32 devices in a mesh: section: 2 (over core), mp: 4 (over y, x), dp: 4 (over z).
Axes of the slice: x: 2, y: 2, z: 4, core: 2. Of those that a mesh axis runs over, the one named last changes fastest.
Arguments:
- token_in: bfloat16 [2, 8192, 1024], P(None, ('dp', 'mp')), may hold values from -6 to 6
- cotangent: bfloat16 [2, 8192, 1024], P(None, ('dp', 'mp')), may hold values from -6 to 6
- w_qkv: bfloat16 [2, 3, 1024, 1024], P('section', None, None, 'mp'), may hold values from -0.1875 to 0.1875
- qv_bias: bfloat16 [2, 2, 1024], P('section', None, 'mp'), may hold values from -1 to 1
- w_attn_out: bfloat16 [2, 1024, 1024], P('section', 'mp'), may hold values from -0.75 to 0.75
- w_ffn_in: bfloat16 [2, 1024, 4096], P('section', None, 'mp'), may hold values from -0.1875 to 0.1875
- ffn_in_bias: bfloat16 [2, 4096], P('section', 'mp'), may hold values from -2.5 to 2.5
- w_ffn_out: bfloat16 [2, 4096, 1024], P('section', 'mp'), may hold values from -0.1875 to 0.1875
- out_biases: float32 [2, 2, 1024], P('section'), may hold values from -2.5 to 2.5
- norm_gains: float32 [2, 2, 1024], P('section'), may hold values from 0.5 to 1.5
- norm_shifts: float32 [2, 2, 1024], P('section'), may hold values from -2.5 to 2.5
Outputs:
- activations: bfloat16 [2, 2, 8192, 1024], P('section', None, ('dp', 'mp'))
- input_grads: bfloat16 [2, 2, 8192, 1024], P('section', None, ('dp', 'mp'))
- grad_w_qkv: float32 [2, 3, 1024, 1024], P('section', None, None, 'mp')
- grad_qv_bias: float32 [2, 2, 1024], P('section', None, 'mp')
- grad_w_attn_out: float32 [2, 1024, 1024], P('section', 'mp')
- grad_w_ffn_in: float32 [2, 1024, 4096], P('section', None, 'mp')
- grad_ffn_in_bias: float32 [2, 4096], P('section', 'mp')
- grad_w_ffn_out: float32 [2, 4096, 1024], P('section', 'mp')
- grad_out_biases: float32 [2, 2, 1024], P('section', None, ('mp', 'dp'))
- grad_norm_gains: float32 [2, 2, 1024], P('section', None, ('mp', 'dp'))
- grad_norm_shifts: float32 [2, 2, 1024], P('section', None, ('mp', 'dp'))
The draws below stay inside these ranges and needn't reach their ends.
All inputs are finite; a program needn't handle non-finite values.
Results may differ from the reference program's by a relative error of at most 0.028.
Values may be sent and summed in bfloat16 or wider, within the bound.
A program may use at most 256 MiB of HBM per device.

```python
import math
import jax
import jax.numpy as jnp
from jax import lax

D = 1024
FF = 4096
HEADS = 16
HEAD_DIM = 64
SEQ = 512
MICRO = 2
ROWS = 8192


def block_scale(rng, dims, split, low, high):
    level, own = 1.0, jax.random.fold_in(rng, 6)
    for dim, shards_of in split:
        heights = jnp.exp(jax.random.uniform(jax.random.fold_in(own, dim), (shards_of,), jnp.float32, low / len(split), high / len(split)))
        level = level * jnp.repeat(heights, dims[dim] // shards_of).reshape([-1 if axis == dim else 1 for axis in range(len(dims))])
    return level


def normal_values(stream_key, extent, spread, reach, split=(), kind=jnp.bfloat16):
    level = block_scale(stream_key, extent, split, -0.22, 0.18) if split else 1.0
    array = jax.random.normal(stream_key, extent, jnp.float32) * spread * level
    return jnp.minimum(jnp.maximum(array, -reach), reach).astype(kind)


def setup_inputs(seed: int = 0) -> dict:
    seeds = jax.random.split(jax.random.key(seed), 12)
    return {
        "token_in": normal_values(seeds[0], (MICRO, ROWS, D), 1.0, 6.0, ((1, 16),)),
        "cotangent": normal_values(seeds[1], (MICRO, ROWS, D), 1.0, 6.0, ((1, 16),)),
        "w_qkv": normal_values(seeds[2], (2, 3, D, D), D ** -0.5, 0.1875, ((0, 2), (3, 4))),
        "qv_bias": normal_values(seeds[3], (2, 2, D), 0.2, 1.0, ((0, 2), (2, 4))),
        "w_attn_out": normal_values(seeds[4], (2, D, D), (D // 16) ** -0.5, 0.75, ((0, 2), (1, 4))),
        "w_ffn_in": normal_values(seeds[5], (2, D, FF), D ** -0.5, 0.1875, ((0, 2), (2, 4))),
        "ffn_in_bias": normal_values(seeds[6], (2, FF), 0.5, 2.5, ((0, 2), (1, 4))),
        "w_ffn_out": normal_values(seeds[7], (2, FF, D), (FF // 4) ** -0.5, 0.1875, ((0, 2), (1, 4))),
        "out_biases": normal_values(seeds[8], (2, 2, D), 0.5, 2.5, ((0, 2),), jnp.float32),
        "norm_gains": jnp.clip(1.0 + 0.1 * jax.random.normal(seeds[9], (2, 2, D), jnp.float32), 0.5, 1.5),
        "norm_shifts": normal_values(seeds[10], (2, 2, D), 0.5, 2.5, ((0, 2),), jnp.float32),
    }


@jax.custom_vjp
def low(v):
    return lax.optimization_barrier(v.astype(jnp.bfloat16)).astype(jnp.float32)

@jax.custom_vjp
def low_back(v):
    return v

def low_keep(v):
    return (low(v), None)

def low_pass(kept, grad):
    return (grad,)

def back_keep(v):
    return (v, None)

def back_low(kept, grad):
    return (low(grad),)
low.defvjp(low_keep, low_pass)
low_back.defvjp(back_keep, back_low)
HIGHEST_PRECISION = lax.Precision.HIGHEST

def norm_rows(values, gain_row, shift_row):
    average = lax.optimization_barrier(jnp.mean(values, axis=-1, keepdims=True))
    centered = values - average
    variance = lax.optimization_barrier(jnp.mean(centered * centered, axis=-1, keepdims=True))
    return centered * lax.rsqrt(variance + 1e-05) * gain_row + shift_row

def layer_forward(section_params, inputs):
    w_qkv, qv_bias, w_attn_out, w_ffn_in, ffn_in_bias, w_ffn_out, out_biases, norm_gains, norm_shifts = section_params
    rows_all = inputs.shape[0]
    page_count = rows_all // SEQ
    scale_factor = 1.0 / math.sqrt(HEAD_DIM)
    token_low = low(inputs)
    bias_full = jnp.stack([qv_bias[0], jnp.zeros_like(qv_bias[0]), qv_bias[1]])
    projected = jnp.einsum('rd,cde->cre', token_low, w_qkv, precision=HIGHEST_PRECISION) + bias_full[:, None, :]
    projected = low(low_back(projected))
    heads_view = projected.reshape(3, page_count, SEQ, HEADS, HEAD_DIM)
    scores = jnp.einsum('pqhe,pkhe->phqk', heads_view[0], heads_view[1], precision=HIGHEST_PRECISION)
    scores = low_back(scores * scale_factor)
    top_score = lax.optimization_barrier(jnp.max(scores, axis=-1, keepdims=True))
    exponent = jnp.exp(scores - top_score)
    weights_soft = exponent / lax.optimization_barrier(jnp.sum(exponent, axis=-1, keepdims=True))
    weights_low = low(weights_soft)
    attended = jnp.einsum('phqk,pkhe->pqhe', weights_low, heads_view[2], precision=HIGHEST_PRECISION)
    attended = low(low_back(attended.reshape(rows_all, D)))
    attn_branch = low_back(jnp.dot(attended, w_attn_out, precision=HIGHEST_PRECISION))
    first = norm_rows(attn_branch + out_biases[0] + inputs, norm_gains[0], norm_shifts[0])
    first_low = low(first)
    pre_act = low_back(jnp.dot(first_low, w_ffn_in, precision=HIGHEST_PRECISION) + ffn_in_bias)
    activated = low(jax.nn.gelu(pre_act, approximate=False))
    ffn_branch = low_back(jnp.dot(activated, w_ffn_out, precision=HIGHEST_PRECISION))
    return norm_rows(ffn_branch + out_biases[1] + first, norm_gains[1], norm_shifts[1])

def two_layers(all_params, inputs, probe_zero):
    first_params = tuple((entry[0] for entry in all_params))
    second_params = tuple((entry[1] for entry in all_params))
    start_rows = low_back(inputs)
    out_one = layer_forward(first_params, start_rows)
    passed = low(low_back(out_one)) + probe_zero
    out_two = layer_forward(second_params, passed)
    return (low(out_two), passed)

def reference(token_in, cotangent, w_qkv, qv_bias, w_attn_out, w_ffn_in, ffn_in_bias, w_ffn_out, out_biases, norm_gains, norm_shifts):
    params = tuple((entry.astype(jnp.float32) for entry in (w_qkv, qv_bias, w_attn_out, w_ffn_in, ffn_in_bias, w_ffn_out, out_biases, norm_gains, norm_shifts)))
    zero_grads = tuple((jnp.zeros(entry.shape, jnp.float32) for entry in params))

    def micro_step(carry, pair):
        token_rows, cot_rows = pair
        final_out, back_fn, passed = jax.vjp(two_layers, params, token_rows.astype(jnp.float32), jnp.zeros(token_rows.shape, jnp.float32), has_aux=True)
        grad_params, grad_rows, grad_probe = back_fn(cot_rows.astype(jnp.float32))
        carry = tuple((total + extra for total, extra in zip(carry, grad_params)))
        return (carry, (passed, final_out, grad_rows, grad_probe))
    grads, outputs = lax.scan(micro_step, zero_grads, (token_in, cotangent))
    passed, final_out, grad_rows, grad_probe = outputs
    activations = jnp.stack([passed, final_out]).astype(jnp.bfloat16)
    input_grads = jnp.stack([grad_rows, grad_probe]).astype(jnp.bfloat16)
    return (activations, input_grads, grads[0], grads[1], grads[2], grads[3], grads[4], grads[5], grads[6], grads[7], grads[8])
```

```python
from functools import partial
import math

import jax
import jax.numpy as jnp
from jax import lax
from jax.sharding import PartitionSpec as P

HEAD_DIM = 64
SEQ = 512


def from_behind(value, axis, by):
    devices = lax.axis_size(axis)
    pairs = [(i, i + by) for i in range(devices) if 0 <= i + by < devices]
    return lax.ppermute(value, axis, pairs)


def norm_rows(values, gain_row, shift_row):
    average = jnp.mean(values, axis=-1, keepdims=True)
    centered = values - average
    variance = jnp.mean(centered * centered, axis=-1, keepdims=True)
    return centered * lax.rsqrt(variance + 1e-05) * gain_row + shift_row


def exact_gelu(values):
    return jax.nn.gelu(values, approximate=False)


def layer_forward(params, token_rows):
    (
        w_qkv,
        qv_bias,
        w_attn_out,
        w_ffn_in,
        ffn_in_bias,
        w_ffn_out,
        out_biases,
        norm_gains,
        norm_shifts,
    ) = params
    gathered = lax.all_gather(token_rows, "mp", axis=0, tiled=True)
    rows_all = gathered.shape[0]
    local_width = w_qkv.shape[2]
    local_heads = local_width // HEAD_DIM
    page_count = rows_all // SEQ
    scale_factor = 1.0 / math.sqrt(HEAD_DIM)
    bias_full = jnp.stack([qv_bias[0], jnp.zeros_like(qv_bias[0]), qv_bias[1]]).astype(jnp.float32)
    projected = (
        jnp.einsum("rd,cde->cre", gathered, w_qkv, preferred_element_type=jnp.float32)
        + bias_full[:, None, :]
    )
    heads_view = projected.astype(jnp.bfloat16).reshape(3, page_count, SEQ, local_heads, HEAD_DIM)
    scores = (
        jnp.einsum(
            "pqhe,pkhe->phqk", heads_view[0], heads_view[1], preferred_element_type=jnp.float32
        )
        * scale_factor
    )
    top_score = jnp.max(scores, axis=-1, keepdims=True)
    exponent = jnp.exp(scores - top_score)
    weights_soft = exponent / jnp.sum(exponent, axis=-1, keepdims=True)
    weights_low = weights_soft.astype(jnp.bfloat16)
    attended = jnp.einsum(
        "phqk,pkhe->pqhe", weights_low, heads_view[2], preferred_element_type=jnp.float32
    )
    attended = attended.reshape(rows_all, local_width).astype(jnp.bfloat16)
    attn_part = jnp.dot(attended, w_attn_out, preferred_element_type=jnp.float32)
    attn_rows = lax.psum_scatter(
        attn_part.astype(jnp.bfloat16), "mp", scatter_dimension=0, tiled=True
    ).astype(jnp.float32)
    residual_one = attn_rows + out_biases[0] + token_rows.astype(jnp.float32)
    first = norm_rows(residual_one, norm_gains[0], norm_shifts[0])
    first_all = lax.all_gather(first.astype(jnp.bfloat16), "mp", axis=0, tiled=True)
    pre_act = jnp.dot(first_all, w_ffn_in, preferred_element_type=jnp.float32) + ffn_in_bias.astype(
        jnp.float32
    )
    activated = exact_gelu(pre_act).astype(jnp.bfloat16)
    ffn_part = jnp.dot(activated, w_ffn_out, preferred_element_type=jnp.float32)
    ffn_rows = lax.psum_scatter(
        ffn_part.astype(jnp.bfloat16), "mp", scatter_dimension=0, tiled=True
    ).astype(jnp.float32)
    residual_two = ffn_rows + out_biases[1] + first
    result = norm_rows(residual_two, norm_gains[1], norm_shifts[1])
    kept_values = (
        gathered,
        heads_view,
        weights_soft,
        attended,
        residual_one,
        first_all,
        pre_act,
        activated,
        residual_two,
    )
    return (result, kept_values)


def layer_backward(params, kept_values, grad_out):
    (
        w_qkv,
        qv_bias,
        w_attn_out,
        w_ffn_in,
        ffn_in_bias,
        w_ffn_out,
        out_biases,
        norm_gains,
        norm_shifts,
    ) = params
    (
        gathered,
        heads_view,
        weights_soft,
        attended,
        residual_one,
        first_all,
        pre_act,
        activated,
        residual_two,
    ) = kept_values
    rows_all = gathered.shape[0]
    local_width = w_qkv.shape[2]
    local_heads = local_width // HEAD_DIM
    page_count = rows_all // SEQ
    scale_factor = 1.0 / math.sqrt(HEAD_DIM)
    unused_two, norm_two_back = jax.vjp(norm_rows, residual_two, norm_gains[1], norm_shifts[1])
    grad_res_two, grad_gain_two, grad_shift_two = norm_two_back(grad_out)
    grad_bias_two = jnp.sum(grad_res_two, axis=0)
    ffn_grad_all = lax.all_gather(grad_res_two.astype(jnp.bfloat16), "mp", axis=0, tiled=True)
    grad_w_ffn_out = jnp.einsum(
        "rf,rd->fd", activated, ffn_grad_all, preferred_element_type=jnp.float32
    )
    grad_act = jnp.einsum("rd,fd->rf", ffn_grad_all, w_ffn_out, preferred_element_type=jnp.float32)
    unused_gelu, gelu_back = jax.vjp(exact_gelu, pre_act)
    grad_pre = gelu_back(grad_act)[0].astype(jnp.bfloat16)
    grad_ffn_in_bias = jnp.sum(grad_pre.astype(jnp.float32), axis=0)
    grad_w_ffn_in = jnp.einsum("rd,rf->df", first_all, grad_pre, preferred_element_type=jnp.float32)
    first_part = jnp.einsum("rf,df->rd", grad_pre, w_ffn_in, preferred_element_type=jnp.float32)
    first_grad_rows = lax.psum_scatter(
        first_part.astype(jnp.bfloat16), "mp", scatter_dimension=0, tiled=True
    ).astype(jnp.float32)
    grad_first = first_grad_rows + grad_res_two
    unused_one, norm_one_back = jax.vjp(norm_rows, residual_one, norm_gains[0], norm_shifts[0])
    grad_res_one, grad_gain_one, grad_shift_one = norm_one_back(grad_first)
    grad_bias_one = jnp.sum(grad_res_one, axis=0)
    attn_grad_all = lax.all_gather(grad_res_one.astype(jnp.bfloat16), "mp", axis=0, tiled=True)
    grad_w_attn_out = jnp.einsum(
        "rk,rd->kd", attended, attn_grad_all, preferred_element_type=jnp.float32
    )
    grad_attended = jnp.einsum(
        "rd,kd->rk", attn_grad_all, w_attn_out, preferred_element_type=jnp.float32
    )
    grad_attended = grad_attended.astype(jnp.bfloat16).reshape(
        page_count, SEQ, local_heads, HEAD_DIM
    )
    weights_low = weights_soft.astype(jnp.bfloat16)
    grad_weights = jnp.einsum(
        "pqhe,pkhe->phqk", grad_attended, heads_view[2], preferred_element_type=jnp.float32
    )
    grad_values = jnp.einsum(
        "phqk,pqhe->pkhe", weights_low, grad_attended, preferred_element_type=jnp.float32
    )
    inner_total = jnp.sum(weights_soft * grad_weights, axis=-1, keepdims=True)
    grad_scores = (weights_soft * (grad_weights - inner_total)).astype(jnp.bfloat16)
    grad_queries = (
        jnp.einsum(
            "phqk,pkhe->pqhe", grad_scores, heads_view[1], preferred_element_type=jnp.float32
        )
        * scale_factor
    )
    grad_keys = (
        jnp.einsum(
            "phqk,pqhe->pkhe", grad_scores, heads_view[0], preferred_element_type=jnp.float32
        )
        * scale_factor
    )
    grad_proj = (
        jnp.stack([grad_queries, grad_keys, grad_values])
        .reshape(3, rows_all, local_width)
        .astype(jnp.bfloat16)
    )
    proj_sums = jnp.sum(grad_proj.astype(jnp.float32), axis=1)
    grad_qv_bias = jnp.stack([proj_sums[0], proj_sums[2]])
    grad_w_qkv = jnp.einsum("rd,cre->cde", gathered, grad_proj, preferred_element_type=jnp.float32)
    input_part = jnp.einsum("cre,cde->rd", grad_proj, w_qkv, preferred_element_type=jnp.float32)
    input_grad_rows = lax.psum_scatter(
        input_part.astype(jnp.bfloat16), "mp", scatter_dimension=0, tiled=True
    ).astype(jnp.float32)
    grad_in = input_grad_rows + grad_res_one
    matrix_grads = (
        grad_w_qkv,
        grad_qv_bias,
        grad_w_attn_out,
        grad_w_ffn_in,
        grad_ffn_in_bias,
        grad_w_ffn_out,
    )
    vector_grads = (
        jnp.stack([grad_bias_one, grad_bias_two]),
        jnp.stack([grad_gain_one, grad_gain_two]),
        jnp.stack([grad_shift_one, grad_shift_two]),
    )
    return (grad_in, matrix_grads, vector_grads)


def pipelined(
    token_in,
    cotangent,
    w_qkv,
    qv_bias,
    w_attn_out,
    w_ffn_in,
    ffn_in_bias,
    w_ffn_out,
    out_biases,
    norm_gains,
    norm_shifts,
):
    params = (
        w_qkv[0],
        qv_bias[0],
        w_attn_out[0],
        w_ffn_in[0],
        ffn_in_bias[0],
        w_ffn_out[0],
        out_biases[0],
        norm_gains[0],
        norm_shifts[0],
    )
    micro_count = token_in.shape[0]
    section_index = lax.axis_index("section")
    is_first = section_index == 0
    zero_rows = jnp.zeros(token_in.shape[1:], jnp.bfloat16)
    run_forward = partial(layer_forward, params)
    run_backward = partial(layer_backward, params)

    def forward_step(step_index, carry):
        received, saved, stored = carry
        own_micro = step_index - section_index
        is_valid = (own_micro >= 0) & (own_micro < micro_count)
        slot_index = jnp.clip(own_micro, 0, micro_count - 1)
        first_rows = lax.dynamic_index_in_dim(
            token_in, jnp.minimum(step_index, micro_count - 1).astype(jnp.int32), 0, keepdims=False
        )
        layer_in = jnp.where(is_first, first_rows, received)
        result, unused_kept = run_forward(layer_in)
        result_low = result.astype(jnp.bfloat16)
        old_saved = lax.dynamic_index_in_dim(saved, slot_index, 0, keepdims=False)
        saved = lax.dynamic_update_index_in_dim(
            saved, jnp.where(is_valid, layer_in, old_saved), slot_index, 0
        )
        old_stored = lax.dynamic_index_in_dim(stored, slot_index, 0, keepdims=False)
        stored = lax.dynamic_update_index_in_dim(
            stored, jnp.where(is_valid, result_low, old_stored), slot_index, 0
        )
        received = from_behind(result_low, "section", 1)
        return (received, saved, stored)

    start_carry = (zero_rows, jnp.zeros_like(token_in), jnp.zeros_like(token_in))
    unused_received, saved, stored = lax.fori_loop(0, micro_count + 1, forward_step, start_carry)
    matrix_zero = tuple((jnp.zeros(entry.shape, jnp.float32) for entry in params[:6]))
    vector_zero = (
        jnp.zeros(out_biases.shape[1:], jnp.float32),
        jnp.zeros(norm_gains.shape[1:], jnp.float32),
        jnp.zeros(norm_shifts.shape[1:], jnp.float32),
    )

    def backward_step(step_index, carry):
        received_grad, grad_store, matrix_sums, vector_sums = carry
        own_micro = step_index - (1 - section_index)
        is_valid = (own_micro >= 0) & (own_micro < micro_count)
        slot_index = jnp.clip(own_micro, 0, micro_count - 1)
        layer_in = lax.dynamic_index_in_dim(saved, slot_index, 0, keepdims=False)
        from_last = lax.dynamic_index_in_dim(cotangent, slot_index, 0, keepdims=False)
        grad_out = jnp.where(is_first, received_grad, from_last).astype(jnp.float32)
        unused_result, kept_values = run_forward(layer_in)
        grad_in, matrix_grads, vector_grads = run_backward(kept_values, grad_out)
        matrix_grads = tuple((jnp.where(is_valid, entry, 0.0) for entry in matrix_grads))
        vector_grads = tuple((jnp.where(is_valid, entry, 0.0) for entry in vector_grads))
        grad_low = grad_in.astype(jnp.bfloat16)
        old_piece = lax.dynamic_index_in_dim(grad_store, slot_index, 0, keepdims=False)
        grad_store = lax.dynamic_update_index_in_dim(
            grad_store, jnp.where(is_valid, grad_low, old_piece), slot_index, 0
        )
        grad_one, grad_two, grad_three, grad_four, grad_five, grad_six = matrix_grads
        matrix_grads = (
            lax.psum(grad_one.astype(jnp.bfloat16), "dp").astype(jnp.float32),
            lax.psum(grad_two.astype(jnp.bfloat16), "dp").astype(jnp.float32),
            lax.psum(grad_three.astype(jnp.bfloat16), "dp").astype(jnp.float32),
            lax.psum(grad_four.astype(jnp.bfloat16), "dp").astype(jnp.float32),
            lax.psum(grad_five.astype(jnp.bfloat16), "dp").astype(jnp.float32),
            lax.psum(grad_six.astype(jnp.bfloat16), "dp").astype(jnp.float32),
        )
        matrix_sums = tuple((total + extra for total, extra in zip(matrix_sums, matrix_grads)))
        vector_sums = tuple((total + extra for total, extra in zip(vector_sums, vector_grads)))
        received_grad = from_behind(grad_low, "section", -1)
        return (received_grad, grad_store, matrix_sums, vector_sums)

    back_carry = (zero_rows, jnp.zeros_like(token_in), matrix_zero, vector_zero)
    unused_grad, grad_store, matrix_sums, vector_sums = lax.fori_loop(
        0, micro_count + 1, backward_step, back_carry
    )
    bias_total, gain_total, shift_total = vector_sums
    bias_part, gain_part, shift_part = (
        lax.psum_scatter(bias_total, ("mp", "dp"), scatter_dimension=1, tiled=True),
        lax.psum_scatter(gain_total, ("mp", "dp"), scatter_dimension=1, tiled=True),
        lax.psum_scatter(shift_total, ("mp", "dp"), scatter_dimension=1, tiled=True),
    )
    return (
        stored[None],
        grad_store[None],
        matrix_sums[0][None],
        matrix_sums[1][None],
        matrix_sums[2][None],
        matrix_sums[3][None],
        matrix_sums[4][None],
        matrix_sums[5][None],
        bias_part[None],
        gain_part[None],
        shift_part[None],
    )


def swapped(value, axis, bit):
    return lax.ppermute(value, axis, [(i, i ^ bit) for i in range(lax.axis_size(axis))])


def swap_x(value):
    return swapped(value, "mp", 1)


def swap_y(value):
    return swapped(value, "mp", 2)


def swap_core(value):
    return swapped(value, "section", 1)


def gather_blocks(own):
    half = own.shape[0] // 2
    by_x = swap_x(own)
    by_y = swap_y(own)
    far_low = swap_x(by_y[:half])
    far_high = swap_y(by_x[half:])
    return [own, by_x, by_y, jnp.concatenate([far_low, far_high], axis=0)]


def gather_layer(own):
    mine = gather_blocks(own)
    other = [swap_core(block) for block in mine]
    return [[a, b] for a, b in zip(mine, other)]


def sum_dp(value):
    devices = lax.axis_size("dp")
    if devices != 4:
        return lax.psum(value.astype(jnp.float32), "dp").astype(jnp.bfloat16)
    place = lax.axis_index("dp")
    is_end = (place == 0) | (place == devices - 1)
    inner = lax.ppermute(value, "dp", [(0, 1), (3, 2)])
    pair = (value.astype(jnp.float32) + inner.astype(jnp.float32)).astype(jnp.bfloat16)
    across = lax.ppermute(pair, "dp", [(1, 2), (2, 1)])
    total = (pair.astype(jnp.float32) + across.astype(jnp.float32)).astype(jnp.bfloat16)
    outer = lax.ppermute(total, "dp", [(1, 0), (2, 3)])
    return jnp.where(is_end, outer, total)


def low(value):
    return value.astype(jnp.bfloat16)


def high(value):
    return value.astype(jnp.float32)


def reduce_blocks(mine, other):
    blocks = [a + high(swap_core(low(b))) for a, b in zip(mine, other)]
    half = blocks[0].shape[0] // 2
    tops = [block[:half] for block in blocks]
    ends = [block[half:] for block in blocks]
    top_two = low(tops[2] + high(swap_x(low(tops[3]))))
    end_one = low(ends[1] + high(swap_y(low(ends[3]))))
    top = tops[0] + high(swap_x(low(tops[1]))) + high(swap_y(top_two))
    end = ends[0] + high(swap_x(end_one)) + high(swap_y(low(ends[2])))
    return sum_dp(jnp.concatenate([low(top), low(end)], axis=0))


def dot(a, b):
    return jnp.dot(a, b, preferred_element_type=jnp.float32)


def dot_tn(a, b):
    return lax.dot_general(a, b, (((0,), (0,)), ((), ())), preferred_element_type=jnp.float32)


def dot_nt(a, b):
    return lax.dot_general(a, b, (((1,), (1,)), ((), ())), preferred_element_type=jnp.float32)


def local_forward(weights, vectors, rows):
    w_qkv, w_attn_out, w_ffn_in, w_ffn_out = weights
    qv_bias, ffn_bias, out_biases, norm_gains, norm_shifts = vectors
    count, width = rows.shape
    pages = count // SEQ
    heads = width // HEAD_DIM
    scale_factor = 1.0 / math.sqrt(HEAD_DIM)
    heads_view = []
    for c in range(3):
        projected = dot(rows, w_qkv[c])
        if c != 1:
            projected = projected + qv_bias[c // 2]
        heads_view.append(low(projected).reshape(pages, SEQ, heads, HEAD_DIM))
    scores = (
        jnp.einsum("pqhe,pkhe->phqk", heads_view[0], heads_view[1], preferred_element_type=jnp.float32)
        * scale_factor
    )
    top_score = jnp.max(scores, axis=-1, keepdims=True)
    exponent = jnp.exp(scores - top_score)
    weights_soft = exponent / jnp.sum(exponent, axis=-1, keepdims=True)
    weights_low = low(weights_soft)
    attended = jnp.einsum("phqk,pkhe->pqhe", weights_low, heads_view[2], preferred_element_type=jnp.float32)
    attended = low(attended.reshape(count, width))
    residual_one = dot(attended, w_attn_out) + out_biases[0] + high(rows)
    first = norm_rows(residual_one, norm_gains[0], norm_shifts[0])
    first_low = low(first)
    ffn_sum = out_biases[1] + first
    pre_acts, activated = [], []
    for r in range(4):
        for h in range(2):
            pre_act = dot(first_low, w_ffn_in[r][h]) + ffn_bias[r][h]
            act = low(exact_gelu(pre_act))
            ffn_sum = ffn_sum + dot(act, w_ffn_out[r][h])
            pre_acts.append(pre_act)
            activated.append(act)
    result = norm_rows(ffn_sum, norm_gains[1], norm_shifts[1])
    kept = (rows, heads_view, weights_soft, attended, residual_one, first_low, pre_acts, activated, ffn_sum)
    return low(result), kept


def local_backward(weights, vectors, kept, grad_out):
    w_qkv, w_attn_out, w_ffn_in, w_ffn_out = weights
    qv_bias, ffn_bias, out_biases, norm_gains, norm_shifts = vectors
    rows, heads_view, weights_soft, attended, residual_one, first_low, pre_acts, activated, residual_two = kept
    count, width = rows.shape
    pages = count // SEQ
    heads = width // HEAD_DIM
    scale_factor = 1.0 / math.sqrt(HEAD_DIM)
    unused_two, norm_two_back = jax.vjp(norm_rows, residual_two, norm_gains[1], norm_shifts[1])
    grad_res_two, grad_gain_two, grad_shift_two = norm_two_back(high(grad_out))
    grad_bias_two = jnp.sum(grad_res_two, axis=0)
    ffn_grad = low(grad_res_two)
    grads_out = [[dot_tn(activated[2 * r + h], ffn_grad) for r in range(4)] for h in range(2)]
    sum_ffn_out = reduce_blocks(*grads_out)
    grad_first = grad_res_two
    grads_in, ffn_bias_grads = [[], []], []
    for r in range(4):
        for h in range(2):
            grad_act = dot_nt(ffn_grad, w_ffn_out[r][h])
            unused_gelu, gelu_back = jax.vjp(exact_gelu, pre_acts[2 * r + h])
            grad_pre = low(gelu_back(grad_act)[0])
            ffn_bias_grads.append(jnp.sum(high(grad_pre), axis=0))
            grads_in[h].append(dot_tn(first_low, grad_pre))
            grad_first = grad_first + dot_nt(grad_pre, w_ffn_in[r][h])
    sum_ffn_in = reduce_blocks(*grads_in)
    unused_one, norm_one_back = jax.vjp(norm_rows, residual_one, norm_gains[0], norm_shifts[0])
    grad_res_one, grad_gain_one, grad_shift_one = norm_one_back(grad_first)
    grad_bias_one = jnp.sum(grad_res_one, axis=0)
    attn_grad = low(grad_res_one)
    grad_w_out = dot_tn(attended, attn_grad).reshape(4, 2, width // 8, width)
    sum_attn_out = reduce_blocks(*[[grad_w_out[r, h] for r in range(4)] for h in range(2)])
    grad_attended = low(dot_nt(attn_grad, w_attn_out)).reshape(pages, SEQ, heads, HEAD_DIM)
    weights_low = low(weights_soft)
    grad_weights = jnp.einsum("pqhe,pkhe->phqk", grad_attended, heads_view[2], preferred_element_type=jnp.float32)
    grad_values = jnp.einsum("phqk,pqhe->pkhe", weights_low, grad_attended, preferred_element_type=jnp.float32)
    inner_total = jnp.sum(weights_soft * grad_weights, axis=-1, keepdims=True)
    grad_scores = low(weights_soft * (grad_weights - inner_total))
    grad_queries = (
        jnp.einsum("phqk,pkhe->pqhe", grad_scores, heads_view[1], preferred_element_type=jnp.float32)
        * scale_factor
    )
    grad_keys = (
        jnp.einsum("phqk,pqhe->pkhe", grad_scores, heads_view[0], preferred_element_type=jnp.float32)
        * scale_factor
    )
    grad_proj = [low(g).reshape(count, width) for g in (grad_queries, grad_keys, grad_values)]
    sums_qkv = []
    for c in range(3):
        whole = dot_tn(rows, grad_proj[c])
        parts = [whole[:, b * (width // 8) : (b + 1) * (width // 8)] for b in range(8)]
        sums_qkv.append(reduce_blocks(parts[0::2], parts[1::2]))
    grad_in = grad_res_one
    for c in range(3):
        grad_in = grad_in + dot_nt(grad_proj[c], w_qkv[c])
    qv_sums = jnp.stack([jnp.sum(high(grad_proj[0]), axis=0), jnp.sum(high(grad_proj[2]), axis=0)])
    vector_grads = (
        qv_sums.reshape(2, 8, width // 8),
        jnp.stack(ffn_bias_grads),
        jnp.stack([grad_bias_one, grad_bias_two]),
        jnp.stack([grad_gain_one, grad_gain_two]),
        jnp.stack([grad_shift_one, grad_shift_two]),
    )
    return low(grad_in), (sums_qkv, sum_attn_out, sum_ffn_in, sum_ffn_out), vector_grads


def by_page(
    token_in,
    cotangent,
    w_qkv,
    qv_bias,
    w_attn_out,
    w_ffn_in,
    ffn_in_bias,
    w_ffn_out,
    out_biases,
    norm_gains,
    norm_shifts,
):
    core = lax.axis_index("section")
    place = lax.axis_index("mp")
    is_first = core == 0
    width = token_in.shape[2]
    own_rows = lax.dynamic_index_in_dim(token_in, core, 0, keepdims=False)
    own_cot = lax.dynamic_index_in_dim(cotangent, core, 0, keepdims=False)

    def by_layer(own, received):
        return [jnp.where(is_first, own, received), jnp.where(is_first, received, own)]

    def halves(shard, axis):
        size = shard.shape[axis] // 2
        return (
            lax.dynamic_slice_in_dim(shard, core * size, size, axis),
            lax.dynamic_slice_in_dim(shard, (1 - core) * size, size, axis),
        )

    def own_halves(shard, axis):
        keep, give = halves(shard, axis)
        return by_layer(keep, swap_core(give))

    eighth = w_qkv.shape[3] // 2
    qkv_keep, qkv_give = halves(w_qkv[0], 2)
    qkv_own = by_layer(qkv_keep.reshape(-1, eighth), swap_core(qkv_give.reshape(-1, eighth)))
    attn_own = own_halves(w_attn_out[0], 0)
    ffn_in_own = own_halves(w_ffn_in[0], 1)
    ffn_out_own = own_halves(w_ffn_out[0], 0)

    ffn_half = ffn_in_bias.shape[1] // 2
    small = jnp.concatenate(
        [
            qv_bias[0].reshape(2, 2, eighth).transpose(1, 0, 2).reshape(2, 2 * eighth),
            ffn_in_bias[0].reshape(2, ffn_half),
        ],
        axis=1,
    )
    small = jnp.stack(by_layer(small, swap_core(small)))
    small = jnp.stack([small, swap_x(small), swap_y(small), swapped(small, "mp", 3)])
    small = high(jnp.where(is_first, small, small[:, :, ::-1]))
    norms = jnp.concatenate([out_biases[0], norm_gains[0], norm_shifts[0]], axis=0)
    norms = by_layer(norms, swap_core(norms))

    layers = []
    for layer in range(2):
        qkv = gather_layer(qkv_own[layer])
        blocks = [block for pair in qkv for block in pair]
        full_qkv = [
            jnp.concatenate([block[c * width : (c + 1) * width] for block in blocks], axis=1) for c in range(3)
        ]
        attn = gather_layer(attn_own[layer])
        full_attn = jnp.concatenate([block for pair in attn for block in pair], axis=0)
        ffn_in = gather_layer(ffn_in_own[layer])
        ffn_out = gather_layer(ffn_out_own[layer])
        own_small = small[:, layer]
        qv = own_small[:, :, : 2 * eighth].reshape(8, 2, eighth).transpose(1, 0, 2).reshape(2, width)
        ffn_bias = own_small[:, :, 2 * eighth :]
        layer_norms = norms[layer]
        layers.append(
            (
                (full_qkv, full_attn, ffn_in, ffn_out),
                (qv, ffn_bias, layer_norms[0:2], layer_norms[2:4], layer_norms[4:6]),
            )
        )

    out_zero, kept_zero = local_forward(*layers[0], own_rows)
    out_one, kept_one = local_forward(*layers[1], out_zero)
    grad_one, sums_one, vectors_one = local_backward(*layers[1], kept_one, own_cot)
    grad_zero, sums_zero, vectors_zero = local_backward(*layers[0], kept_zero, grad_one)

    def trade(first, second):
        own = jnp.where(is_first, first, second)
        received = swap_core(jnp.where(is_first, second, first))
        return jnp.where(is_first, jnp.stack([own, received]), jnp.stack([received, own]))

    activations = trade(out_zero, out_one)
    input_grads = trade(grad_zero, grad_one)

    def joined(zero, one, axis):
        got_one = lax.ppermute(one, "section", [(0, 1)])
        got_zero = lax.ppermute(zero, "section", [(1, 0)])
        low_part = jnp.where(is_first, zero, got_one)
        high_part = jnp.where(is_first, got_zero, one)
        return high(jnp.concatenate([low_part, high_part], axis=axis))

    grad_qkv = jnp.stack([joined(a, b, 1) for a, b in zip(sums_zero[0], sums_one[0])])
    grad_attn = joined(sums_zero[1], sums_one[1], 0)
    grad_ffn_in = joined(sums_zero[2], sums_one[2], 1)
    grad_ffn_out = joined(sums_zero[3], sums_one[3], 0)

    order = jnp.stack([2 * (place ^ (j // 2)) + (core ^ (j % 2)) for j in range(8)])

    def packed(vectors):
        qv, ffn, biases, gains, shifts = vectors
        qv = jnp.take(qv, order, axis=1)
        ffn = jnp.take(ffn, order, axis=0)
        return jnp.concatenate([v.reshape(-1) for v in (qv, ffn, biases, gains, shifts)])

    totals = jnp.stack([packed(vectors_zero), packed(vectors_one)]).reshape(2, -1, 128)
    totals = lax.psum(totals, ("section", "mp", "dp")).reshape(2, -1)
    totals = lax.dynamic_index_in_dim(totals, core, 0, keepdims=False)
    qv_width, ffn_width = 2 * eighth, 2 * ffn_half
    qv_total = totals[: 2 * width].reshape(2, width)
    ffn_total = totals[2 * width : 2 * width + 4 * ffn_width]
    rest = totals[2 * width + 4 * ffn_width :].reshape(3, 2, width)
    piece = width // (lax.axis_size("mp") * lax.axis_size("dp"))
    start = (place * lax.axis_size("dp") + lax.axis_index("dp")) * piece
    rest = lax.dynamic_slice_in_dim(rest, start, piece, 2)
    return (
        activations[None],
        input_grads[None],
        grad_qkv[None],
        lax.dynamic_slice_in_dim(qv_total, place * qv_width, qv_width, 1)[None],
        grad_attn[None],
        grad_ffn_in[None],
        lax.dynamic_slice_in_dim(ffn_total, place * ffn_width, ffn_width, 0)[None],
        grad_ffn_out[None],
        rest[0][None],
        rest[1][None],
        rest[2][None],
    )


def on_device(*args):
    token_in = args[0]
    fits = (
        lax.axis_size("section") == 2
        and lax.axis_size("mp") == 4
        and token_in.shape[0] == 2
        and token_in.shape[1] % SEQ == 0
    )
    return by_page(*args) if fits else pipelined(*args)


def solution(mesh):
    return jax.shard_map(
        on_device,
        mesh=mesh,
        in_specs=(
            P(None, ("dp", "mp"), None),
            P(None, ("dp", "mp"), None),
            P("section", None, None, "mp"),
            P("section", None, "mp"),
            P("section", "mp", None),
            P("section", None, "mp"),
            P("section", "mp"),
            P("section", "mp", None),
            P("section", None, None),
            P("section", None, None),
            P("section", None, None),
        ),
        out_specs=(
            P("section", None, ("dp", "mp"), None),
            P("section", None, ("dp", "mp"), None),
            P("section", None, None, "mp"),
            P("section", None, "mp"),
            P("section", "mp", None),
            P("section", None, "mp"),
            P("section", "mp"),
            P("section", "mp", None),
            P("section", None, ("mp", "dp")),
            P("section", None, ("mp", "dp")),
            P("section", None, ("mp", "dp")),
        ),
        check_vma=False,
    )
```

```python
import functools
from functools import partial
import math

import jax
import jax.numpy as jnp
from jax import lax
from jax.experimental import pallas as pl
from jax.experimental.pallas import tpu as pltpu
from jax.sharding import PartitionSpec as P

HEAD_DIM = 64
SEQ = 512


def from_behind(value, axis, by):
    devices = lax.axis_size(axis)
    pairs = [(i, i + by) for i in range(devices) if 0 <= i + by < devices]
    return lax.ppermute(value, axis, pairs)


def norm_rows(values, gain_row, shift_row):
    average = jnp.mean(values, axis=-1, keepdims=True)
    centered = values - average
    variance = jnp.mean(centered * centered, axis=-1, keepdims=True)
    return centered * lax.rsqrt(variance + 1e-05) * gain_row + shift_row


def exact_gelu(values):
    return jax.nn.gelu(values, approximate=False)


def layer_forward(params, token_rows):
    (
        w_qkv,
        qv_bias,
        w_attn_out,
        w_ffn_in,
        ffn_in_bias,
        w_ffn_out,
        out_biases,
        norm_gains,
        norm_shifts,
    ) = params
    gathered = lax.all_gather(token_rows, "mp", axis=0, tiled=True)
    rows_all = gathered.shape[0]
    local_width = w_qkv.shape[2]
    local_heads = local_width // HEAD_DIM
    page_count = rows_all // SEQ
    scale_factor = 1.0 / math.sqrt(HEAD_DIM)
    bias_full = jnp.stack([qv_bias[0], jnp.zeros_like(qv_bias[0]), qv_bias[1]]).astype(jnp.float32)
    projected = (
        jnp.einsum("rd,cde->cre", gathered, w_qkv, preferred_element_type=jnp.float32)
        + bias_full[:, None, :]
    )
    heads_view = projected.astype(jnp.bfloat16).reshape(3, page_count, SEQ, local_heads, HEAD_DIM)
    scores = (
        jnp.einsum(
            "pqhe,pkhe->phqk", heads_view[0], heads_view[1], preferred_element_type=jnp.float32
        )
        * scale_factor
    )
    top_score = jnp.max(scores, axis=-1, keepdims=True)
    exponent = jnp.exp(scores - top_score)
    weights_soft = exponent / jnp.sum(exponent, axis=-1, keepdims=True)
    weights_low = weights_soft.astype(jnp.bfloat16)
    attended = jnp.einsum(
        "phqk,pkhe->pqhe", weights_low, heads_view[2], preferred_element_type=jnp.float32
    )
    attended = attended.reshape(rows_all, local_width).astype(jnp.bfloat16)
    attn_part = jnp.dot(attended, w_attn_out, preferred_element_type=jnp.float32)
    attn_rows = lax.psum_scatter(
        attn_part.astype(jnp.bfloat16), "mp", scatter_dimension=0, tiled=True
    ).astype(jnp.float32)
    residual_one = attn_rows + out_biases[0] + token_rows.astype(jnp.float32)
    first = norm_rows(residual_one, norm_gains[0], norm_shifts[0])
    first_all = lax.all_gather(first.astype(jnp.bfloat16), "mp", axis=0, tiled=True)
    pre_act = jnp.dot(first_all, w_ffn_in, preferred_element_type=jnp.float32) + ffn_in_bias.astype(
        jnp.float32
    )
    activated = exact_gelu(pre_act).astype(jnp.bfloat16)
    ffn_part = jnp.dot(activated, w_ffn_out, preferred_element_type=jnp.float32)
    ffn_rows = lax.psum_scatter(
        ffn_part.astype(jnp.bfloat16), "mp", scatter_dimension=0, tiled=True
    ).astype(jnp.float32)
    residual_two = ffn_rows + out_biases[1] + first
    result = norm_rows(residual_two, norm_gains[1], norm_shifts[1])
    kept_values = (
        gathered,
        heads_view,
        weights_soft,
        attended,
        residual_one,
        first_all,
        pre_act,
        activated,
        residual_two,
    )
    return (result, kept_values)


def layer_backward(params, kept_values, grad_out):
    (
        w_qkv,
        qv_bias,
        w_attn_out,
        w_ffn_in,
        ffn_in_bias,
        w_ffn_out,
        out_biases,
        norm_gains,
        norm_shifts,
    ) = params
    (
        gathered,
        heads_view,
        weights_soft,
        attended,
        residual_one,
        first_all,
        pre_act,
        activated,
        residual_two,
    ) = kept_values
    rows_all = gathered.shape[0]
    local_width = w_qkv.shape[2]
    local_heads = local_width // HEAD_DIM
    page_count = rows_all // SEQ
    scale_factor = 1.0 / math.sqrt(HEAD_DIM)
    unused_two, norm_two_back = jax.vjp(norm_rows, residual_two, norm_gains[1], norm_shifts[1])
    grad_res_two, grad_gain_two, grad_shift_two = norm_two_back(grad_out)
    grad_bias_two = jnp.sum(grad_res_two, axis=0)
    ffn_grad_all = lax.all_gather(grad_res_two.astype(jnp.bfloat16), "mp", axis=0, tiled=True)
    grad_w_ffn_out = jnp.einsum(
        "rf,rd->fd", activated, ffn_grad_all, preferred_element_type=jnp.float32
    )
    grad_act = jnp.einsum("rd,fd->rf", ffn_grad_all, w_ffn_out, preferred_element_type=jnp.float32)
    unused_gelu, gelu_back = jax.vjp(exact_gelu, pre_act)
    grad_pre = gelu_back(grad_act)[0].astype(jnp.bfloat16)
    grad_ffn_in_bias = jnp.sum(grad_pre.astype(jnp.float32), axis=0)
    grad_w_ffn_in = jnp.einsum("rd,rf->df", first_all, grad_pre, preferred_element_type=jnp.float32)
    first_part = jnp.einsum("rf,df->rd", grad_pre, w_ffn_in, preferred_element_type=jnp.float32)
    first_grad_rows = lax.psum_scatter(
        first_part.astype(jnp.bfloat16), "mp", scatter_dimension=0, tiled=True
    ).astype(jnp.float32)
    grad_first = first_grad_rows + grad_res_two
    unused_one, norm_one_back = jax.vjp(norm_rows, residual_one, norm_gains[0], norm_shifts[0])
    grad_res_one, grad_gain_one, grad_shift_one = norm_one_back(grad_first)
    grad_bias_one = jnp.sum(grad_res_one, axis=0)
    attn_grad_all = lax.all_gather(grad_res_one.astype(jnp.bfloat16), "mp", axis=0, tiled=True)
    grad_w_attn_out = jnp.einsum(
        "rk,rd->kd", attended, attn_grad_all, preferred_element_type=jnp.float32
    )
    grad_attended = jnp.einsum(
        "rd,kd->rk", attn_grad_all, w_attn_out, preferred_element_type=jnp.float32
    )
    grad_attended = grad_attended.astype(jnp.bfloat16).reshape(
        page_count, SEQ, local_heads, HEAD_DIM
    )
    weights_low = weights_soft.astype(jnp.bfloat16)
    grad_weights = jnp.einsum(
        "pqhe,pkhe->phqk", grad_attended, heads_view[2], preferred_element_type=jnp.float32
    )
    grad_values = jnp.einsum(
        "phqk,pqhe->pkhe", weights_low, grad_attended, preferred_element_type=jnp.float32
    )
    inner_total = jnp.sum(weights_soft * grad_weights, axis=-1, keepdims=True)
    grad_scores = (weights_soft * (grad_weights - inner_total)).astype(jnp.bfloat16)
    grad_queries = (
        jnp.einsum(
            "phqk,pkhe->pqhe", grad_scores, heads_view[1], preferred_element_type=jnp.float32
        )
        * scale_factor
    )
    grad_keys = (
        jnp.einsum(
            "phqk,pqhe->pkhe", grad_scores, heads_view[0], preferred_element_type=jnp.float32
        )
        * scale_factor
    )
    grad_proj = (
        jnp.stack([grad_queries, grad_keys, grad_values])
        .reshape(3, rows_all, local_width)
        .astype(jnp.bfloat16)
    )
    proj_sums = jnp.sum(grad_proj.astype(jnp.float32), axis=1)
    grad_qv_bias = jnp.stack([proj_sums[0], proj_sums[2]])
    grad_w_qkv = jnp.einsum("rd,cre->cde", gathered, grad_proj, preferred_element_type=jnp.float32)
    input_part = jnp.einsum("cre,cde->rd", grad_proj, w_qkv, preferred_element_type=jnp.float32)
    input_grad_rows = lax.psum_scatter(
        input_part.astype(jnp.bfloat16), "mp", scatter_dimension=0, tiled=True
    ).astype(jnp.float32)
    grad_in = input_grad_rows + grad_res_one
    matrix_grads = (
        grad_w_qkv,
        grad_qv_bias,
        grad_w_attn_out,
        grad_w_ffn_in,
        grad_ffn_in_bias,
        grad_w_ffn_out,
    )
    vector_grads = (
        jnp.stack([grad_bias_one, grad_bias_two]),
        jnp.stack([grad_gain_one, grad_gain_two]),
        jnp.stack([grad_shift_one, grad_shift_two]),
    )
    return (grad_in, matrix_grads, vector_grads)


def pipelined(
    token_in,
    cotangent,
    w_qkv,
    qv_bias,
    w_attn_out,
    w_ffn_in,
    ffn_in_bias,
    w_ffn_out,
    out_biases,
    norm_gains,
    norm_shifts,
):
    params = (
        w_qkv[0],
        qv_bias[0],
        w_attn_out[0],
        w_ffn_in[0],
        ffn_in_bias[0],
        w_ffn_out[0],
        out_biases[0],
        norm_gains[0],
        norm_shifts[0],
    )
    micro_count = token_in.shape[0]
    section_index = lax.axis_index("section")
    is_first = section_index == 0
    zero_rows = jnp.zeros(token_in.shape[1:], jnp.bfloat16)
    run_forward = partial(layer_forward, params)
    run_backward = partial(layer_backward, params)

    def forward_step(step_index, carry):
        received, saved, stored = carry
        own_micro = step_index - section_index
        is_valid = (own_micro >= 0) & (own_micro < micro_count)
        slot_index = jnp.clip(own_micro, 0, micro_count - 1)
        first_rows = lax.dynamic_index_in_dim(
            token_in, jnp.minimum(step_index, micro_count - 1).astype(jnp.int32), 0, keepdims=False
        )
        layer_in = jnp.where(is_first, first_rows, received)
        result, unused_kept = run_forward(layer_in)
        result_low = result.astype(jnp.bfloat16)
        old_saved = lax.dynamic_index_in_dim(saved, slot_index, 0, keepdims=False)
        saved = lax.dynamic_update_index_in_dim(
            saved, jnp.where(is_valid, layer_in, old_saved), slot_index, 0
        )
        old_stored = lax.dynamic_index_in_dim(stored, slot_index, 0, keepdims=False)
        stored = lax.dynamic_update_index_in_dim(
            stored, jnp.where(is_valid, result_low, old_stored), slot_index, 0
        )
        received = from_behind(result_low, "section", 1)
        return (received, saved, stored)

    start_carry = (zero_rows, jnp.zeros_like(token_in), jnp.zeros_like(token_in))
    unused_received, saved, stored = lax.fori_loop(0, micro_count + 1, forward_step, start_carry)
    matrix_zero = tuple((jnp.zeros(entry.shape, jnp.float32) for entry in params[:6]))
    vector_zero = (
        jnp.zeros(out_biases.shape[1:], jnp.float32),
        jnp.zeros(norm_gains.shape[1:], jnp.float32),
        jnp.zeros(norm_shifts.shape[1:], jnp.float32),
    )

    def backward_step(step_index, carry):
        received_grad, grad_store, matrix_sums, vector_sums = carry
        own_micro = step_index - (1 - section_index)
        is_valid = (own_micro >= 0) & (own_micro < micro_count)
        slot_index = jnp.clip(own_micro, 0, micro_count - 1)
        layer_in = lax.dynamic_index_in_dim(saved, slot_index, 0, keepdims=False)
        from_last = lax.dynamic_index_in_dim(cotangent, slot_index, 0, keepdims=False)
        grad_out = jnp.where(is_first, received_grad, from_last).astype(jnp.float32)
        unused_result, kept_values = run_forward(layer_in)
        grad_in, matrix_grads, vector_grads = run_backward(kept_values, grad_out)
        matrix_grads = tuple((jnp.where(is_valid, entry, 0.0) for entry in matrix_grads))
        vector_grads = tuple((jnp.where(is_valid, entry, 0.0) for entry in vector_grads))
        grad_low = grad_in.astype(jnp.bfloat16)
        old_piece = lax.dynamic_index_in_dim(grad_store, slot_index, 0, keepdims=False)
        grad_store = lax.dynamic_update_index_in_dim(
            grad_store, jnp.where(is_valid, grad_low, old_piece), slot_index, 0
        )
        grad_one, grad_two, grad_three, grad_four, grad_five, grad_six = matrix_grads
        matrix_grads = (
            lax.psum(grad_one.astype(jnp.bfloat16), "dp").astype(jnp.float32),
            lax.psum(grad_two.astype(jnp.bfloat16), "dp").astype(jnp.float32),
            lax.psum(grad_three.astype(jnp.bfloat16), "dp").astype(jnp.float32),
            lax.psum(grad_four.astype(jnp.bfloat16), "dp").astype(jnp.float32),
            lax.psum(grad_five.astype(jnp.bfloat16), "dp").astype(jnp.float32),
            lax.psum(grad_six.astype(jnp.bfloat16), "dp").astype(jnp.float32),
        )
        matrix_sums = tuple((total + extra for total, extra in zip(matrix_sums, matrix_grads)))
        vector_sums = tuple((total + extra for total, extra in zip(vector_sums, vector_grads)))
        received_grad = from_behind(grad_low, "section", -1)
        return (received_grad, grad_store, matrix_sums, vector_sums)

    back_carry = (zero_rows, jnp.zeros_like(token_in), matrix_zero, vector_zero)
    unused_grad, grad_store, matrix_sums, vector_sums = lax.fori_loop(
        0, micro_count + 1, backward_step, back_carry
    )
    bias_total, gain_total, shift_total = vector_sums
    bias_part, gain_part, shift_part = (
        lax.psum_scatter(bias_total, ("mp", "dp"), scatter_dimension=1, tiled=True),
        lax.psum_scatter(gain_total, ("mp", "dp"), scatter_dimension=1, tiled=True),
        lax.psum_scatter(shift_total, ("mp", "dp"), scatter_dimension=1, tiled=True),
    )
    return (
        stored[None],
        grad_store[None],
        matrix_sums[0][None],
        matrix_sums[1][None],
        matrix_sums[2][None],
        matrix_sums[3][None],
        matrix_sums[4][None],
        matrix_sums[5][None],
        bias_part[None],
        gain_part[None],
        shift_part[None],
    )


MESH = pl.DeviceIdType.MESH


def low(value):
    return value.astype(jnp.bfloat16)


def high(value):
    return value.astype(jnp.float32)


def remote(src, dst, send, recv, device):
    return pltpu.make_async_remote_copy(
        src_ref=src, dst_ref=dst, send_sem=send, recv_sem=recv, device_id=device, device_id_type=MESH
    )


def neighbours():
    c, p, d = lax.axis_index("section"), lax.axis_index("mp"), lax.axis_index("dp")
    return {
        "core": (1 - c, p, d),
        "x": (c, p + 1 - 2 * lax.rem(p, 2), d),
        "y": (c, lax.rem(p + 2, 4), d),
        "across": (c, p, 3 - d),
        "inner": (c, p, jnp.where(d == 0, 1, 2)),
        "outer": (c, p, jnp.where(d == 1, 0, 3)),
    }


def places():
    p = lax.axis_index("mp")
    return [p, p + 1 - 2 * lax.rem(p, 2), lax.rem(p + 2, 4), 3 - p]


def greet(near, is_end):
    barrier = pltpu.get_barrier_semaphore()

    def signal(device):
        pl.semaphore_signal(barrier, inc=1, device_id=device, device_id_type=MESH)

    for name in ("core", "x", "y"):
        signal(near[name])

    @pl.when(is_end)
    def _():
        signal(near["inner"])
        pl.semaphore_wait(barrier, 4)

    @pl.when(jnp.logical_not(is_end))
    def _():
        signal(near["outer"])
        signal(near["across"])
        pl.semaphore_wait(barrier, 5)


CHUNKS = 24


def reduce_kernel(
    left, right, out,
    lbuf, rbuf, sendc, recvc, keep, x1s, x1r, y1s, y1r, part, base, x2s, x2r, y2s, y2r, acc,
    zk, zs1, zr1, zs2, zr2, zs3, zr3,
    lsem, cs, cr, x1ss, x1rs, y1ss, y1rs, x2ss, x2rs, y2ss, y2rs, z1ss, z1rs, z2ss, z2rs, z3ss, z3rs, os, orr,
):
    c, d = lax.axis_index("section"), lax.axis_index("dp")
    near = neighbours()
    spots = places()
    is_end = (d == 0) | (d == 3)
    is_mid = jnp.logical_not(is_end)
    greet(near, is_end)
    rows = sendc.shape[2]
    half = rows // 2

    def loads(s):
        layer, k, slot = 1 - s // 12, lax.rem(s, 12), lax.rem(s, 2)
        stride = jnp.where(k < 8, 4, 1)
        first = jnp.where(k < 4, k, jnp.where(k < 8, 12 + k, jnp.where(k == 8, 32, 36 + 4 * (k - 9))))
        kind = jnp.where(k < 4, 0, jnp.where(k < 8, 1, jnp.where(k == 8, 2, 3)))
        copies = [
            pltpu.make_async_copy(left.at[layer, first + stride * p], lbuf.at[slot, p], lsem.at[slot, p])
            for p in range(4)
        ]
        copies.append(pltpu.make_async_copy(right.at[layer, kind], rbuf.at[slot], lsem.at[slot, 4]))
        return copies

    def core_copy(s):
        a, b = lax.rem(s, 2), lax.rem(s, 4)
        return remote(sendc.at[a], recvc.at[b], cs.at[a], cr.at[b], near["core"])

    def link_copy(s, src, dst, ss, rs, name):
        a, b = lax.rem(s, 2), lax.rem(s, 4)
        return remote(src.at[a], dst.at[b], ss.at[a], rs.at[b], near[name])

    x1 = lambda s: link_copy(s, x1s, x1r, x1ss, x1rs, "x")
    y1 = lambda s: link_copy(s, y1s, y1r, y1ss, y1rs, "y")
    x2 = lambda s: link_copy(s, x2s, x2r, x2ss, x2rs, "x")
    y2 = lambda s: link_copy(s, y2s, y2r, y2ss, y2rs, "y")
    z1 = lambda s: link_copy(s, zs1, zr1, z1ss, z1rs, "inner")
    z2 = lambda s: link_copy(s, zs2, zr2, z2ss, z2rs, "across")

    def z3(s):
        b = lax.rem(s, 6)
        return remote(zs3.at[b], zr3.at[b], z3ss.at[b], z3rs.at[b], near["outer"])

    def stage0(s):
        slot = lax.rem(s, 2)
        for copy in loads(s):
            copy.wait()

        @pl.when(s + 1 < CHUNKS)
        def _():
            for copy in loads(s + 1):
                copy.start()

        for r in range(4):
            whole = lax.dot_general(
                lbuf[slot, spots[r]], rbuf[slot], (((0,), (0,)), ((), ())), preferred_element_type=jnp.float32
            )
            keep[slot, r] = jnp.where(c == 0, whole[:rows], whole[rows:])
            sendc[slot, r] = low(jnp.where(c == 0, whole[rows:], whole[:rows]))
        core_copy(s).start()

    def stage1(s):
        a, b = lax.rem(s, 2), lax.rem(s, 4)
        core_copy(s).wait()
        far = keep[a, 3] + high(recvc[b, 3])
        x1s[a, 0] = low(far[:half])
        y1s[a, 0] = low(far[half:])
        by_x = keep[a, 1] + high(recvc[b, 1])
        x1s[a, 1] = low(by_x[:half])
        part[a, 0] = by_x[half:]
        by_y = keep[a, 2] + high(recvc[b, 2])
        y1s[a, 1] = low(by_y[half:])
        part[a, 1] = by_y[:half]
        x1(s).start()
        y1(s).start()
        base[a] = keep[a, 0] + high(recvc[b, 0])

    def stage2(s):
        a, b = lax.rem(s, 2), lax.rem(s, 4)
        x1(s).wait()
        y1(s).wait()
        y2s[a] = low(part[a, 1] + high(x1r[b, 0]))
        x2s[a] = low(part[a, 0] + high(y1r[b, 0]))
        own = base[a]
        acc[a, pl.ds(0, half)] = own[:half] + high(x1r[b, 1])
        acc[a, pl.ds(half, half)] = own[half:] + high(y1r[b, 1])
        x2(s).start()
        y2(s).start()

    def stage3(s):
        a, b = lax.rem(s, 2), lax.rem(s, 4)
        x2(s).wait()
        y2(s).wait()
        own = acc[a]
        top = own[:half] + high(y2r[b])
        end = own[half:] + high(x2r[b])

        @pl.when(is_end)
        def _():
            zs1[a, pl.ds(0, half)] = low(top)
            zs1[a, pl.ds(half, half)] = low(end)
            z1(s).start()

        @pl.when(is_mid)
        def _():
            zk[a, pl.ds(0, half)] = top
            zk[a, pl.ds(half, half)] = end

    def stage4(s):
        a, b = lax.rem(s, 2), lax.rem(s, 4)

        @pl.when(is_end)
        def _():
            z1(s).wait_send()

        @pl.when(is_mid)
        def _():
            z1(s).wait_recv()
            zs2[a] = low(zk[a] + high(zr1[b]))
            z2(s).start()

    def stage5(s):
        a, b = lax.rem(s, 2), lax.rem(s, 4)

        @pl.when(is_mid)
        def _():
            z2(s).wait()
            zs3[lax.rem(s, 6)] = low(high(zs2[a]) + high(zr2[b]))
            z3(s).start()

    def stage6(s, begin):
        layer, k, b = 1 - s // 12, lax.rem(s, 12), lax.rem(s, 6)

        def finish(source):
            @pl.when(layer == c)
            def _():
                copy = pltpu.make_async_copy(source.at[b], out.at[k, c], os.at[b])
                copy.start() if begin else copy.wait()

            @pl.when(layer != c)
            def _():
                copy = remote(source.at[b], out.at[k, c], os.at[b], orr.at[k], near["core"])
                copy.start() if begin else copy.wait_send()

        @pl.when(is_end)
        def _():
            if begin:
                z3(s).wait_recv()
            finish(zr3)

        @pl.when(is_mid)
        def _():
            if begin:
                z3(s).wait_send()
            finish(zs3)

    for copy in loads(0):
        copy.start()

    def step(i, carry):
        def run(stage, lag, *extra):
            @pl.when((i >= lag) & (i < CHUNKS + lag))
            def _():
                stage(i - lag, *extra)

        run(stage1, 1)
        run(stage0, 0)
        run(stage2, 2)
        run(stage3, 3)
        run(stage4, 4)
        run(stage5, 5)
        run(stage6, 6, True)
        run(stage6, 7, False)
        return carry

    lax.fori_loop(0, CHUNKS + 8, step, 0)
    for k in range(12):
        remote(zs3.at[0], out.at[k, 1 - c], os.at[0], orr.at[k], near["core"]).wait_recv()


def grad_reduce(left, right):
    rows, wide = left.shape[2:]
    block, width = wide // 2, right.shape[3]
    half = block // 2
    bf, f32, dma = jnp.bfloat16, jnp.float32, pltpu.SemaphoreType.DMA
    v = pltpu.VMEM
    return pl.pallas_call(
        reduce_kernel,
        out_shape=jax.ShapeDtypeStruct((12, 2, block, width), bf),
        in_specs=[pl.BlockSpec(memory_space=pl.ANY)] * 2,
        out_specs=pl.BlockSpec(memory_space=pl.ANY),
        scratch_shapes=[
            v((2, 4, rows, wide), bf), v((2, rows, width), bf),
            v((2, 4, block, width), bf), v((4, 4, block, width), bf), v((2, 4, block, width), f32),
            v((2, 2, half, width), bf), v((4, 2, half, width), bf), v((2, 2, half, width), bf), v((4, 2, half, width), bf),
            v((2, 2, half, width), f32), v((2, block, width), f32),
            v((2, half, width), bf), v((4, half, width), bf), v((2, half, width), bf), v((4, half, width), bf),
            v((2, block, width), f32),
            v((2, block, width), f32), v((2, block, width), bf), v((4, block, width), bf),
            v((2, block, width), bf), v((4, block, width), bf), v((6, block, width), bf), v((6, block, width), bf),
            dma((2, 5)),
        ] + [dma((n,)) for n in (2, 4) * 7] + [dma((6,)), dma((6,))] + [dma((6,)), dma((12,))],
        compiler_params=pltpu.CompilerParams(collective_id=1, has_side_effects=True, vmem_limit_bytes=50 * 2**20),
    )(left, right)


TRIPLES = 8


def gather_kernel(
    shard, vec, norms, full, vecs, all_norms,
    ini_s, ini_r, loc, x1ss, x1rs, y1ss, y1rs, x2ss, x2rs, y2ss, y2rs, zs, zr, cs, cr, vs, vr, vloc,
):
    c, p, d = lax.axis_index("section"), lax.axis_index("mp"), lax.axis_index("dp")
    near = neighbours()
    near["pair"] = (c, p, d + 1 - 2 * lax.rem(d, 2))
    spots = places()
    rows = shard.shape[1] // 2
    half = rows // 2
    odd = lax.rem(d, 2)
    others = [(cc, spots[r], d) for r in range(4) for cc in (c, 1 - c)][1:]

    barrier = pltpu.get_barrier_semaphore()
    for device in others + [near["pair"]]:
        pl.semaphore_signal(barrier, inc=1, device_id=device, device_id_type=MESH)
    pl.semaphore_wait(barrier, 8)

    def place_of(s, spot, h):
        k = lax.rem(s, 12)
        b, kind = (k - 4) // 2, lax.rem(k, 2)
        row = jnp.where(k < 4, k * 1024 + spot * 256, 4096 + kind * 4096 + spot * 1024 + b * 256) * (rows // 128)
        return s // 12, row + h * rows

    def block(s, spot, h, start=0, size=rows):
        layer, row = place_of(s, spot, h)
        return full.at[layer, pl.ds(pl.multiple_of(row + start, half), size)]

    def init(k):
        layer, row = place_of(12 * c + k, p, 0)
        there = full.at[layer, pl.ds(pl.multiple_of(row, half), 2 * rows)]
        src = shard.at[k]
        return pltpu.make_async_copy(src, there, loc.at[k]), remote(src, there, ini_s.at[k], ini_r.at[k], near["core"])

    def init_wait(k):
        layer, row = place_of(12 * (1 - c) + k, p, 0)
        there = full.at[layer, pl.ds(pl.multiple_of(row, half), 2 * rows)]
        remote(there, there, ini_s.at[k], ini_r.at[k], near["core"]).wait_recv()

    def small():
        copies = [remote(vec, vecs.at[c, p], vs.at[i], vr.at[c, p], device) for i, device in enumerate(others)]
        copies.append(remote(norms, all_norms.at[c], vs.at[7], vr.at[0, 4], near["core"]))
        return copies

    vec_local = pltpu.make_async_copy(vec, vecs.at[c, p], vloc.at[0])
    norm_local = pltpu.make_async_copy(norms, all_norms.at[c], vloc.at[1])

    def first(s, name):
        ss, rs = (x1ss, x1rs) if name == "x" else (y1ss, y1rs)
        b = block(s, p, c)
        return remote(b, b, ss.at[s], rs.at[s], near[name])

    def arrived(s, name):
        ss, rs = (x1ss, x1rs) if name == "x" else (y1ss, y1rs)
        b = block(s, spots[1] if name == "x" else spots[2], c)
        return remote(b, b, ss.at[s], rs.at[s], near[name])

    def relay(s, name):
        if name == "x":
            b = block(s, spots[2], c, 0, half)
            return remote(b, b, x2ss.at[s], x2rs.at[s], near["x"])
        b = block(s, spots[1], c, half, half)
        return remote(b, b, y2ss.at[s], y2rs.at[s], near["y"])

    def relayed(s, name):
        if name == "x":
            b = block(s, spots[3], c, 0, half)
            return remote(b, b, x2ss.at[s], x2rs.at[s], near["x"])
        b = block(s, spots[3], c, half, half)
        return remote(b, b, y2ss.at[s], y2rs.at[s], near["y"])

    def to_pair(s, r):
        b = block(s, spots[r], c)
        return remote(b, b, zs.at[s, r - 1], zr.at[s, r - 1], near["pair"])

    def to_core(s, r):
        b = block(s, spots[r], c)
        return remote(b, b, cs.at[s, r - 1], cr.at[s, r - 1], near["core"])

    def from_core(s, r):
        b = block(s, spots[r], 1 - c)
        return remote(b, b, cs.at[s, r - 1], cr.at[s, r - 1], near["core"])

    def stage_a(t):
        for j in range(3):
            s = 3 * t + j

            @pl.when(s // 12 != c)
            def _():
                init_wait(lax.rem(s, 12))

        for s in (3 * t, 3 * t + 1 + odd):
            first(s, "x").start()
            first(s, "y").start()

    def stage_b(t):
        for n, s in enumerate((3 * t, 3 * t + 1 + odd)):
            arrived(s, "x").wait_recv()
            relay(s, "y").start()
            arrived(s, "y").wait_recv()
            relay(s, "x").start()
            for r in (1, 2):
                to_core(s, r).start()
                if n:
                    to_pair(s, r).start()

    def stage_c(t):
        for n, s in enumerate((3 * t, 3 * t + 1 + odd)):
            relayed(s, "x").wait_recv()
            relayed(s, "y").wait_recv()
            to_core(s, 3).start()
            if n:
                to_pair(s, 3).start()

    def stage_d(t):
        s = 3 * t + 2 - odd
        for r in (1, 2, 3):
            to_pair(s, r).wait_recv()
            to_core(s, r).start()

    def stage_e(t):
        for j in range(3):
            for r in (1, 2, 3):
                from_core(3 * t + j, r).wait_recv()

    def stage_f(t):
        for n, s in enumerate((3 * t, 3 * t + 1 + odd)):
            first(s, "x").wait_send()
            first(s, "y").wait_send()
            relay(s, "x").wait_send()
            relay(s, "y").wait_send()
            for r in (1, 2, 3):
                if n:
                    to_pair(s, r).wait_send()
        for j in range(3):
            for r in (1, 2, 3):
                to_core(3 * t + j, r).wait_send()

    def begin(k, carry):
        for copy in init(k):
            copy.start()
        return carry

    lax.fori_loop(0, 12, begin, 0)
    vec_local.start()
    norm_local.start()
    for copy in small():
        copy.start()

    def local_done(k, carry):
        init(k)[0].wait()
        return carry

    lax.fori_loop(0, 12, local_done, 0)

    def step(i, carry):
        def run(stage, lag):
            @pl.when((i >= lag) & (i < TRIPLES + lag))
            def _():
                stage(i - lag)

        for lag, stage in enumerate((stage_a, stage_b, stage_c, stage_d, stage_e, stage_f)):
            run(stage, lag)
        return carry

    lax.fori_loop(0, TRIPLES + 5, step, 0)

    def sent(k, carry):
        init(k)[1].wait_send()
        return carry

    lax.fori_loop(0, 12, sent, 0)
    vec_local.wait()
    norm_local.wait()
    for copy in small():
        copy.wait_send()
    for cc, spot in [(cc, spots[r]) for r in range(4) for cc in (c, 1 - c)][1:]:
        remote(vec, vecs.at[cc, spot], vs.at[0], vr.at[cc, spot], near["core"]).wait_recv()
    remote(norms, all_norms.at[1 - c], vs.at[7], vr.at[0, 4], near["core"]).wait_recv()


def weight_gather(shard, vec, norms):
    block, width = shard.shape[2:]
    dma = pltpu.SemaphoreType.DMA
    return pl.pallas_call(
        gather_kernel,
        out_shape=(
            jax.ShapeDtypeStruct((2, 96 * block, width), shard.dtype),
            jax.ShapeDtypeStruct((2, 4) + vec.shape, vec.dtype),
            jax.ShapeDtypeStruct((2,) + norms.shape, norms.dtype),
        ),
        in_specs=[pl.BlockSpec(memory_space=pltpu.VMEM)] + [pl.BlockSpec(memory_space=pl.ANY)] * 2,
        out_specs=[pl.BlockSpec(memory_space=pl.ANY)] * 3,
        scratch_shapes=[dma((12,))] * 3 + [dma((24,))] * 8 + [dma((24, 3))] * 4 + [dma((8,)), dma((2, 5)), dma((2,))],
        compiler_params=pltpu.CompilerParams(collective_id=0, has_side_effects=True, vmem_limit_bytes=16 * 2**20),
    )(shard.reshape(12, 2 * block, width), vec, norms)


SCALE = 0.125


def dot(a, b):
    return jnp.dot(a, b, preferred_element_type=jnp.float32)


def dot_tn(a, b):
    return lax.dot_general(a, b, (((0,), (0,)), ((), ())), preferred_element_type=jnp.float32)


def dot_nt(a, b):
    return lax.dot_general(a, b, (((1,), (1,)), ((), ())), preferred_element_type=jnp.float32)


def standard(values):
    average = jnp.mean(values, axis=-1, keepdims=True)
    centered = values - average
    variance = jnp.mean(centered * centered, axis=-1, keepdims=True)
    scale = lax.rsqrt(variance + 1e-05)
    return centered * scale, scale


def softmax(q, k):
    scores = dot_nt(q * jnp.asarray(SCALE, q.dtype), k)
    exponent = jnp.exp(scores - jnp.max(scores, axis=-1, keepdims=True))
    return exponent * (1.0 / jnp.sum(exponent, axis=-1, keepdims=True))


def by_rows(rows, step, body):
    def run(i, carry):
        body(pl.ds(pl.multiple_of(i * step, step), step))
        return carry

    lax.fori_loop(0, rows // step, run, 0)


def attention_block(x, w, vec, save, acc, dim):
    rows = x[...]
    q = low(dot_nt(rows, w[0]) + vec[0:1])
    k = low(dot_nt(rows, w[1]))
    v = low(dot_nt(rows, w[2]) + vec[1:2])
    save[0], save[1], save[2] = q, k, v
    for j in range(q.shape[1] // dim):
        cols = slice(j * dim, (j + 1) * dim)
        save[3, :, cols] = low(dot(low(softmax(q[:, cols], k[:, cols])), v[:, cols]))
    acc[...] += dot(save[3], w[3])


def ffn_block(hb, w, bias, save, acc):
    z = dot_nt(hb[...], w[0]) + bias
    inner = 0.5 + 0.5 * lax.erf(z * math.sqrt(0.5))
    g = low(z * inner)
    save[0] = g
    save[1] = low(inner + z * jnp.exp(-0.5 * z * z) * (1.0 / math.sqrt(2.0 * math.pi)))
    acc[...] += dot(g, w[1])


def first_norm(x, nrm, acc, u1, hb):
    def run(rows):
        u = acc[rows] + nrm[0:1] + high(x[rows])
        u1[rows] = u
        h = standard(u)[0] * nrm[2:3] + nrm[4:5]
        hb[rows] = low(h)
        acc[rows] = h + nrm[1:2]

    by_rows(acc.shape[0], 64, run)


def second_norm(nrm, acc, u2, out):
    def run(rows):
        u = acc[rows]
        u2[rows] = u
        out[rows] = low(standard(u)[0] * nrm[3:4] + nrm[5:6])

    by_rows(acc.shape[0], 64, run)


def norm_back(u, grad, gain, sums, at, out_low, out_acc):
    def run(rows):
        g = high(grad[rows])
        xhat, scale = standard(u[rows])
        scaled = g * gain
        du = scale * (
            scaled
            - jnp.mean(scaled, axis=-1, keepdims=True)
            - xhat * jnp.mean(scaled * xhat, axis=-1, keepdims=True)
        )
        out_low[rows] = low(du)
        out_acc[rows] = du
        for row, term in ((at[0], du), (at[1], g * xhat), (at[2], g)):
            sums[row : row + 1] += jnp.sum(term, axis=0, keepdims=True)

    by_rows(u.shape[0], 64, run)


def ffn_back_block(dfb, w, gd, acc, dz_out):
    dz = low(dot_nt(dfb[...], w[1]) * high(gd))
    dz_out[...] = dz
    acc[...] += dot(dz, w[0])
    return jnp.sum(high(dz), axis=0, keepdims=True)


def attention_back_block(dab, w, qkv, dq_out, dk_out, dv_out, acc, dim):
    dob = low(dot_nt(dab[...], w[3]))
    for j in range(dob.shape[1] // dim):
        cols = slice(j * dim, (j + 1) * dim)
        q, k, v, do = qkv[0, :, cols], qkv[1, :, cols], qkv[2, :, cols], dob[:, cols]
        a = softmax(q, k)
        da = dot_nt(do, v)
        ds = low(a * (da - jnp.sum(a * da, axis=-1, keepdims=True)))
        dv_out[:, cols] = low(dot_tn(low(a), do))
        dq_out[:, cols] = low(dot(ds, k) * SCALE)
        dk_out[:, cols] = low(dot_tn(ds, q) * SCALE)
    acc[...] += dot(dq_out[...], w[0]) + dot(dk_out[...], w[1]) + dot(dv_out[...], w[2])


def weight_copies(full, layer, kind, p, b, buf, sem, rows):
    width = 4 * rows
    if kind == 0:
        starts = [c * width + p * rows for c in range(4)]
    else:
        starts = [4 * width + t * 4 * width + p * width + b * rows for t in range(2)]
    return [
        pltpu.make_async_copy(full.at[layer, pl.ds(pl.multiple_of(start, rows), rows)], buf.at[n], sem.at[n])
        for n, start in enumerate(starts)
    ]


def forward_kernel(dim, x_in, full, vecs, norms, qkvo, gd, us, hbs, outs,
                   x, acc, u, hb, wa, wf, sa, sf, wasem, wfsem, sasem, sfsem, usem):
    rows = wa.shape[2]
    x[...] = x_in[...]

    def one(copy):
        copy.start()
        copy.wait()

    def layer_step(l, carry):
        nrm = norms.at[l]
        acc[...] = jnp.zeros_like(acc)

        def attn(p, slot):
            return weight_copies(full, l, 0, p, 0, wa.at[slot], wasem.at[slot], rows)

        def ffn(n, slot):
            return weight_copies(full, l, 1, lax.rem(n, 4), n // 4, wf.at[slot], wfsem.at[slot], rows)

        for copy in attn(0, 0) + ffn(0, 0):
            copy.start()

        def attn_step(p, carry):
            slot = lax.rem(p, 2)
            for copy in attn(p, slot):
                copy.wait()

            @pl.when(p < 3)
            def _():
                for copy in attn(p + 1, 1 - slot):
                    copy.start()

            attention_block(x, wa.at[slot], vecs[l, p], sa, acc, dim)
            one(pltpu.make_async_copy(sa, qkvo.at[l, p], sasem))
            return carry

        lax.fori_loop(0, 4, attn_step, 0)
        first_norm(x, nrm, acc, u, hb)
        one(pltpu.make_async_copy(u, us.at[l, 0], usem))
        one(pltpu.make_async_copy(hb, hbs.at[l], usem))

        def ffn_step(n, carry):
            slot = lax.rem(n, 2)
            for copy in ffn(n, slot):
                copy.wait()

            @pl.when(n < 15)
            def _():
                for copy in ffn(n + 1, 1 - slot):
                    copy.start()

            p, b = lax.rem(n, 4), n // 4
            ffn_block(hb, wf.at[slot], vecs[l, p, pl.ds(2 + b, 1)], sf, acc)
            one(pltpu.make_async_copy(sf, gd.at[l, 4 * p + b], sfsem))
            return carry

        lax.fori_loop(0, 16, ffn_step, 0)
        second_norm(nrm, acc, u, x)
        one(pltpu.make_async_copy(u, us.at[l, 1], usem))
        one(pltpu.make_async_copy(x, outs.at[l], usem))
        return carry

    lax.fori_loop(0, 2, layer_step, 0)


def forward(dim, x, full, vecs, norms):
    seq, width = x.shape
    rows = width // 4
    bf, f32, dma, v = jnp.bfloat16, jnp.float32, pltpu.SemaphoreType.DMA, pltpu.VMEM
    hbm, vmem = pl.BlockSpec(memory_space=pl.ANY), pl.BlockSpec(memory_space=pltpu.VMEM)
    S = jax.ShapeDtypeStruct
    return pl.pallas_call(
        functools.partial(forward_kernel, dim),
        out_shape=(S((2, 4, 4, seq, rows), bf), S((2, 16, 2, seq, rows), bf), S((2, 2, seq, width), f32),
                   S((2, seq, width), bf), S((2, seq, width), bf)),
        in_specs=[vmem, hbm, vmem, vmem],
        out_specs=[hbm] * 5,
        scratch_shapes=[v((seq, width), bf), v((seq, width), f32), v((seq, width), f32), v((seq, width), bf),
                        v((2, 4, rows, width), bf), v((2, 2, rows, width), bf), v((4, seq, rows), bf), v((2, seq, rows), bf),
                        dma((2, 4)), dma((2, 2)), dma(()), dma(()), dma(())],
        compiler_params=pltpu.CompilerParams(vmem_limit_bytes=50 * 2**20),
    )(x, full, vecs, norms)


def backward_kernel(dim, x_in, cot, full, vecs, norms, qkvo, gd, us, hbs, outs, left, right, dxs, sums, vgrads,
                    L, R, acc, g, u, wa, wf, da, df, wasem, wfsem, dasem, dfsem, lsem, osem):
    rows = wa.shape[2]
    sums[...] = jnp.zeros_like(sums)
    vgrads[...] = jnp.zeros_like(vgrads)

    def one(copy):
        copy.start()
        copy.wait()

    def layer_step(i, carry):
        l = 1 - i
        nrm, sm, vg = norms.at[l], sums.at[l], vgrads.at[l]

        @pl.when(i == 0)
        def _():
            one(pltpu.make_async_copy(cot, g, osem))
            one(pltpu.make_async_copy(outs.at[0], R.at[3], osem))

        @pl.when(i == 1)
        def _():
            one(pltpu.make_async_copy(x_in, R.at[3], osem))

        one(pltpu.make_async_copy(hbs.at[l], R.at[1], osem))

        def ld(n, carry):
            one(pltpu.make_async_copy(gd.at[l, n, 0], L.at[n], osem))
            return carry

        lax.fori_loop(0, 16, ld, 0)

        def ldo(n, carry):
            one(pltpu.make_async_copy(qkvo.at[l, n, 3], L.at[32 + n], osem))
            return carry

        lax.fori_loop(0, 4, ldo, 0)
        one(pltpu.make_async_copy(us.at[l, 1], u, osem))
        norm_back(u, g, nrm[3:4], sm, (1, 3, 5), R.at[0], acc)

        def attn(p, slot):
            return weight_copies(full, l, 0, p, 0, wa.at[slot], wasem.at[slot], rows) + [
                pltpu.make_async_copy(qkvo.at[l, p], da.at[slot], dasem.at[slot])
            ]

        def ffn(n, slot):
            return weight_copies(full, l, 1, lax.rem(n, 4), n // 4, wf.at[slot], wfsem.at[slot], rows) + [
                pltpu.make_async_copy(gd.at[l, 4 * lax.rem(n, 4) + n // 4, 1], df.at[slot], dfsem.at[slot])
            ]

        for copy in attn(0, 0) + ffn(0, 0):
            copy.start()

        def ffn_step(n, carry):
            slot = lax.rem(n, 2)
            for copy in ffn(n, slot):
                copy.wait()

            @pl.when(n < 15)
            def _():
                for copy in ffn(n + 1, 1 - slot):
                    copy.start()

            p, b = lax.rem(n, 4), n // 4
            vg[p, pl.ds(2 + b, 1)] = ffn_back_block(R.at[0], wf.at[slot], df[slot], acc, L.at[16 + 4 * p + b])
            return carry

        lax.fori_loop(0, 16, ffn_step, 0)
        one(pltpu.make_async_copy(us.at[l, 0], u, osem))
        norm_back(u, acc, nrm[2:3], sm, (0, 2, 4), R.at[2], acc)

        def attn_step(p, carry):
            slot = lax.rem(p, 2)
            for copy in attn(p, slot):
                copy.wait()

            @pl.when(p < 3)
            def _():
                for copy in attn(p + 1, 1 - slot):
                    copy.start()

            attention_back_block(
                R.at[2], wa.at[slot], da.at[slot], L.at[36 + p], L.at[40 + p], L.at[44 + p], acc, dim
            )
            vg[p, 0:1] = jnp.sum(high(L[36 + p]), axis=0, keepdims=True)
            vg[p, 1:2] = jnp.sum(high(L[44 + p]), axis=0, keepdims=True)
            return carry

        lax.fori_loop(0, 4, attn_step, 0)
        by_rows(acc.shape[0], 64, lambda r: g.__setitem__(r, low(acc[r])))
        one(pltpu.make_async_copy(g, dxs.at[l], osem))
        one(pltpu.make_async_copy(L, left.at[l], osem))
        one(pltpu.make_async_copy(R, right.at[l], osem))
        return carry

    lax.fori_loop(0, 2, layer_step, 0)


def backward(dim, x, cot, full, vecs, norms, saved):
    seq, width = x.shape
    rows = width // 4
    bf, f32, dma, v = jnp.bfloat16, jnp.float32, pltpu.SemaphoreType.DMA, pltpu.VMEM
    hbm, vmem = pl.BlockSpec(memory_space=pl.ANY), pl.BlockSpec(memory_space=pltpu.VMEM)
    S = jax.ShapeDtypeStruct
    return pl.pallas_call(
        functools.partial(backward_kernel, dim),
        out_shape=(S((2, 48, seq, rows), bf), S((2, 4, seq, width), bf), S((2, seq, width), bf),
                   S((2, 8, width), f32), S((2, 4, 8, rows), f32)),
        in_specs=[hbm, hbm, hbm, vmem, vmem] + [hbm] * 5,
        out_specs=[hbm, hbm, hbm, vmem, vmem],
        scratch_shapes=[v((48, seq, rows), bf), v((4, seq, width), bf), v((seq, width), f32), v((seq, width), bf),
                        v((seq, width), f32),
                        v((2, 4, rows, width), bf), v((2, 2, rows, width), bf), v((2, 4, seq, rows), bf), v((2, seq, rows), bf),
                        dma((2, 4)), dma((2, 2)), dma((2,)), dma((2,)), dma(()), dma(())],
        compiler_params=pltpu.CompilerParams(vmem_limit_bytes=56 * 2**20),
    )(x, cot, full, vecs, norms, *saved)


def butterfly(value):
    for axis, bits in (("section", 1), ("mp", 2), ("dp", 2)):
        for bit in range(bits):
            pairs = [(i, i ^ (1 << bit)) for i in range(lax.axis_size(axis))]
            value = value + lax.ppermute(value, axis, pairs)
    return value


def by_page(
    token_in,
    cotangent,
    w_qkv,
    qv_bias,
    w_attn_out,
    w_ffn_in,
    ffn_in_bias,
    w_ffn_out,
    out_biases,
    norm_gains,
    norm_shifts,
):
    core, place = lax.axis_index("section"), lax.axis_index("mp")
    is_first = core == 0
    width = token_in.shape[2]
    quarter = width // 4
    x = lax.dynamic_index_in_dim(token_in, core, 0, keepdims=False)
    cot = lax.dynamic_index_in_dim(cotangent, core, 0, keepdims=False)
    ffn_in_t = w_ffn_in[0].T.reshape(4, 1, quarter, width)
    ffn = jnp.concatenate([ffn_in_t, w_ffn_out[0].reshape(4, 1, quarter, width)], axis=1)
    shard = jnp.concatenate(
        [w_qkv[0].transpose(0, 2, 1), w_attn_out, ffn.reshape(8, quarter, width)], axis=0
    ).reshape(12, 2, quarter // 2, width)
    vec = high(jnp.concatenate([qv_bias[0], ffn_in_bias[0].reshape(4, quarter)], axis=0))
    vec = jnp.pad(vec, ((0, 2), (0, 0)))
    norms = jnp.concatenate([out_biases[0], norm_gains[0], norm_shifts[0]], axis=0)
    norms = jnp.pad(norms, ((0, 2), (0, 0)))
    full, vecs, all_norms = weight_gather(shard, vec, norms)
    saved = forward(HEAD_DIM, x, full, vecs, all_norms)
    left, right, grads, sums, vector_grads = backward(HEAD_DIM, x, cot, full, vecs, all_norms, saved)
    parts = grad_reduce(left, right)
    outs = saved[4]

    def trade(both):
        own = lax.dynamic_index_in_dim(both, core, 0)
        received = swap_core(lax.dynamic_index_in_dim(both, 1 - core, 0))
        return jnp.where(is_first, jnp.concatenate([own, received]), jnp.concatenate([received, own]))

    flat = jnp.concatenate([vector_grads.reshape(2, -1), sums.reshape(2, -1)], axis=1).reshape(2, -1, quarter)
    flat = lax.dynamic_index_in_dim(butterfly(flat), core, 0, keepdims=False)
    own = lax.dynamic_slice_in_dim(flat, place * 8, 8, 0)
    rows = flat[32:].reshape(8, width)
    piece = width // (lax.axis_size("mp") * lax.axis_size("dp"))
    begin = (place * lax.axis_size("dp") + lax.axis_index("dp")) * piece
    rows = lax.dynamic_slice_in_dim(rows, begin, piece, 1)
    parts = parts.reshape(12, quarter, width)
    return (
        trade(outs)[None],
        trade(grads)[None],
        high(parts[9:12].transpose(0, 2, 1))[None],
        own[0:2][None],
        high(parts[8])[None],
        high(parts[4:8].reshape(width, width).T)[None],
        own[2:6].reshape(1, width),
        high(parts[0:4].reshape(width, width))[None],
        rows[0:2][None],
        rows[2:4][None],
        rows[4:6][None],
    )


def swap_core(value):
    return lax.ppermute(value, "section", [(0, 1), (1, 0)])


def on_device(*args):
    token_in, w_qkv, ffn_in = args[0], args[2], args[5]
    fits = (
        lax.axis_size("section") == 2
        and lax.axis_size("mp") == 4
        and lax.axis_size("dp") == 4
        and token_in.shape == (2, SEQ, 1024)
        and w_qkv.shape[3] == 256
        and ffn_in.shape[2] == 1024
    )
    return by_page(*args) if fits else pipelined(*args)


def solution(mesh):
    return jax.shard_map(
        on_device,
        mesh=mesh,
        in_specs=(
            P(None, ("dp", "mp"), None),
            P(None, ("dp", "mp"), None),
            P("section", None, None, "mp"),
            P("section", None, "mp"),
            P("section", "mp", None),
            P("section", None, "mp"),
            P("section", "mp"),
            P("section", "mp", None),
            P("section", None, None),
            P("section", None, None),
            P("section", None, None),
        ),
        out_specs=(
            P("section", None, ("dp", "mp"), None),
            P("section", None, ("dp", "mp"), None),
            P("section", None, None, "mp"),
            P("section", None, "mp"),
            P("section", "mp", None),
            P("section", None, "mp"),
            P("section", "mp"),
            P("section", "mp", None),
            P("section", None, ("mp", "dp")),
            P("section", None, ("mp", "dp")),
            P("section", None, ("mp", "dp")),
        ),
        check_vma=False,
    )
```

```python
import functools
from functools import partial
import math

import jax
import jax.numpy as jnp
from jax import lax
from jax.experimental import pallas as pl
from jax.experimental.pallas import tpu as pltpu
from jax.sharding import PartitionSpec as P

HEAD_DIM = 64
SEQ = 512


def from_behind(value, axis, by):
    devices = lax.axis_size(axis)
    pairs = [(i, i + by) for i in range(devices) if 0 <= i + by < devices]
    return lax.ppermute(value, axis, pairs)


def norm_rows(values, gain_row, shift_row):
    average = jnp.mean(values, axis=-1, keepdims=True)
    centered = values - average
    variance = jnp.mean(centered * centered, axis=-1, keepdims=True)
    return centered * lax.rsqrt(variance + 1e-05) * gain_row + shift_row


def exact_gelu(values):
    return jax.nn.gelu(values, approximate=False)


def layer_forward(params, token_rows):
    (
        w_qkv,
        qv_bias,
        w_attn_out,
        w_ffn_in,
        ffn_in_bias,
        w_ffn_out,
        out_biases,
        norm_gains,
        norm_shifts,
    ) = params
    gathered = lax.all_gather(token_rows, "mp", axis=0, tiled=True)
    rows_all = gathered.shape[0]
    local_width = w_qkv.shape[2]
    local_heads = local_width // HEAD_DIM
    page_count = rows_all // SEQ
    scale_factor = 1.0 / math.sqrt(HEAD_DIM)
    bias_full = jnp.stack([qv_bias[0], jnp.zeros_like(qv_bias[0]), qv_bias[1]]).astype(jnp.float32)
    projected = (
        jnp.einsum("rd,cde->cre", gathered, w_qkv, preferred_element_type=jnp.float32)
        + bias_full[:, None, :]
    )
    heads_view = projected.astype(jnp.bfloat16).reshape(3, page_count, SEQ, local_heads, HEAD_DIM)
    scores = (
        jnp.einsum(
            "pqhe,pkhe->phqk", heads_view[0], heads_view[1], preferred_element_type=jnp.float32
        )
        * scale_factor
    )
    top_score = jnp.max(scores, axis=-1, keepdims=True)
    exponent = jnp.exp(scores - top_score)
    weights_soft = exponent / jnp.sum(exponent, axis=-1, keepdims=True)
    weights_low = weights_soft.astype(jnp.bfloat16)
    attended = jnp.einsum(
        "phqk,pkhe->pqhe", weights_low, heads_view[2], preferred_element_type=jnp.float32
    )
    attended = attended.reshape(rows_all, local_width).astype(jnp.bfloat16)
    attn_part = jnp.dot(attended, w_attn_out, preferred_element_type=jnp.float32)
    attn_rows = lax.psum_scatter(
        attn_part.astype(jnp.bfloat16), "mp", scatter_dimension=0, tiled=True
    ).astype(jnp.float32)
    residual_one = attn_rows + out_biases[0] + token_rows.astype(jnp.float32)
    first = norm_rows(residual_one, norm_gains[0], norm_shifts[0])
    first_all = lax.all_gather(first.astype(jnp.bfloat16), "mp", axis=0, tiled=True)
    pre_act = jnp.dot(first_all, w_ffn_in, preferred_element_type=jnp.float32) + ffn_in_bias.astype(
        jnp.float32
    )
    activated = exact_gelu(pre_act).astype(jnp.bfloat16)
    ffn_part = jnp.dot(activated, w_ffn_out, preferred_element_type=jnp.float32)
    ffn_rows = lax.psum_scatter(
        ffn_part.astype(jnp.bfloat16), "mp", scatter_dimension=0, tiled=True
    ).astype(jnp.float32)
    residual_two = ffn_rows + out_biases[1] + first
    result = norm_rows(residual_two, norm_gains[1], norm_shifts[1])
    kept_values = (
        gathered,
        heads_view,
        weights_soft,
        attended,
        residual_one,
        first_all,
        pre_act,
        activated,
        residual_two,
    )
    return (result, kept_values)


def layer_backward(params, kept_values, grad_out):
    (
        w_qkv,
        qv_bias,
        w_attn_out,
        w_ffn_in,
        ffn_in_bias,
        w_ffn_out,
        out_biases,
        norm_gains,
        norm_shifts,
    ) = params
    (
        gathered,
        heads_view,
        weights_soft,
        attended,
        residual_one,
        first_all,
        pre_act,
        activated,
        residual_two,
    ) = kept_values
    rows_all = gathered.shape[0]
    local_width = w_qkv.shape[2]
    local_heads = local_width // HEAD_DIM
    page_count = rows_all // SEQ
    scale_factor = 1.0 / math.sqrt(HEAD_DIM)
    unused_two, norm_two_back = jax.vjp(norm_rows, residual_two, norm_gains[1], norm_shifts[1])
    grad_res_two, grad_gain_two, grad_shift_two = norm_two_back(grad_out)
    grad_bias_two = jnp.sum(grad_res_two, axis=0)
    ffn_grad_all = lax.all_gather(grad_res_two.astype(jnp.bfloat16), "mp", axis=0, tiled=True)
    grad_w_ffn_out = jnp.einsum(
        "rf,rd->fd", activated, ffn_grad_all, preferred_element_type=jnp.float32
    )
    grad_act = jnp.einsum("rd,fd->rf", ffn_grad_all, w_ffn_out, preferred_element_type=jnp.float32)
    unused_gelu, gelu_back = jax.vjp(exact_gelu, pre_act)
    grad_pre = gelu_back(grad_act)[0].astype(jnp.bfloat16)
    grad_ffn_in_bias = jnp.sum(grad_pre.astype(jnp.float32), axis=0)
    grad_w_ffn_in = jnp.einsum("rd,rf->df", first_all, grad_pre, preferred_element_type=jnp.float32)
    first_part = jnp.einsum("rf,df->rd", grad_pre, w_ffn_in, preferred_element_type=jnp.float32)
    first_grad_rows = lax.psum_scatter(
        first_part.astype(jnp.bfloat16), "mp", scatter_dimension=0, tiled=True
    ).astype(jnp.float32)
    grad_first = first_grad_rows + grad_res_two
    unused_one, norm_one_back = jax.vjp(norm_rows, residual_one, norm_gains[0], norm_shifts[0])
    grad_res_one, grad_gain_one, grad_shift_one = norm_one_back(grad_first)
    grad_bias_one = jnp.sum(grad_res_one, axis=0)
    attn_grad_all = lax.all_gather(grad_res_one.astype(jnp.bfloat16), "mp", axis=0, tiled=True)
    grad_w_attn_out = jnp.einsum(
        "rk,rd->kd", attended, attn_grad_all, preferred_element_type=jnp.float32
    )
    grad_attended = jnp.einsum(
        "rd,kd->rk", attn_grad_all, w_attn_out, preferred_element_type=jnp.float32
    )
    grad_attended = grad_attended.astype(jnp.bfloat16).reshape(
        page_count, SEQ, local_heads, HEAD_DIM
    )
    weights_low = weights_soft.astype(jnp.bfloat16)
    grad_weights = jnp.einsum(
        "pqhe,pkhe->phqk", grad_attended, heads_view[2], preferred_element_type=jnp.float32
    )
    grad_values = jnp.einsum(
        "phqk,pqhe->pkhe", weights_low, grad_attended, preferred_element_type=jnp.float32
    )
    inner_total = jnp.sum(weights_soft * grad_weights, axis=-1, keepdims=True)
    grad_scores = (weights_soft * (grad_weights - inner_total)).astype(jnp.bfloat16)
    grad_queries = (
        jnp.einsum(
            "phqk,pkhe->pqhe", grad_scores, heads_view[1], preferred_element_type=jnp.float32
        )
        * scale_factor
    )
    grad_keys = (
        jnp.einsum(
            "phqk,pqhe->pkhe", grad_scores, heads_view[0], preferred_element_type=jnp.float32
        )
        * scale_factor
    )
    grad_proj = (
        jnp.stack([grad_queries, grad_keys, grad_values])
        .reshape(3, rows_all, local_width)
        .astype(jnp.bfloat16)
    )
    proj_sums = jnp.sum(grad_proj.astype(jnp.float32), axis=1)
    grad_qv_bias = jnp.stack([proj_sums[0], proj_sums[2]])
    grad_w_qkv = jnp.einsum("rd,cre->cde", gathered, grad_proj, preferred_element_type=jnp.float32)
    input_part = jnp.einsum("cre,cde->rd", grad_proj, w_qkv, preferred_element_type=jnp.float32)
    input_grad_rows = lax.psum_scatter(
        input_part.astype(jnp.bfloat16), "mp", scatter_dimension=0, tiled=True
    ).astype(jnp.float32)
    grad_in = input_grad_rows + grad_res_one
    matrix_grads = (
        grad_w_qkv,
        grad_qv_bias,
        grad_w_attn_out,
        grad_w_ffn_in,
        grad_ffn_in_bias,
        grad_w_ffn_out,
    )
    vector_grads = (
        jnp.stack([grad_bias_one, grad_bias_two]),
        jnp.stack([grad_gain_one, grad_gain_two]),
        jnp.stack([grad_shift_one, grad_shift_two]),
    )
    return (grad_in, matrix_grads, vector_grads)


def pipelined(
    token_in,
    cotangent,
    w_qkv,
    qv_bias,
    w_attn_out,
    w_ffn_in,
    ffn_in_bias,
    w_ffn_out,
    out_biases,
    norm_gains,
    norm_shifts,
):
    params = (
        w_qkv[0],
        qv_bias[0],
        w_attn_out[0],
        w_ffn_in[0],
        ffn_in_bias[0],
        w_ffn_out[0],
        out_biases[0],
        norm_gains[0],
        norm_shifts[0],
    )
    micro_count = token_in.shape[0]
    section_index = lax.axis_index("section")
    is_first = section_index == 0
    zero_rows = jnp.zeros(token_in.shape[1:], jnp.bfloat16)
    run_forward = partial(layer_forward, params)
    run_backward = partial(layer_backward, params)

    def forward_step(step_index, carry):
        received, saved, stored = carry
        own_micro = step_index - section_index
        is_valid = (own_micro >= 0) & (own_micro < micro_count)
        slot_index = jnp.clip(own_micro, 0, micro_count - 1)
        first_rows = lax.dynamic_index_in_dim(
            token_in, jnp.minimum(step_index, micro_count - 1).astype(jnp.int32), 0, keepdims=False
        )
        layer_in = jnp.where(is_first, first_rows, received)
        result, unused_kept = run_forward(layer_in)
        result_low = result.astype(jnp.bfloat16)
        old_saved = lax.dynamic_index_in_dim(saved, slot_index, 0, keepdims=False)
        saved = lax.dynamic_update_index_in_dim(
            saved, jnp.where(is_valid, layer_in, old_saved), slot_index, 0
        )
        old_stored = lax.dynamic_index_in_dim(stored, slot_index, 0, keepdims=False)
        stored = lax.dynamic_update_index_in_dim(
            stored, jnp.where(is_valid, result_low, old_stored), slot_index, 0
        )
        received = from_behind(result_low, "section", 1)
        return (received, saved, stored)

    start_carry = (zero_rows, jnp.zeros_like(token_in), jnp.zeros_like(token_in))
    unused_received, saved, stored = lax.fori_loop(0, micro_count + 1, forward_step, start_carry)
    matrix_zero = tuple((jnp.zeros(entry.shape, jnp.float32) for entry in params[:6]))
    vector_zero = (
        jnp.zeros(out_biases.shape[1:], jnp.float32),
        jnp.zeros(norm_gains.shape[1:], jnp.float32),
        jnp.zeros(norm_shifts.shape[1:], jnp.float32),
    )

    def backward_step(step_index, carry):
        received_grad, grad_store, matrix_sums, vector_sums = carry
        own_micro = step_index - (1 - section_index)
        is_valid = (own_micro >= 0) & (own_micro < micro_count)
        slot_index = jnp.clip(own_micro, 0, micro_count - 1)
        layer_in = lax.dynamic_index_in_dim(saved, slot_index, 0, keepdims=False)
        from_last = lax.dynamic_index_in_dim(cotangent, slot_index, 0, keepdims=False)
        grad_out = jnp.where(is_first, received_grad, from_last).astype(jnp.float32)
        unused_result, kept_values = run_forward(layer_in)
        grad_in, matrix_grads, vector_grads = run_backward(kept_values, grad_out)
        matrix_grads = tuple((jnp.where(is_valid, entry, 0.0) for entry in matrix_grads))
        vector_grads = tuple((jnp.where(is_valid, entry, 0.0) for entry in vector_grads))
        grad_low = grad_in.astype(jnp.bfloat16)
        old_piece = lax.dynamic_index_in_dim(grad_store, slot_index, 0, keepdims=False)
        grad_store = lax.dynamic_update_index_in_dim(
            grad_store, jnp.where(is_valid, grad_low, old_piece), slot_index, 0
        )
        grad_one, grad_two, grad_three, grad_four, grad_five, grad_six = matrix_grads
        matrix_grads = (
            lax.psum(grad_one.astype(jnp.bfloat16), "dp").astype(jnp.float32),
            lax.psum(grad_two.astype(jnp.bfloat16), "dp").astype(jnp.float32),
            lax.psum(grad_three.astype(jnp.bfloat16), "dp").astype(jnp.float32),
            lax.psum(grad_four.astype(jnp.bfloat16), "dp").astype(jnp.float32),
            lax.psum(grad_five.astype(jnp.bfloat16), "dp").astype(jnp.float32),
            lax.psum(grad_six.astype(jnp.bfloat16), "dp").astype(jnp.float32),
        )
        matrix_sums = tuple((total + extra for total, extra in zip(matrix_sums, matrix_grads)))
        vector_sums = tuple((total + extra for total, extra in zip(vector_sums, vector_grads)))
        received_grad = from_behind(grad_low, "section", -1)
        return (received_grad, grad_store, matrix_sums, vector_sums)

    back_carry = (zero_rows, jnp.zeros_like(token_in), matrix_zero, vector_zero)
    unused_grad, grad_store, matrix_sums, vector_sums = lax.fori_loop(
        0, micro_count + 1, backward_step, back_carry
    )
    bias_total, gain_total, shift_total = vector_sums
    bias_part, gain_part, shift_part = (
        lax.psum_scatter(bias_total, ("mp", "dp"), scatter_dimension=1, tiled=True),
        lax.psum_scatter(gain_total, ("mp", "dp"), scatter_dimension=1, tiled=True),
        lax.psum_scatter(shift_total, ("mp", "dp"), scatter_dimension=1, tiled=True),
    )
    return (
        stored[None],
        grad_store[None],
        matrix_sums[0][None],
        matrix_sums[1][None],
        matrix_sums[2][None],
        matrix_sums[3][None],
        matrix_sums[4][None],
        matrix_sums[5][None],
        bias_part[None],
        gain_part[None],
        shift_part[None],
    )


MESH = pl.DeviceIdType.MESH
CHUNKS = 24
TRIPLES = 8
SCALE = 0.125


def low(value):
    return value.astype(jnp.bfloat16)


def high(value):
    return value.astype(jnp.float32)


def remote(src, dst, send, recv, device):
    return pltpu.make_async_remote_copy(
        src_ref=src, dst_ref=dst, send_sem=send, recv_sem=recv, device_id=device, device_id_type=MESH
    )


def neighbours():
    c, p, d = lax.axis_index("section"), lax.axis_index("mp"), lax.axis_index("dp")
    return {
        "core": (1 - c, p, d),
        "x": (c, p + 1 - 2 * lax.rem(p, 2), d),
        "y": (c, lax.rem(p + 2, 4), d),
        "across": (c, p, 3 - d),
        "inner": (c, p, jnp.where(d == 0, 1, 2)),
        "outer": (c, p, jnp.where(d == 1, 0, 3)),
    }


def places():
    p = lax.axis_index("mp")
    return [p, p + 1 - 2 * lax.rem(p, 2), lax.rem(p + 2, 4), 3 - p]


def dot(a, b):
    return jnp.dot(a, b, preferred_element_type=jnp.float32)


def dot_tn(a, b):
    return lax.dot_general(a, b, (((0,), (0,)), ((), ())), preferred_element_type=jnp.float32)


def dot_nt(a, b):
    return lax.dot_general(a, b, (((1,), (1,)), ((), ())), preferred_element_type=jnp.float32)


def standard(values):
    average = jnp.mean(values, axis=-1, keepdims=True)
    centered = values - average
    variance = jnp.mean(centered * centered, axis=-1, keepdims=True)
    scale = lax.rsqrt(variance + 1e-05)
    return centered * scale, scale


def softmax(q, k):
    scores = dot_nt(q * jnp.asarray(SCALE, q.dtype), k)
    exponent = jnp.exp(scores - jnp.max(scores, axis=-1, keepdims=True))
    return exponent * (1.0 / jnp.sum(exponent, axis=-1, keepdims=True))


def by_rows(rows, step, body):
    def run(i, carry):
        body(pl.ds(pl.multiple_of(i * step, step), step))
        return carry

    lax.fori_loop(0, rows // step, run, 0)


def ffn_block(hb, w, bias, save, acc):
    z = dot_nt(hb[...], w[0]) + bias
    inner = 0.5 + 0.5 * lax.erf(z * math.sqrt(0.5))
    g = low(z * inner)
    save[0] = g
    save[1] = low(inner + z * jnp.exp(-0.5 * z * z) * (1.0 / math.sqrt(2.0 * math.pi)))
    acc[...] += dot(g, w[1])


def first_norm(x, nrm, acc, u1, hb):
    def run(rows):
        u = acc[rows] + nrm[0:1] + high(x[rows])
        u1[rows] = u
        h = standard(u)[0] * nrm[2:3] + nrm[4:5]
        hb[rows] = low(h)
        acc[rows] = h + nrm[1:2]

    by_rows(acc.shape[0], 64, run)


def second_norm(nrm, acc, u2, out):
    def run(rows):
        u = acc[rows]
        u2[rows] = u
        out[rows] = low(standard(u)[0] * nrm[3:4] + nrm[5:6])

    by_rows(acc.shape[0], 64, run)


def norm_back(u, grad, gain, sums, at, out_low, out_acc):
    def run(rows):
        g = high(grad[rows])
        xhat, scale = standard(u[rows])
        scaled = g * gain
        du = scale * (
            scaled
            - jnp.mean(scaled, axis=-1, keepdims=True)
            - xhat * jnp.mean(scaled * xhat, axis=-1, keepdims=True)
        )
        out_low[rows] = low(du)
        out_acc[rows] = du
        for row, term in ((at[0], du), (at[1], g * xhat), (at[2], g)):
            sums[row : row + 1] += jnp.sum(term, axis=0, keepdims=True)

    by_rows(u.shape[0], 64, run)


def ffn_back_block(dfb, w, gd, acc, dz_out):
    dz = low(dot_nt(dfb[...], w[1]) * high(gd))
    dz_out[...] = dz
    acc[...] += dot(dz, w[0])
    return jnp.sum(high(dz), axis=0, keepdims=True)


def attention_back_block(dab, w, qkv, dq_out, dk_out, dv_out, acc, dim):
    dob = low(dot_nt(dab[...], w[3]))
    for j in range(dob.shape[1] // dim):
        cols = slice(j * dim, (j + 1) * dim)
        q, k, v, do = qkv[0, :, cols], qkv[1, :, cols], qkv[2, :, cols], dob[:, cols]
        a = softmax(q, k)
        da = dot_nt(do, v)
        ds = low(a * (da - jnp.sum(a * da, axis=-1, keepdims=True)))
        dv_out[:, cols] = low(dot_tn(low(a), do))
        dq_out[:, cols] = low(dot(ds, k) * SCALE)
        dk_out[:, cols] = low(dot_tn(ds, q) * SCALE)
    acc[...] += dot(dq_out[...], w[0]) + dot(dk_out[...], w[1]) + dot(dv_out[...], w[2])


def weight_copies(full, layer, kind, p, b, buf, sem, rows):
    width = 4 * rows
    if kind == 0:
        starts = [c * width + p * rows for c in range(4)]
    else:
        starts = [4 * width + t * 4 * width + p * width + b * rows for t in range(2)]
    return [
        pltpu.make_async_copy(full.at[layer, pl.ds(pl.multiple_of(start, rows), rows)], buf.at[n], sem.at[n])
        for n, start in enumerate(starts)
    ]


def project_block(x, w, vec, save, dim):
    rows = x[...]
    q = low(dot_nt(rows, w[0]) + vec[0:1])
    k = low(dot_nt(rows, w[1]))
    v = low(dot_nt(rows, w[2]) + vec[1:2])
    save[0], save[1], save[2] = q, k, v
    for j in range(q.shape[1] // dim):
        cols = slice(j * dim, (j + 1) * dim)
        save[3, :, cols] = low(dot(low(softmax(q[:, cols], k[:, cols])), v[:, cols]))


def gather_forward_kernel(
    dim, x_in, shard, vec, norm_in, full, vecs, norms, qkvo, gd, us, hbs, outs,
    x, acc, u, hb, wa, wf, sa, sf, wasem, wfsem, sasem, sfsem, usem,
    ini_s, ini_r, loc, x1ss, x1rs, y1ss, y1rs, x2ss, x2rs, y2ss, y2rs, zs, zr, cs, cr, vs, vr, vloc,
):
    c, p, d = lax.axis_index("section"), lax.axis_index("mp"), lax.axis_index("dp")
    near = neighbours()
    near["pair"] = (c, p, d + 1 - 2 * lax.rem(d, 2))
    spots = places()
    rows = shard.shape[1] // 2
    half = rows // 2
    odd = lax.rem(d, 2)
    others = [(cc, spots[r], d) for r in range(4) for cc in (c, 1 - c)][1:]

    barrier = pltpu.get_barrier_semaphore()
    for device in others + [near["pair"]]:
        pl.semaphore_signal(barrier, inc=1, device_id=device, device_id_type=MESH)
    pl.semaphore_wait(barrier, 8)

    def place_of(s, spot, h):
        k = lax.rem(s, 12)
        b, kind = (k - 4) // 2, lax.rem(k, 2)
        row = jnp.where(k < 4, k * 8 + spot * 2, 32 + kind * 32 + spot * 8 + b * 2)
        return s // 12, (row + h) * rows

    def block(s, spot, h, start=0, size=rows):
        layer, row = place_of(s, spot, h)
        return full.at[layer, pl.ds(pl.multiple_of(row + start, half), size)]

    def init_place(k, layer):
        row = place_of(12 * layer + k, p, 0)[1]
        return full.at[layer, pl.ds(pl.multiple_of(row, half), 2 * rows)]

    def init_local(k):
        return pltpu.make_async_copy(shard.at[k], init_place(k, c), loc.at[k])

    def init_remote(k):
        return remote(shard.at[k], init_place(k, c), ini_s.at[k], ini_r.at[k], near["core"])

    def init_wait(k):
        there = init_place(k, 1 - c)
        remote(there, there, ini_s.at[k], ini_r.at[k], near["core"]).wait_recv()

    def small():
        copies = [remote(vec, vecs.at[c, p], vs.at[i], vr.at[c, p], device) for i, device in enumerate(others)]
        copies.append(remote(norm_in, norms.at[c], vs.at[7], vr.at[0, 4], near["core"]))
        return copies

    def small_local():
        return [
            pltpu.make_async_copy(vec, vecs.at[c, p], vloc.at[0]),
            pltpu.make_async_copy(norm_in, norms.at[c], vloc.at[1]),
        ]

    def hop(s, spot, name, pick):
        ss, rs = (x1ss, x1rs) if pick == "x" else (y1ss, y1rs)
        b = block(s, spot, c)
        return remote(b, b, ss.at[s], rs.at[s], near[name])

    def first(s, name):
        return hop(s, p, name, name)

    def arrived(s, name):
        return hop(s, spots[1] if name == "x" else spots[2], name, name)

    def relay(s, name, spot=None):
        if name == "x":
            b = block(s, spots[2] if spot is None else spot, c, 0, half)
            return remote(b, b, x2ss.at[s], x2rs.at[s], near["x"])
        b = block(s, spots[1] if spot is None else spot, c, half, half)
        return remote(b, b, y2ss.at[s], y2rs.at[s], near["y"])

    def relayed(s, name):
        return relay(s, name, spots[3])

    def to_pair(s, r):
        b = block(s, spots[r], c)
        return remote(b, b, zs.at[s, r - 1], zr.at[s, r - 1], near["pair"])

    def to_core(s, r):
        b = block(s, spots[r], c)
        return remote(b, b, cs.at[s, r - 1], cr.at[s, r - 1], near["core"])

    def from_core(s, r):
        b = block(s, spots[r], 1 - c)
        return remote(b, b, cs.at[s, r - 1], cr.at[s, r - 1], near["core"])

    def stage_a(t):
        for j in range(3):
            s = 3 * t + j

            @pl.when(s // 12 != c)
            def _():
                init_wait(lax.rem(s, 12))

        for s in (3 * t, 3 * t + 1 + odd):
            first(s, "x").start()
            first(s, "y").start()

    def stage_b(t):
        for n, s in enumerate((3 * t, 3 * t + 1 + odd)):
            arrived(s, "x").wait_recv()
            relay(s, "y").start()
            arrived(s, "y").wait_recv()
            relay(s, "x").start()
            for r in (1, 2):
                to_core(s, r).start()
                if n:
                    to_pair(s, r).start()

    def stage_c(t):
        for n, s in enumerate((3 * t, 3 * t + 1 + odd)):
            relayed(s, "x").wait_recv()
            relayed(s, "y").wait_recv()
            to_core(s, 3).start()
            if n:
                to_pair(s, 3).start()

    def stage_d(t):
        s = 3 * t + 2 - odd
        for r in (1, 2, 3):
            to_pair(s, r).wait_recv()
            to_core(s, r).start()

    def stage_e(t):
        for j in range(3):
            for r in (1, 2, 3):
                from_core(3 * t + j, r).wait_recv()

    def stage_f(t):
        for n, s in enumerate((3 * t, 3 * t + 1 + odd)):
            first(s, "x").wait_send()
            first(s, "y").wait_send()
            relay(s, "x").wait_send()
            relay(s, "y").wait_send()
            for r in (1, 2, 3):
                if n:
                    to_pair(s, r).wait_send()
        for j in range(3):
            for r in (1, 2, 3):
                to_core(3 * t + j, r).wait_send()

    wide = 2 * rows

    def attn(l, q, slot):
        return weight_copies(full, l, 0, q, 0, wa.at[slot], wasem.at[slot], wide)[:3]

    def attn_out(l, q, slot):
        return weight_copies(full, l, 0, q, 0, wa.at[slot], wasem.at[slot], wide)[3]

    def ffn(l, n, slot):
        return weight_copies(full, l, 1, lax.rem(n, 4), n // 4, wf.at[slot], wfsem.at[slot], wide)

    def save_attn(l, q, slot):
        return pltpu.make_async_copy(sa.at[q], qkvo.at[l, q], sasem.at[slot])

    def save_ffn(l, n, slot):
        return pltpu.make_async_copy(sf.at[slot], gd.at[l, 4 * lax.rem(n, 4) + n // 4], sfsem.at[slot])

    def attention_segment(l):
        for copy in attn(l, 0, 0):
            copy.start()

        def run(q, carry):
            slot = lax.rem(q, 2)
            for copy in attn(l, q, slot):
                copy.wait()

            @pl.when(q < 3)
            def _():
                for copy in attn(l, q + 1, 1 - slot):
                    copy.start()

            project_block(x, wa.at[slot], vecs[l, q], sa.at[q], dim)
            save_attn(l, q, q).start()
            return carry

        lax.fori_loop(0, 4, run, 0)

    def ffn_segment(l, begin, count):
        for copy in ffn(l, begin, 0):
            copy.start()

        def run(m, carry):
            slot = lax.rem(m, 2)
            n = begin + m
            for copy in ffn(l, n, slot):
                copy.wait()

            @pl.when(m < count - 1)
            def _():
                for copy in ffn(l, n + 1, 1 - slot):
                    copy.start()

            @pl.when(m >= 2)
            def _():
                save_ffn(l, n - 2, slot).wait()

            ffn_block(hb, wf.at[slot], vecs[l, lax.rem(n, 4), pl.ds(2 + n // 4, 1)], sf.at[slot], acc)
            save_ffn(l, n, slot).start()
            return carry

        lax.fori_loop(0, count, run, 0)
        for m in (count - 2, count - 1):
            save_ffn(l, begin + m, m % 2).wait()

    def keep(l, which):
        if which == 2:
            return pltpu.make_async_copy(hb, hbs.at[l], usem.at[2])
        if which == 3:
            return pltpu.make_async_copy(x, outs.at[l], usem.at[3])
        return pltpu.make_async_copy(u, us.at[l, which], usem.at[which])

    def out_segment(l):
        for q in range(2):
            attn_out(l, q, q).start()
        acc[...] = jnp.zeros_like(acc)
        for q in range(4):
            attn_out(l, q, q % 2).wait()
            acc[...] += dot(sa[q, 3], wa[q % 2, 3])
            if q < 2:
                attn_out(l, q + 2, q).start()
        for q in range(4):
            save_attn(l, q, q).wait()

        @pl.when(l == 1)
        def _():
            keep(0, 1).wait()

        first_norm(x, norms.at[l], acc, u, hb)
        keep(l, 0).start()
        keep(l, 2).start()

    def end_segment(l):
        keep(l, 0).wait()
        keep(l, 2).wait()

        @pl.when(l == 1)
        def _():
            keep(0, 3).wait()

        second_norm(norms.at[l], acc, u, x)
        keep(l, 1).start()
        keep(l, 3).start()

    def compute(t):
        l, part = t // 4, lax.rem(t, 4)

        @pl.when(t == 0)
        def _():
            for copy in small_local():
                copy.wait()
            for copy in small():
                copy.wait_send()
            for cc, spot in [(cc, spots[r]) for r in range(4) for cc in (c, 1 - c)][1:]:
                remote(vec, vecs.at[cc, spot], vs.at[0], vr.at[cc, spot], near["core"]).wait_recv()
            remote(norm_in, norms.at[1 - c], vs.at[7], vr.at[0, 4], near["core"]).wait_recv()

        @pl.when(part == 0)
        def _():
            attention_segment(l)

        @pl.when(part == 1)
        def _():
            out_segment(l)

        @pl.when(part > 0)
        def _():
            ffn_segment(l, 4 * (part - 1), 4)

        @pl.when(part == 3)
        def _():
            ffn_segment(l, 12, 4)
            end_segment(l)

    def begin(k, carry):
        init_local(k).start()
        init_remote(k).start()
        return carry

    lax.fori_loop(0, 12, begin, 0)
    for copy in small_local() + small():
        copy.start()
    x[...] = x_in[...]

    def local_done(k, carry):
        init_local(k).wait()
        return carry

    lax.fori_loop(0, 12, local_done, 0)

    def step(i, carry):
        def run(stage, lag):
            @pl.when((i >= lag) & (i < TRIPLES + lag))
            def _():
                stage(i - lag)

        for lag, stage in enumerate((stage_a, stage_b, stage_c, stage_d, stage_e)):
            run(stage, lag)
        run(compute, 4)
        run(stage_f, 5)
        return carry

    lax.fori_loop(0, TRIPLES + 5, step, 0)

    def sent(k, carry):
        init_remote(k).wait_send()
        return carry

    lax.fori_loop(0, 12, sent, 0)
    keep(1, 1).wait()
    keep(1, 3).wait()


def gather_forward(dim, x, shard, vec, norms):
    rows, width = shard.shape[1:]
    seq = x.shape[0]
    bf, f32, dma, v = jnp.bfloat16, jnp.float32, pltpu.SemaphoreType.DMA, pltpu.VMEM
    hbm, vmem = pl.BlockSpec(memory_space=pl.ANY), pl.BlockSpec(memory_space=pltpu.VMEM)
    S = jax.ShapeDtypeStruct
    return pl.pallas_call(
        functools.partial(gather_forward_kernel, dim),
        out_shape=(
            S((2, 48 * rows, width), bf), S((2, 4) + vec.shape, f32), S((2,) + norms.shape, f32),
            S((2, 4, 4, seq, rows), bf), S((2, 16, 2, seq, rows), bf), S((2, 2, seq, width), f32),
            S((2, seq, width), bf), S((2, seq, width), bf),
        ),
        in_specs=[vmem, vmem, vmem, vmem],
        out_specs=[hbm, vmem, vmem] + [hbm] * 5,
        scratch_shapes=[
            v((seq, width), bf), v((seq, width), f32), v((seq, width), f32), v((seq, width), bf),
            v((2, 4, rows, width), bf), v((2, 2, rows, width), bf), v((4, 4, seq, rows), bf), v((2, 2, seq, rows), bf),
            dma((2, 4)), dma((2, 2)), dma((4,)), dma((2,)), dma((4,)),
        ] + [dma((12,))] * 3 + [dma((24,))] * 8 + [dma((24, 3))] * 4 + [dma((8,)), dma((2, 5)), dma((2,))],
        compiler_params=pltpu.CompilerParams(collective_id=0, has_side_effects=True, vmem_limit_bytes=56 * 2**20),
    )(x, shard, vec, norms)


def backward_reduce_kernel(
    dim, x_in, cot, full, vecs, norms, qkvo, gd, us, hbs, outs, out, dxs, totals,
    left, right, acc, g, u, wa, wf, da, df, trades,
    sendc, recvc, keep, x1s, x1r, y1s, y1r, part, base, x2s, x2r, y2s, y2r, mid,
    zk, zs1, zr1, zs2, zr2, zs3, zr3,
    wasem, wfsem, dasem, dfsem, gsem, osem4, bsem, tss, trs,
    cs, cr, x1ss, x1rs, y1ss, y1rs, x2ss, x2rs, y2ss, y2rs, z1ss, z1rs, z2ss, z2rs, z3ss, z3rs, os, orr,
):
    c, p, d = lax.axis_index("section"), lax.axis_index("mp"), lax.axis_index("dp")
    near = neighbours()
    near["pair"] = (c, p, d + 1 - 2 * lax.rem(d, 2))
    near["far"] = (c, p, lax.rem(d + 2, 4))
    spots = places()
    is_end = (d == 0) | (d == 3)
    is_mid = jnp.logical_not(is_end)
    rows = sendc.shape[2]
    half = rows // 2
    wide = 2 * rows

    barrier = pltpu.get_barrier_semaphore()

    def signal(device):
        pl.semaphore_signal(barrier, inc=1, device_id=device, device_id_type=MESH)

    for name in ("core", "x", "y", "pair", "far"):
        signal(near[name])

    @pl.when(is_end)
    def _():
        pl.semaphore_wait(barrier, 5)

    @pl.when(is_mid)
    def _():
        signal(near["across"])
        pl.semaphore_wait(barrier, 6)

    def core_copy(s):
        a, b = lax.rem(s, 2), lax.rem(s, 4)
        return remote(sendc.at[a], recvc.at[b], cs.at[a], cr.at[b], near["core"])

    def link_copy(s, src, dst, ss, rs, name):
        a, b = lax.rem(s, 2), lax.rem(s, 4)
        return remote(src.at[a], dst.at[b], ss.at[a], rs.at[b], near[name])

    x1 = lambda s: link_copy(s, x1s, x1r, x1ss, x1rs, "x")
    y1 = lambda s: link_copy(s, y1s, y1r, y1ss, y1rs, "y")
    x2 = lambda s: link_copy(s, x2s, x2r, x2ss, x2rs, "x")
    y2 = lambda s: link_copy(s, y2s, y2r, y2ss, y2rs, "y")
    z1 = lambda s: link_copy(s, zs1, zr1, z1ss, z1rs, "inner")
    z2 = lambda s: link_copy(s, zs2, zr2, z2ss, z2rs, "across")

    def z3(s):
        b = lax.rem(s, 6)
        return remote(zs3.at[b], zr3.at[b], z3ss.at[b], z3rs.at[b], near["outer"])

    def stage0(s):
        k, slot = lax.rem(s, 12), lax.rem(s, 2)
        stride = jnp.where(k < 8, 4, 1)
        first = jnp.where(k < 4, k, jnp.where(k < 8, 12 + k, jnp.where(k == 8, 32, 36 + 4 * (k - 9))))
        kind = jnp.where(k < 4, 0, jnp.where(k < 8, 1, jnp.where(k == 8, 2, 3)))
        for r in range(4):
            whole = dot_tn(left[first + stride * spots[r]], right[kind])
            keep[slot, r] = jnp.where(c == 0, whole[:rows], whole[rows:])
            sendc[slot, r] = low(jnp.where(c == 0, whole[rows:], whole[:rows]))
        core_copy(s).start()

    def stage1(s):
        a, b = lax.rem(s, 2), lax.rem(s, 4)
        core_copy(s).wait()
        far = keep[a, 3] + high(recvc[b, 3])
        x1s[a, 0] = low(far[:half])
        y1s[a, 0] = low(far[half:])
        by_x = keep[a, 1] + high(recvc[b, 1])
        x1s[a, 1] = low(by_x[:half])
        part[a, 0] = by_x[half:]
        by_y = keep[a, 2] + high(recvc[b, 2])
        y1s[a, 1] = low(by_y[half:])
        part[a, 1] = by_y[:half]
        x1(s).start()
        y1(s).start()
        base[a] = keep[a, 0] + high(recvc[b, 0])

    def stage2(s):
        a, b = lax.rem(s, 2), lax.rem(s, 4)
        x1(s).wait()
        y1(s).wait()
        y2s[a] = low(part[a, 1] + high(x1r[b, 0]))
        x2s[a] = low(part[a, 0] + high(y1r[b, 0]))
        own = base[a]
        mid[a, pl.ds(0, half)] = own[:half] + high(x1r[b, 1])
        mid[a, pl.ds(half, half)] = own[half:] + high(y1r[b, 1])
        x2(s).start()
        y2(s).start()

    def stage3(s):
        a, b = lax.rem(s, 2), lax.rem(s, 4)
        x2(s).wait()
        y2(s).wait()
        own = mid[a]
        top = own[:half] + high(y2r[b])
        end = own[half:] + high(x2r[b])

        @pl.when(is_end)
        def _():
            zs1[a, pl.ds(0, half)] = low(top)
            zs1[a, pl.ds(half, half)] = low(end)
            z1(s).start()

        @pl.when(is_mid)
        def _():
            zk[a, pl.ds(0, half)] = top
            zk[a, pl.ds(half, half)] = end

    def stage4(s):
        a, b = lax.rem(s, 2), lax.rem(s, 4)

        @pl.when(is_end)
        def _():
            z1(s).wait_send()

        @pl.when(is_mid)
        def _():
            z1(s).wait_recv()
            zs2[a] = low(zk[a] + high(zr1[b]))
            z2(s).start()

    def stage5(s):
        a, b = lax.rem(s, 2), lax.rem(s, 4)

        @pl.when(is_mid)
        def _():
            z2(s).wait()
            zs3[lax.rem(s, 6)] = low(high(zs2[a]) + high(zr2[b]))
            z3(s).start()

    def stage6(s, begin):
        layer, k, b = 1 - s // 12, lax.rem(s, 12), lax.rem(s, 6)

        def finish(source):
            @pl.when(layer == c)
            def _():
                copy = pltpu.make_async_copy(source.at[b], out.at[k, c], os.at[b])
                copy.start() if begin else copy.wait()

            @pl.when(layer != c)
            def _():
                copy = remote(source.at[b], out.at[k, c], os.at[b], orr.at[k], near["core"])
                copy.start() if begin else copy.wait_send()

        @pl.when(is_end)
        def _():
            if begin:
                z3(s).wait_recv()
            finish(zr3)

        @pl.when(is_mid)
        def _():
            if begin:
                z3(s).wait_send()
            finish(zs3)

    def load_g(l, n):
        return pltpu.make_async_copy(gd.at[l, n, 0], left.at[n], gsem.at[n])

    def load_o(l, n):
        return pltpu.make_async_copy(qkvo.at[l, n, 3], left.at[32 + n], osem4.at[n])

    def load_h(l):
        return pltpu.make_async_copy(hbs.at[l], right.at[1], bsem.at[0])

    def load_x(source):
        return pltpu.make_async_copy(source, right.at[3], bsem.at[1])

    def load_u(l, which):
        return pltpu.make_async_copy(us.at[l, which], u, bsem.at[2])

    def ffn(l, n, slot):
        return weight_copies(full, l, 1, lax.rem(n, 4), n // 4, wf.at[slot], wfsem.at[slot], wide) + [
            pltpu.make_async_copy(gd.at[l, 4 * lax.rem(n, 4) + n // 4, 1], df.at[slot], dfsem.at[slot])
        ]

    def attn(l, q, slot):
        return weight_copies(full, l, 0, q, 0, wa.at[slot], wasem.at[slot], wide) + [
            pltpu.make_async_copy(qkvo.at[l, q], da.at[slot], dasem.at[slot])
        ]

    def store_dx(l):
        return pltpu.make_async_copy(g, dxs.at[l], bsem.at[3])

    def ahead(l):
        load_u(l, 1).start()
        for copy in ffn(l, 0, 0) + attn(l, 0, 0):
            copy.start()

    def operands(l):
        def run(n, carry):
            load_g(l, n).start()
            return carry

        lax.fori_loop(0, 16, run, 0)
        for n in range(4):
            load_o(l, n).start()
        load_h(l).start()

    def operands_there(l):
        def run(n, carry):
            load_g(l, n).wait()
            return carry

        lax.fori_loop(0, 16, run, 0)
        for n in range(4):
            load_o(l, n).wait()
        load_h(l).wait()

    def top_segment(l):
        load_u(l, 1).wait()
        norm_back(u, g, norms[l, 3:4], totals.at[l], (1, 3, 5), right.at[0], acc)
        load_u(l, 0).start()

        @pl.when(l == 1)
        def _():
            operands_there(1)

    def ffn_segment(l, b):
        def run(q, carry):
            n = 4 * b + q
            slot = lax.rem(n, 2)
            for copy in ffn(l, n, slot):
                copy.wait()

            @pl.when(n < 15)
            def _():
                for copy in ffn(l, n + 1, 1 - slot):
                    copy.start()

            row = ffn_back_block(right.at[0], wf.at[slot], df[slot], acc, left.at[16 + 4 * q + b])
            totals[l, pl.ds(10 + b, 1), pl.ds(pl.multiple_of(q * wide, wide), wide)] = row
            return carry

        lax.fori_loop(0, 4, run, 0)

    def middle_segment(l):
        load_u(l, 0).wait()
        norm_back(u, acc, norms[l, 2:3], totals.at[l], (0, 2, 4), right.at[2], acc)

    def attention_segment(l, q):
        slot = lax.rem(q, 2)
        for copy in attn(l, q, slot):
            copy.wait()

        @pl.when(q < 3)
        def _():
            for copy in attn(l, q + 1, 1 - slot):
                copy.start()

        dq, dk, dv = left.at[36 + q], left.at[40 + q], left.at[44 + q]
        attention_back_block(right.at[2], wa.at[slot], da.at[slot], dq, dk, dv, acc, dim)
        cols = pl.ds(pl.multiple_of(q * wide, wide), wide)
        totals[l, 8:9, cols] = jnp.sum(high(dq[...]), axis=0, keepdims=True)
        totals[l, 9:10, cols] = jnp.sum(high(dv[...]), axis=0, keepdims=True)

    def end_segment(l):
        by_rows(acc.shape[0], 64, lambda r: g.__setitem__(r, low(acc[r])))
        store_dx(l).start()

        @pl.when(l == 1)
        def _():
            ahead(0)

    def segment(i):
        l, j = 1 - i // 9, lax.rem(i, 9)

        @pl.when(i == 9)
        def _():
            operands(0)
            store_dx(1).wait()

        @pl.when(j == 0)
        def _():
            top_segment(l)

        @pl.when(j < 4)
        def _():
            ffn_segment(l, j)

        @pl.when(j == 4)
        def _():
            middle_segment(l)

        @pl.when((j >= 4) & (j < 8))
        def _():
            attention_segment(l, j - 4)

        @pl.when(j == 8)
        def _():
            end_segment(l)

        @pl.when(i == 8)
        def _():
            load_x(outs.at[0]).wait()

        @pl.when(i == 12)
        def _():
            operands_there(0)
            load_x(x_in).start()

        @pl.when(i == 16)
        def _():
            load_x(x_in).wait()

    def trade(k, name):
        copy = remote(totals, trades.at[k], tss.at[k], trs.at[k], near[name])
        copy.start()
        copy.wait()
        totals[...] += trades[k]

    first_rows = pltpu.make_async_copy(cot, g, bsem.at[3])
    first_rows.start()
    ahead(1)
    operands(1)
    load_x(outs.at[0]).start()
    totals[...] = jnp.zeros_like(totals)
    first_rows.wait()

    def step(i, carry):
        def run(stage, lag, *extra):
            @pl.when((i >= lag) & (i < CHUNKS + lag))
            def _():
                stage(i - lag, *extra)

        run(stage1, 1)

        @pl.when(i < 18)
        def _():
            segment(i)

        run(stage0, 0)
        run(stage2, 2)
        run(stage3, 3)
        run(stage4, 4)
        run(stage5, 5)
        run(stage6, 6, True)
        run(stage6, 7, False)
        for k, name in enumerate(("core", "x", "y", "pair", "far")):

            @pl.when(i == 19 + k)
            def _():
                trade(k, name)

        return carry

    lax.fori_loop(0, CHUNKS + 8, step, 0)
    store_dx(0).wait()
    for k in range(12):
        remote(zs3.at[0], out.at[k, 1 - c], os.at[0], orr.at[k], near["core"]).wait_recv()


def backward_reduce(dim, x, cot, full, vecs, norms, saved):
    seq, width = x.shape
    wide = width // 4
    block, half = wide // 2, wide // 4
    bf, f32, dma, v = jnp.bfloat16, jnp.float32, pltpu.SemaphoreType.DMA, pltpu.VMEM
    hbm, vmem = pl.BlockSpec(memory_space=pl.ANY), pl.BlockSpec(memory_space=pltpu.VMEM)
    S = jax.ShapeDtypeStruct
    return pl.pallas_call(
        functools.partial(backward_reduce_kernel, dim),
        out_shape=(S((12, 2, block, width), bf), S((2, seq, width), bf), S((2, 16, width), f32)),
        in_specs=[hbm, hbm, hbm, vmem, vmem] + [hbm] * 5,
        out_specs=[hbm, hbm, vmem],
        scratch_shapes=[
            v((48, seq, wide), bf), v((4, seq, width), bf), v((seq, width), f32), v((seq, width), bf),
            v((seq, width), f32),
            v((2, 4, wide, width), bf), v((2, 2, wide, width), bf), v((2, 4, seq, wide), bf), v((2, seq, wide), bf),
            v((5, 2, 16, width), f32),
            v((2, 4, block, width), bf), v((4, 4, block, width), bf), v((2, 4, block, width), f32),
            v((2, 2, half, width), bf), v((4, 2, half, width), bf), v((2, 2, half, width), bf), v((4, 2, half, width), bf),
            v((2, 2, half, width), f32), v((2, block, width), f32),
            v((2, half, width), bf), v((4, half, width), bf), v((2, half, width), bf), v((4, half, width), bf),
            v((2, block, width), f32),
            v((2, block, width), f32), v((2, block, width), bf), v((4, block, width), bf),
            v((2, block, width), bf), v((4, block, width), bf), v((6, block, width), bf), v((6, block, width), bf),
            dma((2, 4)), dma((2, 2)), dma((2,)), dma((2,)), dma((16,)), dma((4,)), dma((4,)), dma((5,)), dma((5,)),
        ] + [dma((n,)) for n in (2, 4) * 7] + [dma((6,)), dma((6,))] + [dma((6,)), dma((12,))],
        compiler_params=pltpu.CompilerParams(collective_id=1, has_side_effects=True, vmem_limit_bytes=63 * 2**20),
    )(x, cot, full, vecs, norms, *saved)


def swap_core(value):
    return lax.ppermute(value, "section", [(0, 1), (1, 0)])


def by_page(
    token_in,
    cotangent,
    w_qkv,
    qv_bias,
    w_attn_out,
    w_ffn_in,
    ffn_in_bias,
    w_ffn_out,
    out_biases,
    norm_gains,
    norm_shifts,
):
    core, place = lax.axis_index("section"), lax.axis_index("mp")
    is_first = core == 0
    width = token_in.shape[2]
    quarter = width // 4
    x = lax.dynamic_index_in_dim(token_in, core, 0, keepdims=False)
    cot = lax.dynamic_index_in_dim(cotangent, core, 0, keepdims=False)
    ffn_in_t = w_ffn_in[0].T.reshape(4, 1, quarter, width)
    ffn = jnp.concatenate([ffn_in_t, w_ffn_out[0].reshape(4, 1, quarter, width)], axis=1)
    shard = jnp.concatenate(
        [w_qkv[0].transpose(0, 2, 1), w_attn_out, ffn.reshape(8, quarter, width)], axis=0
    )
    vec = high(jnp.concatenate([qv_bias[0], ffn_in_bias[0].reshape(4, quarter)], axis=0))
    vec = jnp.pad(vec, ((0, 2), (0, 0)))
    norms = jnp.concatenate([out_biases[0], norm_gains[0], norm_shifts[0]], axis=0)
    norms = jnp.pad(norms, ((0, 2), (0, 0)))
    full, vecs, all_norms, *saved = gather_forward(HEAD_DIM, x, shard, vec, norms)
    parts, grads, totals = backward_reduce(HEAD_DIM, x, cot, full, vecs, all_norms, saved)
    outs = saved[4]

    def trade(both):
        own = lax.dynamic_index_in_dim(both, core, 0)
        received = swap_core(lax.dynamic_index_in_dim(both, 1 - core, 0))
        return jnp.where(is_first, jnp.concatenate([own, received]), jnp.concatenate([received, own]))

    totals = lax.dynamic_index_in_dim(totals, core, 0, keepdims=False)
    own = lax.dynamic_slice_in_dim(totals[8:], place * quarter, quarter, 1)
    piece = width // (lax.axis_size("mp") * lax.axis_size("dp"))
    begin = (place * lax.axis_size("dp") + lax.axis_index("dp")) * piece
    rows = lax.dynamic_slice_in_dim(totals[:8], begin, piece, 1)
    parts = parts.reshape(12, quarter, width)
    return (
        trade(outs)[None],
        trade(grads)[None],
        high(parts[9:12].transpose(0, 2, 1))[None],
        own[0:2][None],
        high(parts[8])[None],
        high(parts[4:8].reshape(width, width).T)[None],
        own[2:6].reshape(1, width),
        high(parts[0:4].reshape(width, width))[None],
        rows[0:2][None],
        rows[2:4][None],
        rows[4:6][None],
    )


def on_device(*args):
    token_in, w_qkv, ffn_in = args[0], args[2], args[5]
    fits = (
        lax.axis_size("section") == 2
        and lax.axis_size("mp") == 4
        and lax.axis_size("dp") == 4
        and token_in.shape == (2, SEQ, 1024)
        and w_qkv.shape[3] == 256
        and ffn_in.shape[2] == 1024
    )
    return by_page(*args) if fits else pipelined(*args)


def solution(mesh):
    return jax.shard_map(
        on_device,
        mesh=mesh,
        in_specs=(
            P(None, ("dp", "mp"), None),
            P(None, ("dp", "mp"), None),
            P("section", None, None, "mp"),
            P("section", None, "mp"),
            P("section", "mp", None),
            P("section", None, "mp"),
            P("section", "mp"),
            P("section", "mp", None),
            P("section", None, None),
            P("section", None, None),
            P("section", None, None),
        ),
        out_specs=(
            P("section", None, ("dp", "mp"), None),
            P("section", None, ("dp", "mp"), None),
            P("section", None, None, "mp"),
            P("section", None, "mp"),
            P("section", "mp", None),
            P("section", None, "mp"),
            P("section", "mp"),
            P("section", "mp", None),
            P("section", None, ("mp", "dp")),
            P("section", None, ("mp", "dp")),
            P("section", None, ("mp", "dp")),
        ),
        check_vma=False,
    )
```

```python
import functools
from functools import partial
import math

import jax
import jax.numpy as jnp
from jax import lax
from jax.experimental import pallas as pl
from jax.experimental.pallas import tpu as pltpu
from jax.sharding import PartitionSpec as P

HEAD_DIM = 64
SEQ = 512


def from_behind(value, axis, by):
    devices = lax.axis_size(axis)
    pairs = [(i, i + by) for i in range(devices) if 0 <= i + by < devices]
    return lax.ppermute(value, axis, pairs)


def norm_rows(values, gain_row, shift_row):
    average = jnp.mean(values, axis=-1, keepdims=True)
    centered = values - average
    variance = jnp.mean(centered * centered, axis=-1, keepdims=True)
    return centered * lax.rsqrt(variance + 1e-05) * gain_row + shift_row


def exact_gelu(values):
    return jax.nn.gelu(values, approximate=False)


def layer_forward(params, token_rows):
    (
        w_qkv,
        qv_bias,
        w_attn_out,
        w_ffn_in,
        ffn_in_bias,
        w_ffn_out,
        out_biases,
        norm_gains,
        norm_shifts,
    ) = params
    gathered = lax.all_gather(token_rows, "mp", axis=0, tiled=True)
    rows_all = gathered.shape[0]
    local_width = w_qkv.shape[2]
    local_heads = local_width // HEAD_DIM
    page_count = rows_all // SEQ
    scale_factor = 1.0 / math.sqrt(HEAD_DIM)
    bias_full = jnp.stack([qv_bias[0], jnp.zeros_like(qv_bias[0]), qv_bias[1]]).astype(jnp.float32)
    projected = (
        jnp.einsum("rd,cde->cre", gathered, w_qkv, preferred_element_type=jnp.float32)
        + bias_full[:, None, :]
    )
    heads_view = projected.astype(jnp.bfloat16).reshape(3, page_count, SEQ, local_heads, HEAD_DIM)
    scores = (
        jnp.einsum(
            "pqhe,pkhe->phqk", heads_view[0], heads_view[1], preferred_element_type=jnp.float32
        )
        * scale_factor
    )
    top_score = jnp.max(scores, axis=-1, keepdims=True)
    exponent = jnp.exp(scores - top_score)
    weights_soft = exponent / jnp.sum(exponent, axis=-1, keepdims=True)
    weights_low = weights_soft.astype(jnp.bfloat16)
    attended = jnp.einsum(
        "phqk,pkhe->pqhe", weights_low, heads_view[2], preferred_element_type=jnp.float32
    )
    attended = attended.reshape(rows_all, local_width).astype(jnp.bfloat16)
    attn_part = jnp.dot(attended, w_attn_out, preferred_element_type=jnp.float32)
    attn_rows = lax.psum_scatter(
        attn_part.astype(jnp.bfloat16), "mp", scatter_dimension=0, tiled=True
    ).astype(jnp.float32)
    residual_one = attn_rows + out_biases[0] + token_rows.astype(jnp.float32)
    first = norm_rows(residual_one, norm_gains[0], norm_shifts[0])
    first_all = lax.all_gather(first.astype(jnp.bfloat16), "mp", axis=0, tiled=True)
    pre_act = jnp.dot(first_all, w_ffn_in, preferred_element_type=jnp.float32) + ffn_in_bias.astype(
        jnp.float32
    )
    activated = exact_gelu(pre_act).astype(jnp.bfloat16)
    ffn_part = jnp.dot(activated, w_ffn_out, preferred_element_type=jnp.float32)
    ffn_rows = lax.psum_scatter(
        ffn_part.astype(jnp.bfloat16), "mp", scatter_dimension=0, tiled=True
    ).astype(jnp.float32)
    residual_two = ffn_rows + out_biases[1] + first
    result = norm_rows(residual_two, norm_gains[1], norm_shifts[1])
    kept_values = (
        gathered,
        heads_view,
        weights_soft,
        attended,
        residual_one,
        first_all,
        pre_act,
        activated,
        residual_two,
    )
    return (result, kept_values)


def layer_backward(params, kept_values, grad_out):
    (
        w_qkv,
        qv_bias,
        w_attn_out,
        w_ffn_in,
        ffn_in_bias,
        w_ffn_out,
        out_biases,
        norm_gains,
        norm_shifts,
    ) = params
    (
        gathered,
        heads_view,
        weights_soft,
        attended,
        residual_one,
        first_all,
        pre_act,
        activated,
        residual_two,
    ) = kept_values
    rows_all = gathered.shape[0]
    local_width = w_qkv.shape[2]
    local_heads = local_width // HEAD_DIM
    page_count = rows_all // SEQ
    scale_factor = 1.0 / math.sqrt(HEAD_DIM)
    unused_two, norm_two_back = jax.vjp(norm_rows, residual_two, norm_gains[1], norm_shifts[1])
    grad_res_two, grad_gain_two, grad_shift_two = norm_two_back(grad_out)
    grad_bias_two = jnp.sum(grad_res_two, axis=0)
    ffn_grad_all = lax.all_gather(grad_res_two.astype(jnp.bfloat16), "mp", axis=0, tiled=True)
    grad_w_ffn_out = jnp.einsum(
        "rf,rd->fd", activated, ffn_grad_all, preferred_element_type=jnp.float32
    )
    grad_act = jnp.einsum("rd,fd->rf", ffn_grad_all, w_ffn_out, preferred_element_type=jnp.float32)
    unused_gelu, gelu_back = jax.vjp(exact_gelu, pre_act)
    grad_pre = gelu_back(grad_act)[0].astype(jnp.bfloat16)
    grad_ffn_in_bias = jnp.sum(grad_pre.astype(jnp.float32), axis=0)
    grad_w_ffn_in = jnp.einsum("rd,rf->df", first_all, grad_pre, preferred_element_type=jnp.float32)
    first_part = jnp.einsum("rf,df->rd", grad_pre, w_ffn_in, preferred_element_type=jnp.float32)
    first_grad_rows = lax.psum_scatter(
        first_part.astype(jnp.bfloat16), "mp", scatter_dimension=0, tiled=True
    ).astype(jnp.float32)
    grad_first = first_grad_rows + grad_res_two
    unused_one, norm_one_back = jax.vjp(norm_rows, residual_one, norm_gains[0], norm_shifts[0])
    grad_res_one, grad_gain_one, grad_shift_one = norm_one_back(grad_first)
    grad_bias_one = jnp.sum(grad_res_one, axis=0)
    attn_grad_all = lax.all_gather(grad_res_one.astype(jnp.bfloat16), "mp", axis=0, tiled=True)
    grad_w_attn_out = jnp.einsum(
        "rk,rd->kd", attended, attn_grad_all, preferred_element_type=jnp.float32
    )
    grad_attended = jnp.einsum(
        "rd,kd->rk", attn_grad_all, w_attn_out, preferred_element_type=jnp.float32
    )
    grad_attended = grad_attended.astype(jnp.bfloat16).reshape(
        page_count, SEQ, local_heads, HEAD_DIM
    )
    weights_low = weights_soft.astype(jnp.bfloat16)
    grad_weights = jnp.einsum(
        "pqhe,pkhe->phqk", grad_attended, heads_view[2], preferred_element_type=jnp.float32
    )
    grad_values = jnp.einsum(
        "phqk,pqhe->pkhe", weights_low, grad_attended, preferred_element_type=jnp.float32
    )
    inner_total = jnp.sum(weights_soft * grad_weights, axis=-1, keepdims=True)
    grad_scores = (weights_soft * (grad_weights - inner_total)).astype(jnp.bfloat16)
    grad_queries = (
        jnp.einsum(
            "phqk,pkhe->pqhe", grad_scores, heads_view[1], preferred_element_type=jnp.float32
        )
        * scale_factor
    )
    grad_keys = (
        jnp.einsum(
            "phqk,pqhe->pkhe", grad_scores, heads_view[0], preferred_element_type=jnp.float32
        )
        * scale_factor
    )
    grad_proj = (
        jnp.stack([grad_queries, grad_keys, grad_values])
        .reshape(3, rows_all, local_width)
        .astype(jnp.bfloat16)
    )
    proj_sums = jnp.sum(grad_proj.astype(jnp.float32), axis=1)
    grad_qv_bias = jnp.stack([proj_sums[0], proj_sums[2]])
    grad_w_qkv = jnp.einsum("rd,cre->cde", gathered, grad_proj, preferred_element_type=jnp.float32)
    input_part = jnp.einsum("cre,cde->rd", grad_proj, w_qkv, preferred_element_type=jnp.float32)
    input_grad_rows = lax.psum_scatter(
        input_part.astype(jnp.bfloat16), "mp", scatter_dimension=0, tiled=True
    ).astype(jnp.float32)
    grad_in = input_grad_rows + grad_res_one
    matrix_grads = (
        grad_w_qkv,
        grad_qv_bias,
        grad_w_attn_out,
        grad_w_ffn_in,
        grad_ffn_in_bias,
        grad_w_ffn_out,
    )
    vector_grads = (
        jnp.stack([grad_bias_one, grad_bias_two]),
        jnp.stack([grad_gain_one, grad_gain_two]),
        jnp.stack([grad_shift_one, grad_shift_two]),
    )
    return (grad_in, matrix_grads, vector_grads)


def pipelined(
    token_in,
    cotangent,
    w_qkv,
    qv_bias,
    w_attn_out,
    w_ffn_in,
    ffn_in_bias,
    w_ffn_out,
    out_biases,
    norm_gains,
    norm_shifts,
):
    params = (
        w_qkv[0],
        qv_bias[0],
        w_attn_out[0],
        w_ffn_in[0],
        ffn_in_bias[0],
        w_ffn_out[0],
        out_biases[0],
        norm_gains[0],
        norm_shifts[0],
    )
    micro_count = token_in.shape[0]
    section_index = lax.axis_index("section")
    is_first = section_index == 0
    zero_rows = jnp.zeros(token_in.shape[1:], jnp.bfloat16)
    run_forward = partial(layer_forward, params)
    run_backward = partial(layer_backward, params)

    def forward_step(step_index, carry):
        received, saved, stored = carry
        own_micro = step_index - section_index
        is_valid = (own_micro >= 0) & (own_micro < micro_count)
        slot_index = jnp.clip(own_micro, 0, micro_count - 1)
        first_rows = lax.dynamic_index_in_dim(
            token_in, jnp.minimum(step_index, micro_count - 1).astype(jnp.int32), 0, keepdims=False
        )
        layer_in = jnp.where(is_first, first_rows, received)
        result, unused_kept = run_forward(layer_in)
        result_low = result.astype(jnp.bfloat16)
        old_saved = lax.dynamic_index_in_dim(saved, slot_index, 0, keepdims=False)
        saved = lax.dynamic_update_index_in_dim(
            saved, jnp.where(is_valid, layer_in, old_saved), slot_index, 0
        )
        old_stored = lax.dynamic_index_in_dim(stored, slot_index, 0, keepdims=False)
        stored = lax.dynamic_update_index_in_dim(
            stored, jnp.where(is_valid, result_low, old_stored), slot_index, 0
        )
        received = from_behind(result_low, "section", 1)
        return (received, saved, stored)

    start_carry = (zero_rows, jnp.zeros_like(token_in), jnp.zeros_like(token_in))
    unused_received, saved, stored = lax.fori_loop(0, micro_count + 1, forward_step, start_carry)
    matrix_zero = tuple((jnp.zeros(entry.shape, jnp.float32) for entry in params[:6]))
    vector_zero = (
        jnp.zeros(out_biases.shape[1:], jnp.float32),
        jnp.zeros(norm_gains.shape[1:], jnp.float32),
        jnp.zeros(norm_shifts.shape[1:], jnp.float32),
    )

    def backward_step(step_index, carry):
        received_grad, grad_store, matrix_sums, vector_sums = carry
        own_micro = step_index - (1 - section_index)
        is_valid = (own_micro >= 0) & (own_micro < micro_count)
        slot_index = jnp.clip(own_micro, 0, micro_count - 1)
        layer_in = lax.dynamic_index_in_dim(saved, slot_index, 0, keepdims=False)
        from_last = lax.dynamic_index_in_dim(cotangent, slot_index, 0, keepdims=False)
        grad_out = jnp.where(is_first, received_grad, from_last).astype(jnp.float32)
        unused_result, kept_values = run_forward(layer_in)
        grad_in, matrix_grads, vector_grads = run_backward(kept_values, grad_out)
        matrix_grads = tuple((jnp.where(is_valid, entry, 0.0) for entry in matrix_grads))
        vector_grads = tuple((jnp.where(is_valid, entry, 0.0) for entry in vector_grads))
        grad_low = grad_in.astype(jnp.bfloat16)
        old_piece = lax.dynamic_index_in_dim(grad_store, slot_index, 0, keepdims=False)
        grad_store = lax.dynamic_update_index_in_dim(
            grad_store, jnp.where(is_valid, grad_low, old_piece), slot_index, 0
        )
        grad_one, grad_two, grad_three, grad_four, grad_five, grad_six = matrix_grads
        matrix_grads = (
            lax.psum(grad_one.astype(jnp.bfloat16), "dp").astype(jnp.float32),
            lax.psum(grad_two.astype(jnp.bfloat16), "dp").astype(jnp.float32),
            lax.psum(grad_three.astype(jnp.bfloat16), "dp").astype(jnp.float32),
            lax.psum(grad_four.astype(jnp.bfloat16), "dp").astype(jnp.float32),
            lax.psum(grad_five.astype(jnp.bfloat16), "dp").astype(jnp.float32),
            lax.psum(grad_six.astype(jnp.bfloat16), "dp").astype(jnp.float32),
        )
        matrix_sums = tuple((total + extra for total, extra in zip(matrix_sums, matrix_grads)))
        vector_sums = tuple((total + extra for total, extra in zip(vector_sums, vector_grads)))
        received_grad = from_behind(grad_low, "section", -1)
        return (received_grad, grad_store, matrix_sums, vector_sums)

    back_carry = (zero_rows, jnp.zeros_like(token_in), matrix_zero, vector_zero)
    unused_grad, grad_store, matrix_sums, vector_sums = lax.fori_loop(
        0, micro_count + 1, backward_step, back_carry
    )
    bias_total, gain_total, shift_total = vector_sums
    bias_part, gain_part, shift_part = (
        lax.psum_scatter(bias_total, ("mp", "dp"), scatter_dimension=1, tiled=True),
        lax.psum_scatter(gain_total, ("mp", "dp"), scatter_dimension=1, tiled=True),
        lax.psum_scatter(shift_total, ("mp", "dp"), scatter_dimension=1, tiled=True),
    )
    return (
        stored[None],
        grad_store[None],
        matrix_sums[0][None],
        matrix_sums[1][None],
        matrix_sums[2][None],
        matrix_sums[3][None],
        matrix_sums[4][None],
        matrix_sums[5][None],
        bias_part[None],
        gain_part[None],
        shift_part[None],
    )


MESH = pl.DeviceIdType.MESH
CHUNKS = 24
TRIPLES = 8
SCALE = 0.125


def low(value):
    return value.astype(jnp.bfloat16)


def high(value):
    return value.astype(jnp.float32)


def remote(src, dst, send, recv, device):
    return pltpu.make_async_remote_copy(
        src_ref=src, dst_ref=dst, send_sem=send, recv_sem=recv, device_id=device, device_id_type=MESH
    )


def neighbours():
    c, p, d = lax.axis_index("section"), lax.axis_index("mp"), lax.axis_index("dp")
    return {
        "core": (1 - c, p, d),
        "x": (c, p + 1 - 2 * lax.rem(p, 2), d),
        "y": (c, lax.rem(p + 2, 4), d),
        "across": (c, p, 3 - d),
        "inner": (c, p, jnp.where(d == 0, 1, 2)),
        "outer": (c, p, jnp.where(d == 1, 0, 3)),
    }


def places():
    p = lax.axis_index("mp")
    return [p, p + 1 - 2 * lax.rem(p, 2), lax.rem(p + 2, 4), 3 - p]


def dot(a, b):
    return jnp.dot(a, b, preferred_element_type=jnp.float32)


def dot_tn(a, b):
    return lax.dot_general(a, b, (((0,), (0,)), ((), ())), preferred_element_type=jnp.float32)


def dot_nt(a, b):
    return lax.dot_general(a, b, (((1,), (1,)), ((), ())), preferred_element_type=jnp.float32)


def standard(values):
    average = jnp.mean(values, axis=-1, keepdims=True)
    centered = values - average
    variance = jnp.mean(centered * centered, axis=-1, keepdims=True)
    scale = lax.rsqrt(variance + 1e-05)
    return centered * scale, scale


def softmax(q, k):
    scores = dot_nt(q * jnp.asarray(SCALE, q.dtype), k)
    exponent = jnp.exp(scores - jnp.max(scores, axis=-1, keepdims=True))
    return exponent * (1.0 / jnp.sum(exponent, axis=-1, keepdims=True))


def by_rows(rows, step, body):
    def run(i, carry):
        body(pl.ds(pl.multiple_of(i * step, step), step))
        return carry

    lax.fori_loop(0, rows // step, run, 0)


def first_norm(x, nrm, acc, u1, hb):
    def run(rows):
        u = acc[rows] + nrm[0:1] + high(x[rows])
        u1[rows] = u
        h = standard(u)[0] * nrm[2:3] + nrm[4:5]
        hb[rows] = low(h)
        acc[rows] = h + nrm[1:2]

    by_rows(acc.shape[0], 64, run)


def second_norm(nrm, acc, u2, out):
    def run(rows):
        u = acc[rows]
        u2[rows] = u
        out[rows] = low(standard(u)[0] * nrm[3:4] + nrm[5:6])

    by_rows(acc.shape[0], 64, run)


def norm_back(u, grad, gain, sums, at, out_low, out_acc):
    def run(rows):
        g = high(grad[rows])
        xhat, scale = standard(u[rows])
        scaled = g * gain
        du = scale * (
            scaled
            - jnp.mean(scaled, axis=-1, keepdims=True)
            - xhat * jnp.mean(scaled * xhat, axis=-1, keepdims=True)
        )
        out_low[rows] = low(du)
        out_acc[rows] = du
        for row, term in ((at[0], du), (at[1], g * xhat), (at[2], g)):
            sums[row : row + 1] += jnp.sum(term, axis=0, keepdims=True)

    by_rows(u.shape[0], 64, run)


def ffn_back_block(dfb, w, gd, acc, dz_out):
    dz = low(dot_nt(dfb[...], w[1]) * high(gd))
    dz_out[...] = dz
    acc[...] += dot(dz, w[0])
    return jnp.sum(high(dz), axis=0, keepdims=True)


def attention_back_block(dab, w, qkv, dq_out, dk_out, dv_out, acc, dim):
    dob = low(dot_nt(dab[...], w[3]))
    for j in range(dob.shape[1] // dim):
        cols = slice(j * dim, (j + 1) * dim)
        q, k, v, do = qkv[0, :, cols], qkv[1, :, cols], qkv[2, :, cols], dob[:, cols]
        a = softmax(q, k)
        da = dot_nt(do, v)
        ds = low(a * (da - jnp.sum(a * da, axis=-1, keepdims=True)))
        dv_out[:, cols] = low(dot_tn(low(a), do))
        dq_out[:, cols] = low(dot(ds, k) * SCALE)
        dk_out[:, cols] = low(dot_tn(ds, q) * SCALE)
    acc[...] += dot(dq_out[...], w[0]) + dot(dk_out[...], w[1]) + dot(dv_out[...], w[2])


def weight_copies(full, layer, kind, p, b, buf, sem, rows):
    width = 4 * rows
    if kind == 0:
        starts = [c * width + p * rows for c in range(4)]
    else:
        starts = [4 * width + t * 4 * width + p * width + b * rows for t in range(2)]
    return [
        pltpu.make_async_copy(full.at[layer, pl.ds(pl.multiple_of(start, rows), rows)], buf.at[n], sem.at[n])
        for n, start in enumerate(starts)
    ]


def project_block(x, w, vec, save, dim):
    rows = x[...]
    q = low(dot_nt(rows, w[0]) + vec[0:1])
    k = low(dot_nt(rows, w[1]))
    v = low(dot_nt(rows, w[2]) + vec[1:2])
    save[0], save[1], save[2] = q, k, v
    for j in range(q.shape[1] // dim):
        cols = slice(j * dim, (j + 1) * dim)
        save[3, :, cols] = low(dot(low(softmax(q[:, cols], k[:, cols])), v[:, cols]))


def unit_values(hb, w, bias):
    z = dot_nt(hb[...], w) + bias
    inner = 0.5 + 0.5 * lax.erf(z * math.sqrt(0.5))
    slope = inner + z * jnp.exp(-0.5 * z * z) * (1.0 / math.sqrt(2.0 * math.pi))
    return low(z * inner), low(slope)


def gather_forward_kernel(
    dim, tokens, w_qkv, w_out, w_up, w_down, vec, norm_in, full, vecs, norms, qkvo, gd, us, hbs, between, acts,
    turned, x, acc, u, hb, wa, wf, sa, gb, sd, wasem, wfsem, sasem, gbsem, sdsem, usem,
    ini_s, ini_r, loc, x1ss, x1rs, y1ss, y1rs, x2ss, x2rs, y2ss, y2rs, zs, zr, cs, cr, vs, vr, vloc, as_, ar,
):
    c, p, d = lax.axis_index("section"), lax.axis_index("mp"), lax.axis_index("dp")
    near = neighbours()
    near["pair"] = (c, p, d + 1 - 2 * lax.rem(d, 2))
    spots = places()
    rows = w_out.shape[0] // 2
    half = rows // 2
    odd = lax.rem(d, 2)
    others = [(cc, spots[r], d) for r in range(4) for cc in (c, 1 - c)][1:]

    barrier = pltpu.get_barrier_semaphore()
    for device in others + [near["pair"]]:
        pl.semaphore_signal(barrier, inc=1, device_id=device, device_id_type=MESH)
    pl.semaphore_wait(barrier, 8)

    def place_of(s, spot, h):
        k = lax.rem(s, 12)
        row = jnp.where(k < 4, k * 8 + spot * 2, 32 + (k // 4 - 1) * 32 + spot * 8 + lax.rem(k, 4) * 2)
        return s // 12, (row + h) * rows

    def block(s, spot, h, start=0, size=rows):
        layer, row = place_of(s, spot, h)
        return full.at[layer, pl.ds(pl.multiple_of(row + start, half), size)]

    def init_place(k, layer):
        row = place_of(12 * layer + k, p, 0)[1]
        return full.at[layer, pl.ds(pl.multiple_of(row, half), 2 * rows)]

    def turn(k):
        if k < 3:
            turned[k] = w_qkv[k].T
        elif 4 <= k < 8:
            turned[k - 1] = w_up[:, 2 * rows * (k - 4) : 2 * rows * (k - 3)].T

    def chunk(k):
        if k == 3:
            return w_out
        if k < 8:
            return turned.at[k if k < 3 else k - 1]
        return w_down.at[pl.ds(2 * rows * (k - 8), 2 * rows)]

    def init_start(k):
        turn(k)
        pltpu.make_async_copy(chunk(k), init_place(k, c), loc.at[k]).start()
        remote(chunk(k), init_place(k, c), ini_s.at[k], ini_r.at[k], near["core"]).start()

    def init_local(k):
        return pltpu.make_async_copy(init_place(k, c), init_place(k, c), loc.at[k])

    def init_wait(k):
        there = init_place(k, 1 - c)
        remote(there, there, ini_s.at[k], ini_r.at[k], near["core"]).wait_recv()

    def small():
        copies = [remote(vec, vecs.at[c, p], vs.at[i], vr.at[c, p], device) for i, device in enumerate(others)]
        copies.append(remote(norm_in, norms.at[c], vs.at[7], vr.at[0, 4], near["core"]))
        return copies

    def small_local():
        return [
            pltpu.make_async_copy(vec, vecs.at[c, p], vloc.at[0]),
            pltpu.make_async_copy(norm_in, norms.at[c], vloc.at[1]),
        ]

    def hop(s, spot, name, pick):
        ss, rs = (x1ss, x1rs) if pick == "x" else (y1ss, y1rs)
        b = block(s, spot, c)
        return remote(b, b, ss.at[s], rs.at[s], near[name])

    def first(s, name):
        return hop(s, p, name, name)

    def arrived(s, name):
        return hop(s, spots[1] if name == "x" else spots[2], name, name)

    def relay(s, name, spot=None):
        if name == "x":
            b = block(s, spots[2] if spot is None else spot, c, 0, half)
            return remote(b, b, x2ss.at[s], x2rs.at[s], near["x"])
        b = block(s, spots[1] if spot is None else spot, c, half, half)
        return remote(b, b, y2ss.at[s], y2rs.at[s], near["y"])

    def relayed(s, name):
        return relay(s, name, spots[3])

    def to_pair(s, r):
        b = block(s, spots[r], c)
        return remote(b, b, zs.at[s, r - 1], zr.at[s, r - 1], near["pair"])

    def to_core(s, r):
        b = block(s, spots[r], c)
        return remote(b, b, cs.at[s, r - 1], cr.at[s, r - 1], near["core"])

    def from_core(s, r):
        b = block(s, spots[r], 1 - c)
        return remote(b, b, cs.at[s, r - 1], cr.at[s, r - 1], near["core"])

    def sent_chunk(j):
        t, n = j // 2, lax.rem(j, 2)
        return 3 * t + (1 - n) * (1 + odd), n == 0

    def stage_a(j):
        s = sent_chunk(j)[0]
        for m in range(3):
            own = 3 * (j // 2) + m

            @pl.when((own // 12 != c) & (lax.rem(j, 2) == 0))
            def _():
                init_wait(lax.rem(own, 12))

            @pl.when((own // 12 == c) & (lax.rem(j, 2) == 0))
            def _():
                init_local(lax.rem(own, 12)).wait()

        first(s, "x").start()
        first(s, "y").start()

    def stage_b(j):
        s, shared = sent_chunk(j)
        arrived(s, "x").wait_recv()
        relay(s, "y").start()
        arrived(s, "y").wait_recv()
        relay(s, "x").start()
        for r in (1, 2):
            to_core(s, r).start()

        @pl.when(shared)
        def _():
            for r in (1, 2):
                to_pair(s, r).start()

    def stage_c(j):
        s, shared = sent_chunk(j)
        relayed(s, "x").wait_recv()
        relayed(s, "y").wait_recv()
        to_core(s, 3).start()

        @pl.when(shared)
        def _():
            to_pair(s, 3).start()

    def stage_d(t):
        s = 3 * t + 2 - odd
        for r in (1, 2, 3):
            to_pair(s, r).wait_recv()
            to_core(s, r).start()

    def stage_e(t):
        for j in range(3):
            for r in (1, 2, 3):
                from_core(3 * t + j, r).wait_recv()

    def stage_f(t):
        for n, s in enumerate((3 * t, 3 * t + 1 + odd)):
            first(s, "x").wait_send()
            first(s, "y").wait_send()
            relay(s, "x").wait_send()
            relay(s, "y").wait_send()
            for r in (1, 2, 3):
                if n:
                    to_pair(s, r).wait_send()
        for j in range(3):
            for r in (1, 2, 3):
                to_core(3 * t + j, r).wait_send()

    wide = 2 * rows

    def weights(l, number, place, sem):
        begin = pl.multiple_of(number * wide, wide)
        return pltpu.make_async_copy(full.at[l, pl.ds(begin, wide)], place, sem)

    def load_qkv(l, q):
        return [weights(l, 4 * n + q, wa.at[q, n], wasem.at[q, n]) for n in range(3)]

    def load(l, number, slot):
        return weights(l, number, wf.at[slot], wfsem.at[slot])

    def load_out(l, q):
        return load(l, 12 + q, q)

    def load_in(l, b, q, slot):
        return load(l, 16 + 4 * q + b, slot)

    def load_down(l, b, q, slot):
        return load(l, 32 + 4 * q + b, slot)

    def save_attn(l, q):
        return pltpu.make_async_copy(sa.at[q], qkvo.at[l, q], sasem.at[q])

    def save_g(l, n):
        return pltpu.make_async_copy(gb.at[n], gd.at[l, n, 0], gbsem.at[n])

    def save_d(l, n, slot):
        return pltpu.make_async_copy(sd.at[slot], gd.at[l, n, 1], sdsem.at[slot])

    def keep(l, which):
        if which == 2:
            return pltpu.make_async_copy(hb, hbs.at[l], usem.at[2])
        if which == 3:
            return pltpu.make_async_copy(x, between, usem.at[3])
        return pltpu.make_async_copy(u, us.at[l, which], usem.at[which])

    def give(l, begin):
        @pl.when(l == c)
        def _():
            copy = pltpu.make_async_copy(x, acts.at[c], as_.at[0])
            copy.start() if begin else copy.wait()

        @pl.when(l != c)
        def _():
            copy = remote(x, acts.at[c], as_.at[0], ar.at[0], near["core"])
            copy.start() if begin else copy.wait_send()

    def kept(l):
        @pl.when(l == 0)
        def _():
            keep(0, 3).wait()

        give(l, False)

    def each(count, body):
        def run(q, carry):
            body(q)
            return carry

        lax.fori_loop(0, count, run, 0)

    def attention_segment(l, q):
        for copy in load_qkv(l, q):
            copy.wait()
        project_block(x, wa.at[q], vecs[l, q], sa.at[q], dim)
        save_attn(l, q).start()

    def out_segment(l):
        @pl.when(l == 1)
        def _():
            keep(0, 1).wait()

        acc[...] = jnp.zeros_like(acc)

        def branch(q):
            load_out(l, q).wait()
            acc[...] += dot(sa[q, 3], wf[q])
            load_in(l, 1, q, q).start()

        each(4, branch)
        first_norm(x, norms.at[l], acc, u, hb)
        keep(l, 0).start()
        keep(l, 2).start()

    def up_segment(l, b, slot):
        def run(q):
            load_in(l, b, q, slot + q).wait()
            n, two = 4 * q + b, lax.rem(q, 2)

            @pl.when(q >= 2)
            def _():
                save_d(l, n - 8, two).wait()

            g, slope = unit_values(hb, wf[slot + q], vecs[l, q, pl.ds(2 + b, 1)])
            gb[n] = g
            sd[two] = slope
            save_g(l, n).start()
            save_d(l, n, two).start()

        each(4, run)
        for q in (2, 3):
            save_d(l, 4 * q + b, q % 2).wait()

    def down_segment(l, b, slot):
        def run(q):
            load_down(l, b, q, slot + q).wait()
            acc[...] += dot(gb[4 * q + b], wf[slot + q])

        each(4, run)

    def end_segment(l):
        keep(l, 0).wait()
        keep(l, 2).wait()
        each(4, lambda q: save_attn(l, q).wait())
        each(16, lambda n: save_g(l, n).wait())

        @pl.when(l == 1)
        def _():
            kept(0)

        second_norm(norms.at[l], acc, u, x)
        keep(l, 1).start()
        give(l, True)

        @pl.when(l == 0)
        def _():
            keep(0, 3).start()

    def small_there():
        for copy in small_local():
            copy.wait()
        for copy in small():
            copy.wait_send()
        for cc, spot in [(cc, spots[r]) for r in range(4) for cc in (c, 1 - c)][1:]:
            remote(vec, vecs.at[cc, spot], vs.at[0], vr.at[cc, spot], near["core"]).wait_recv()
        remote(norm_in, norms.at[1 - c], vs.at[7], vr.at[0, 4], near["core"]).wait_recv()

    def compute(m):
        l, part = m // 8, lax.rem(m, 8)

        def at(number, body):
            @pl.when(part == number)
            def _():
                body()

        def attention_first():
            for q in range(4):
                for copy in load_qkv(l, q):
                    copy.start()

            @pl.when(m == 0)
            def _():
                small_there()
                first_rows.wait()

        def attention_half(begin):
            each(2, lambda q: attention_segment(l, begin + q))

        def out_part():
            for q in range(4):
                load_out(l, q).start()
            for q in range(4):
                load_in(l, 0, q, 4 + q).start()
            out_segment(l)

        def up_part():
            for q in range(4):
                load_in(l, 2, q, q).start()
            for q in range(4):
                load_in(l, 3, q, 4 + q).start()
            up_segment(l, 2, 0)
            for q in range(4):
                load_down(l, 0, q, q).start()

        def turn_part():
            up_segment(l, 3, 4)
            down_segment(l, 0, 0)

        def down_part():
            for b in (1, 2):
                for q in range(4):
                    load_down(l, b, q, 4 * (b - 1) + q).start()
            down_segment(l, 1, 0)
            for q in range(4):
                load_down(l, 3, q, q).start()
            down_segment(l, 2, 4)

        def end_part():
            down_segment(l, 3, 0)
            end_segment(l)

        at(0, attention_first)

        @pl.when(part < 2)
        def _():
            attention_half(2 * part)

        at(2, out_part)

        @pl.when((part == 2) | (part == 3))
        def _():
            b = part - 2
            up_segment(l, b, 4 - 4 * b)

        at(4, up_part)
        at(5, turn_part)
        at(6, down_part)
        at(7, end_part)

    first_rows = pltpu.make_async_copy(tokens.at[c], x, usem.at[4])
    first_rows.start()
    for k in range(3):
        init_start(k)
    for copy in small_local() + small():
        copy.start()

    def step(count, carry):
        i = count - 1

        def run(stage, lag):
            @pl.when((i >= lag) & (i < 2 * TRIPLES + lag))
            def _():
                stage(i - lag)

        def run_late(stage, lag):
            @pl.when((i >= lag) & (i < 2 * TRIPLES + lag) & (lax.rem(i - lag, 2) == 0))
            def _():
                stage((i - lag) // 2)

        run(stage_a, -1)
        run(stage_b, 1)
        run(stage_c, 2)
        run_late(stage_d, 4)
        run_late(stage_e, 5)
        run_late(stage_f, 6)
        for t in range(3):

            @pl.when(i == 2 * t)
            def _():
                for k in range(3 * t + 3, 3 * t + 6):
                    init_start(k)

        run(compute, 5)
        return carry

    lax.fori_loop(0, 2 * TRIPLES + 6, step, 0)

    for k in range(12):
        remote(chunk(k), init_place(k, c), ini_s.at[k], ini_r.at[k], near["core"]).wait_send()
    keep(1, 1).wait()
    kept(1)
    remote(x, acts.at[1 - c], as_.at[0], ar.at[0], near["core"]).wait_recv()


def gather_forward(dim, tokens, w_qkv, w_out, w_up, w_down, vec, norms):
    rows, width = w_out.shape
    seq = tokens.shape[1]
    bf, f32, dma, v = jnp.bfloat16, jnp.float32, pltpu.SemaphoreType.DMA, pltpu.VMEM
    hbm, vmem = pl.BlockSpec(memory_space=pl.ANY), pl.BlockSpec(memory_space=pltpu.VMEM)
    S = jax.ShapeDtypeStruct
    return pl.pallas_call(
        functools.partial(gather_forward_kernel, dim),
        out_shape=(
            S((2, 48 * rows, width), bf), S((2, 4) + vec.shape, f32), S((2,) + norms.shape, f32),
            S((2, 4, 4, seq, rows), bf), S((2, 16, 2, seq, rows), bf), S((2, 2, seq, width), f32),
            S((2, seq, width), bf), S((seq, width), bf), S((2, seq, width), bf),
        ),
        in_specs=[hbm] + [vmem] * 6,
        out_specs=[hbm, vmem, vmem] + [hbm] * 6,
        scratch_shapes=[
            v((7, rows, width), bf),
            v((seq, width), bf), v((seq, width), f32), v((seq, width), f32), v((seq, width), bf),
            v((4, 3, rows, width), bf), v((8, rows, width), bf), v((4, 4, seq, rows), bf), v((16, seq, rows), bf),
            v((2, seq, rows), bf), dma((4, 3)), dma((8,)), dma((4,)), dma((16,)), dma((2,)), dma((5,)),
        ] + [dma((12,))] * 3 + [dma((24,))] * 8 + [dma((24, 3))] * 4
        + [dma((8,)), dma((2, 5)), dma((2,)), dma((1,)), dma((1,))],
        compiler_params=pltpu.CompilerParams(collective_id=0, has_side_effects=True, vmem_limit_bytes=60 * 2**20),
    )(tokens, w_qkv, w_out, w_up, w_down, vec, norms)


def backward_reduce_kernel(
    dim, tokens, cots, full, norms, qkvo, gd, us, hbs, between, out, grads, totals,
    left, right, acc, g, u, wa, wf, da, df, trades,
    sendc, recvc, keep, x1s, x1r, y1s, y1r, part, base, x2s, x2r, y2s, y2r, mid,
    zk, zs1, zr1, zs2, zr2, zs3, zr3,
    wasem, wfsem, dasem, dfsem, gsem, osem4, bsem, gds, gdr, tss, trs,
    cs, cr, x1ss, x1rs, y1ss, y1rs, x2ss, x2rs, y2ss, y2rs, z1ss, z1rs, z2ss, z2rs, z3ss, z3rs, os, orr,
):
    c, p, d = lax.axis_index("section"), lax.axis_index("mp"), lax.axis_index("dp")
    near = neighbours()
    near["pair"] = (c, p, d + 1 - 2 * lax.rem(d, 2))
    near["far"] = (c, p, lax.rem(d + 2, 4))
    spots = places()
    is_end = (d == 0) | (d == 3)
    is_mid = jnp.logical_not(is_end)
    rows = sendc.shape[2]
    half = rows // 2
    wide = 2 * rows

    barrier = pltpu.get_barrier_semaphore()

    def signal(device):
        pl.semaphore_signal(barrier, inc=1, device_id=device, device_id_type=MESH)

    for name in ("core", "x", "y", "pair", "far"):
        signal(near[name])

    @pl.when(is_end)
    def _():
        pl.semaphore_wait(barrier, 5)

    @pl.when(is_mid)
    def _():
        signal(near["across"])
        pl.semaphore_wait(barrier, 6)

    def core_copy(s):
        a, b = lax.rem(s, 2), lax.rem(s, 4)
        return remote(sendc.at[a], recvc.at[b], cs.at[a], cr.at[b], near["core"])

    def link_copy(s, src, dst, ss, rs, name):
        a, b = lax.rem(s, 2), lax.rem(s, 4)
        return remote(src.at[a], dst.at[b], ss.at[a], rs.at[b], near[name])

    x1 = lambda s: link_copy(s, x1s, x1r, x1ss, x1rs, "x")
    y1 = lambda s: link_copy(s, y1s, y1r, y1ss, y1rs, "y")
    x2 = lambda s: link_copy(s, x2s, x2r, x2ss, x2rs, "x")
    y2 = lambda s: link_copy(s, y2s, y2r, y2ss, y2rs, "y")
    z1 = lambda s: link_copy(s, zs1, zr1, z1ss, z1rs, "inner")
    z2 = lambda s: link_copy(s, zs2, zr2, z2ss, z2rs, "across")

    def z3(s):
        b = lax.rem(s, 6)
        return remote(zs3.at[b], zr3.at[b], z3ss.at[b], z3rs.at[b], near["outer"])

    def stage0(s):
        k, slot = lax.rem(s, 12), lax.rem(s, 2)
        stride = jnp.where(k < 8, 4, 1)
        first = jnp.where(k < 4, k, jnp.where(k < 8, 12 + k, jnp.where(k == 8, 32, 36 + 4 * (k - 9))))
        kind = jnp.where(k < 4, 0, jnp.where(k < 8, 1, jnp.where(k == 8, 2, 3)))
        for r in range(4):
            whole = dot_tn(left[first + stride * spots[r]], right[kind])
            keep[slot, r] = jnp.where(c == 0, whole[:rows], whole[rows:])
            sendc[slot, r] = low(jnp.where(c == 0, whole[rows:], whole[:rows]))
        core_copy(s).start()

    def stage1(s):
        a, b = lax.rem(s, 2), lax.rem(s, 4)
        core_copy(s).wait()
        far = keep[a, 3] + high(recvc[b, 3])
        x1s[a, 0] = low(far[:half])
        y1s[a, 0] = low(far[half:])
        by_x = keep[a, 1] + high(recvc[b, 1])
        x1s[a, 1] = low(by_x[:half])
        part[a, 0] = by_x[half:]
        by_y = keep[a, 2] + high(recvc[b, 2])
        y1s[a, 1] = low(by_y[half:])
        part[a, 1] = by_y[:half]
        x1(s).start()
        y1(s).start()
        base[a] = keep[a, 0] + high(recvc[b, 0])

    def stage2(s):
        a, b = lax.rem(s, 2), lax.rem(s, 4)
        x1(s).wait()
        y1(s).wait()
        y2s[a] = low(part[a, 1] + high(x1r[b, 0]))
        x2s[a] = low(part[a, 0] + high(y1r[b, 0]))
        own = base[a]
        mid[a, pl.ds(0, half)] = own[:half] + high(x1r[b, 1])
        mid[a, pl.ds(half, half)] = own[half:] + high(y1r[b, 1])
        x2(s).start()
        y2(s).start()

    def stage3(s):
        a, b = lax.rem(s, 2), lax.rem(s, 4)
        x2(s).wait()
        y2(s).wait()
        own = mid[a]
        top = own[:half] + high(y2r[b])
        end = own[half:] + high(x2r[b])

        @pl.when(is_end)
        def _():
            zs1[a, pl.ds(0, half)] = low(top)
            zs1[a, pl.ds(half, half)] = low(end)
            z1(s).start()

        @pl.when(is_mid)
        def _():
            zk[a, pl.ds(0, half)] = top
            zk[a, pl.ds(half, half)] = end

    def stage4(s):
        a, b = lax.rem(s, 2), lax.rem(s, 4)

        @pl.when(is_end)
        def _():
            z1(s).wait_send()

        @pl.when(is_mid)
        def _():
            z1(s).wait_recv()
            zs2[a] = low(zk[a] + high(zr1[b]))
            z2(s).start()

    def stage5(s):
        a, b = lax.rem(s, 2), lax.rem(s, 4)

        @pl.when(is_mid)
        def _():
            z2(s).wait()
            zs3[lax.rem(s, 6)] = low(high(zs2[a]) + high(zr2[b]))
            z3(s).start()

    def stage6(s, begin):
        layer, k, b = 1 - s // 12, lax.rem(s, 12), lax.rem(s, 6)

        def finish(source):
            @pl.when(layer == c)
            def _():
                copy = pltpu.make_async_copy(source.at[b], out.at[k, c], os.at[b])
                copy.start() if begin else copy.wait()

            @pl.when(layer != c)
            def _():
                copy = remote(source.at[b], out.at[k, c], os.at[b], orr.at[k], near["core"])
                copy.start() if begin else copy.wait_send()

        @pl.when(is_end)
        def _():
            if begin:
                z3(s).wait_recv()
            finish(zr3)

        @pl.when(is_mid)
        def _():
            if begin:
                z3(s).wait_send()
            finish(zs3)

    def load_g(l, n):
        return pltpu.make_async_copy(gd.at[l, n, 0], left.at[n], gsem.at[n])

    def load_o(l, n):
        return pltpu.make_async_copy(qkvo.at[l, n, 3], left.at[32 + n], osem4.at[n])

    def load_h(l):
        return pltpu.make_async_copy(hbs.at[l], right.at[1], bsem.at[0])

    def load_x(source):
        return pltpu.make_async_copy(source, right.at[3], bsem.at[1])

    def load_u(l, which):
        return pltpu.make_async_copy(us.at[l, which], u, bsem.at[2])

    def ffn(l, n, slot):
        return weight_copies(full, l, 1, lax.rem(n, 4), n // 4, wf.at[slot], wfsem.at[slot], wide) + [
            pltpu.make_async_copy(gd.at[l, 4 * lax.rem(n, 4) + n // 4, 1], df.at[slot], dfsem.at[slot])
        ]

    def attn(l, q, slot):
        return weight_copies(full, l, 0, q, 0, wa.at[slot], wasem.at[slot], wide) + [
            pltpu.make_async_copy(qkvo.at[l, q], da.at[slot], dasem.at[slot])
        ]

    def store_dx(l, begin):
        @pl.when(l == c)
        def _():
            copy = pltpu.make_async_copy(g, grads.at[c], gds.at[0])
            copy.start() if begin else copy.wait()

        @pl.when(l != c)
        def _():
            copy = remote(g, grads.at[c], gds.at[0], gdr.at[0], near["core"])
            copy.start() if begin else copy.wait_send()

    def ahead(l):
        load_u(l, 1).start()
        for copy in ffn(l, 0, 0) + attn(l, 0, 0):
            copy.start()

    def operands(l):
        def run(n, carry):
            load_g(l, n).start()
            return carry

        lax.fori_loop(0, 16, run, 0)
        for n in range(4):
            load_o(l, n).start()
        load_h(l).start()

    def operands_there(l):
        def run(n, carry):
            load_g(l, n).wait()
            return carry

        lax.fori_loop(0, 16, run, 0)
        for n in range(4):
            load_o(l, n).wait()
        load_h(l).wait()

    def top_segment(l):
        load_u(l, 1).wait()
        norm_back(u, g, norms[l, 3:4], totals.at[l], (1, 3, 5), right.at[0], acc)
        load_u(l, 0).start()

        @pl.when(l == 1)
        def _():
            operands_there(1)

    def ffn_segment(l, b):
        def run(q, carry):
            n = 4 * b + q
            slot = lax.rem(n, 2)
            for copy in ffn(l, n, slot):
                copy.wait()

            @pl.when(n < 15)
            def _():
                for copy in ffn(l, n + 1, 1 - slot):
                    copy.start()

            row = ffn_back_block(right.at[0], wf.at[slot], df[slot], acc, left.at[16 + 4 * q + b])
            totals[l, pl.ds(10 + b, 1), pl.ds(pl.multiple_of(q * wide, wide), wide)] = row
            return carry

        lax.fori_loop(0, 4, run, 0)

    def middle_segment(l):
        load_u(l, 0).wait()
        norm_back(u, acc, norms[l, 2:3], totals.at[l], (0, 2, 4), right.at[2], acc)

    def attention_segment(l, q):
        slot = lax.rem(q, 2)
        for copy in attn(l, q, slot):
            copy.wait()

        @pl.when(q < 3)
        def _():
            for copy in attn(l, q + 1, 1 - slot):
                copy.start()

        dq, dk, dv = left.at[36 + q], left.at[40 + q], left.at[44 + q]
        attention_back_block(right.at[2], wa.at[slot], da.at[slot], dq, dk, dv, acc, dim)
        cols = pl.ds(pl.multiple_of(q * wide, wide), wide)
        totals[l, 8:9, cols] = jnp.sum(high(dq[...]), axis=0, keepdims=True)
        totals[l, 9:10, cols] = jnp.sum(high(dv[...]), axis=0, keepdims=True)

    def end_segment(l):
        by_rows(acc.shape[0], 64, lambda r: g.__setitem__(r, low(acc[r])))
        store_dx(l, True)

        @pl.when(l == 1)
        def _():
            ahead(0)

    def segment(i):
        l, j = 1 - i // 9, lax.rem(i, 9)

        @pl.when(i == 9)
        def _():
            operands(0)
            store_dx(1, False)

        @pl.when(j == 0)
        def _():
            top_segment(l)

        @pl.when(j < 4)
        def _():
            ffn_segment(l, j)

        @pl.when(j == 4)
        def _():
            middle_segment(l)

        @pl.when((j >= 4) & (j < 8))
        def _():
            attention_segment(l, j - 4)

        @pl.when(j == 8)
        def _():
            end_segment(l)

        @pl.when(i == 8)
        def _():
            load_x(between).wait()

        @pl.when(i == 12)
        def _():
            operands_there(0)
            load_x(tokens.at[c]).start()

        @pl.when(i == 16)
        def _():
            load_x(tokens.at[c]).wait()

    def trade(k):
        return remote(totals, trades.at[k], tss.at[k], trs.at[k], near[("core", "x", "y", "pair", "far")[k]])

    first_rows = pltpu.make_async_copy(cots.at[c], g, bsem.at[3])
    first_rows.start()
    ahead(1)
    operands(1)
    load_x(between).start()
    totals[...] = jnp.zeros_like(totals)
    first_rows.wait()

    def step(count, carry):
        i = count - 1

        def run(stage, lag, *extra):
            @pl.when((i >= lag) & (i < CHUNKS + lag))
            def _():
                stage(i - lag, *extra)

        for lag, stage in enumerate((stage1, stage2, stage3, stage4, stage5)):
            run(stage, lag + 1)
        run(stage6, 6, True)
        run(stage6, 7, False)
        for k in range(6):

            @pl.when(i == 18 + k)
            def _():
                if k:
                    trade(k - 1).wait()
                    totals[...] += trades[k - 1]
                if k < 5:
                    trade(k).start()

        run(stage0, 0)

        @pl.when(i < 17)
        def _():
            segment(i + 1)

        return carry

    lax.fori_loop(0, CHUNKS + 9, step, 0)
    store_dx(0, False)
    remote(g, grads.at[1 - c], gds.at[0], gdr.at[0], near["core"]).wait_recv()
    for k in range(12):
        remote(zs3.at[0], out.at[k, 1 - c], os.at[0], orr.at[k], near["core"]).wait_recv()


def backward_reduce(dim, tokens, cots, full, norms, saved):
    seq, width = tokens.shape[1:]
    wide = width // 4
    block, half = wide // 2, wide // 4
    bf, f32, dma, v = jnp.bfloat16, jnp.float32, pltpu.SemaphoreType.DMA, pltpu.VMEM
    hbm, vmem = pl.BlockSpec(memory_space=pl.ANY), pl.BlockSpec(memory_space=pltpu.VMEM)
    S = jax.ShapeDtypeStruct
    return pl.pallas_call(
        functools.partial(backward_reduce_kernel, dim),
        out_shape=(S((12, 2, block, width), bf), S((2, seq, width), bf), S((2, 16, width), f32)),
        in_specs=[hbm, hbm, hbm, vmem] + [hbm] * 5,
        out_specs=[hbm, hbm, vmem],
        scratch_shapes=[
            v((48, seq, wide), bf), v((4, seq, width), bf), v((seq, width), f32), v((seq, width), bf),
            v((seq, width), f32),
            v((2, 4, wide, width), bf), v((2, 2, wide, width), bf), v((2, 4, seq, wide), bf), v((2, seq, wide), bf),
            v((5, 2, 16, width), f32),
            v((2, 4, block, width), bf), v((4, 4, block, width), bf), v((2, 4, block, width), f32),
            v((2, 2, half, width), bf), v((4, 2, half, width), bf), v((2, 2, half, width), bf), v((4, 2, half, width), bf),
            v((2, 2, half, width), f32), v((2, block, width), f32),
            v((2, half, width), bf), v((4, half, width), bf), v((2, half, width), bf), v((4, half, width), bf),
            v((2, block, width), f32),
            v((2, block, width), f32), v((2, block, width), bf), v((4, block, width), bf),
            v((2, block, width), bf), v((4, block, width), bf), v((6, block, width), bf), v((6, block, width), bf),
            dma((2, 4)), dma((2, 2)), dma((2,)), dma((2,)), dma((16,)), dma((4,)), dma((4,)), dma((1,)), dma((1,)), dma((5,)), dma((5,)),
        ] + [dma((n,)) for n in (2, 4) * 7] + [dma((6,)), dma((6,))] + [dma((6,)), dma((12,))],
        compiler_params=pltpu.CompilerParams(collective_id=1, has_side_effects=True, vmem_limit_bytes=63 * 2**20),
    )(tokens, cots, full, norms, *saved)


def finish_kernel(parts, acts_in, grads_in, acts, grads, g_qkv, g_out, g_up, g_down,
                  pb, ab, gb, qb, ob, ub, db, psem, asem, osem):
    def load(k):
        return pltpu.make_async_copy(parts.at[k], pb.at[k], psem.at[k])

    others = [(acts_in, ab, acts, 0), (grads_in, gb, grads, 1)]
    for k in range(12):
        load(k).start()
    for source, buffer, place, n in others:
        pltpu.make_async_copy(source, buffer, asem.at[n]).start()
    stores = []
    rows = pb.shape[1]

    def store(source, place):
        copy = pltpu.make_async_copy(source, place, osem.at[len(stores)])
        copy.start()
        stores.append(copy)

    for k in range(12):
        load(k).wait()
        if k < 4:
            span = pl.ds(k * rows, rows)
            db[span] = high(pb[k])
            store(db.at[span], g_down.at[span])
        elif k < 8:
            ub[:, pl.ds((k - 4) * rows, rows)] = high(pb[k]).T
            if k == 7:
                store(ub, g_up)
        elif k == 8:
            ob[...] = high(pb[k])
            store(ob, g_out)
        else:
            qb[k - 9] = high(pb[k]).T
            store(qb.at[k - 9], g_qkv.at[k - 9])
    for source, buffer, place, n in others:
        pltpu.make_async_copy(source, buffer, asem.at[n]).wait()
        store(buffer, place)
    for copy in stores:
        copy.wait()


def finish(parts, acts, grads):
    count, rows, width = parts.shape
    bf, f32, dma, v = jnp.bfloat16, jnp.float32, pltpu.SemaphoreType.DMA, pltpu.VMEM
    S = jax.ShapeDtypeStruct
    shapes = [(3, width, rows), (rows, width), (width, width), (width, width)]
    hbm = pl.BlockSpec(memory_space=pl.ANY)
    return pl.pallas_call(
        finish_kernel,
        out_shape=[S(acts.shape, bf), S(grads.shape, bf)] + [S(shape, f32) for shape in shapes],
        in_specs=[hbm] * 3,
        out_specs=[hbm] * 6,
        scratch_shapes=[v(parts.shape, bf), v(acts.shape, bf), v(grads.shape, bf)] + [v(shape, f32) for shape in shapes]
        + [dma((12,)), dma((2,)), dma((11,))],
        compiler_params=pltpu.CompilerParams(vmem_limit_bytes=40 * 2**20),
    )(parts, acts, grads)


def by_page(
    token_in,
    cotangent,
    w_qkv,
    qv_bias,
    w_attn_out,
    w_ffn_in,
    ffn_in_bias,
    w_ffn_out,
    out_biases,
    norm_gains,
    norm_shifts,
):
    core, place = lax.axis_index("section"), lax.axis_index("mp")
    width = token_in.shape[2]
    quarter = width // 4
    vec = high(jnp.concatenate([qv_bias[0], ffn_in_bias[0].reshape(4, quarter)], axis=0))
    vec = jnp.pad(vec, ((0, 2), (0, 0)))
    norms = jnp.concatenate([out_biases[0], norm_gains[0], norm_shifts[0]], axis=0)
    norms = jnp.pad(norms, ((0, 2), (0, 0)))
    full, vecs, norms, *saved, acts = gather_forward(
        HEAD_DIM, token_in, w_qkv[0], w_attn_out[0], w_ffn_in[0], w_ffn_out[0], vec, norms
    )
    parts, grads, totals = backward_reduce(HEAD_DIM, token_in, cotangent, full, norms, saved)
    parts = parts.reshape(12, quarter, width)
    acts, grads, grad_qkv, grad_out, grad_up, grad_down = finish(parts, acts, grads)
    totals = lax.dynamic_index_in_dim(totals, core, 0, keepdims=False)
    own = lax.dynamic_slice_in_dim(totals[8:], place * quarter, quarter, 1)
    piece = width // (lax.axis_size("mp") * lax.axis_size("dp"))
    begin = (place * lax.axis_size("dp") + lax.axis_index("dp")) * piece
    rows = lax.dynamic_slice_in_dim(totals[:8], begin, piece, 1)
    return (
        acts[None],
        grads[None],
        grad_qkv[None],
        own[0:2][None],
        grad_out[None],
        grad_up[None],
        own[2:6].reshape(1, width),
        grad_down[None],
        rows[0:2][None],
        rows[2:4][None],
        rows[4:6][None],
    )


def on_device(*args):
    token_in, w_qkv, ffn_in = args[0], args[2], args[5]
    fits = (
        lax.axis_size("section") == 2
        and lax.axis_size("mp") == 4
        and lax.axis_size("dp") == 4
        and token_in.shape == (2, SEQ, 1024)
        and w_qkv.shape[3] == 256
        and ffn_in.shape[2] == 1024
    )
    return by_page(*args) if fits else pipelined(*args)


def solution(mesh):
    return jax.shard_map(
        on_device,
        mesh=mesh,
        in_specs=(
            P(None, ("dp", "mp"), None),
            P(None, ("dp", "mp"), None),
            P("section", None, None, "mp"),
            P("section", None, "mp"),
            P("section", "mp", None),
            P("section", None, "mp"),
            P("section", "mp"),
            P("section", "mp", None),
            P("section", None, None),
            P("section", None, None),
            P("section", None, None),
        ),
        out_specs=(
            P("section", None, ("dp", "mp"), None),
            P("section", None, ("dp", "mp"), None),
            P("section", None, None, "mp"),
            P("section", None, "mp"),
            P("section", "mp", None),
            P("section", None, "mp"),
            P("section", "mp"),
            P("section", "mp", None),
            P("section", None, ("mp", "dp")),
            P("section", None, ("mp", "dp")),
            P("section", None, ("mp", "dp")),
        ),
        check_vma=False,
    )
```

```python
import functools
from functools import partial
import math

import jax
import jax.numpy as jnp
from jax import lax
from jax.experimental import pallas as pl
from jax.experimental.pallas import tpu as pltpu
from jax.sharding import PartitionSpec as P

HEAD_DIM = 64
SEQ = 512


def from_behind(value, axis, by):
    devices = lax.axis_size(axis)
    pairs = [(i, i + by) for i in range(devices) if 0 <= i + by < devices]
    return lax.ppermute(value, axis, pairs)


def norm_rows(values, gain_row, shift_row):
    average = jnp.mean(values, axis=-1, keepdims=True)
    centered = values - average
    variance = jnp.mean(centered * centered, axis=-1, keepdims=True)
    return centered * lax.rsqrt(variance + 1e-05) * gain_row + shift_row


def exact_gelu(values):
    return jax.nn.gelu(values, approximate=False)


def layer_forward(params, token_rows):
    (
        w_qkv,
        qv_bias,
        w_attn_out,
        w_ffn_in,
        ffn_in_bias,
        w_ffn_out,
        out_biases,
        norm_gains,
        norm_shifts,
    ) = params
    gathered = lax.all_gather(token_rows, "mp", axis=0, tiled=True)
    rows_all = gathered.shape[0]
    local_width = w_qkv.shape[2]
    local_heads = local_width // HEAD_DIM
    page_count = rows_all // SEQ
    scale_factor = 1.0 / math.sqrt(HEAD_DIM)
    bias_full = jnp.stack([qv_bias[0], jnp.zeros_like(qv_bias[0]), qv_bias[1]]).astype(jnp.float32)
    projected = (
        jnp.einsum("rd,cde->cre", gathered, w_qkv, preferred_element_type=jnp.float32)
        + bias_full[:, None, :]
    )
    heads_view = projected.astype(jnp.bfloat16).reshape(3, page_count, SEQ, local_heads, HEAD_DIM)
    scores = (
        jnp.einsum(
            "pqhe,pkhe->phqk", heads_view[0], heads_view[1], preferred_element_type=jnp.float32
        )
        * scale_factor
    )
    top_score = jnp.max(scores, axis=-1, keepdims=True)
    exponent = jnp.exp(scores - top_score)
    weights_soft = exponent / jnp.sum(exponent, axis=-1, keepdims=True)
    weights_low = weights_soft.astype(jnp.bfloat16)
    attended = jnp.einsum(
        "phqk,pkhe->pqhe", weights_low, heads_view[2], preferred_element_type=jnp.float32
    )
    attended = attended.reshape(rows_all, local_width).astype(jnp.bfloat16)
    attn_part = jnp.dot(attended, w_attn_out, preferred_element_type=jnp.float32)
    attn_rows = lax.psum_scatter(
        attn_part.astype(jnp.bfloat16), "mp", scatter_dimension=0, tiled=True
    ).astype(jnp.float32)
    residual_one = attn_rows + out_biases[0] + token_rows.astype(jnp.float32)
    first = norm_rows(residual_one, norm_gains[0], norm_shifts[0])
    first_all = lax.all_gather(first.astype(jnp.bfloat16), "mp", axis=0, tiled=True)
    pre_act = jnp.dot(first_all, w_ffn_in, preferred_element_type=jnp.float32) + ffn_in_bias.astype(
        jnp.float32
    )
    activated = exact_gelu(pre_act).astype(jnp.bfloat16)
    ffn_part = jnp.dot(activated, w_ffn_out, preferred_element_type=jnp.float32)
    ffn_rows = lax.psum_scatter(
        ffn_part.astype(jnp.bfloat16), "mp", scatter_dimension=0, tiled=True
    ).astype(jnp.float32)
    residual_two = ffn_rows + out_biases[1] + first
    result = norm_rows(residual_two, norm_gains[1], norm_shifts[1])
    kept_values = (
        gathered,
        heads_view,
        weights_soft,
        attended,
        residual_one,
        first_all,
        pre_act,
        activated,
        residual_two,
    )
    return (result, kept_values)


def layer_backward(params, kept_values, grad_out):
    (
        w_qkv,
        qv_bias,
        w_attn_out,
        w_ffn_in,
        ffn_in_bias,
        w_ffn_out,
        out_biases,
        norm_gains,
        norm_shifts,
    ) = params
    (
        gathered,
        heads_view,
        weights_soft,
        attended,
        residual_one,
        first_all,
        pre_act,
        activated,
        residual_two,
    ) = kept_values
    rows_all = gathered.shape[0]
    local_width = w_qkv.shape[2]
    local_heads = local_width // HEAD_DIM
    page_count = rows_all // SEQ
    scale_factor = 1.0 / math.sqrt(HEAD_DIM)
    unused_two, norm_two_back = jax.vjp(norm_rows, residual_two, norm_gains[1], norm_shifts[1])
    grad_res_two, grad_gain_two, grad_shift_two = norm_two_back(grad_out)
    grad_bias_two = jnp.sum(grad_res_two, axis=0)
    ffn_grad_all = lax.all_gather(grad_res_two.astype(jnp.bfloat16), "mp", axis=0, tiled=True)
    grad_w_ffn_out = jnp.einsum(
        "rf,rd->fd", activated, ffn_grad_all, preferred_element_type=jnp.float32
    )
    grad_act = jnp.einsum("rd,fd->rf", ffn_grad_all, w_ffn_out, preferred_element_type=jnp.float32)
    unused_gelu, gelu_back = jax.vjp(exact_gelu, pre_act)
    grad_pre = gelu_back(grad_act)[0].astype(jnp.bfloat16)
    grad_ffn_in_bias = jnp.sum(grad_pre.astype(jnp.float32), axis=0)
    grad_w_ffn_in = jnp.einsum("rd,rf->df", first_all, grad_pre, preferred_element_type=jnp.float32)
    first_part = jnp.einsum("rf,df->rd", grad_pre, w_ffn_in, preferred_element_type=jnp.float32)
    first_grad_rows = lax.psum_scatter(
        first_part.astype(jnp.bfloat16), "mp", scatter_dimension=0, tiled=True
    ).astype(jnp.float32)
    grad_first = first_grad_rows + grad_res_two
    unused_one, norm_one_back = jax.vjp(norm_rows, residual_one, norm_gains[0], norm_shifts[0])
    grad_res_one, grad_gain_one, grad_shift_one = norm_one_back(grad_first)
    grad_bias_one = jnp.sum(grad_res_one, axis=0)
    attn_grad_all = lax.all_gather(grad_res_one.astype(jnp.bfloat16), "mp", axis=0, tiled=True)
    grad_w_attn_out = jnp.einsum(
        "rk,rd->kd", attended, attn_grad_all, preferred_element_type=jnp.float32
    )
    grad_attended = jnp.einsum(
        "rd,kd->rk", attn_grad_all, w_attn_out, preferred_element_type=jnp.float32
    )
    grad_attended = grad_attended.astype(jnp.bfloat16).reshape(
        page_count, SEQ, local_heads, HEAD_DIM
    )
    weights_low = weights_soft.astype(jnp.bfloat16)
    grad_weights = jnp.einsum(
        "pqhe,pkhe->phqk", grad_attended, heads_view[2], preferred_element_type=jnp.float32
    )
    grad_values = jnp.einsum(
        "phqk,pqhe->pkhe", weights_low, grad_attended, preferred_element_type=jnp.float32
    )
    inner_total = jnp.sum(weights_soft * grad_weights, axis=-1, keepdims=True)
    grad_scores = (weights_soft * (grad_weights - inner_total)).astype(jnp.bfloat16)
    grad_queries = (
        jnp.einsum(
            "phqk,pkhe->pqhe", grad_scores, heads_view[1], preferred_element_type=jnp.float32
        )
        * scale_factor
    )
    grad_keys = (
        jnp.einsum(
            "phqk,pqhe->pkhe", grad_scores, heads_view[0], preferred_element_type=jnp.float32
        )
        * scale_factor
    )
    grad_proj = (
        jnp.stack([grad_queries, grad_keys, grad_values])
        .reshape(3, rows_all, local_width)
        .astype(jnp.bfloat16)
    )
    proj_sums = jnp.sum(grad_proj.astype(jnp.float32), axis=1)
    grad_qv_bias = jnp.stack([proj_sums[0], proj_sums[2]])
    grad_w_qkv = jnp.einsum("rd,cre->cde", gathered, grad_proj, preferred_element_type=jnp.float32)
    input_part = jnp.einsum("cre,cde->rd", grad_proj, w_qkv, preferred_element_type=jnp.float32)
    input_grad_rows = lax.psum_scatter(
        input_part.astype(jnp.bfloat16), "mp", scatter_dimension=0, tiled=True
    ).astype(jnp.float32)
    grad_in = input_grad_rows + grad_res_one
    matrix_grads = (
        grad_w_qkv,
        grad_qv_bias,
        grad_w_attn_out,
        grad_w_ffn_in,
        grad_ffn_in_bias,
        grad_w_ffn_out,
    )
    vector_grads = (
        jnp.stack([grad_bias_one, grad_bias_two]),
        jnp.stack([grad_gain_one, grad_gain_two]),
        jnp.stack([grad_shift_one, grad_shift_two]),
    )
    return (grad_in, matrix_grads, vector_grads)


def pipelined(
    token_in,
    cotangent,
    w_qkv,
    qv_bias,
    w_attn_out,
    w_ffn_in,
    ffn_in_bias,
    w_ffn_out,
    out_biases,
    norm_gains,
    norm_shifts,
):
    params = (
        w_qkv[0],
        qv_bias[0],
        w_attn_out[0],
        w_ffn_in[0],
        ffn_in_bias[0],
        w_ffn_out[0],
        out_biases[0],
        norm_gains[0],
        norm_shifts[0],
    )
    micro_count = token_in.shape[0]
    section_index = lax.axis_index("section")
    is_first = section_index == 0
    zero_rows = jnp.zeros(token_in.shape[1:], jnp.bfloat16)
    run_forward = partial(layer_forward, params)
    run_backward = partial(layer_backward, params)

    def forward_step(step_index, carry):
        received, saved, stored = carry
        own_micro = step_index - section_index
        is_valid = (own_micro >= 0) & (own_micro < micro_count)
        slot_index = jnp.clip(own_micro, 0, micro_count - 1)
        first_rows = lax.dynamic_index_in_dim(
            token_in, jnp.minimum(step_index, micro_count - 1).astype(jnp.int32), 0, keepdims=False
        )
        layer_in = jnp.where(is_first, first_rows, received)
        result, unused_kept = run_forward(layer_in)
        result_low = result.astype(jnp.bfloat16)
        old_saved = lax.dynamic_index_in_dim(saved, slot_index, 0, keepdims=False)
        saved = lax.dynamic_update_index_in_dim(
            saved, jnp.where(is_valid, layer_in, old_saved), slot_index, 0
        )
        old_stored = lax.dynamic_index_in_dim(stored, slot_index, 0, keepdims=False)
        stored = lax.dynamic_update_index_in_dim(
            stored, jnp.where(is_valid, result_low, old_stored), slot_index, 0
        )
        received = from_behind(result_low, "section", 1)
        return (received, saved, stored)

    start_carry = (zero_rows, jnp.zeros_like(token_in), jnp.zeros_like(token_in))
    unused_received, saved, stored = lax.fori_loop(0, micro_count + 1, forward_step, start_carry)
    matrix_zero = tuple((jnp.zeros(entry.shape, jnp.float32) for entry in params[:6]))
    vector_zero = (
        jnp.zeros(out_biases.shape[1:], jnp.float32),
        jnp.zeros(norm_gains.shape[1:], jnp.float32),
        jnp.zeros(norm_shifts.shape[1:], jnp.float32),
    )

    def backward_step(step_index, carry):
        received_grad, grad_store, matrix_sums, vector_sums = carry
        own_micro = step_index - (1 - section_index)
        is_valid = (own_micro >= 0) & (own_micro < micro_count)
        slot_index = jnp.clip(own_micro, 0, micro_count - 1)
        layer_in = lax.dynamic_index_in_dim(saved, slot_index, 0, keepdims=False)
        from_last = lax.dynamic_index_in_dim(cotangent, slot_index, 0, keepdims=False)
        grad_out = jnp.where(is_first, received_grad, from_last).astype(jnp.float32)
        unused_result, kept_values = run_forward(layer_in)
        grad_in, matrix_grads, vector_grads = run_backward(kept_values, grad_out)
        matrix_grads = tuple((jnp.where(is_valid, entry, 0.0) for entry in matrix_grads))
        vector_grads = tuple((jnp.where(is_valid, entry, 0.0) for entry in vector_grads))
        grad_low = grad_in.astype(jnp.bfloat16)
        old_piece = lax.dynamic_index_in_dim(grad_store, slot_index, 0, keepdims=False)
        grad_store = lax.dynamic_update_index_in_dim(
            grad_store, jnp.where(is_valid, grad_low, old_piece), slot_index, 0
        )
        grad_one, grad_two, grad_three, grad_four, grad_five, grad_six = matrix_grads
        matrix_grads = (
            lax.psum(grad_one.astype(jnp.bfloat16), "dp").astype(jnp.float32),
            lax.psum(grad_two.astype(jnp.bfloat16), "dp").astype(jnp.float32),
            lax.psum(grad_three.astype(jnp.bfloat16), "dp").astype(jnp.float32),
            lax.psum(grad_four.astype(jnp.bfloat16), "dp").astype(jnp.float32),
            lax.psum(grad_five.astype(jnp.bfloat16), "dp").astype(jnp.float32),
            lax.psum(grad_six.astype(jnp.bfloat16), "dp").astype(jnp.float32),
        )
        matrix_sums = tuple((total + extra for total, extra in zip(matrix_sums, matrix_grads)))
        vector_sums = tuple((total + extra for total, extra in zip(vector_sums, vector_grads)))
        received_grad = from_behind(grad_low, "section", -1)
        return (received_grad, grad_store, matrix_sums, vector_sums)

    back_carry = (zero_rows, jnp.zeros_like(token_in), matrix_zero, vector_zero)
    unused_grad, grad_store, matrix_sums, vector_sums = lax.fori_loop(
        0, micro_count + 1, backward_step, back_carry
    )
    bias_total, gain_total, shift_total = vector_sums
    bias_part, gain_part, shift_part = (
        lax.psum_scatter(bias_total, ("mp", "dp"), scatter_dimension=1, tiled=True),
        lax.psum_scatter(gain_total, ("mp", "dp"), scatter_dimension=1, tiled=True),
        lax.psum_scatter(shift_total, ("mp", "dp"), scatter_dimension=1, tiled=True),
    )
    return (
        stored[None],
        grad_store[None],
        matrix_sums[0][None],
        matrix_sums[1][None],
        matrix_sums[2][None],
        matrix_sums[3][None],
        matrix_sums[4][None],
        matrix_sums[5][None],
        bias_part[None],
        gain_part[None],
        shift_part[None],
    )


MESH = pl.DeviceIdType.MESH
CHUNKS = 24
TRIPLES = 8
SCALE = 0.125


def low(value):
    return value.astype(jnp.bfloat16)


def high(value):
    return value.astype(jnp.float32)


def remote(src, dst, send, recv, device):
    return pltpu.make_async_remote_copy(
        src_ref=src, dst_ref=dst, send_sem=send, recv_sem=recv, device_id=device, device_id_type=MESH
    )


def neighbours():
    c, p, d = lax.axis_index("section"), lax.axis_index("mp"), lax.axis_index("dp")
    return {
        "core": (1 - c, p, d),
        "x": (c, p + 1 - 2 * lax.rem(p, 2), d),
        "y": (c, lax.rem(p + 2, 4), d),
        "across": (c, p, 3 - d),
        "inner": (c, p, jnp.where(d == 0, 1, 2)),
        "outer": (c, p, jnp.where(d == 1, 0, 3)),
    }


def places():
    p = lax.axis_index("mp")
    return [p, p + 1 - 2 * lax.rem(p, 2), lax.rem(p + 2, 4), 3 - p]


def dot(a, b):
    return jnp.dot(a, b, preferred_element_type=jnp.float32)


def dot_tn(a, b):
    return lax.dot_general(a, b, (((0,), (0,)), ((), ())), preferred_element_type=jnp.float32)


def dot_nt(a, b):
    return lax.dot_general(a, b, (((1,), (1,)), ((), ())), preferred_element_type=jnp.float32)


def standard(values):
    average = jnp.mean(values, axis=-1, keepdims=True)
    centered = values - average
    variance = jnp.mean(centered * centered, axis=-1, keepdims=True)
    scale = lax.rsqrt(variance + 1e-05)
    return centered * scale, scale


def softmax(q, k):
    scores = dot_nt(q * jnp.asarray(SCALE, q.dtype), k)
    exponent = jnp.exp(scores - jnp.max(scores, axis=-1, keepdims=True))
    return exponent * (1.0 / jnp.sum(exponent, axis=-1, keepdims=True))


def by_rows(rows, step, body):
    def run(i, carry):
        body(pl.ds(pl.multiple_of(i * step, step), step))
        return carry

    lax.fori_loop(0, rows // step, run, 0)


def first_norm(x, nrm, acc, u1, hb):
    def run(rows):
        u = acc[rows] + nrm[0:1] + high(x[rows])
        u1[rows] = u
        h = standard(u)[0] * nrm[2:3] + nrm[4:5]
        hb[rows] = low(h)
        acc[rows] = h + nrm[1:2]

    by_rows(acc.shape[0], 64, run)


def second_norm(nrm, acc, u2, out):
    def run(rows):
        u = acc[rows]
        u2[rows] = u
        out[rows] = low(standard(u)[0] * nrm[3:4] + nrm[5:6])

    by_rows(acc.shape[0], 64, run)


def norm_back(u, grad, gain, sums, at, out_low, out_acc):
    def run(rows):
        g = high(grad[rows])
        xhat, scale = standard(u[rows])
        scaled = g * gain
        du = scale * (
            scaled
            - jnp.mean(scaled, axis=-1, keepdims=True)
            - xhat * jnp.mean(scaled * xhat, axis=-1, keepdims=True)
        )
        out_low[rows] = low(du)
        out_acc[rows] = du
        for row, term in ((at[0], du), (at[1], g * xhat), (at[2], g)):
            sums[row : row + 1] += jnp.sum(term, axis=0, keepdims=True)

    by_rows(u.shape[0], 64, run)


def ffn_back_block(dfb, w, gd, acc, dz_out):
    dz = low(dot_nt(dfb[...], w[1]) * high(gd))
    dz_out[...] = dz
    acc[...] += dot(dz, w[0])
    return jnp.sum(high(dz), axis=0, keepdims=True)


def attention_back_block(dab, w, qkv, dq_out, dk_out, dv_out, acc, dim):
    dob = low(dot_nt(dab[...], w[3]))
    for j in range(dob.shape[1] // dim):
        cols = slice(j * dim, (j + 1) * dim)
        q, k, v, do = qkv[0, :, cols], qkv[1, :, cols], qkv[2, :, cols], dob[:, cols]
        a = softmax(q, k)
        da = dot_nt(do, v)
        ds = low(a * (da - jnp.sum(a * da, axis=-1, keepdims=True)))
        dv_out[:, cols] = low(dot_tn(low(a), do))
        dq_out[:, cols] = low(dot(ds, k) * SCALE)
        dk_out[:, cols] = low(dot_tn(ds, q) * SCALE)
    acc[...] += dot(dq_out[...], w[0]) + dot(dk_out[...], w[1]) + dot(dv_out[...], w[2])


def weight_copies(full, layer, kind, p, b, buf, sem, rows):
    width = 4 * rows
    if kind == 0:
        starts = [c * width + p * rows for c in range(4)]
    else:
        starts = [4 * width + t * 4 * width + p * width + b * rows for t in range(2)]
    return [
        pltpu.make_async_copy(full.at[layer, pl.ds(pl.multiple_of(start, rows), rows)], buf.at[n], sem.at[n])
        for n, start in enumerate(starts)
    ]


def project_block(x, w, vec, save, dim):
    rows = x[...]
    q = low(dot_nt(rows, w[0]) + vec[0:1])
    k = low(dot_nt(rows, w[1]))
    v = low(dot_nt(rows, w[2]) + vec[1:2])
    save[0], save[1], save[2] = q, k, v
    for j in range(q.shape[1] // dim):
        cols = slice(j * dim, (j + 1) * dim)
        save[3, :, cols] = low(dot(low(softmax(q[:, cols], k[:, cols])), v[:, cols]))


def unit_values(hb, w, bias):
    z = dot_nt(hb[...], w) + bias
    inner = 0.5 + 0.5 * lax.erf(z * math.sqrt(0.5))
    slope = inner + z * jnp.exp(-0.5 * z * z) * (1.0 / math.sqrt(2.0 * math.pi))
    return low(z * inner), low(slope)


def gather_forward_kernel(
    dim, tokens, w_qkv, w_out, w_up, w_down, vec, norm_in, full, vecs, norms, qkvo, gd, us, hbs, between, acts,
    turned, x, acc, u, hb, wa, wf, sa, gb, sd, wasem, wfsem, sasem, gbsem, sdsem, usem,
    ini_s, ini_r, loc, x1ss, x1rs, y1ss, y1rs, x2ss, x2rs, y2ss, y2rs, zs, zr, cs, cr, vs, vr, vloc, as_, ar,
):
    c, p, d = lax.axis_index("section"), lax.axis_index("mp"), lax.axis_index("dp")
    near = neighbours()
    near["pair"] = (c, p, d + 1 - 2 * lax.rem(d, 2))
    spots = places()
    rows = w_out.shape[0] // 2
    half = rows // 2
    odd = lax.rem(d, 2)
    others = [(cc, spots[r], d) for r in range(4) for cc in (c, 1 - c)][1:]

    barrier = pltpu.get_barrier_semaphore()
    for device in others + [near["pair"]]:
        pl.semaphore_signal(barrier, inc=1, device_id=device, device_id_type=MESH)
    pl.semaphore_wait(barrier, 8)

    def place_of(s, spot, h):
        k = lax.rem(s, 12)
        row = jnp.where(k < 4, k * 8 + spot * 2, 32 + (k // 4 - 1) * 32 + spot * 8 + lax.rem(k, 4) * 2)
        return s // 12, (row + h) * rows

    def block(s, spot, h, start=0, size=rows):
        layer, row = place_of(s, spot, h)
        return full.at[layer, pl.ds(pl.multiple_of(row + start, half), size)]

    def init_place(k, layer):
        row = place_of(12 * layer + k, p, 0)[1]
        return full.at[layer, pl.ds(pl.multiple_of(row, half), 2 * rows)]

    def turn(k):
        if k < 3:
            turned[k] = w_qkv[k].T
        elif 4 <= k < 8:
            turned[k - 1] = w_up[:, 2 * rows * (k - 4) : 2 * rows * (k - 3)].T

    def chunk(k):
        if k == 3:
            return w_out
        if k < 8:
            return turned.at[k if k < 3 else k - 1]
        return w_down.at[pl.ds(2 * rows * (k - 8), 2 * rows)]

    def init_start(k):
        turn(k)
        pltpu.make_async_copy(chunk(k), init_place(k, c), loc.at[k]).start()
        remote(chunk(k), init_place(k, c), ini_s.at[k], ini_r.at[k], near["core"]).start()

    def init_local(k):
        return pltpu.make_async_copy(init_place(k, c), init_place(k, c), loc.at[k])

    def init_wait(k):
        there = init_place(k, 1 - c)
        remote(there, there, ini_s.at[k], ini_r.at[k], near["core"]).wait_recv()

    def small():
        copies = [remote(vec, vecs.at[c, p], vs.at[i], vr.at[c, p], device) for i, device in enumerate(others)]
        copies.append(remote(norm_in, norms.at[c], vs.at[7], vr.at[0, 4], near["core"]))
        return copies

    def small_local():
        return [
            pltpu.make_async_copy(vec, vecs.at[c, p], vloc.at[0]),
            pltpu.make_async_copy(norm_in, norms.at[c], vloc.at[1]),
        ]

    def hop(s, spot, name, pick):
        ss, rs = (x1ss, x1rs) if pick == "x" else (y1ss, y1rs)
        b = block(s, spot, c)
        return remote(b, b, ss.at[s], rs.at[s], near[name])

    def first(s, name):
        return hop(s, p, name, name)

    def arrived(s, name):
        return hop(s, spots[1] if name == "x" else spots[2], name, name)

    def relay(s, name, spot=None):
        if name == "x":
            b = block(s, spots[2] if spot is None else spot, c, 0, half)
            return remote(b, b, x2ss.at[s], x2rs.at[s], near["x"])
        b = block(s, spots[1] if spot is None else spot, c, half, half)
        return remote(b, b, y2ss.at[s], y2rs.at[s], near["y"])

    def relayed(s, name):
        return relay(s, name, spots[3])

    def to_pair(s, r):
        b = block(s, spots[r], c)
        return remote(b, b, zs.at[s, r - 1], zr.at[s, r - 1], near["pair"])

    def to_core(s, r):
        b = block(s, spots[r], c)
        return remote(b, b, cs.at[s, r - 1], cr.at[s, r - 1], near["core"])

    def from_core(s, r):
        b = block(s, spots[r], 1 - c)
        return remote(b, b, cs.at[s, r - 1], cr.at[s, r - 1], near["core"])

    def sent_chunk(j):
        t, n = j // 2, lax.rem(j, 2)
        return 3 * t + (1 - n) * (1 + odd), n == 0

    def stage_a(j):
        s = sent_chunk(j)[0]
        for m in range(3):
            own = 3 * (j // 2) + m

            @pl.when((own // 12 != c) & (lax.rem(j, 2) == 0))
            def _():
                init_wait(lax.rem(own, 12))

            @pl.when((own // 12 == c) & (lax.rem(j, 2) == 0))
            def _():
                init_local(lax.rem(own, 12)).wait()

        first(s, "x").start()
        first(s, "y").start()

    def stage_b(j):
        s, shared = sent_chunk(j)
        arrived(s, "x").wait_recv()
        relay(s, "y").start()
        arrived(s, "y").wait_recv()
        relay(s, "x").start()
        for r in (1, 2):
            to_core(s, r).start()

        @pl.when(shared)
        def _():
            for r in (1, 2):
                to_pair(s, r).start()

    def stage_c(j):
        s, shared = sent_chunk(j)
        relayed(s, "x").wait_recv()
        relayed(s, "y").wait_recv()
        to_core(s, 3).start()

        @pl.when(shared)
        def _():
            to_pair(s, 3).start()

    def stage_d(t):
        s = 3 * t + 2 - odd
        for r in (1, 2, 3):
            to_pair(s, r).wait_recv()
            to_core(s, r).start()

    def stage_e(t):
        for j in range(3):
            for r in (1, 2, 3):
                from_core(3 * t + j, r).wait_recv()

    def stage_f(t):
        for n, s in enumerate((3 * t, 3 * t + 1 + odd)):
            first(s, "x").wait_send()
            first(s, "y").wait_send()
            relay(s, "x").wait_send()
            relay(s, "y").wait_send()
            for r in (1, 2, 3):
                if n:
                    to_pair(s, r).wait_send()
        for j in range(3):
            for r in (1, 2, 3):
                to_core(3 * t + j, r).wait_send()

    wide = 2 * rows

    def weights(l, number, place, sem):
        begin = pl.multiple_of(number * wide, wide)
        return pltpu.make_async_copy(full.at[l, pl.ds(begin, wide)], place, sem)

    def load_qkv(l, q):
        return [weights(l, 4 * n + q, wa.at[q, n], wasem.at[q, n]) for n in range(3)]

    def load(l, number, slot):
        return weights(l, number, wf.at[slot], wfsem.at[slot])

    def load_out(l, q):
        return load(l, 12 + q, q)

    def load_in(l, b, q, slot):
        return load(l, 16 + 4 * q + b, slot)

    def load_down(l, b, q, slot):
        return load(l, 32 + 4 * q + b, slot)

    def save_attn(l, q):
        return pltpu.make_async_copy(sa.at[q], qkvo.at[l, q], sasem.at[q])

    def save_g(l, n):
        return pltpu.make_async_copy(gb.at[n], gd.at[l, n, 0], gbsem.at[n])

    def save_d(l, n, slot):
        return pltpu.make_async_copy(sd.at[slot], gd.at[l, n, 1], sdsem.at[slot])

    def keep(l, which):
        if which == 2:
            return pltpu.make_async_copy(hb, hbs.at[l], usem.at[2])
        if which == 3:
            return pltpu.make_async_copy(x, between, usem.at[3])
        return pltpu.make_async_copy(u, us.at[l, which], usem.at[which])

    def give(l, begin):
        @pl.when(l == c)
        def _():
            copy = pltpu.make_async_copy(x, acts.at[c], as_.at[0])
            copy.start() if begin else copy.wait()

        @pl.when(l != c)
        def _():
            copy = remote(x, acts.at[c], as_.at[0], ar.at[0], near["core"])
            copy.start() if begin else copy.wait_send()

    def kept(l):
        @pl.when(l == 0)
        def _():
            keep(0, 3).wait()

        give(l, False)

    def each(count, body):
        def run(q, carry):
            body(q)
            return carry

        lax.fori_loop(0, count, run, 0)

    def attention_segment(l, q):
        for copy in load_qkv(l, q):
            copy.wait()
        project_block(x, wa.at[q], vecs[l, q], sa.at[q], dim)
        save_attn(l, q).start()

    def out_segment(l):
        @pl.when(l == 1)
        def _():
            keep(0, 1).wait()

        acc[...] = jnp.zeros_like(acc)

        def branch(q):
            load_out(l, q).wait()
            acc[...] += dot(sa[q, 3], wf[q])
            load_in(l, 1, q, q).start()

        each(4, branch)
        first_norm(x, norms.at[l], acc, u, hb)
        keep(l, 0).start()
        keep(l, 2).start()

    def up_segment(l, b, slot):
        def run(q):
            load_in(l, b, q, slot + q).wait()
            n, two = 4 * q + b, lax.rem(q, 2)

            @pl.when(q >= 2)
            def _():
                save_d(l, n - 8, two).wait()

            g, slope = unit_values(hb, wf[slot + q], vecs[l, q, pl.ds(2 + b, 1)])
            gb[n] = g
            sd[two] = slope
            save_g(l, n).start()
            save_d(l, n, two).start()

        each(4, run)
        for q in (2, 3):
            save_d(l, 4 * q + b, q % 2).wait()

    def down_segment(l, b, slot):
        def run(q):
            load_down(l, b, q, slot + q).wait()
            acc[...] += dot(gb[4 * q + b], wf[slot + q])

        each(4, run)

    def end_segment(l):
        keep(l, 0).wait()
        keep(l, 2).wait()
        each(4, lambda q: save_attn(l, q).wait())
        each(16, lambda n: save_g(l, n).wait())

        @pl.when(l == 1)
        def _():
            kept(0)

        second_norm(norms.at[l], acc, u, x)
        keep(l, 1).start()
        give(l, True)

        @pl.when(l == 0)
        def _():
            keep(0, 3).start()

    def small_there():
        for copy in small_local():
            copy.wait()
        for copy in small():
            copy.wait_send()
        for cc, spot in [(cc, spots[r]) for r in range(4) for cc in (c, 1 - c)][1:]:
            remote(vec, vecs.at[cc, spot], vs.at[0], vr.at[cc, spot], near["core"]).wait_recv()
        remote(norm_in, norms.at[1 - c], vs.at[7], vr.at[0, 4], near["core"]).wait_recv()

    def compute(m):
        l, part = m // 8, lax.rem(m, 8)

        def at(number, body):
            @pl.when(part == number)
            def _():
                body()

        def attention_first():
            for q in range(4):
                for copy in load_qkv(l, q):
                    copy.start()

            @pl.when(m == 0)
            def _():
                small_there()
                first_rows.wait()

        def attention_half(begin):
            each(2, lambda q: attention_segment(l, begin + q))

        def out_part():
            for q in range(4):
                load_out(l, q).start()
            for q in range(4):
                load_in(l, 0, q, 4 + q).start()
            out_segment(l)

        def up_part():
            for q in range(4):
                load_in(l, 2, q, q).start()
            for q in range(4):
                load_in(l, 3, q, 4 + q).start()
            up_segment(l, 2, 0)
            for q in range(4):
                load_down(l, 0, q, q).start()

        def turn_part():
            up_segment(l, 3, 4)
            down_segment(l, 0, 0)

        def down_part():
            for b in (1, 2):
                for q in range(4):
                    load_down(l, b, q, 4 * (b - 1) + q).start()
            down_segment(l, 1, 0)
            for q in range(4):
                load_down(l, 3, q, q).start()
            down_segment(l, 2, 4)

        def end_part():
            down_segment(l, 3, 0)
            end_segment(l)

        at(0, attention_first)

        @pl.when(part < 2)
        def _():
            attention_half(2 * part)

        at(2, out_part)

        @pl.when((part == 2) | (part == 3))
        def _():
            b = part - 2
            up_segment(l, b, 4 - 4 * b)

        at(4, up_part)
        at(5, turn_part)
        at(6, down_part)
        at(7, end_part)

    first_rows = pltpu.make_async_copy(tokens.at[c], x, usem.at[4])
    first_rows.start()
    for k in range(3):
        init_start(k)
    for copy in small_local() + small():
        copy.start()

    def step(count, carry):
        i = count - 1

        def run(stage, lag):
            @pl.when((i >= lag) & (i < 2 * TRIPLES + lag))
            def _():
                stage(i - lag)

        def run_late(stage, lag):
            @pl.when((i >= lag) & (i < 2 * TRIPLES + lag) & (lax.rem(i - lag, 2) == 0))
            def _():
                stage((i - lag) // 2)

        run(stage_a, -1)
        run(stage_b, 1)
        run(stage_c, 2)
        run_late(stage_d, 4)
        run_late(stage_e, 5)
        run_late(stage_f, 6)
        for t in range(3):

            @pl.when(i == 2 * t)
            def _():
                for k in range(3 * t + 3, 3 * t + 6):
                    init_start(k)

        run(compute, 5)
        return carry

    lax.fori_loop(0, 2 * TRIPLES + 6, step, 0)

    for k in range(12):
        remote(chunk(k), init_place(k, c), ini_s.at[k], ini_r.at[k], near["core"]).wait_send()
    keep(1, 1).wait()
    kept(1)
    remote(x, acts.at[1 - c], as_.at[0], ar.at[0], near["core"]).wait_recv()


def gather_forward(dim, tokens, w_qkv, w_out, w_up, w_down, vec, norms):
    rows, width = w_out.shape
    seq = tokens.shape[1]
    bf, f32, dma, v = jnp.bfloat16, jnp.float32, pltpu.SemaphoreType.DMA, pltpu.VMEM
    hbm, vmem = pl.BlockSpec(memory_space=pl.ANY), pl.BlockSpec(memory_space=pltpu.VMEM)
    S = jax.ShapeDtypeStruct
    return pl.pallas_call(
        functools.partial(gather_forward_kernel, dim),
        out_shape=(
            S((2, 48 * rows, width), bf), S((2, 4) + vec.shape, f32), S((2,) + norms.shape, f32),
            S((2, 4, 4, seq, rows), bf), S((2, 16, 2, seq, rows), bf), S((2, 2, seq, width), f32),
            S((2, seq, width), bf), S((seq, width), bf), S((2, seq, width), bf),
        ),
        in_specs=[hbm] + [vmem] * 6,
        out_specs=[hbm, vmem, vmem] + [hbm] * 6,
        scratch_shapes=[
            v((7, rows, width), bf),
            v((seq, width), bf), v((seq, width), f32), v((seq, width), f32), v((seq, width), bf),
            v((4, 3, rows, width), bf), v((8, rows, width), bf), v((4, 4, seq, rows), bf), v((16, seq, rows), bf),
            v((2, seq, rows), bf), dma((4, 3)), dma((8,)), dma((4,)), dma((16,)), dma((2,)), dma((5,)),
        ] + [dma((12,))] * 3 + [dma((24,))] * 8 + [dma((24, 3))] * 4
        + [dma((8,)), dma((2, 5)), dma((2,)), dma((1,)), dma((1,))],
        compiler_params=pltpu.CompilerParams(collective_id=0, has_side_effects=True, vmem_limit_bytes=60 * 2**20),
    )(tokens, w_qkv, w_out, w_up, w_down, vec, norms)


def backward_reduce_kernel(
    dim, tokens, cots, full, norms, qkvo, gd, us, hbs, between, out, grads, totals,
    left, right, acc, g, u, wa, wf, da, df, trades,
    sendc, recvc, keep, x1s, x1r, y1s, y1r, part, base, x2s, x2r, y2s, y2r, mid,
    zk, zs1, zr1, zs2, zr2, zs3, zr3,
    wasem, wfsem, dasem, dfsem, gsem, osem4, bsem, gds, gdr, tss, trs,
    cs, cr, x1ss, x1rs, y1ss, y1rs, x2ss, x2rs, y2ss, y2rs, z1ss, z1rs, z2ss, z2rs, z3ss, z3rs, os, orr,
):
    c, p, d = lax.axis_index("section"), lax.axis_index("mp"), lax.axis_index("dp")
    near = neighbours()
    near["pair"] = (c, p, d + 1 - 2 * lax.rem(d, 2))
    near["far"] = (c, p, lax.rem(d + 2, 4))
    spots = places()
    is_end = (d == 0) | (d == 3)
    is_mid = jnp.logical_not(is_end)
    rows = sendc.shape[2]
    half = rows // 2
    wide = 2 * rows

    barrier = pltpu.get_barrier_semaphore()

    def signal(device):
        pl.semaphore_signal(barrier, inc=1, device_id=device, device_id_type=MESH)

    for name in ("core", "x", "y", "pair", "far"):
        signal(near[name])

    @pl.when(is_end)
    def _():
        pl.semaphore_wait(barrier, 5)

    @pl.when(is_mid)
    def _():
        signal(near["across"])
        pl.semaphore_wait(barrier, 6)

    def core_copy(s):
        a, b = lax.rem(s, 2), lax.rem(s, 4)
        return remote(sendc.at[a], recvc.at[b], cs.at[a], cr.at[b], near["core"])

    def link_copy(s, src, dst, ss, rs, name):
        a, b = lax.rem(s, 2), lax.rem(s, 4)
        return remote(src.at[a], dst.at[b], ss.at[a], rs.at[b], near[name])

    def first_copy(s, n, src, dst, ss, rs, name):
        a, b = lax.rem(s, 2), lax.rem(s, 4)
        return remote(src.at[a, n], dst.at[b, n], ss.at[a, n], rs.at[b, n], near[name])

    x1 = lambda s, n: first_copy(s, n, x1s, x1r, x1ss, x1rs, "x")
    y1 = lambda s, n: first_copy(s, n, y1s, y1r, y1ss, y1rs, "y")
    x2 = lambda s: link_copy(s, x2s, x2r, x2ss, x2rs, "x")
    y2 = lambda s: link_copy(s, y2s, y2r, y2ss, y2rs, "y")
    z1 = lambda s, n: first_copy(s, n, zs1, zr1, z1ss, z1rs, "inner")
    z2 = lambda s, n: first_copy(s, n, zs2, zr2, z2ss, z2rs, "across")

    def z3(s, n):
        b = lax.rem(s, 6)
        return remote(zs3.at[b, n], zr3.at[b, n], z3ss.at[b, n], z3rs.at[b, n], near["outer"])

    def stage0(s):
        k, slot = lax.rem(s, 12), lax.rem(s, 2)
        stride = jnp.where(k < 8, 4, 1)
        first = jnp.where(k < 4, k, jnp.where(k < 8, 12 + k, jnp.where(k == 8, 32, 36 + 4 * (k - 9))))
        kind = jnp.where(k < 4, 0, jnp.where(k < 8, 1, jnp.where(k == 8, 2, 3)))
        for r in range(4):
            whole = dot_tn(left[first + stride * spots[r]], right[kind])
            keep[slot, r] = jnp.where(c == 0, whole[:rows], whole[rows:])
            sendc[slot, r] = low(jnp.where(c == 0, whole[rows:], whole[:rows]))
        core_copy(s).start()

    def stage1(s):
        a, b = lax.rem(s, 2), lax.rem(s, 4)
        core_copy(s).wait()
        far = keep[a, 3] + high(recvc[b, 3])
        x1s[a, 0] = low(far[:half])
        y1s[a, 0] = low(far[half:])
        x1(s, 0).start()
        y1(s, 0).start()
        by_x = keep[a, 1] + high(recvc[b, 1])
        x1s[a, 1] = low(by_x[:half])
        part[a, 0] = by_x[half:]
        by_y = keep[a, 2] + high(recvc[b, 2])
        y1s[a, 1] = low(by_y[half:])
        part[a, 1] = by_y[:half]
        x1(s, 1).start()
        y1(s, 1).start()
        base[a] = keep[a, 0] + high(recvc[b, 0])

    def stage2(s):
        a, b = lax.rem(s, 2), lax.rem(s, 4)
        x1(s, 0).wait()
        y2s[a] = low(part[a, 1] + high(x1r[b, 0]))
        y2(s).start()
        y1(s, 0).wait()
        x2s[a] = low(part[a, 0] + high(y1r[b, 0]))
        x2(s).start()
        x1(s, 1).wait()
        y1(s, 1).wait()
        own = base[a]
        mid[a, 0] = own[:half] + high(x1r[b, 1])
        mid[a, 1] = own[half:] + high(y1r[b, 1])

    def stage3(s):
        a, b = lax.rem(s, 2), lax.rem(s, 4)
        for n, copy, got in ((0, y2, y2r), (1, x2, x2r)):
            copy(s).wait()
            total = mid[a, n] + high(got[b])

            @pl.when(is_end)
            def _():
                zs1[a, n] = low(total)
                z1(s, n).start()

            @pl.when(is_mid)
            def _():
                zk[a, n] = total

    def stage4(s):
        a, b = lax.rem(s, 2), lax.rem(s, 4)
        for n in range(2):

            @pl.when(is_end)
            def _():
                z1(s, n).wait_send()

            @pl.when(is_mid)
            def _():
                z1(s, n).wait_recv()
                zs2[a, n] = low(zk[a, n] + high(zr1[b, n]))
                z2(s, n).start()

    def stage5(s):
        a, b, to = lax.rem(s, 2), lax.rem(s, 4), lax.rem(s, 6)

        @pl.when(is_mid)
        def _():
            for n in range(2):
                z2(s, n).wait()
                zs3[to, n] = low(high(zs2[a, n]) + high(zr2[b, n]))
                z3(s, n).start()

    def stage6(s, begin):
        layer, k, b = 1 - s // 12, lax.rem(s, 12), lax.rem(s, 6)

        def finish(source):
            @pl.when(layer == c)
            def _():
                copy = pltpu.make_async_copy(source.at[b], out.at[k, c], os.at[b])
                copy.start() if begin else copy.wait()

            @pl.when(layer != c)
            def _():
                copy = remote(source.at[b], out.at[k, c], os.at[b], orr.at[k], near["core"])
                copy.start() if begin else copy.wait_send()

        @pl.when(is_end)
        def _():
            if begin:
                for n in range(2):
                    z3(s, n).wait_recv()
            finish(zr3)

        @pl.when(is_mid)
        def _():
            if begin:
                for n in range(2):
                    z3(s, n).wait_send()
            finish(zs3)

    def load_g(l, n):
        return pltpu.make_async_copy(gd.at[l, n, 0], left.at[n], gsem.at[n])

    def load_o(l, n):
        return pltpu.make_async_copy(qkvo.at[l, n, 3], left.at[32 + n], osem4.at[n])

    def load_h(l):
        return pltpu.make_async_copy(hbs.at[l], right.at[1], bsem.at[0])

    def load_x(source):
        return pltpu.make_async_copy(source, right.at[3], bsem.at[1])

    def load_u(l, which):
        return pltpu.make_async_copy(us.at[l, which], u, bsem.at[2])

    def ffn(l, n, slot):
        return weight_copies(full, l, 1, lax.rem(n, 4), n // 4, wf.at[slot], wfsem.at[slot], wide) + [
            pltpu.make_async_copy(gd.at[l, 4 * lax.rem(n, 4) + n // 4, 1], df.at[slot], dfsem.at[slot])
        ]

    def attn(l, q, slot):
        return weight_copies(full, l, 0, q, 0, wa.at[slot], wasem.at[slot], wide) + [
            pltpu.make_async_copy(qkvo.at[l, q], da.at[slot], dasem.at[slot])
        ]

    def store_dx(l, begin):
        @pl.when(l == c)
        def _():
            copy = pltpu.make_async_copy(g, grads.at[c], gds.at[0])
            copy.start() if begin else copy.wait()

        @pl.when(l != c)
        def _():
            copy = remote(g, grads.at[c], gds.at[0], gdr.at[0], near["core"])
            copy.start() if begin else copy.wait_send()

    def ahead(l):
        load_u(l, 1).start()
        for copy in ffn(l, 0, 0) + attn(l, 0, 0):
            copy.start()

    def operands(l):
        def run(n, carry):
            load_g(l, n).start()
            return carry

        lax.fori_loop(0, 16, run, 0)
        for n in range(4):
            load_o(l, n).start()
        load_h(l).start()

    def operands_there(l):
        def run(n, carry):
            load_g(l, n).wait()
            return carry

        lax.fori_loop(0, 16, run, 0)
        for n in range(4):
            load_o(l, n).wait()
        load_h(l).wait()

    def top_segment(l):
        load_u(l, 1).wait()
        norm_back(u, g, norms[l, 3:4], totals.at[l], (1, 3, 5), right.at[0], acc)
        load_u(l, 0).start()

        @pl.when(l == 1)
        def _():
            operands_there(1)

    def ffn_segment(l, b):
        def run(q, carry):
            n = 4 * b + q
            slot = lax.rem(n, 2)
            for copy in ffn(l, n, slot):
                copy.wait()

            @pl.when(n < 15)
            def _():
                for copy in ffn(l, n + 1, 1 - slot):
                    copy.start()

            row = ffn_back_block(right.at[0], wf.at[slot], df[slot], acc, left.at[16 + 4 * q + b])
            totals[l, pl.ds(10 + b, 1), pl.ds(pl.multiple_of(q * wide, wide), wide)] = row
            return carry

        lax.fori_loop(0, 4, run, 0)

    def middle_segment(l):
        load_u(l, 0).wait()
        norm_back(u, acc, norms[l, 2:3], totals.at[l], (0, 2, 4), right.at[2], acc)

    def attention_segment(l, q):
        slot = lax.rem(q, 2)
        for copy in attn(l, q, slot):
            copy.wait()

        @pl.when(q < 3)
        def _():
            for copy in attn(l, q + 1, 1 - slot):
                copy.start()

        dq, dk, dv = left.at[36 + q], left.at[40 + q], left.at[44 + q]
        attention_back_block(right.at[2], wa.at[slot], da.at[slot], dq, dk, dv, acc, dim)
        cols = pl.ds(pl.multiple_of(q * wide, wide), wide)
        totals[l, 8:9, cols] = jnp.sum(high(dq[...]), axis=0, keepdims=True)
        totals[l, 9:10, cols] = jnp.sum(high(dv[...]), axis=0, keepdims=True)

    def end_segment(l):
        by_rows(acc.shape[0], 64, lambda r: g.__setitem__(r, low(acc[r])))
        store_dx(l, True)
        if l == 1:
            ahead(0)

    def segment(i):
        l = jnp.where(i < 8, 1, 0)
        j = jnp.where(i < 8, i, i - 9)

        @pl.when(i == 8)
        def _():
            end_segment(1)
            operands(0)
            load_x(between).wait()
            store_dx(1, False)

        @pl.when(j == -1)
        def _():
            top_segment(l)

        @pl.when((j >= 0) & (j < 4))
        def _():
            ffn_segment(l, j)

        @pl.when(j == 3)
        def _():
            middle_segment(l)

        @pl.when((j >= 4) & (j < 8))
        def _():
            attention_segment(l, j - 4)

        @pl.when(i == 17)
        def _():
            end_segment(0)

        @pl.when(i == 11)
        def _():
            operands_there(0)

        @pl.when(i == 12)
        def _():
            load_x(tokens.at[c]).start()

        @pl.when(i == 16)
        def _():
            load_x(tokens.at[c]).wait()

    def trade(k):
        return remote(totals, trades.at[k], tss.at[k], trs.at[k], near[("core", "x", "y", "pair", "far")[k]])

    first_rows = pltpu.make_async_copy(cots.at[c], g, bsem.at[3])
    first_rows.start()
    ahead(1)
    operands(1)
    load_x(between).start()
    totals[...] = jnp.zeros_like(totals)
    first_rows.wait()

    def step(count, carry):
        i = count - 1

        def run(stage, lag, *extra):
            @pl.when((i >= lag) & (i < CHUNKS + lag))
            def _():
                stage(i - lag, *extra)

        for lag, stage in enumerate((stage1, stage2, stage3, stage4, stage5)):
            run(stage, lag + 1)
        run(stage6, 6, True)
        run(stage6, 7, False)
        for k in range(6):

            @pl.when(i == 19 + k)
            def _():
                if k:
                    trade(k - 1).wait()
                    totals[...] += trades[k - 1]
                if k < 5:
                    trade(k).start()

        run(stage0, 0)

        @pl.when(i < 18)
        def _():
            segment(i)

        return carry

    lax.fori_loop(0, CHUNKS + 9, step, 0)
    store_dx(0, False)
    remote(g, grads.at[1 - c], gds.at[0], gdr.at[0], near["core"]).wait_recv()
    for k in range(12):
        remote(zs3.at[0], out.at[k, 1 - c], os.at[0], orr.at[k], near["core"]).wait_recv()


def backward_reduce(dim, tokens, cots, full, norms, saved):
    seq, width = tokens.shape[1:]
    wide = width // 4
    block, half = wide // 2, wide // 4
    bf, f32, dma, v = jnp.bfloat16, jnp.float32, pltpu.SemaphoreType.DMA, pltpu.VMEM
    hbm, vmem = pl.BlockSpec(memory_space=pl.ANY), pl.BlockSpec(memory_space=pltpu.VMEM)
    S = jax.ShapeDtypeStruct
    return pl.pallas_call(
        functools.partial(backward_reduce_kernel, dim),
        out_shape=(S((12, 2, 2, half, width), bf), S((2, seq, width), bf), S((2, 16, width), f32)),
        in_specs=[hbm, hbm, hbm, vmem] + [hbm] * 5,
        out_specs=[hbm, hbm, vmem],
        scratch_shapes=[
            v((48, seq, wide), bf), v((4, seq, width), bf), v((seq, width), f32), v((seq, width), bf),
            v((seq, width), f32),
            v((2, 4, wide, width), bf), v((2, 2, wide, width), bf), v((2, 4, seq, wide), bf), v((2, seq, wide), bf),
            v((5, 2, 16, width), f32),
            v((2, 4, block, width), bf), v((4, 4, block, width), bf), v((2, 4, block, width), f32),
            v((2, 2, half, width), bf), v((4, 2, half, width), bf), v((2, 2, half, width), bf), v((4, 2, half, width), bf),
            v((2, 2, half, width), f32), v((2, block, width), f32),
            v((2, half, width), bf), v((4, half, width), bf), v((2, half, width), bf), v((4, half, width), bf),
            v((2, 2, half, width), f32),
            v((2, 2, half, width), f32), v((2, 2, half, width), bf), v((4, 2, half, width), bf),
            v((2, 2, half, width), bf), v((4, 2, half, width), bf), v((6, 2, half, width), bf), v((6, 2, half, width), bf),
            dma((2, 4)), dma((2, 2)), dma((2,)), dma((2,)), dma((16,)), dma((4,)), dma((4,)), dma((1,)), dma((1,)), dma((5,)), dma((5,)),
        ] + [dma((n,)) for n in (2, 4)] + [dma((n, 2)) for n in (2, 4) * 2] + [dma((n,)) for n in (2, 4) * 2]
        + [dma((n, 2)) for n in (2, 4, 2, 4, 6, 6)] + [dma((6,)), dma((12,))],
        compiler_params=pltpu.CompilerParams(collective_id=1, has_side_effects=True, vmem_limit_bytes=63 * 2**20),
    )(tokens, cots, full, norms, *saved)


def finish_kernel(parts, acts_in, grads_in, acts, grads, g_qkv, g_out, g_up, g_down,
                  pb, ab, gb, qb, ob, ub, db, psem, asem, osem):
    def load(k):
        return pltpu.make_async_copy(parts.at[k], pb.at[k], psem.at[k])

    others = [(acts_in, ab, acts, 0), (grads_in, gb, grads, 1)]
    for k in range(12):
        load(k).start()
    for source, buffer, place, n in others:
        pltpu.make_async_copy(source, buffer, asem.at[n]).start()
    stores = []
    rows = pb.shape[1]

    def store(source, place):
        copy = pltpu.make_async_copy(source, place, osem.at[len(stores)])
        copy.start()
        stores.append(copy)

    for k in range(12):
        load(k).wait()
        if k < 4:
            span = pl.ds(k * rows, rows)
            db[span] = high(pb[k])
            store(db.at[span], g_down.at[span])
        elif k < 8:
            ub[:, pl.ds((k - 4) * rows, rows)] = high(pb[k]).T
            if k == 7:
                store(ub, g_up)
        elif k == 8:
            ob[...] = high(pb[k])
            store(ob, g_out)
        else:
            qb[k - 9] = high(pb[k]).T
            store(qb.at[k - 9], g_qkv.at[k - 9])
    for source, buffer, place, n in others:
        pltpu.make_async_copy(source, buffer, asem.at[n]).wait()
        store(buffer, place)
    for copy in stores:
        copy.wait()


def finish(parts, acts, grads):
    count, rows, width = parts.shape
    bf, f32, dma, v = jnp.bfloat16, jnp.float32, pltpu.SemaphoreType.DMA, pltpu.VMEM
    S = jax.ShapeDtypeStruct
    shapes = [(3, width, rows), (rows, width), (width, width), (width, width)]
    hbm = pl.BlockSpec(memory_space=pl.ANY)
    return pl.pallas_call(
        finish_kernel,
        out_shape=[S(acts.shape, bf), S(grads.shape, bf)] + [S(shape, f32) for shape in shapes],
        in_specs=[hbm] * 3,
        out_specs=[hbm] * 6,
        scratch_shapes=[v(parts.shape, bf), v(acts.shape, bf), v(grads.shape, bf)] + [v(shape, f32) for shape in shapes]
        + [dma((12,)), dma((2,)), dma((11,))],
        compiler_params=pltpu.CompilerParams(vmem_limit_bytes=63 * 2**20),
    )(parts, acts, grads)


def by_page(
    token_in,
    cotangent,
    w_qkv,
    qv_bias,
    w_attn_out,
    w_ffn_in,
    ffn_in_bias,
    w_ffn_out,
    out_biases,
    norm_gains,
    norm_shifts,
):
    core, place = lax.axis_index("section"), lax.axis_index("mp")
    width = token_in.shape[2]
    quarter = width // 4
    vec = high(jnp.concatenate([qv_bias[0], ffn_in_bias[0].reshape(4, quarter)], axis=0))
    vec = jnp.pad(vec, ((0, 2), (0, 0)))
    norms = jnp.concatenate([out_biases[0], norm_gains[0], norm_shifts[0]], axis=0)
    norms = jnp.pad(norms, ((0, 2), (0, 0)))
    full, vecs, norms, *saved, acts = gather_forward(
        HEAD_DIM, token_in, w_qkv[0], w_attn_out[0], w_ffn_in[0], w_ffn_out[0], vec, norms
    )
    parts, grads, totals = backward_reduce(HEAD_DIM, token_in, cotangent, full, norms, saved)
    parts = parts.reshape(12, quarter, width)
    acts, grads, grad_qkv, grad_out, grad_up, grad_down = finish(parts, acts, grads)
    totals = lax.dynamic_index_in_dim(totals, core, 0, keepdims=False)
    own = lax.dynamic_slice_in_dim(totals[8:], place * quarter, quarter, 1)
    piece = width // (lax.axis_size("mp") * lax.axis_size("dp"))
    begin = (place * lax.axis_size("dp") + lax.axis_index("dp")) * piece
    rows = lax.dynamic_slice_in_dim(totals[:8], begin, piece, 1)
    return (
        acts[None],
        grads[None],
        grad_qkv[None],
        own[0:2][None],
        grad_out[None],
        grad_up[None],
        own[2:6].reshape(1, width),
        grad_down[None],
        rows[0:2][None],
        rows[2:4][None],
        rows[4:6][None],
    )


def on_device(*args):
    token_in, w_qkv, ffn_in = args[0], args[2], args[5]
    fits = (
        lax.axis_size("section") == 2
        and lax.axis_size("mp") == 4
        and lax.axis_size("dp") == 4
        and token_in.shape == (2, SEQ, 1024)
        and w_qkv.shape[3] == 256
        and ffn_in.shape[2] == 1024
    )
    return by_page(*args) if fits else pipelined(*args)


def solution(mesh):
    return jax.shard_map(
        on_device,
        mesh=mesh,
        in_specs=(
            P(None, ("dp", "mp"), None),
            P(None, ("dp", "mp"), None),
            P("section", None, None, "mp"),
            P("section", None, "mp"),
            P("section", "mp", None),
            P("section", None, "mp"),
            P("section", "mp"),
            P("section", "mp", None),
            P("section", None, None),
            P("section", None, None),
            P("section", None, None),
        ),
        out_specs=(
            P("section", None, ("dp", "mp"), None),
            P("section", None, ("dp", "mp"), None),
            P("section", None, None, "mp"),
            P("section", None, "mp"),
            P("section", "mp", None),
            P("section", None, "mp"),
            P("section", "mp"),
            P("section", "mp", None),
            P("section", None, ("mp", "dp")),
            P("section", None, ("mp", "dp")),
            P("section", None, ("mp", "dp")),
        ),
        check_vma=False,
    )
```

```python
import functools
from functools import partial
import math

import jax
import jax.numpy as jnp
from jax import lax
from jax.experimental import pallas as pl
from jax.experimental.pallas import tpu as pltpu
from jax.sharding import PartitionSpec as P

HEAD_DIM = 64
SEQ = 512


def from_behind(value, axis, by):
    devices = lax.axis_size(axis)
    pairs = [(i, i + by) for i in range(devices) if 0 <= i + by < devices]
    return lax.ppermute(value, axis, pairs)


def norm_rows(values, gain_row, shift_row):
    average = jnp.mean(values, axis=-1, keepdims=True)
    centered = values - average
    variance = jnp.mean(centered * centered, axis=-1, keepdims=True)
    return centered * lax.rsqrt(variance + 1e-05) * gain_row + shift_row


def exact_gelu(values):
    return jax.nn.gelu(values, approximate=False)


def layer_forward(params, token_rows):
    (
        w_qkv,
        qv_bias,
        w_attn_out,
        w_ffn_in,
        ffn_in_bias,
        w_ffn_out,
        out_biases,
        norm_gains,
        norm_shifts,
    ) = params
    gathered = lax.all_gather(token_rows, "mp", axis=0, tiled=True)
    rows_all = gathered.shape[0]
    local_width = w_qkv.shape[2]
    local_heads = local_width // HEAD_DIM
    page_count = rows_all // SEQ
    scale_factor = 1.0 / math.sqrt(HEAD_DIM)
    bias_full = jnp.stack([qv_bias[0], jnp.zeros_like(qv_bias[0]), qv_bias[1]]).astype(jnp.float32)
    projected = (
        jnp.einsum("rd,cde->cre", gathered, w_qkv, preferred_element_type=jnp.float32)
        + bias_full[:, None, :]
    )
    heads_view = projected.astype(jnp.bfloat16).reshape(3, page_count, SEQ, local_heads, HEAD_DIM)
    scores = (
        jnp.einsum(
            "pqhe,pkhe->phqk", heads_view[0], heads_view[1], preferred_element_type=jnp.float32
        )
        * scale_factor
    )
    top_score = jnp.max(scores, axis=-1, keepdims=True)
    exponent = jnp.exp(scores - top_score)
    weights_soft = exponent / jnp.sum(exponent, axis=-1, keepdims=True)
    weights_low = weights_soft.astype(jnp.bfloat16)
    attended = jnp.einsum(
        "phqk,pkhe->pqhe", weights_low, heads_view[2], preferred_element_type=jnp.float32
    )
    attended = attended.reshape(rows_all, local_width).astype(jnp.bfloat16)
    attn_part = jnp.dot(attended, w_attn_out, preferred_element_type=jnp.float32)
    attn_rows = lax.psum_scatter(
        attn_part.astype(jnp.bfloat16), "mp", scatter_dimension=0, tiled=True
    ).astype(jnp.float32)
    residual_one = attn_rows + out_biases[0] + token_rows.astype(jnp.float32)
    first = norm_rows(residual_one, norm_gains[0], norm_shifts[0])
    first_all = lax.all_gather(first.astype(jnp.bfloat16), "mp", axis=0, tiled=True)
    pre_act = jnp.dot(first_all, w_ffn_in, preferred_element_type=jnp.float32) + ffn_in_bias.astype(
        jnp.float32
    )
    activated = exact_gelu(pre_act).astype(jnp.bfloat16)
    ffn_part = jnp.dot(activated, w_ffn_out, preferred_element_type=jnp.float32)
    ffn_rows = lax.psum_scatter(
        ffn_part.astype(jnp.bfloat16), "mp", scatter_dimension=0, tiled=True
    ).astype(jnp.float32)
    residual_two = ffn_rows + out_biases[1] + first
    result = norm_rows(residual_two, norm_gains[1], norm_shifts[1])
    kept_values = (
        gathered,
        heads_view,
        weights_soft,
        attended,
        residual_one,
        first_all,
        pre_act,
        activated,
        residual_two,
    )
    return (result, kept_values)


def layer_backward(params, kept_values, grad_out):
    (
        w_qkv,
        qv_bias,
        w_attn_out,
        w_ffn_in,
        ffn_in_bias,
        w_ffn_out,
        out_biases,
        norm_gains,
        norm_shifts,
    ) = params
    (
        gathered,
        heads_view,
        weights_soft,
        attended,
        residual_one,
        first_all,
        pre_act,
        activated,
        residual_two,
    ) = kept_values
    rows_all = gathered.shape[0]
    local_width = w_qkv.shape[2]
    local_heads = local_width // HEAD_DIM
    page_count = rows_all // SEQ
    scale_factor = 1.0 / math.sqrt(HEAD_DIM)
    unused_two, norm_two_back = jax.vjp(norm_rows, residual_two, norm_gains[1], norm_shifts[1])
    grad_res_two, grad_gain_two, grad_shift_two = norm_two_back(grad_out)
    grad_bias_two = jnp.sum(grad_res_two, axis=0)
    ffn_grad_all = lax.all_gather(grad_res_two.astype(jnp.bfloat16), "mp", axis=0, tiled=True)
    grad_w_ffn_out = jnp.einsum(
        "rf,rd->fd", activated, ffn_grad_all, preferred_element_type=jnp.float32
    )
    grad_act = jnp.einsum("rd,fd->rf", ffn_grad_all, w_ffn_out, preferred_element_type=jnp.float32)
    unused_gelu, gelu_back = jax.vjp(exact_gelu, pre_act)
    grad_pre = gelu_back(grad_act)[0].astype(jnp.bfloat16)
    grad_ffn_in_bias = jnp.sum(grad_pre.astype(jnp.float32), axis=0)
    grad_w_ffn_in = jnp.einsum("rd,rf->df", first_all, grad_pre, preferred_element_type=jnp.float32)
    first_part = jnp.einsum("rf,df->rd", grad_pre, w_ffn_in, preferred_element_type=jnp.float32)
    first_grad_rows = lax.psum_scatter(
        first_part.astype(jnp.bfloat16), "mp", scatter_dimension=0, tiled=True
    ).astype(jnp.float32)
    grad_first = first_grad_rows + grad_res_two
    unused_one, norm_one_back = jax.vjp(norm_rows, residual_one, norm_gains[0], norm_shifts[0])
    grad_res_one, grad_gain_one, grad_shift_one = norm_one_back(grad_first)
    grad_bias_one = jnp.sum(grad_res_one, axis=0)
    attn_grad_all = lax.all_gather(grad_res_one.astype(jnp.bfloat16), "mp", axis=0, tiled=True)
    grad_w_attn_out = jnp.einsum(
        "rk,rd->kd", attended, attn_grad_all, preferred_element_type=jnp.float32
    )
    grad_attended = jnp.einsum(
        "rd,kd->rk", attn_grad_all, w_attn_out, preferred_element_type=jnp.float32
    )
    grad_attended = grad_attended.astype(jnp.bfloat16).reshape(
        page_count, SEQ, local_heads, HEAD_DIM
    )
    weights_low = weights_soft.astype(jnp.bfloat16)
    grad_weights = jnp.einsum(
        "pqhe,pkhe->phqk", grad_attended, heads_view[2], preferred_element_type=jnp.float32
    )
    grad_values = jnp.einsum(
        "phqk,pqhe->pkhe", weights_low, grad_attended, preferred_element_type=jnp.float32
    )
    inner_total = jnp.sum(weights_soft * grad_weights, axis=-1, keepdims=True)
    grad_scores = (weights_soft * (grad_weights - inner_total)).astype(jnp.bfloat16)
    grad_queries = (
        jnp.einsum(
            "phqk,pkhe->pqhe", grad_scores, heads_view[1], preferred_element_type=jnp.float32
        )
        * scale_factor
    )
    grad_keys = (
        jnp.einsum(
            "phqk,pqhe->pkhe", grad_scores, heads_view[0], preferred_element_type=jnp.float32
        )
        * scale_factor
    )
    grad_proj = (
        jnp.stack([grad_queries, grad_keys, grad_values])
        .reshape(3, rows_all, local_width)
        .astype(jnp.bfloat16)
    )
    proj_sums = jnp.sum(grad_proj.astype(jnp.float32), axis=1)
    grad_qv_bias = jnp.stack([proj_sums[0], proj_sums[2]])
    grad_w_qkv = jnp.einsum("rd,cre->cde", gathered, grad_proj, preferred_element_type=jnp.float32)
    input_part = jnp.einsum("cre,cde->rd", grad_proj, w_qkv, preferred_element_type=jnp.float32)
    input_grad_rows = lax.psum_scatter(
        input_part.astype(jnp.bfloat16), "mp", scatter_dimension=0, tiled=True
    ).astype(jnp.float32)
    grad_in = input_grad_rows + grad_res_one
    matrix_grads = (
        grad_w_qkv,
        grad_qv_bias,
        grad_w_attn_out,
        grad_w_ffn_in,
        grad_ffn_in_bias,
        grad_w_ffn_out,
    )
    vector_grads = (
        jnp.stack([grad_bias_one, grad_bias_two]),
        jnp.stack([grad_gain_one, grad_gain_two]),
        jnp.stack([grad_shift_one, grad_shift_two]),
    )
    return (grad_in, matrix_grads, vector_grads)


def pipelined(
    token_in,
    cotangent,
    w_qkv,
    qv_bias,
    w_attn_out,
    w_ffn_in,
    ffn_in_bias,
    w_ffn_out,
    out_biases,
    norm_gains,
    norm_shifts,
):
    params = (
        w_qkv[0],
        qv_bias[0],
        w_attn_out[0],
        w_ffn_in[0],
        ffn_in_bias[0],
        w_ffn_out[0],
        out_biases[0],
        norm_gains[0],
        norm_shifts[0],
    )
    micro_count = token_in.shape[0]
    section_index = lax.axis_index("section")
    is_first = section_index == 0
    zero_rows = jnp.zeros(token_in.shape[1:], jnp.bfloat16)
    run_forward = partial(layer_forward, params)
    run_backward = partial(layer_backward, params)

    def forward_step(step_index, carry):
        received, saved, stored = carry
        own_micro = step_index - section_index
        is_valid = (own_micro >= 0) & (own_micro < micro_count)
        slot_index = jnp.clip(own_micro, 0, micro_count - 1)
        first_rows = lax.dynamic_index_in_dim(
            token_in, jnp.minimum(step_index, micro_count - 1).astype(jnp.int32), 0, keepdims=False
        )
        layer_in = jnp.where(is_first, first_rows, received)
        result, unused_kept = run_forward(layer_in)
        result_low = result.astype(jnp.bfloat16)
        old_saved = lax.dynamic_index_in_dim(saved, slot_index, 0, keepdims=False)
        saved = lax.dynamic_update_index_in_dim(
            saved, jnp.where(is_valid, layer_in, old_saved), slot_index, 0
        )
        old_stored = lax.dynamic_index_in_dim(stored, slot_index, 0, keepdims=False)
        stored = lax.dynamic_update_index_in_dim(
            stored, jnp.where(is_valid, result_low, old_stored), slot_index, 0
        )
        received = from_behind(result_low, "section", 1)
        return (received, saved, stored)

    start_carry = (zero_rows, jnp.zeros_like(token_in), jnp.zeros_like(token_in))
    unused_received, saved, stored = lax.fori_loop(0, micro_count + 1, forward_step, start_carry)
    matrix_zero = tuple((jnp.zeros(entry.shape, jnp.float32) for entry in params[:6]))
    vector_zero = (
        jnp.zeros(out_biases.shape[1:], jnp.float32),
        jnp.zeros(norm_gains.shape[1:], jnp.float32),
        jnp.zeros(norm_shifts.shape[1:], jnp.float32),
    )

    def backward_step(step_index, carry):
        received_grad, grad_store, matrix_sums, vector_sums = carry
        own_micro = step_index - (1 - section_index)
        is_valid = (own_micro >= 0) & (own_micro < micro_count)
        slot_index = jnp.clip(own_micro, 0, micro_count - 1)
        layer_in = lax.dynamic_index_in_dim(saved, slot_index, 0, keepdims=False)
        from_last = lax.dynamic_index_in_dim(cotangent, slot_index, 0, keepdims=False)
        grad_out = jnp.where(is_first, received_grad, from_last).astype(jnp.float32)
        unused_result, kept_values = run_forward(layer_in)
        grad_in, matrix_grads, vector_grads = run_backward(kept_values, grad_out)
        matrix_grads = tuple((jnp.where(is_valid, entry, 0.0) for entry in matrix_grads))
        vector_grads = tuple((jnp.where(is_valid, entry, 0.0) for entry in vector_grads))
        grad_low = grad_in.astype(jnp.bfloat16)
        old_piece = lax.dynamic_index_in_dim(grad_store, slot_index, 0, keepdims=False)
        grad_store = lax.dynamic_update_index_in_dim(
            grad_store, jnp.where(is_valid, grad_low, old_piece), slot_index, 0
        )
        grad_one, grad_two, grad_three, grad_four, grad_five, grad_six = matrix_grads
        matrix_grads = (
            lax.psum(grad_one.astype(jnp.bfloat16), "dp").astype(jnp.float32),
            lax.psum(grad_two.astype(jnp.bfloat16), "dp").astype(jnp.float32),
            lax.psum(grad_three.astype(jnp.bfloat16), "dp").astype(jnp.float32),
            lax.psum(grad_four.astype(jnp.bfloat16), "dp").astype(jnp.float32),
            lax.psum(grad_five.astype(jnp.bfloat16), "dp").astype(jnp.float32),
            lax.psum(grad_six.astype(jnp.bfloat16), "dp").astype(jnp.float32),
        )
        matrix_sums = tuple((total + extra for total, extra in zip(matrix_sums, matrix_grads)))
        vector_sums = tuple((total + extra for total, extra in zip(vector_sums, vector_grads)))
        received_grad = from_behind(grad_low, "section", -1)
        return (received_grad, grad_store, matrix_sums, vector_sums)

    back_carry = (zero_rows, jnp.zeros_like(token_in), matrix_zero, vector_zero)
    unused_grad, grad_store, matrix_sums, vector_sums = lax.fori_loop(
        0, micro_count + 1, backward_step, back_carry
    )
    bias_total, gain_total, shift_total = vector_sums
    bias_part, gain_part, shift_part = (
        lax.psum_scatter(bias_total, ("mp", "dp"), scatter_dimension=1, tiled=True),
        lax.psum_scatter(gain_total, ("mp", "dp"), scatter_dimension=1, tiled=True),
        lax.psum_scatter(shift_total, ("mp", "dp"), scatter_dimension=1, tiled=True),
    )
    return (
        stored[None],
        grad_store[None],
        matrix_sums[0][None],
        matrix_sums[1][None],
        matrix_sums[2][None],
        matrix_sums[3][None],
        matrix_sums[4][None],
        matrix_sums[5][None],
        bias_part[None],
        gain_part[None],
        shift_part[None],
    )


MESH = pl.DeviceIdType.MESH
CHUNKS = 24
TRIPLES = 8
SCALE = 0.125


def low(value):
    return value.astype(jnp.bfloat16)


def high(value):
    return value.astype(jnp.float32)


def remote(src, dst, send, recv, device):
    return pltpu.make_async_remote_copy(
        src_ref=src, dst_ref=dst, send_sem=send, recv_sem=recv, device_id=device, device_id_type=MESH
    )


def neighbours():
    c, p, d = lax.axis_index("section"), lax.axis_index("mp"), lax.axis_index("dp")
    return {
        "core": (1 - c, p, d),
        "x": (c, p + 1 - 2 * lax.rem(p, 2), d),
        "y": (c, lax.rem(p + 2, 4), d),
        "across": (c, p, 3 - d),
        "inner": (c, p, jnp.where(d == 0, 1, 2)),
        "outer": (c, p, jnp.where(d == 1, 0, 3)),
    }


def places():
    p = lax.axis_index("mp")
    return [p, p + 1 - 2 * lax.rem(p, 2), lax.rem(p + 2, 4), 3 - p]


def dot(a, b):
    return jnp.dot(a, b, preferred_element_type=jnp.float32)


def dot_tn(a, b):
    return lax.dot_general(a, b, (((0,), (0,)), ((), ())), preferred_element_type=jnp.float32)


def dot_nt(a, b):
    return lax.dot_general(a, b, (((1,), (1,)), ((), ())), preferred_element_type=jnp.float32)


def standard(values):
    average = jnp.mean(values, axis=-1, keepdims=True)
    centered = values - average
    variance = jnp.mean(centered * centered, axis=-1, keepdims=True)
    scale = lax.rsqrt(variance + 1e-05)
    return centered * scale, scale


def softmax(q, k):
    scores = dot_nt(q * jnp.asarray(SCALE, q.dtype), k)
    top = jnp.max(scores, axis=-1, keepdims=True)
    exponent = jnp.exp(scores - top)
    total = jnp.sum(exponent, axis=-1, keepdims=True)
    return exponent * (1.0 / total), top + jnp.log(total)


def by_rows(rows, step, body):
    def run(i, carry):
        body(pl.ds(pl.multiple_of(i * step, step), step))
        return carry

    lax.fori_loop(0, rows // step, run, 0)


def first_norm(x, nrm, acc, u1, hb):
    def run(rows):
        u = acc[rows] + nrm[0:1] + high(x[rows])
        u1[rows] = u
        h = standard(u)[0] * nrm[2:3] + nrm[4:5]
        hb[rows] = low(h)
        acc[rows] = h + nrm[1:2]

    by_rows(acc.shape[0], 64, run)


def second_norm(nrm, acc, u2, out):
    def run(rows):
        u = acc[rows]
        u2[rows] = u
        out[rows] = low(standard(u)[0] * nrm[3:4] + nrm[5:6])

    by_rows(acc.shape[0], 64, run)


def norm_back(u, grad, gain, sums, at, out_low, out_acc):
    def run(rows):
        g = high(grad[rows])
        xhat, scale = standard(u[rows])
        scaled = g * gain
        du = scale * (
            scaled
            - jnp.mean(scaled, axis=-1, keepdims=True)
            - xhat * jnp.mean(scaled * xhat, axis=-1, keepdims=True)
        )
        out_low[rows] = low(du)
        out_acc[rows] = du
        for row, term in ((at[0], du), (at[1], g * xhat), (at[2], g)):
            sums[row : row + 1] += jnp.sum(term, axis=0, keepdims=True)

    by_rows(u.shape[0], 64, run)


def ffn_back_block(dfb, w, gd, acc, dz_out):
    dz = low(dot_nt(dfb[...], w[1]) * high(gd))
    dz_out[...] = dz
    acc[...] += dot(dz, w[0])
    return jnp.sum(high(dz), axis=0, keepdims=True)


def attention_back_block(dab, w, qkv, logs, dq_out, dk_out, dv_out, acc, dim):
    dob = low(dot_nt(dab[...], w[3]))
    for j in range(dob.shape[1] // dim):
        cols = slice(j * dim, (j + 1) * dim)
        q, k, v, do = qkv[0, :, cols], qkv[1, :, cols], qkv[2, :, cols], dob[:, cols]
        a = jnp.exp(dot_nt(q * jnp.asarray(SCALE, q.dtype), k) - logs[:, j : j + 1])
        da = dot_nt(do, v)
        ds = low(a * (da - jnp.sum(a * da, axis=-1, keepdims=True)))
        dv_out[:, cols] = low(dot_tn(low(a), do))
        dq_out[:, cols] = low(dot(ds, k) * SCALE)
        dk_out[:, cols] = low(dot_tn(ds, q) * SCALE)
    acc[...] += dot(dq_out[...], w[0]) + dot(dk_out[...], w[1]) + dot(dv_out[...], w[2])


def weight_copies(full, layer, kind, p, b, buf, sem, rows):
    width = 4 * rows
    if kind == 0:
        starts = [c * width + p * rows for c in range(4)]
    else:
        starts = [4 * width + t * 4 * width + p * width + b * rows for t in range(2)]
    return [
        pltpu.make_async_copy(full.at[layer, pl.ds(pl.multiple_of(start, rows), rows)], buf.at[n], sem.at[n])
        for n, start in enumerate(starts)
    ]


def project_block(x, w, vec, save, logs, dim):
    rows = x[...]
    q = low(dot_nt(rows, w[0]) + vec[0:1])
    k = low(dot_nt(rows, w[1]))
    v = low(dot_nt(rows, w[2]) + vec[1:2])
    save[0], save[1], save[2] = q, k, v
    for j in range(q.shape[1] // dim):
        cols = slice(j * dim, (j + 1) * dim)
        soft, logs[:, j : j + 1] = softmax(q[:, cols], k[:, cols])
        save[3, :, cols] = low(dot(low(soft), v[:, cols]))


def unit_values(hb, w, bias):
    z = dot_nt(hb[...], w) + bias
    inner = 0.5 + 0.5 * lax.erf(z * math.sqrt(0.5))
    slope = inner + z * jnp.exp(-0.5 * z * z) * (1.0 / math.sqrt(2.0 * math.pi))
    return low(z * inner), low(slope)


def gather_forward_kernel(
    dim, tokens, w_qkv, w_out, w_up, w_down, qv, up_bias, biases, gains, shifts, full, vecs, norms, qkvo, logs, gd, us, hbs, between, acts,
    turned, x, acc, u, hb, wa, wf, sa, gb, sd, wasem, wfsem, sasem, gbsem, sdsem, usem, vec, norm_in, lb, lbsem,
    ini_s, ini_r, loc, x1ss, x1rs, y1ss, y1rs, x2ss, x2rs, y2ss, y2rs, zs, zr, cs, cr, vs, vr, vloc, as_, ar,
):
    c, p, d = lax.axis_index("section"), lax.axis_index("mp"), lax.axis_index("dp")
    near = neighbours()
    near["pair"] = (c, p, d + 1 - 2 * lax.rem(d, 2))
    spots = places()
    rows = w_out.shape[0] // 2
    half = rows // 2
    odd = lax.rem(d, 2)
    others = [(cc, spots[r], d) for r in range(4) for cc in (c, 1 - c)][1:]

    def place_of(s, spot, h):
        k = lax.rem(s, 12)
        row = jnp.where(k < 4, k * 8 + spot * 2, 32 + (k // 4 - 1) * 32 + spot * 8 + lax.rem(k, 4) * 2)
        return s // 12, (row + h) * rows

    def block(s, spot, h, start=0, size=rows):
        layer, row = place_of(s, spot, h)
        return full.at[layer, pl.ds(pl.multiple_of(row + start, half), size)]

    def init_place(k, layer):
        row = place_of(12 * layer + k, p, 0)[1]
        return full.at[layer, pl.ds(pl.multiple_of(row, half), 2 * rows)]

    def turn(k):
        if k < 3:
            turned[k] = w_qkv[k].T
        elif 4 <= k < 8:
            turned[k - 1] = w_up[:, 2 * rows * (k - 4) : 2 * rows * (k - 3)].T

    def chunk(k):
        if k == 3:
            return w_out
        if k < 8:
            return turned.at[k if k < 3 else k - 1]
        return w_down.at[pl.ds(2 * rows * (k - 8), 2 * rows)]

    def init_start(k):
        if k > 2:
            turn(k)
        pltpu.make_async_copy(chunk(k), init_place(k, c), loc.at[k]).start()
        remote(chunk(k), init_place(k, c), ini_s.at[k], ini_r.at[k], near["core"]).start()

    def init_local(k):
        return pltpu.make_async_copy(init_place(k, c), init_place(k, c), loc.at[k])

    def init_wait(k):
        there = init_place(k, 1 - c)
        remote(there, there, ini_s.at[k], ini_r.at[k], near["core"]).wait_recv()

    def small():
        copies = [remote(vec, vecs.at[c, p], vs.at[i], vr.at[c, p], device) for i, device in enumerate(others)]
        copies.append(remote(norm_in, norms.at[c], vs.at[7], vr.at[0, 4], near["core"]))
        return copies

    def small_local():
        return [
            pltpu.make_async_copy(vec, vecs.at[c, p], vloc.at[0]),
            pltpu.make_async_copy(norm_in, norms.at[c], vloc.at[1]),
        ]

    def hop(s, spot, name, pick):
        ss, rs = (x1ss, x1rs) if pick == "x" else (y1ss, y1rs)
        b = block(s, spot, c)
        return remote(b, b, ss.at[s], rs.at[s], near[name])

    def first(s, name):
        return hop(s, p, name, name)

    def arrived(s, name):
        return hop(s, spots[1] if name == "x" else spots[2], name, name)

    def relay(s, name, spot=None):
        if name == "x":
            b = block(s, spots[2] if spot is None else spot, c, 0, half)
            return remote(b, b, x2ss.at[s], x2rs.at[s], near["x"])
        b = block(s, spots[1] if spot is None else spot, c, half, half)
        return remote(b, b, y2ss.at[s], y2rs.at[s], near["y"])

    def relayed(s, name):
        return relay(s, name, spots[3])

    def to_pair(s, r):
        b = block(s, spots[r], c)
        return remote(b, b, zs.at[s, r - 1], zr.at[s, r - 1], near["pair"])

    def to_core(s, r):
        b = block(s, spots[r], c)
        return remote(b, b, cs.at[s, r - 1], cr.at[s, r - 1], near["core"])

    def from_core(s, r):
        b = block(s, spots[r], 1 - c)
        return remote(b, b, cs.at[s, r - 1], cr.at[s, r - 1], near["core"])

    def sent_chunk(j):
        t, n = j // 2, lax.rem(j, 2)
        return 3 * t + (1 - n) * (1 + odd), n == 0

    def stage_a(j):
        s = sent_chunk(j)[0]
        for m in range(3):
            own = 3 * (j // 2) + m

            @pl.when((own // 12 != c) & (lax.rem(j, 2) == 0))
            def _():
                init_wait(lax.rem(own, 12))

            @pl.when((own // 12 == c) & (lax.rem(j, 2) == 0))
            def _():
                init_local(lax.rem(own, 12)).wait()

        first(s, "x").start()
        first(s, "y").start()

    def stage_b(j):
        s, shared = sent_chunk(j)
        arrived(s, "x").wait_recv()
        relay(s, "y").start()
        arrived(s, "y").wait_recv()
        relay(s, "x").start()
        for r in (1, 2):
            to_core(s, r).start()

        @pl.when(shared)
        def _():
            for r in (1, 2):
                to_pair(s, r).start()

    def stage_c(j):
        s, shared = sent_chunk(j)
        relayed(s, "x").wait_recv()
        relayed(s, "y").wait_recv()
        to_core(s, 3).start()

        @pl.when(shared)
        def _():
            to_pair(s, 3).start()

    def stage_d(t):
        s = 3 * t + 2 - odd
        for r in (1, 2, 3):
            to_pair(s, r).wait_recv()
            to_core(s, r).start()

    def stage_e(t):
        for j in range(3):
            for r in (1, 2, 3):
                from_core(3 * t + j, r).wait_recv()

    def stage_f(t):
        for n, s in enumerate((3 * t, 3 * t + 1 + odd)):
            first(s, "x").wait_send()
            first(s, "y").wait_send()
            relay(s, "x").wait_send()
            relay(s, "y").wait_send()
            for r in (1, 2, 3):
                if n:
                    to_pair(s, r).wait_send()
        for j in range(3):
            for r in (1, 2, 3):
                to_core(3 * t + j, r).wait_send()

    wide = 2 * rows

    def weights(l, number, place, sem):
        begin = pl.multiple_of(number * wide, wide)
        return pltpu.make_async_copy(full.at[l, pl.ds(begin, wide)], place, sem)

    def load_qkv(l, q):
        return [weights(l, 4 * n + q, wa.at[q, n], wasem.at[q, n]) for n in range(3)]

    def load(l, number, slot):
        return weights(l, number, wf.at[slot], wfsem.at[slot])

    def load_out(l, q):
        return load(l, 12 + q, q)

    def load_in(l, b, q, slot):
        return load(l, 16 + 4 * q + b, slot)

    def load_down(l, b, q, slot):
        return load(l, 32 + 4 * q + b, slot)

    def load_last(l, q):
        return weights(l, 32 + 4 * q + 3, wa.at[q, 0], wasem.at[q, 0])

    def save_attn(l, q):
        return pltpu.make_async_copy(sa.at[q], qkvo.at[l, q], sasem.at[q])

    def save_logs(l, q):
        return pltpu.make_async_copy(lb.at[q], logs.at[l, q], lbsem.at[q])

    def save_g(l, n):
        return pltpu.make_async_copy(gb.at[n], gd.at[l, n, 0], gbsem.at[n])

    def save_d(l, n, slot):
        return pltpu.make_async_copy(sd.at[slot], gd.at[l, n, 1], sdsem.at[slot])

    def keep(l, which):
        if which == 2:
            return pltpu.make_async_copy(hb, hbs.at[l], usem.at[2])
        if which == 3:
            return pltpu.make_async_copy(x, between, usem.at[3])
        return pltpu.make_async_copy(u, us.at[l, which], usem.at[which])

    def give(l, begin):
        @pl.when(l == c)
        def _():
            copy = pltpu.make_async_copy(x, acts.at[c], as_.at[0])
            copy.start() if begin else copy.wait()

        @pl.when(l != c)
        def _():
            copy = remote(x, acts.at[c], as_.at[0], ar.at[0], near["core"])
            copy.start() if begin else copy.wait_send()

    def kept(l):
        @pl.when(l == 0)
        def _():
            keep(0, 3).wait()

        give(l, False)

    def each(count, body):
        def run(q, carry):
            body(q)
            return carry

        lax.fori_loop(0, count, run, 0)

    def attention_segment(l, q):
        for copy in load_qkv(l, q):
            copy.wait()
        project_block(x, wa.at[q], vecs[l, q], sa.at[q], lb.at[q], dim)
        save_attn(l, q).start()
        save_logs(l, q).start()

    def out_segment(l):
        @pl.when(l == 1)
        def _():
            keep(0, 1).wait()

        acc[...] = jnp.zeros_like(acc)

        def branch(q):
            load_out(l, q).wait()
            acc[...] += dot(sa[q, 3], wf[q])
            load_in(l, 1, q, q).start()

        each(4, branch)
        first_norm(x, norms.at[l], acc, u, hb)
        keep(l, 0).start()
        keep(l, 2).start()

    def up_segment(l, b, slot):
        for q in range(4):
            load_in(l, b, q, slot + q).wait()
        for q in range(4):
            g, slope = unit_values(hb, wf[slot + q], vecs[l, q, pl.ds(2 + b, 1)])
            gb[4 * q + b] = g
            sd[q] = slope
        for q in range(4):
            save_g(l, 4 * q + b).start()
            save_d(l, 4 * q + b, q).start()

    def up_saved(l, b):
        for q in range(4):
            save_d(l, 4 * q + b, q).wait()

    def down_segment(l, b, slot):
        for q in range(4):
            load_down(l, b, q, slot + q).wait()
        first_two = dot(gb[b], wf[slot]) + dot(gb[4 + b], wf[slot + 1])
        acc[...] += first_two + dot(gb[8 + b], wf[slot + 2]) + dot(gb[12 + b], wf[slot + 3])

    def end_segment(l):
        keep(l, 0).wait()
        keep(l, 2).wait()
        each(4, lambda q: save_attn(l, q).wait())
        each(4, lambda q: save_logs(l, q).wait())
        each(16, lambda n: save_g(l, n).wait())

        @pl.when(l == 1)
        def _():
            kept(0)

        second_norm(norms.at[l], acc, u, x)
        keep(l, 1).start()
        give(l, True)

        @pl.when(l == 0)
        def _():
            keep(0, 3).start()

    def small_there():
        for copy in small_local():
            copy.wait()
        for copy in small():
            copy.wait_send()
        for cc, spot in [(cc, spots[r]) for r in range(4) for cc in (c, 1 - c)][1:]:
            remote(vec, vecs.at[cc, spot], vs.at[0], vr.at[cc, spot], near["core"]).wait_recv()
        remote(norm_in, norms.at[1 - c], vs.at[7], vr.at[0, 4], near["core"]).wait_recv()

    def compute(m):
        l, part = m // 8, lax.rem(m, 8)

        def at(number, body):
            @pl.when(part == number)
            def _():
                body()

        def attention_first():
            for q in range(4):
                for copy in load_qkv(l, q):
                    copy.start()

            @pl.when(m == 0)
            def _():
                small_there()
                first_rows.wait()

        def attention_half(begin):
            each(2, lambda q: attention_segment(l, begin + q))

        def out_part():
            for q in range(4):
                load_out(l, q).start()
            for q in range(4):
                load_in(l, 0, q, 4 + q).start()
            out_segment(l)

        def up_part():
            for q in range(4):
                load_in(l, 2, q, q).start()
            for q in range(4):
                load_in(l, 3, q, 4 + q).start()
            up_saved(l, 1)
            up_segment(l, 2, 0)
            for q in range(4):
                load_down(l, 0, q, q).start()

        def turn_part():
            up_saved(l, 2)
            up_segment(l, 3, 4)
            down_segment(l, 0, 0)

        def down_part():
            for b in (1, 2):
                for q in range(4):
                    load_down(l, b, q, 4 * (b - 1) + q).start()
            for q in range(4):
                load_last(l, q).start()
            up_saved(l, 3)
            down_segment(l, 1, 0)
            down_segment(l, 2, 4)

        def end_part():
            for q in range(4):
                load_last(l, q).wait()
            first_two = dot(gb[3], wa[0, 0]) + dot(gb[7], wa[1, 0])
            acc[...] += first_two + dot(gb[11], wa[2, 0]) + dot(gb[15], wa[3, 0])
            end_segment(l)

        at(0, attention_first)

        @pl.when(part < 2)
        def _():
            attention_half(2 * part)

        at(2, out_part)

        @pl.when((part == 2) | (part == 3))
        def _():
            b = part - 2

            @pl.when(b == 1)
            def _():
                up_saved(l, 0)

            up_segment(l, b, 4 - 4 * b)

        at(4, up_part)
        at(5, turn_part)
        at(6, down_part)
        at(7, end_part)

    first_rows = pltpu.make_async_copy(tokens.at[c], x, usem.at[4])
    first_rows.start()
    vec[...] = jnp.zeros_like(vec)
    vec[0:2] = high(qv[...])
    for b in range(4):
        vec[2 + b : 3 + b] = high(up_bias[:, 2 * rows * b : 2 * rows * (b + 1)])
    norm_in[...] = jnp.zeros_like(norm_in)
    norm_in[0:2], norm_in[2:4], norm_in[4:6] = biases[...], gains[...], shifts[...]
    barrier = pltpu.get_barrier_semaphore()
    for device in others + [near["pair"]]:
        pl.semaphore_signal(barrier, inc=1, device_id=device, device_id_type=MESH)
    for k in range(3):
        turn(k)
    pl.semaphore_wait(barrier, 8)
    for k in range(3):
        init_start(k)
    for copy in small_local() + small():
        copy.start()

    def step(count, carry):
        i = count - 1

        def run(stage, lag):
            @pl.when((i >= lag) & (i < 2 * TRIPLES + lag))
            def _():
                stage(i - lag)

        def run_late(stage, lag):
            @pl.when((i >= lag) & (i < 2 * TRIPLES + lag) & (lax.rem(i - lag, 2) == 0))
            def _():
                stage((i - lag) // 2)

        run(stage_a, -1)
        run(stage_b, 1)
        run(stage_c, 2)
        run_late(stage_e, 4)
        run_late(stage_f, 6)
        for t in range(3):

            @pl.when(i == 2 * t)
            def _():
                for k in range(3 * t + 3, 3 * t + 6):
                    init_start(k)

        run(compute, 4)
        run_late(stage_d, 3)
        return carry

    lax.fori_loop(0, 2 * TRIPLES + 6, step, 0)

    for k in range(12):
        remote(chunk(k), init_place(k, c), ini_s.at[k], ini_r.at[k], near["core"]).wait_send()
    keep(1, 1).wait()
    kept(1)
    remote(x, acts.at[1 - c], as_.at[0], ar.at[0], near["core"]).wait_recv()


def gather_forward(dim, tokens, w_qkv, w_out, w_up, w_down, qv, up_bias, biases, gains, shifts):
    rows, width = w_out.shape
    seq = tokens.shape[1]
    bf, f32, dma, v = jnp.bfloat16, jnp.float32, pltpu.SemaphoreType.DMA, pltpu.VMEM
    hbm, vmem = pl.BlockSpec(memory_space=pl.ANY), pl.BlockSpec(memory_space=pltpu.VMEM)
    S = jax.ShapeDtypeStruct
    return pl.pallas_call(
        functools.partial(gather_forward_kernel, dim),
        out_shape=(
            S((2, 48 * rows, width), bf), S((2, 4, 8, rows), f32), S((2, 8, width), f32),
            S((2, 4, 4, seq, rows), bf), S((2, 4, seq, 128), f32), S((2, 16, 2, seq, rows), bf), S((2, 2, seq, width), f32),
            S((2, seq, width), bf), S((seq, width), bf), S((2, seq, width), bf),
        ),
        in_specs=[hbm] + [vmem] * 9,
        out_specs=[hbm, vmem, vmem] + [hbm] * 7,
        scratch_shapes=[
            v((7, rows, width), bf),
            v((seq, width), bf), v((seq, width), f32), v((seq, width), f32), v((seq, width), bf),
            v((4, 3, rows, width), bf), v((8, rows, width), bf), v((4, 4, seq, rows), bf), v((16, seq, rows), bf),
            v((4, seq, rows), bf), dma((4, 3)), dma((8,)), dma((4,)), dma((16,)), dma((4,)), dma((5,)),
            v((8, rows), f32), v((8, width), f32), v((4, seq, 128), f32), dma((4,)),
        ] + [dma((12,))] * 3 + [dma((24,))] * 8 + [dma((24, 3))] * 4
        + [dma((8,)), dma((2, 5)), dma((2,)), dma((1,)), dma((1,))],
        compiler_params=pltpu.CompilerParams(collective_id=0, has_side_effects=True, vmem_limit_bytes=60 * 2**20),
    )(tokens, w_qkv, w_out, w_up, w_down, qv, up_bias, biases, gains, shifts)


def backward_reduce_kernel(
    dim, tokens, cots, full, norms, qkvo, logs, gd, us, hbs, between, out, grads, totals,
    left, right, acc, g, u, wa, wf, da, df, dl, dlsem, trades,
    sendc, recvc, keep, x1s, x1r, y1s, y1r, part, base, x2s, x2r, y2s, y2r, mid,
    zk, zs1, zr1, zs2, zr2, zs3, zr3,
    wasem, wfsem, dasem, dfsem, gsem, osem4, bsem, gds, gdr, tss, trs,
    cs, cr, x1ss, x1rs, y1ss, y1rs, x2ss, x2rs, y2ss, y2rs, z1ss, z1rs, z2ss, z2rs, z3ss, z3rs, os, orr,
):
    c, p, d = lax.axis_index("section"), lax.axis_index("mp"), lax.axis_index("dp")
    near = neighbours()
    near["pair"] = (c, p, d + 1 - 2 * lax.rem(d, 2))
    near["far"] = (c, p, lax.rem(d + 2, 4))
    spots = places()
    is_end = (d == 0) | (d == 3)
    is_mid = jnp.logical_not(is_end)
    rows = sendc.shape[2]
    half = rows // 2
    wide = 2 * rows

    def core_copy(s):
        a, b = lax.rem(s, 2), lax.rem(s, 4)
        return remote(sendc.at[a], recvc.at[b], cs.at[a], cr.at[b], near["core"])

    def link_copy(s, src, dst, ss, rs, name):
        a, b = lax.rem(s, 2), lax.rem(s, 4)
        return remote(src.at[a], dst.at[b], ss.at[a], rs.at[b], near[name])

    def first_copy(s, n, src, dst, ss, rs, name):
        a, b = lax.rem(s, 2), lax.rem(s, 4)
        return remote(src.at[a, n], dst.at[b, n], ss.at[a, n], rs.at[b, n], near[name])

    x1 = lambda s, n: first_copy(s, n, x1s, x1r, x1ss, x1rs, "x")
    y1 = lambda s, n: first_copy(s, n, y1s, y1r, y1ss, y1rs, "y")
    x2 = lambda s: link_copy(s, x2s, x2r, x2ss, x2rs, "x")
    y2 = lambda s: link_copy(s, y2s, y2r, y2ss, y2rs, "y")
    z1 = lambda s, n: first_copy(s, n, zs1, zr1, z1ss, z1rs, "inner")
    z2 = lambda s, n: first_copy(s, n, zs2, zr2, z2ss, z2rs, "across")

    def z3(s, n):
        b = lax.rem(s, 6)
        return remote(zs3.at[b, n], zr3.at[b, n], z3ss.at[b, n], z3rs.at[b, n], near["outer"])

    def stage0(s):
        k, slot = lax.rem(s, 12), lax.rem(s, 2)
        stride = jnp.where(k < 8, 4, 1)
        first = jnp.where(k < 4, k, jnp.where(k < 8, 12 + k, jnp.where(k == 8, 32, 36 + 4 * (k - 9))))
        kind = jnp.where(k < 4, 0, jnp.where(k < 8, 1, jnp.where(k == 8, 2, 3)))
        for r in range(4):
            whole = dot_tn(left[first + stride * spots[r]], right[kind])
            keep[slot, r] = jnp.where(c == 0, whole[:rows], whole[rows:])
            sendc[slot, r] = low(jnp.where(c == 0, whole[rows:], whole[:rows]))
        core_copy(s).start()

    def stage1(s):
        a, b = lax.rem(s, 2), lax.rem(s, 4)
        core_copy(s).wait()
        far = keep[a, 3] + high(recvc[b, 3])
        x1s[a, 0] = low(far[:half])
        y1s[a, 0] = low(far[half:])
        x1(s, 0).start()
        y1(s, 0).start()
        by_x = keep[a, 1] + high(recvc[b, 1])
        x1s[a, 1] = low(by_x[:half])
        part[a, 0] = by_x[half:]
        by_y = keep[a, 2] + high(recvc[b, 2])
        y1s[a, 1] = low(by_y[half:])
        part[a, 1] = by_y[:half]
        x1(s, 1).start()
        y1(s, 1).start()
        base[a] = keep[a, 0] + high(recvc[b, 0])

    def stage2(s):
        a, b = lax.rem(s, 2), lax.rem(s, 4)
        x1(s, 0).wait()
        y2s[a] = low(part[a, 1] + high(x1r[b, 0]))
        y2(s).start()
        y1(s, 0).wait()
        x2s[a] = low(part[a, 0] + high(y1r[b, 0]))
        x2(s).start()
        x1(s, 1).wait()
        y1(s, 1).wait()
        own = base[a]
        mid[a, 0] = own[:half] + high(x1r[b, 1])
        mid[a, 1] = own[half:] + high(y1r[b, 1])

    def stage3(s):
        a, b = lax.rem(s, 2), lax.rem(s, 4)
        for n, copy, got in ((0, y2, y2r), (1, x2, x2r)):
            copy(s).wait()
            total = mid[a, n] + high(got[b])

            @pl.when(is_end)
            def _():
                zs1[a, n] = low(total)
                z1(s, n).start()

            @pl.when(is_mid)
            def _():
                zk[a, n] = total

    def stage4(s):
        a, b = lax.rem(s, 2), lax.rem(s, 4)
        for n in range(2):

            @pl.when(is_end)
            def _():
                z1(s, n).wait_send()

            @pl.when(is_mid)
            def _():
                z1(s, n).wait_recv()
                zs2[a, n] = low(zk[a, n] + high(zr1[b, n]))
                z2(s, n).start()

    def stage5(s):
        a, b, to = lax.rem(s, 2), lax.rem(s, 4), lax.rem(s, 6)

        @pl.when(is_mid)
        def _():
            for n in range(2):
                z2(s, n).wait()
                zs3[to, n] = low(high(zs2[a, n]) + high(zr2[b, n]))
                z3(s, n).start()

    def stage6(s, begin):
        layer, k, b = 1 - s // 12, lax.rem(s, 12), lax.rem(s, 6)

        def finish(source):
            @pl.when(layer == c)
            def _():
                copy = pltpu.make_async_copy(source.at[b], out.at[k, c], os.at[b])
                copy.start() if begin else copy.wait()

            @pl.when(layer != c)
            def _():
                copy = remote(source.at[b], out.at[k, c], os.at[b], orr.at[k], near["core"])
                copy.start() if begin else copy.wait_send()

        @pl.when(is_end)
        def _():
            if begin:
                for n in range(2):
                    z3(s, n).wait_recv()
            finish(zr3)

        @pl.when(is_mid)
        def _():
            if begin:
                for n in range(2):
                    z3(s, n).wait_send()
            finish(zs3)

    def load_g(l, n):
        return pltpu.make_async_copy(gd.at[l, n, 0], left.at[n], gsem.at[n])

    def load_o(l, n):
        return pltpu.make_async_copy(qkvo.at[l, n, 3], left.at[32 + n], osem4.at[n])

    def load_h(l):
        return pltpu.make_async_copy(hbs.at[l], right.at[1], bsem.at[0])

    def load_x(source):
        return pltpu.make_async_copy(source, right.at[3], bsem.at[1])

    def load_u(l, which):
        return pltpu.make_async_copy(us.at[l, which], u, bsem.at[2])

    def ffn(l, n, slot):
        return weight_copies(full, l, 1, lax.rem(n, 4), n // 4, wf.at[slot], wfsem.at[slot], wide) + [
            pltpu.make_async_copy(gd.at[l, 4 * lax.rem(n, 4) + n // 4, 1], df.at[slot], dfsem.at[slot])
        ]

    def attn(l, q, slot):
        return weight_copies(full, l, 0, q, 0, wa.at[slot], wasem.at[slot], wide) + [
            pltpu.make_async_copy(qkvo.at[l, q], da.at[slot], dasem.at[slot]),
            pltpu.make_async_copy(logs.at[l, q], dl.at[slot], dlsem.at[slot]),
        ]

    def store_dx(l, begin):
        @pl.when(l == c)
        def _():
            copy = pltpu.make_async_copy(g, grads.at[c], gds.at[0])
            copy.start() if begin else copy.wait()

        @pl.when(l != c)
        def _():
            copy = remote(g, grads.at[c], gds.at[0], gdr.at[0], near["core"])
            copy.start() if begin else copy.wait_send()

    def ahead(l):
        load_u(l, 1).start()
        for copy in ffn(l, 0, 0) + attn(l, 0, 0):
            copy.start()

    def operands(l):
        def run(n, carry):
            load_g(l, n).start()
            return carry

        lax.fori_loop(0, 16, run, 0)
        for n in range(4):
            load_o(l, n).start()
        load_h(l).start()

    def operands_there(l):
        def run(n, carry):
            load_g(l, n).wait()
            return carry

        lax.fori_loop(0, 16, run, 0)
        for n in range(4):
            load_o(l, n).wait()
        load_h(l).wait()

    def top_segment(l):
        load_u(l, 1).wait()
        norm_back(u, g, norms[l, 3:4], totals.at[l], (1, 3, 5), right.at[0], acc)
        load_u(l, 0).start()

        @pl.when(l == 1)
        def _():
            operands_there(1)

    def ffn_segment(l, b):
        def run(q, carry):
            n = 4 * b + q
            slot = lax.rem(n, 2)
            for copy in ffn(l, n, slot):
                copy.wait()

            @pl.when(n < 15)
            def _():
                for copy in ffn(l, n + 1, 1 - slot):
                    copy.start()

            row = ffn_back_block(right.at[0], wf.at[slot], df[slot], acc, left.at[16 + 4 * q + b])
            totals[l, pl.ds(10 + b, 1), pl.ds(pl.multiple_of(q * wide, wide), wide)] = row
            return carry

        lax.fori_loop(0, 4, run, 0)

    def middle_segment(l):
        load_u(l, 0).wait()
        norm_back(u, acc, norms[l, 2:3], totals.at[l], (0, 2, 4), right.at[2], acc)

    def attention_segment(l, q):
        slot = lax.rem(q, 2)
        for copy in attn(l, q, slot):
            copy.wait()

        @pl.when(q < 3)
        def _():
            for copy in attn(l, q + 1, 1 - slot):
                copy.start()

        dq, dk, dv = left.at[36 + q], left.at[40 + q], left.at[44 + q]
        attention_back_block(right.at[2], wa.at[slot], da.at[slot], dl[slot], dq, dk, dv, acc, dim)
        cols = pl.ds(pl.multiple_of(q * wide, wide), wide)
        totals[l, 8:9, cols] = jnp.sum(high(dq[...]), axis=0, keepdims=True)
        totals[l, 9:10, cols] = jnp.sum(high(dv[...]), axis=0, keepdims=True)

    def end_segment(l):
        by_rows(acc.shape[0], 64, lambda r: g.__setitem__(r, low(acc[r])))
        store_dx(l, True)
        if l == 1:
            ahead(0)

    def segment(i):
        l = jnp.where(i < 8, 1, 0)
        j = jnp.where(i < 8, i, i - 9)

        @pl.when(i == 8)
        def _():
            end_segment(1)
            operands(0)
            store_dx(1, False)

        @pl.when(i == 7)
        def _():
            load_x(between).wait()

        @pl.when(j == -1)
        def _():
            top_segment(l)

        @pl.when((j >= 0) & (j < 4))
        def _():
            ffn_segment(l, j)

        @pl.when(j == 3)
        def _():
            middle_segment(l)

        @pl.when((j >= 4) & (j < 8))
        def _():
            attention_segment(l, j - 4)

        @pl.when(i == 17)
        def _():
            end_segment(0)

        @pl.when(i == 10)
        def _():
            operands_there(0)

        @pl.when(i == 12)
        def _():
            load_x(tokens.at[c]).start()

        @pl.when(i == 16)
        def _():
            load_x(tokens.at[c]).wait()

    def trade(k):
        return remote(totals, trades.at[k], tss.at[k], trs.at[k], near[("core", "x", "y", "pair", "far")[k]])

    first_rows = pltpu.make_async_copy(cots.at[c], g, bsem.at[3])
    first_rows.start()
    ahead(1)
    operands(1)
    load_x(between).start()
    totals[...] = jnp.zeros_like(totals)
    barrier = pltpu.get_barrier_semaphore()

    def signal(device):
        pl.semaphore_signal(barrier, inc=1, device_id=device, device_id_type=MESH)

    for name in ("core", "x", "y", "pair", "far"):
        signal(near[name])

    @pl.when(is_end)
    def _():
        pl.semaphore_wait(barrier, 5)

    @pl.when(is_mid)
    def _():
        signal(near["across"])
        pl.semaphore_wait(barrier, 6)

    first_rows.wait()

    def step(count, carry):
        i = count - 1

        def run(stage, lag, *extra):
            @pl.when((i >= lag) & (i < CHUNKS + lag))
            def _():
                stage(i - lag, *extra)

        for lag, stage in enumerate((stage1, stage2, stage3, stage4, stage5)):
            run(stage, lag + 1)
        run(stage6, 6, True)
        run(stage6, 7, False)
        for k in range(6):

            @pl.when(i == 19 + k)
            def _():
                if k:
                    trade(k - 1).wait()
                    totals[...] += trades[k - 1]
                if k < 5:
                    trade(k).start()

        run(stage0, 0)

        @pl.when((i < 19) & (i != 0))
        def _():
            segment(jnp.where(i < 0, i, i - 1))

        return carry

    lax.fori_loop(0, CHUNKS + 9, step, 0)
    store_dx(0, False)
    remote(g, grads.at[1 - c], gds.at[0], gdr.at[0], near["core"]).wait_recv()
    for k in range(12):
        remote(zs3.at[0], out.at[k, 1 - c], os.at[0], orr.at[k], near["core"]).wait_recv()


def backward_reduce(dim, tokens, cots, full, norms, saved):
    seq, width = tokens.shape[1:]
    wide = width // 4
    block, half = wide // 2, wide // 4
    bf, f32, dma, v = jnp.bfloat16, jnp.float32, pltpu.SemaphoreType.DMA, pltpu.VMEM
    hbm, vmem = pl.BlockSpec(memory_space=pl.ANY), pl.BlockSpec(memory_space=pltpu.VMEM)
    S = jax.ShapeDtypeStruct
    return pl.pallas_call(
        functools.partial(backward_reduce_kernel, dim),
        out_shape=(S((12, 2, 2, half, width), bf), S((2, seq, width), bf), S((2, 16, width), f32)),
        in_specs=[hbm, hbm, hbm, vmem] + [hbm] * 6,
        out_specs=[hbm, hbm, vmem],
        scratch_shapes=[
            v((48, seq, wide), bf), v((4, seq, width), bf), v((seq, width), f32), v((seq, width), bf),
            v((seq, width), f32),
            v((2, 4, wide, width), bf), v((2, 2, wide, width), bf), v((2, 4, seq, wide), bf), v((2, seq, wide), bf),
            v((2, seq, 128), f32), dma((2,)), v((5, 2, 16, width), f32),
            v((2, 4, block, width), bf), v((4, 4, block, width), bf), v((2, 4, block, width), f32),
            v((2, 2, half, width), bf), v((4, 2, half, width), bf), v((2, 2, half, width), bf), v((4, 2, half, width), bf),
            v((2, 2, half, width), f32), v((2, block, width), f32),
            v((2, half, width), bf), v((4, half, width), bf), v((2, half, width), bf), v((4, half, width), bf),
            v((2, 2, half, width), f32),
            v((2, 2, half, width), f32), v((2, 2, half, width), bf), v((4, 2, half, width), bf),
            v((2, 2, half, width), bf), v((4, 2, half, width), bf), v((6, 2, half, width), bf), v((6, 2, half, width), bf),
            dma((2, 4)), dma((2, 2)), dma((2,)), dma((2,)), dma((16,)), dma((4,)), dma((4,)), dma((1,)), dma((1,)), dma((5,)), dma((5,)),
        ] + [dma((n,)) for n in (2, 4)] + [dma((n, 2)) for n in (2, 4) * 2] + [dma((n,)) for n in (2, 4) * 2]
        + [dma((n, 2)) for n in (2, 4, 2, 4, 6, 6)] + [dma((6,)), dma((12,))],
        compiler_params=pltpu.CompilerParams(collective_id=1, has_side_effects=True, vmem_limit_bytes=63 * 2**20),
    )(tokens, cots, full, norms, *saved)


def finish_kernel(parts, acts_in, grads_in, totals, acts, grads, g_qkv, g_out, g_up, g_down, g_qv, g_bias,
                  g_biases, g_gains, g_shifts, pb, ab, gb, qb, ob, ub, db, psem, asem, osem):
    def load(k):
        return pltpu.make_async_copy(parts.at[k], pb.at[k], psem.at[k])

    others = [(acts_in, ab, acts, 0), (grads_in, gb, grads, 1)]
    for k in range(12):
        load(k).start()
    for source, buffer, place, n in others:
        pltpu.make_async_copy(source, buffer, asem.at[n]).start()
    stores = []
    rows = pb.shape[1]
    c, p, d = lax.axis_index("section"), lax.axis_index("mp"), lax.axis_index("dp")
    mine = totals.at[c]
    own = mine[8:16, pl.ds(pl.multiple_of(p * rows, rows), rows)]
    g_qv[...] = own[0:2]
    for b in range(4):
        g_bias[:, b * rows : (b + 1) * rows] = own[2 + b : 3 + b]
    piece = g_gains.shape[1]
    both = mine[0:8, pl.ds(pl.multiple_of(p * rows + d // 2 * 2 * piece, 2 * piece), 2 * piece)]
    both = jnp.where(lax.rem(d, 2) == 0, both[:, :piece], both[:, piece:])
    g_biases[...], g_gains[...], g_shifts[...] = both[0:2], both[2:4], both[4:6]

    def store(source, place):
        copy = pltpu.make_async_copy(source, place, osem.at[len(stores)])
        copy.start()
        stores.append(copy)

    for k in range(12):
        load(k).wait()
        if k < 4:
            span = pl.ds(k * rows, rows)
            db[span] = high(pb[k])
            store(db.at[span], g_down.at[span])
        elif k < 8:
            ub[:, pl.ds((k - 4) * rows, rows)] = high(pb[k]).T
            if k == 7:
                store(ub, g_up)
        elif k == 8:
            ob[...] = high(pb[k])
            store(ob, g_out)
        else:
            qb[k - 9] = high(pb[k]).T
            store(qb.at[k - 9], g_qkv.at[k - 9])
    for source, buffer, place, n in others:
        pltpu.make_async_copy(source, buffer, asem.at[n]).wait()
        store(buffer, place)
    for copy in stores:
        copy.wait()


def finish(parts, acts, grads, totals):
    count, rows, width = parts.shape
    bf, f32, dma, v = jnp.bfloat16, jnp.float32, pltpu.SemaphoreType.DMA, pltpu.VMEM
    S = jax.ShapeDtypeStruct
    shapes = [(3, width, rows), (rows, width), (width, width), (width, width)]
    piece = width // (lax.axis_size("mp") * lax.axis_size("dp"))
    hbm, vmem = pl.BlockSpec(memory_space=pl.ANY), pl.BlockSpec(memory_space=pltpu.VMEM)
    vectors = [(2, rows), (1, 4 * rows)] + [(2, piece)] * 3
    return pl.pallas_call(
        finish_kernel,
        out_shape=[S(acts.shape, bf), S(grads.shape, bf)] + [S(shape, f32) for shape in shapes + vectors],
        in_specs=[hbm] * 3 + [vmem],
        out_specs=[hbm] * 6 + [vmem] * 5,
        scratch_shapes=[v(parts.shape, bf), v(acts.shape, bf), v(grads.shape, bf)] + [v(shape, f32) for shape in shapes]
        + [dma((12,)), dma((2,)), dma((11,))],
        compiler_params=pltpu.CompilerParams(vmem_limit_bytes=63 * 2**20),
    )(parts, acts, grads, totals)


def by_page(
    token_in,
    cotangent,
    w_qkv,
    qv_bias,
    w_attn_out,
    w_ffn_in,
    ffn_in_bias,
    w_ffn_out,
    out_biases,
    norm_gains,
    norm_shifts,
):
    width = token_in.shape[2]
    full, vecs, norms, *saved, acts = gather_forward(
        HEAD_DIM,
        token_in,
        w_qkv[0],
        w_attn_out[0],
        w_ffn_in[0],
        w_ffn_out[0],
        qv_bias[0],
        ffn_in_bias,
        out_biases[0],
        norm_gains[0],
        norm_shifts[0],
    )
    parts, grads, totals = backward_reduce(HEAD_DIM, token_in, cotangent, full, norms, saved)
    results = finish(parts.reshape(12, width // 4, width), acts, grads, totals)
    acts, grads, grad_qkv, grad_out, grad_up, grad_down, grad_qv, grad_bias, *rows = results
    return (
        acts[None],
        grads[None],
        grad_qkv[None],
        grad_qv[None],
        grad_out[None],
        grad_up[None],
        grad_bias,
        grad_down[None],
    ) + tuple(row[None] for row in rows)


def on_device(*args):
    token_in, w_qkv, ffn_in = args[0], args[2], args[5]
    fits = (
        lax.axis_size("section") == 2
        and lax.axis_size("mp") == 4
        and lax.axis_size("dp") == 4
        and token_in.shape == (2, SEQ, 1024)
        and w_qkv.shape[3] == 256
        and ffn_in.shape[2] == 1024
    )
    return by_page(*args) if fits else pipelined(*args)


def solution(mesh):
    return jax.shard_map(
        on_device,
        mesh=mesh,
        in_specs=(
            P(None, ("dp", "mp"), None),
            P(None, ("dp", "mp"), None),
            P("section", None, None, "mp"),
            P("section", None, "mp"),
            P("section", "mp", None),
            P("section", None, "mp"),
            P("section", "mp"),
            P("section", "mp", None),
            P("section", None, None),
            P("section", None, None),
            P("section", None, None),
        ),
        out_specs=(
            P("section", None, ("dp", "mp"), None),
            P("section", None, ("dp", "mp"), None),
            P("section", None, None, "mp"),
            P("section", None, "mp"),
            P("section", "mp", None),
            P("section", None, "mp"),
            P("section", "mp"),
            P("section", "mp", None),
            P("section", None, ("mp", "dp")),
            P("section", None, ("mp", "dp")),
            P("section", None, ("mp", "dp")),
        ),
        check_vma=False,
    )
```

```python
import functools
from functools import partial
import math

import jax
import jax.numpy as jnp
from jax import lax
from jax.experimental import pallas as pl
from jax.experimental.pallas import tpu as pltpu
from jax.sharding import PartitionSpec as P

HEAD_DIM = 64
SEQ = 512


def from_behind(value, axis, by):
    devices = lax.axis_size(axis)
    pairs = [(i, i + by) for i in range(devices) if 0 <= i + by < devices]
    return lax.ppermute(value, axis, pairs)


def norm_rows(values, gain_row, shift_row):
    average = jnp.mean(values, axis=-1, keepdims=True)
    centered = values - average
    variance = jnp.mean(centered * centered, axis=-1, keepdims=True)
    return centered * lax.rsqrt(variance + 1e-05) * gain_row + shift_row


def exact_gelu(values):
    return jax.nn.gelu(values, approximate=False)


def layer_forward(params, token_rows):
    (
        w_qkv,
        qv_bias,
        w_attn_out,
        w_ffn_in,
        ffn_in_bias,
        w_ffn_out,
        out_biases,
        norm_gains,
        norm_shifts,
    ) = params
    gathered = lax.all_gather(token_rows, "mp", axis=0, tiled=True)
    rows_all = gathered.shape[0]
    local_width = w_qkv.shape[2]
    local_heads = local_width // HEAD_DIM
    page_count = rows_all // SEQ
    scale_factor = 1.0 / math.sqrt(HEAD_DIM)
    bias_full = jnp.stack([qv_bias[0], jnp.zeros_like(qv_bias[0]), qv_bias[1]]).astype(jnp.float32)
    projected = (
        jnp.einsum("rd,cde->cre", gathered, w_qkv, preferred_element_type=jnp.float32)
        + bias_full[:, None, :]
    )
    heads_view = projected.astype(jnp.bfloat16).reshape(3, page_count, SEQ, local_heads, HEAD_DIM)
    scores = (
        jnp.einsum(
            "pqhe,pkhe->phqk", heads_view[0], heads_view[1], preferred_element_type=jnp.float32
        )
        * scale_factor
    )
    top_score = jnp.max(scores, axis=-1, keepdims=True)
    exponent = jnp.exp(scores - top_score)
    weights_soft = exponent / jnp.sum(exponent, axis=-1, keepdims=True)
    weights_low = weights_soft.astype(jnp.bfloat16)
    attended = jnp.einsum(
        "phqk,pkhe->pqhe", weights_low, heads_view[2], preferred_element_type=jnp.float32
    )
    attended = attended.reshape(rows_all, local_width).astype(jnp.bfloat16)
    attn_part = jnp.dot(attended, w_attn_out, preferred_element_type=jnp.float32)
    attn_rows = lax.psum_scatter(
        attn_part.astype(jnp.bfloat16), "mp", scatter_dimension=0, tiled=True
    ).astype(jnp.float32)
    residual_one = attn_rows + out_biases[0] + token_rows.astype(jnp.float32)
    first = norm_rows(residual_one, norm_gains[0], norm_shifts[0])
    first_all = lax.all_gather(first.astype(jnp.bfloat16), "mp", axis=0, tiled=True)
    pre_act = jnp.dot(first_all, w_ffn_in, preferred_element_type=jnp.float32) + ffn_in_bias.astype(
        jnp.float32
    )
    activated = exact_gelu(pre_act).astype(jnp.bfloat16)
    ffn_part = jnp.dot(activated, w_ffn_out, preferred_element_type=jnp.float32)
    ffn_rows = lax.psum_scatter(
        ffn_part.astype(jnp.bfloat16), "mp", scatter_dimension=0, tiled=True
    ).astype(jnp.float32)
    residual_two = ffn_rows + out_biases[1] + first
    result = norm_rows(residual_two, norm_gains[1], norm_shifts[1])
    kept_values = (
        gathered,
        heads_view,
        weights_soft,
        attended,
        residual_one,
        first_all,
        pre_act,
        activated,
        residual_two,
    )
    return (result, kept_values)


def layer_backward(params, kept_values, grad_out):
    (
        w_qkv,
        qv_bias,
        w_attn_out,
        w_ffn_in,
        ffn_in_bias,
        w_ffn_out,
        out_biases,
        norm_gains,
        norm_shifts,
    ) = params
    (
        gathered,
        heads_view,
        weights_soft,
        attended,
        residual_one,
        first_all,
        pre_act,
        activated,
        residual_two,
    ) = kept_values
    rows_all = gathered.shape[0]
    local_width = w_qkv.shape[2]
    local_heads = local_width // HEAD_DIM
    page_count = rows_all // SEQ
    scale_factor = 1.0 / math.sqrt(HEAD_DIM)
    unused_two, norm_two_back = jax.vjp(norm_rows, residual_two, norm_gains[1], norm_shifts[1])
    grad_res_two, grad_gain_two, grad_shift_two = norm_two_back(grad_out)
    grad_bias_two = jnp.sum(grad_res_two, axis=0)
    ffn_grad_all = lax.all_gather(grad_res_two.astype(jnp.bfloat16), "mp", axis=0, tiled=True)
    grad_w_ffn_out = jnp.einsum(
        "rf,rd->fd", activated, ffn_grad_all, preferred_element_type=jnp.float32
    )
    grad_act = jnp.einsum("rd,fd->rf", ffn_grad_all, w_ffn_out, preferred_element_type=jnp.float32)
    unused_gelu, gelu_back = jax.vjp(exact_gelu, pre_act)
    grad_pre = gelu_back(grad_act)[0].astype(jnp.bfloat16)
    grad_ffn_in_bias = jnp.sum(grad_pre.astype(jnp.float32), axis=0)
    grad_w_ffn_in = jnp.einsum("rd,rf->df", first_all, grad_pre, preferred_element_type=jnp.float32)
    first_part = jnp.einsum("rf,df->rd", grad_pre, w_ffn_in, preferred_element_type=jnp.float32)
    first_grad_rows = lax.psum_scatter(
        first_part.astype(jnp.bfloat16), "mp", scatter_dimension=0, tiled=True
    ).astype(jnp.float32)
    grad_first = first_grad_rows + grad_res_two
    unused_one, norm_one_back = jax.vjp(norm_rows, residual_one, norm_gains[0], norm_shifts[0])
    grad_res_one, grad_gain_one, grad_shift_one = norm_one_back(grad_first)
    grad_bias_one = jnp.sum(grad_res_one, axis=0)
    attn_grad_all = lax.all_gather(grad_res_one.astype(jnp.bfloat16), "mp", axis=0, tiled=True)
    grad_w_attn_out = jnp.einsum(
        "rk,rd->kd", attended, attn_grad_all, preferred_element_type=jnp.float32
    )
    grad_attended = jnp.einsum(
        "rd,kd->rk", attn_grad_all, w_attn_out, preferred_element_type=jnp.float32
    )
    grad_attended = grad_attended.astype(jnp.bfloat16).reshape(
        page_count, SEQ, local_heads, HEAD_DIM
    )
    weights_low = weights_soft.astype(jnp.bfloat16)
    grad_weights = jnp.einsum(
        "pqhe,pkhe->phqk", grad_attended, heads_view[2], preferred_element_type=jnp.float32
    )
    grad_values = jnp.einsum(
        "phqk,pqhe->pkhe", weights_low, grad_attended, preferred_element_type=jnp.float32
    )
    inner_total = jnp.sum(weights_soft * grad_weights, axis=-1, keepdims=True)
    grad_scores = (weights_soft * (grad_weights - inner_total)).astype(jnp.bfloat16)
    grad_queries = (
        jnp.einsum(
            "phqk,pkhe->pqhe", grad_scores, heads_view[1], preferred_element_type=jnp.float32
        )
        * scale_factor
    )
    grad_keys = (
        jnp.einsum(
            "phqk,pqhe->pkhe", grad_scores, heads_view[0], preferred_element_type=jnp.float32
        )
        * scale_factor
    )
    grad_proj = (
        jnp.stack([grad_queries, grad_keys, grad_values])
        .reshape(3, rows_all, local_width)
        .astype(jnp.bfloat16)
    )
    proj_sums = jnp.sum(grad_proj.astype(jnp.float32), axis=1)
    grad_qv_bias = jnp.stack([proj_sums[0], proj_sums[2]])
    grad_w_qkv = jnp.einsum("rd,cre->cde", gathered, grad_proj, preferred_element_type=jnp.float32)
    input_part = jnp.einsum("cre,cde->rd", grad_proj, w_qkv, preferred_element_type=jnp.float32)
    input_grad_rows = lax.psum_scatter(
        input_part.astype(jnp.bfloat16), "mp", scatter_dimension=0, tiled=True
    ).astype(jnp.float32)
    grad_in = input_grad_rows + grad_res_one
    matrix_grads = (
        grad_w_qkv,
        grad_qv_bias,
        grad_w_attn_out,
        grad_w_ffn_in,
        grad_ffn_in_bias,
        grad_w_ffn_out,
    )
    vector_grads = (
        jnp.stack([grad_bias_one, grad_bias_two]),
        jnp.stack([grad_gain_one, grad_gain_two]),
        jnp.stack([grad_shift_one, grad_shift_two]),
    )
    return (grad_in, matrix_grads, vector_grads)


def pipelined(
    token_in,
    cotangent,
    w_qkv,
    qv_bias,
    w_attn_out,
    w_ffn_in,
    ffn_in_bias,
    w_ffn_out,
    out_biases,
    norm_gains,
    norm_shifts,
):
    params = (
        w_qkv[0],
        qv_bias[0],
        w_attn_out[0],
        w_ffn_in[0],
        ffn_in_bias[0],
        w_ffn_out[0],
        out_biases[0],
        norm_gains[0],
        norm_shifts[0],
    )
    micro_count = token_in.shape[0]
    section_index = lax.axis_index("section")
    is_first = section_index == 0
    zero_rows = jnp.zeros(token_in.shape[1:], jnp.bfloat16)
    run_forward = partial(layer_forward, params)
    run_backward = partial(layer_backward, params)

    def forward_step(step_index, carry):
        received, saved, stored = carry
        own_micro = step_index - section_index
        is_valid = (own_micro >= 0) & (own_micro < micro_count)
        slot_index = jnp.clip(own_micro, 0, micro_count - 1)
        first_rows = lax.dynamic_index_in_dim(
            token_in, jnp.minimum(step_index, micro_count - 1).astype(jnp.int32), 0, keepdims=False
        )
        layer_in = jnp.where(is_first, first_rows, received)
        result, unused_kept = run_forward(layer_in)
        result_low = result.astype(jnp.bfloat16)
        old_saved = lax.dynamic_index_in_dim(saved, slot_index, 0, keepdims=False)
        saved = lax.dynamic_update_index_in_dim(
            saved, jnp.where(is_valid, layer_in, old_saved), slot_index, 0
        )
        old_stored = lax.dynamic_index_in_dim(stored, slot_index, 0, keepdims=False)
        stored = lax.dynamic_update_index_in_dim(
            stored, jnp.where(is_valid, result_low, old_stored), slot_index, 0
        )
        received = from_behind(result_low, "section", 1)
        return (received, saved, stored)

    start_carry = (zero_rows, jnp.zeros_like(token_in), jnp.zeros_like(token_in))
    unused_received, saved, stored = lax.fori_loop(0, micro_count + 1, forward_step, start_carry)
    matrix_zero = tuple((jnp.zeros(entry.shape, jnp.float32) for entry in params[:6]))
    vector_zero = (
        jnp.zeros(out_biases.shape[1:], jnp.float32),
        jnp.zeros(norm_gains.shape[1:], jnp.float32),
        jnp.zeros(norm_shifts.shape[1:], jnp.float32),
    )

    def backward_step(step_index, carry):
        received_grad, grad_store, matrix_sums, vector_sums = carry
        own_micro = step_index - (1 - section_index)
        is_valid = (own_micro >= 0) & (own_micro < micro_count)
        slot_index = jnp.clip(own_micro, 0, micro_count - 1)
        layer_in = lax.dynamic_index_in_dim(saved, slot_index, 0, keepdims=False)
        from_last = lax.dynamic_index_in_dim(cotangent, slot_index, 0, keepdims=False)
        grad_out = jnp.where(is_first, received_grad, from_last).astype(jnp.float32)
        unused_result, kept_values = run_forward(layer_in)
        grad_in, matrix_grads, vector_grads = run_backward(kept_values, grad_out)
        matrix_grads = tuple((jnp.where(is_valid, entry, 0.0) for entry in matrix_grads))
        vector_grads = tuple((jnp.where(is_valid, entry, 0.0) for entry in vector_grads))
        grad_low = grad_in.astype(jnp.bfloat16)
        old_piece = lax.dynamic_index_in_dim(grad_store, slot_index, 0, keepdims=False)
        grad_store = lax.dynamic_update_index_in_dim(
            grad_store, jnp.where(is_valid, grad_low, old_piece), slot_index, 0
        )
        grad_one, grad_two, grad_three, grad_four, grad_five, grad_six = matrix_grads
        matrix_grads = (
            lax.psum(grad_one.astype(jnp.bfloat16), "dp").astype(jnp.float32),
            lax.psum(grad_two.astype(jnp.bfloat16), "dp").astype(jnp.float32),
            lax.psum(grad_three.astype(jnp.bfloat16), "dp").astype(jnp.float32),
            lax.psum(grad_four.astype(jnp.bfloat16), "dp").astype(jnp.float32),
            lax.psum(grad_five.astype(jnp.bfloat16), "dp").astype(jnp.float32),
            lax.psum(grad_six.astype(jnp.bfloat16), "dp").astype(jnp.float32),
        )
        matrix_sums = tuple((total + extra for total, extra in zip(matrix_sums, matrix_grads)))
        vector_sums = tuple((total + extra for total, extra in zip(vector_sums, vector_grads)))
        received_grad = from_behind(grad_low, "section", -1)
        return (received_grad, grad_store, matrix_sums, vector_sums)

    back_carry = (zero_rows, jnp.zeros_like(token_in), matrix_zero, vector_zero)
    unused_grad, grad_store, matrix_sums, vector_sums = lax.fori_loop(
        0, micro_count + 1, backward_step, back_carry
    )
    bias_total, gain_total, shift_total = vector_sums
    bias_part, gain_part, shift_part = (
        lax.psum_scatter(bias_total, ("mp", "dp"), scatter_dimension=1, tiled=True),
        lax.psum_scatter(gain_total, ("mp", "dp"), scatter_dimension=1, tiled=True),
        lax.psum_scatter(shift_total, ("mp", "dp"), scatter_dimension=1, tiled=True),
    )
    return (
        stored[None],
        grad_store[None],
        matrix_sums[0][None],
        matrix_sums[1][None],
        matrix_sums[2][None],
        matrix_sums[3][None],
        matrix_sums[4][None],
        matrix_sums[5][None],
        bias_part[None],
        gain_part[None],
        shift_part[None],
    )


MESH = pl.DeviceIdType.MESH
CHUNKS = 24
TRIPLES = 8
SCALE = 0.125


def low(value):
    return value.astype(jnp.bfloat16)


def high(value):
    return value.astype(jnp.float32)


def remote(src, dst, send, recv, device):
    return pltpu.make_async_remote_copy(
        src_ref=src, dst_ref=dst, send_sem=send, recv_sem=recv, device_id=device, device_id_type=MESH
    )


def neighbours():
    c, p, d = lax.axis_index("section"), lax.axis_index("mp"), lax.axis_index("dp")
    return {
        "core": (1 - c, p, d),
        "x": (c, p + 1 - 2 * lax.rem(p, 2), d),
        "y": (c, lax.rem(p + 2, 4), d),
        "across": (c, p, 3 - d),
        "inner": (c, p, jnp.where(d == 0, 1, 2)),
        "outer": (c, p, jnp.where(d == 1, 0, 3)),
    }


def places():
    p = lax.axis_index("mp")
    return [p, p + 1 - 2 * lax.rem(p, 2), lax.rem(p + 2, 4), 3 - p]


def dot(a, b):
    return jnp.dot(a, b, preferred_element_type=jnp.float32)


def dot_tn(a, b):
    return lax.dot_general(a, b, (((0,), (0,)), ((), ())), preferred_element_type=jnp.float32)


def dot_nt(a, b):
    return lax.dot_general(a, b, (((1,), (1,)), ((), ())), preferred_element_type=jnp.float32)


def standard(values):
    average = jnp.mean(values, axis=-1, keepdims=True)
    centered = values - average
    variance = jnp.mean(centered * centered, axis=-1, keepdims=True)
    scale = lax.rsqrt(variance + 1e-05)
    return centered * scale, scale


def softmax(q, k):
    scores = dot_nt(q * jnp.asarray(SCALE, q.dtype), k)
    top = jnp.max(scores, axis=-1, keepdims=True)
    exponent = jnp.exp(scores - top)
    total = jnp.sum(exponent, axis=-1, keepdims=True)
    return exponent * (1.0 / total), top + jnp.log(total)


def by_rows(rows, step, body):
    def run(i, carry):
        body(pl.ds(pl.multiple_of(i * step, step), step))
        return carry

    lax.fori_loop(0, rows // step, run, 0)


def first_norm(x, nrm, acc, u1, hb):
    def run(rows):
        u = acc[rows] + nrm[0:1] + high(x[rows])
        u1[rows] = u
        h = standard(u)[0] * nrm[2:3] + nrm[4:5]
        hb[rows] = low(h)
        acc[rows] = h + nrm[1:2]

    by_rows(acc.shape[0], 64, run)


def second_norm(nrm, acc, u2, out):
    def run(rows):
        u = acc[rows]
        u2[rows] = u
        out[rows] = low(standard(u)[0] * nrm[3:4] + nrm[5:6])

    by_rows(acc.shape[0], 64, run)


def norm_back(u, grad, gain, sums, at, out_low, out_acc):
    def run(rows):
        g = high(grad[rows])
        xhat, scale = standard(u[rows])
        scaled = g * gain
        du = scale * (
            scaled
            - jnp.mean(scaled, axis=-1, keepdims=True)
            - xhat * jnp.mean(scaled * xhat, axis=-1, keepdims=True)
        )
        out_low[rows] = low(du)
        out_acc[rows] = du
        for row, term in ((at[0], du), (at[1], g * xhat), (at[2], g)):
            sums[row : row + 1] += jnp.sum(term, axis=0, keepdims=True)

    by_rows(u.shape[0], 64, run)


def ffn_back_block(dfb, w, gd, acc, dz_out):
    dz = low(dot_nt(dfb[...], w[1]) * high(gd))
    dz_out[...] = dz
    acc[...] += dot(dz, w[0])
    return jnp.sum(high(dz), axis=0, keepdims=True)


def attention_back_block(dab, w, qkv, logs, dq_out, dk_out, dv_out, acc, dim):
    dob = low(dot_nt(dab[...], w[3]))
    for j in range(dob.shape[1] // dim):
        cols = slice(j * dim, (j + 1) * dim)
        q, k, v, do = qkv[0, :, cols], qkv[1, :, cols], qkv[2, :, cols], dob[:, cols]
        a = jnp.exp(dot_nt(q * jnp.asarray(SCALE, q.dtype), k) - logs[:, j : j + 1])
        da = dot_nt(do, v)
        ds = low(a * (da - jnp.sum(a * da, axis=-1, keepdims=True)))
        dv_out[:, cols] = low(dot_tn(low(a), do))
        dq_out[:, cols] = low(dot(ds, k) * SCALE)
        dk_out[:, cols] = low(dot_tn(ds, q) * SCALE)
    acc[...] += dot(dq_out[...], w[0]) + dot(dk_out[...], w[1]) + dot(dv_out[...], w[2])


def weight_copies(full, layer, kind, p, b, buf, sem, rows):
    width = 4 * rows
    if kind == 0:
        starts = [c * width + p * rows for c in range(4)]
    else:
        starts = [4 * width + t * 4 * width + p * width + b * rows for t in range(2)]
    return [
        pltpu.make_async_copy(full.at[layer, pl.ds(pl.multiple_of(start, rows), rows)], buf.at[n], sem.at[n])
        for n, start in enumerate(starts)
    ]


def project_block(x, w, vec, save, logs, dim):
    rows = x[...]
    q = low(dot_nt(rows, w[0]) + vec[0:1])
    k = low(dot_nt(rows, w[1]))
    v = low(dot_nt(rows, w[2]) + vec[1:2])
    save[0], save[1], save[2] = q, k, v
    for j in range(q.shape[1] // dim):
        cols = slice(j * dim, (j + 1) * dim)
        soft, logs[:, j : j + 1] = softmax(q[:, cols], k[:, cols])
        save[3, :, cols] = low(dot(low(soft), v[:, cols]))


def unit_values(hb, w, bias):
    z = dot_nt(hb[...], w) + bias
    inner = 0.5 + 0.5 * lax.erf(z * math.sqrt(0.5))
    slope = inner + z * jnp.exp(-0.5 * z * z) * (1.0 / math.sqrt(2.0 * math.pi))
    return low(z * inner), low(slope)


def gather_forward_kernel(
    dim, tokens, qkv_in, out_in, up_in, down_in, qv, up_bias, biases, gains, shifts, full, vecs, norms, qkvo, logs, gd, us, hbs, between, acts,
    turned, x, acc, u, hb, wa, wf, sa, gb, sd, wasem, wfsem, sasem, gbsem, sdsem, usem, vec, norm_in, lb, lbsem,
    w_qkv, w_out, w_up, w_down, rawsem,
    ini_s, ini_r, loc, x1ss, x1rs, y1ss, y1rs, x2ss, x2rs, y2ss, y2rs, zs, zr, cs, cr, vs, vr, vloc, as_, ar,
):
    c, p, d = lax.axis_index("section"), lax.axis_index("mp"), lax.axis_index("dp")
    near = neighbours()
    near["pair"] = (c, p, d + 1 - 2 * lax.rem(d, 2))
    spots = places()
    rows = w_out.shape[0] // 2
    half = rows // 2
    odd = lax.rem(d, 2)
    others = [(cc, spots[r], d) for r in range(4) for cc in (c, 1 - c)][1:]

    def place_of(s, spot, h):
        k = lax.rem(s, 12)
        row = jnp.where(k < 4, k * 8 + spot * 2, 32 + (k // 4 - 1) * 32 + spot * 8 + lax.rem(k, 4) * 2)
        return s // 12, (row + h) * rows

    def block(s, spot, h, start=0, size=rows):
        layer, row = place_of(s, spot, h)
        return full.at[layer, pl.ds(pl.multiple_of(row + start, half), size)]

    def init_place(k, layer):
        row = place_of(12 * layer + k, p, 0)[1]
        return full.at[layer, pl.ds(pl.multiple_of(row, half), 2 * rows)]

    def turn(k):
        if k < 3:
            turned[k] = w_qkv[k].T
        elif 4 <= k < 8:
            turned[k - 1] = w_up[:, 2 * rows * (k - 4) : 2 * rows * (k - 3)].T

    def chunk(k):
        if k == 3:
            return w_out
        if k < 8:
            return turned.at[k if k < 3 else k - 1]
        return w_down.at[pl.ds(2 * rows * (k - 8), 2 * rows)]

    def init_start(k):
        if k > 2:
            turn(k)
        pltpu.make_async_copy(chunk(k), init_place(k, c), loc.at[k]).start()
        remote(chunk(k), init_place(k, c), ini_s.at[k], ini_r.at[k], near["core"]).start()

    def init_local(k):
        return pltpu.make_async_copy(init_place(k, c), init_place(k, c), loc.at[k])

    def init_wait(k):
        there = init_place(k, 1 - c)
        remote(there, there, ini_s.at[k], ini_r.at[k], near["core"]).wait_recv()

    def small():
        copies = [remote(vec, vecs.at[c, p], vs.at[i], vr.at[c, p], device) for i, device in enumerate(others)]
        copies.append(remote(norm_in, norms.at[c], vs.at[7], vr.at[0, 4], near["core"]))
        return copies

    def small_local():
        return [
            pltpu.make_async_copy(vec, vecs.at[c, p], vloc.at[0]),
            pltpu.make_async_copy(norm_in, norms.at[c], vloc.at[1]),
        ]

    def hop(s, spot, name, pick):
        ss, rs = (x1ss, x1rs) if pick == "x" else (y1ss, y1rs)
        b = block(s, spot, c)
        return remote(b, b, ss.at[s], rs.at[s], near[name])

    def first(s, name):
        return hop(s, p, name, name)

    def arrived(s, name):
        return hop(s, spots[1] if name == "x" else spots[2], name, name)

    def relay(s, name, spot=None):
        if name == "x":
            b = block(s, spots[2] if spot is None else spot, c, 0, half)
            return remote(b, b, x2ss.at[s], x2rs.at[s], near["x"])
        b = block(s, spots[1] if spot is None else spot, c, half, half)
        return remote(b, b, y2ss.at[s], y2rs.at[s], near["y"])

    def relayed(s, name):
        return relay(s, name, spots[3])

    def to_pair(s, r):
        b = block(s, spots[r], c)
        return remote(b, b, zs.at[s, r - 1], zr.at[s, r - 1], near["pair"])

    def to_core(s, r):
        b = block(s, spots[r], c)
        return remote(b, b, cs.at[s, r - 1], cr.at[s, r - 1], near["core"])

    def from_core(s, r):
        b = block(s, spots[r], 1 - c)
        return remote(b, b, cs.at[s, r - 1], cr.at[s, r - 1], near["core"])

    def sent_chunk(j):
        t, n = j // 2, lax.rem(j, 2)
        return 3 * t + (1 - n) * (1 + odd), n == 0

    def stage_a(j):
        s = sent_chunk(j)[0]
        for m in range(3):
            own = 3 * (j // 2) + m

            @pl.when((own // 12 != c) & (lax.rem(j, 2) == 0))
            def _():
                init_wait(lax.rem(own, 12))

            @pl.when((own // 12 == c) & (lax.rem(j, 2) == 0))
            def _():
                init_local(lax.rem(own, 12)).wait()

        first(s, "x").start()
        first(s, "y").start()

    def stage_b(j):
        s, shared = sent_chunk(j)
        arrived(s, "x").wait_recv()
        relay(s, "y").start()
        arrived(s, "y").wait_recv()
        relay(s, "x").start()
        for r in (1, 2):
            to_core(s, r).start()

        @pl.when(shared)
        def _():
            for r in (1, 2):
                to_pair(s, r).start()

    def stage_c(j):
        s, shared = sent_chunk(j)
        relayed(s, "x").wait_recv()
        relayed(s, "y").wait_recv()
        to_core(s, 3).start()

        @pl.when(shared)
        def _():
            to_pair(s, 3).start()

    def stage_d(t):
        s = 3 * t + 2 - odd
        for r in (1, 2, 3):
            to_pair(s, r).wait_recv()
            to_core(s, r).start()

    def stage_e(t):
        for j in range(3):
            for r in (1, 2, 3):
                from_core(3 * t + j, r).wait_recv()

    def stage_f(t):
        for n, s in enumerate((3 * t, 3 * t + 1 + odd)):
            first(s, "x").wait_send()
            first(s, "y").wait_send()
            relay(s, "x").wait_send()
            relay(s, "y").wait_send()
            for r in (1, 2, 3):
                if n:
                    to_pair(s, r).wait_send()
        for j in range(3):
            for r in (1, 2, 3):
                to_core(3 * t + j, r).wait_send()

    wide = 2 * rows

    def weights(l, number, place, sem):
        begin = pl.multiple_of(number * wide, wide)
        return pltpu.make_async_copy(full.at[l, pl.ds(begin, wide)], place, sem)

    def load_qkv(l, q):
        return [weights(l, 4 * n + q, wa.at[q, n], wasem.at[q, n]) for n in range(3)]

    def load(l, number, slot):
        return weights(l, number, wf.at[slot], wfsem.at[slot])

    def load_out(l, q):
        return load(l, 12 + q, q)

    def load_in(l, b, q, slot):
        return load(l, 16 + 4 * q + b, slot)

    def load_down(l, b, q, slot):
        return load(l, 32 + 4 * q + b, slot)

    def load_last(l, q):
        return weights(l, 32 + 4 * q + 3, wa.at[q, 0], wasem.at[q, 0])

    def save_attn(l, q):
        return pltpu.make_async_copy(sa.at[q], qkvo.at[l, q], sasem.at[q])

    def save_logs(l, q):
        return pltpu.make_async_copy(lb.at[q], logs.at[l, q], lbsem.at[q])

    def save_g(l, n):
        return pltpu.make_async_copy(gb.at[n], gd.at[l, n, 0], gbsem.at[n])

    def save_d(l, n, slot):
        return pltpu.make_async_copy(sd.at[slot], gd.at[l, n, 1], sdsem.at[slot])

    def keep(l, which):
        if which == 2:
            return pltpu.make_async_copy(hb, hbs.at[l], usem.at[2])
        if which == 3:
            return pltpu.make_async_copy(x, between, usem.at[3])
        return pltpu.make_async_copy(u, us.at[l, which], usem.at[which])

    def give(begin):
        @pl.when(c == 0)
        def _():
            copy = pltpu.make_async_copy(x, acts.at[0], as_.at[0])
            copy.start() if begin else copy.wait()

        @pl.when(c == 1)
        def _():
            copy = remote(x, acts.at[1], as_.at[0], ar.at[0], near["core"])
            copy.start() if begin else copy.wait_send()

    def last_sum():
        return pltpu.make_async_copy(acc, us.at[1, 1], usem.at[1])

    def each(count, body):
        def run(q, carry):
            body(q)
            return carry

        lax.fori_loop(0, count, run, 0)

    def attention_segment(l, q):
        for copy in load_qkv(l, q):
            copy.wait()
        project_block(x, wa.at[q], vecs[l, q], sa.at[q], lb.at[q], dim)
        save_attn(l, q).start()
        save_logs(l, q).start()

    def out_segment(l):
        @pl.when(l == 1)
        def _():
            keep(0, 1).wait()

        acc[...] = jnp.zeros_like(acc)

        def branch(q):
            load_out(l, q).wait()
            acc[...] += dot(sa[q, 3], wf[q])
            load_in(l, 1, q, q).start()

        each(4, branch)
        first_norm(x, norms.at[l], acc, u, hb)
        keep(l, 0).start()
        keep(l, 2).start()

    def up_segment(l, b, slot):
        for q in range(4):
            load_in(l, b, q, slot + q).wait()
        for q in range(4):
            g, slope = unit_values(hb, wf[slot + q], vecs[l, q, pl.ds(2 + b, 1)])
            gb[4 * q + b] = g
            sd[q] = slope
        for q in range(4):
            save_g(l, 4 * q + b).start()
            save_d(l, 4 * q + b, q).start()

    def up_saved(l, b):
        for q in range(4):
            save_d(l, 4 * q + b, q).wait()

    def down_segment(l, b, slot):
        for q in range(4):
            load_down(l, b, q, slot + q).wait()
        first_two = dot(gb[b], wf[slot]) + dot(gb[4 + b], wf[slot + 1])
        acc[...] += first_two + dot(gb[8 + b], wf[slot + 2]) + dot(gb[12 + b], wf[slot + 3])

    def end_segment(l):
        keep(l, 0).wait()
        keep(l, 2).wait()
        each(4, lambda q: save_attn(l, q).wait())
        each(4, lambda q: save_logs(l, q).wait())
        each(16, lambda n: save_g(l, n).wait())

        @pl.when(l == 0)
        def _():
            second_norm(norms.at[0], acc, u, x)
            keep(0, 1).start()
            give(True)
            keep(0, 3).start()

        @pl.when(l == 1)
        def _():
            last_sum().start()

    def small_there():
        for copy in small_local():
            copy.wait()
        for copy in small():
            copy.wait_send()
        for cc, spot in [(cc, spots[r]) for r in range(4) for cc in (c, 1 - c)][1:]:
            remote(vec, vecs.at[cc, spot], vs.at[0], vr.at[cc, spot], near["core"]).wait_recv()
        remote(norm_in, norms.at[1 - c], vs.at[7], vr.at[0, 4], near["core"]).wait_recv()

    def compute(m):
        l, part = m // 8, lax.rem(m, 8)

        def at(number, body):
            @pl.when(part == number)
            def _():
                body()

        def attention_first():
            for q in range(4):
                for copy in load_qkv(l, q):
                    copy.start()

            @pl.when(m == 0)
            def _():
                small_there()
                first_rows.wait()

        def attention_half(begin):
            each(2, lambda q: attention_segment(l, begin + q))

        def out_part():
            for q in range(4):
                load_out(l, q).start()
            for q in range(4):
                load_in(l, 0, q, 4 + q).start()
            out_segment(l)

        def up_part():
            for q in range(4):
                load_in(l, 2, q, q).start()
            for q in range(4):
                load_in(l, 3, q, 4 + q).start()
            up_saved(l, 1)
            up_segment(l, 2, 0)
            for q in range(4):
                load_down(l, 0, q, q).start()

        def turn_part():
            up_saved(l, 2)
            up_segment(l, 3, 4)
            down_segment(l, 0, 0)

        def down_part():
            for b in (1, 2):
                for q in range(4):
                    load_down(l, b, q, 4 * (b - 1) + q).start()
            for q in range(4):
                load_last(l, q).start()
            up_saved(l, 3)
            down_segment(l, 1, 0)
            down_segment(l, 2, 4)

        def end_part():
            for q in range(4):
                load_last(l, q).wait()
            first_two = dot(gb[3], wa[0, 0]) + dot(gb[7], wa[1, 0])
            acc[...] += first_two + dot(gb[11], wa[2, 0]) + dot(gb[15], wa[3, 0])
            end_segment(l)

        at(0, attention_first)

        @pl.when(part < 2)
        def _():
            attention_half(2 * part)

        at(2, out_part)

        @pl.when((part == 2) | (part == 3))
        def _():
            b = part - 2

            @pl.when(b == 1)
            def _():
                up_saved(l, 0)

            up_segment(l, b, 4 - 4 * b)

        at(4, up_part)
        at(5, turn_part)
        at(6, down_part)
        at(7, end_part)

    first_rows = pltpu.make_async_copy(tokens.at[c], x, usem.at[4])
    raw = [
        pltpu.make_async_copy(source, place, rawsem.at[n])
        for n, (source, place) in enumerate(
            ((qkv_in, w_qkv), (out_in, w_out), (up_in, w_up), (down_in, w_down))
        )
    ]
    for copy in raw:
        copy.start()
    first_rows.start()
    vec[...] = jnp.zeros_like(vec)
    vec[0:2] = high(qv[...])
    for b in range(4):
        vec[2 + b : 3 + b] = high(up_bias[:, 2 * rows * b : 2 * rows * (b + 1)])
    norm_in[...] = jnp.zeros_like(norm_in)
    norm_in[0:2], norm_in[2:4], norm_in[4:6] = biases[...], gains[...], shifts[...]
    barrier = pltpu.get_barrier_semaphore()
    for device in others + [near["pair"]]:
        pl.semaphore_signal(barrier, inc=1, device_id=device, device_id_type=MESH)
    raw[0].wait()
    for k in range(3):
        turn(k)
    pl.semaphore_wait(barrier, 8)
    for k in range(3):
        init_start(k)
    for copy in small_local() + small():
        copy.start()

    def step(count, carry):
        i = count - 1

        def run(stage, lag):
            @pl.when((i >= lag) & (i < 2 * TRIPLES + lag))
            def _():
                stage(i - lag)

        def run_late(stage, lag):
            @pl.when((i >= lag) & (i < 2 * TRIPLES + lag) & (lax.rem(i - lag, 2) == 0))
            def _():
                stage((i - lag) // 2)

        run(stage_a, -1)
        run(stage_b, 1)
        run(stage_c, 2)
        run_late(stage_e, 4)
        run_late(stage_f, 6)
        for t in range(3):

            @pl.when(i == 2 * t)
            def _():
                if t == 0:
                    for copy in raw[1:]:
                        copy.wait()
                for k in range(3 * t + 3, 3 * t + 6):
                    init_start(k)

        run(compute, 4)
        run_late(stage_d, 3)
        return carry

    lax.fori_loop(0, 2 * TRIPLES + 6, step, 0)

    for k in range(12):
        remote(chunk(k), init_place(k, c), ini_s.at[k], ini_r.at[k], near["core"]).wait_send()
    keep(0, 3).wait()
    give(False)
    last_sum().wait()

    @pl.when(c == 0)
    def _():
        remote(x, acts.at[1], as_.at[0], ar.at[0], near["core"]).wait_recv()


def gather_forward(dim, tokens, w_qkv, w_out, w_up, w_down, qv, up_bias, biases, gains, shifts):
    rows, width = w_out.shape
    seq = tokens.shape[1]
    bf, f32, dma, v = jnp.bfloat16, jnp.float32, pltpu.SemaphoreType.DMA, pltpu.VMEM
    hbm, vmem = pl.BlockSpec(memory_space=pl.ANY), pl.BlockSpec(memory_space=pltpu.VMEM)
    S = jax.ShapeDtypeStruct
    return pl.pallas_call(
        functools.partial(gather_forward_kernel, dim),
        out_shape=(
            S((2, 48 * rows, width), bf), S((2, 4, 8, rows), f32), S((2, 8, width), f32),
            S((2, 4, 4, seq, rows), bf), S((2, 4, seq, 128), f32), S((2, 16, 2, seq, rows), bf), S((2, 2, seq, width), f32),
            S((2, seq, width), bf), S((seq, width), bf), S((2, seq, width), bf),
        ),
        in_specs=[hbm] * 5 + [vmem] * 5,
        out_specs=[hbm, vmem, vmem] + [hbm] * 7,
        scratch_shapes=[
            v((7, rows, width), bf),
            v((seq, width), bf), v((seq, width), f32), v((seq, width), f32), v((seq, width), bf),
            v((4, 3, rows, width), bf), v((8, rows, width), bf), v((4, 4, seq, rows), bf), v((16, seq, rows), bf),
            v((4, seq, rows), bf), dma((4, 3)), dma((8,)), dma((4,)), dma((16,)), dma((4,)), dma((5,)),
            v((8, rows), f32), v((8, width), f32), v((4, seq, 128), f32), dma((4,)),
            v(w_qkv.shape, bf), v(w_out.shape, bf), v(w_up.shape, bf), v(w_down.shape, bf), dma((4,)),
        ] + [dma((12,))] * 3 + [dma((24,))] * 8 + [dma((24, 3))] * 4
        + [dma((8,)), dma((2, 5)), dma((2,)), dma((1,)), dma((1,))],
        compiler_params=pltpu.CompilerParams(collective_id=0, has_side_effects=True, vmem_limit_bytes=60 * 2**20),
    )(tokens, w_qkv, w_out, w_up, w_down, qv, up_bias, biases, gains, shifts)


def backward_reduce_kernel(
    dim, tokens, cots, full, norms, qkvo, logs, gd, us, hbs, between, out, grads, acts, totals,
    left, right, acc, g, u, wa, wf, da, df, dl, dlsem, trades,
    sendc, recvc, keep, x1s, x1r, y1s, y1r, part, base, x2s, x2r, y2s, y2r, mid,
    zk, zs1, zr1, zs2, zr2, zs3, zr3,
    wasem, wfsem, dasem, dfsem, gsem, osem4, bsem, gds, gdr, as_, ar, tss, trs,
    cs, cr, x1ss, x1rs, y1ss, y1rs, x2ss, x2rs, y2ss, y2rs, z1ss, z1rs, z2ss, z2rs, z3ss, z3rs, os, orr,
):
    c, p, d = lax.axis_index("section"), lax.axis_index("mp"), lax.axis_index("dp")
    near = neighbours()
    near["pair"] = (c, p, d + 1 - 2 * lax.rem(d, 2))
    near["far"] = (c, p, lax.rem(d + 2, 4))
    spots = places()
    is_end = (d == 0) | (d == 3)
    is_mid = jnp.logical_not(is_end)
    rows = sendc.shape[2]
    half = rows // 2
    wide = 2 * rows

    def core_copy(s):
        a, b = lax.rem(s, 2), lax.rem(s, 4)
        return remote(sendc.at[a], recvc.at[b], cs.at[a], cr.at[b], near["core"])

    def link_copy(s, src, dst, ss, rs, name):
        a, b = lax.rem(s, 2), lax.rem(s, 4)
        return remote(src.at[a], dst.at[b], ss.at[a], rs.at[b], near[name])

    def first_copy(s, n, src, dst, ss, rs, name):
        a, b = lax.rem(s, 2), lax.rem(s, 4)
        return remote(src.at[a, n], dst.at[b, n], ss.at[a, n], rs.at[b, n], near[name])

    x1 = lambda s, n: first_copy(s, n, x1s, x1r, x1ss, x1rs, "x")
    y1 = lambda s, n: first_copy(s, n, y1s, y1r, y1ss, y1rs, "y")
    x2 = lambda s: link_copy(s, x2s, x2r, x2ss, x2rs, "x")
    y2 = lambda s: link_copy(s, y2s, y2r, y2ss, y2rs, "y")
    z1 = lambda s, n: first_copy(s, n, zs1, zr1, z1ss, z1rs, "inner")
    z2 = lambda s, n: first_copy(s, n, zs2, zr2, z2ss, z2rs, "across")

    def z3(s, n):
        b = lax.rem(s, 6)
        return remote(zs3.at[b, n], zr3.at[b, n], z3ss.at[b, n], z3rs.at[b, n], near["outer"])

    def stage0(s):
        k, slot = lax.rem(s, 12), lax.rem(s, 2)
        stride = jnp.where(k < 8, 4, 1)
        first = jnp.where(k < 4, k, jnp.where(k < 8, 12 + k, jnp.where(k == 8, 32, 36 + 4 * (k - 9))))
        kind = jnp.where(k < 4, 0, jnp.where(k < 8, 1, jnp.where(k == 8, 2, 3)))
        for r in range(4):
            whole = dot_tn(left[first + stride * spots[r]], right[kind])
            keep[slot, r] = jnp.where(c == 0, whole[:rows], whole[rows:])
            sendc[slot, r] = low(jnp.where(c == 0, whole[rows:], whole[:rows]))
        core_copy(s).start()

    def stage1(s):
        a, b = lax.rem(s, 2), lax.rem(s, 4)
        core_copy(s).wait()
        far = keep[a, 3] + high(recvc[b, 3])
        x1s[a, 0] = low(far[:half])
        y1s[a, 0] = low(far[half:])
        x1(s, 0).start()
        y1(s, 0).start()
        by_x = keep[a, 1] + high(recvc[b, 1])
        x1s[a, 1] = low(by_x[:half])
        part[a, 0] = by_x[half:]
        by_y = keep[a, 2] + high(recvc[b, 2])
        y1s[a, 1] = low(by_y[half:])
        part[a, 1] = by_y[:half]
        x1(s, 1).start()
        y1(s, 1).start()
        base[a] = keep[a, 0] + high(recvc[b, 0])

    def stage2(s):
        a, b = lax.rem(s, 2), lax.rem(s, 4)
        x1(s, 0).wait()
        y2s[a] = low(part[a, 1] + high(x1r[b, 0]))
        y2(s).start()
        y1(s, 0).wait()
        x2s[a] = low(part[a, 0] + high(y1r[b, 0]))
        x2(s).start()
        x1(s, 1).wait()
        y1(s, 1).wait()
        own = base[a]
        mid[a, 0] = own[:half] + high(x1r[b, 1])
        mid[a, 1] = own[half:] + high(y1r[b, 1])

    def stage3(s):
        a, b = lax.rem(s, 2), lax.rem(s, 4)
        for n, copy, got in ((0, y2, y2r), (1, x2, x2r)):
            copy(s).wait()
            total = mid[a, n] + high(got[b])

            @pl.when(is_end)
            def _():
                zs1[a, n] = low(total)
                z1(s, n).start()

            @pl.when(is_mid)
            def _():
                zk[a, n] = total

    def stage4(s):
        a, b = lax.rem(s, 2), lax.rem(s, 4)
        for n in range(2):

            @pl.when(is_end)
            def _():
                z1(s, n).wait_send()

            @pl.when(is_mid)
            def _():
                z1(s, n).wait_recv()
                zs2[a, n] = low(zk[a, n] + high(zr1[b, n]))
                z2(s, n).start()

    def stage5(s):
        a, b, to = lax.rem(s, 2), lax.rem(s, 4), lax.rem(s, 6)

        @pl.when(is_mid)
        def _():
            for n in range(2):
                z2(s, n).wait()
                zs3[to, n] = low(high(zs2[a, n]) + high(zr2[b, n]))
                z3(s, n).start()

    def stage6(s, begin):
        layer, k, b = 1 - s // 12, lax.rem(s, 12), lax.rem(s, 6)

        def finish(source):
            @pl.when(layer == c)
            def _():
                copy = pltpu.make_async_copy(source.at[b], out.at[k, c], os.at[b])
                copy.start() if begin else copy.wait()

            @pl.when(layer != c)
            def _():
                copy = remote(source.at[b], out.at[k, c], os.at[b], orr.at[k], near["core"])
                copy.start() if begin else copy.wait_send()

        @pl.when(is_end)
        def _():
            if begin:
                for n in range(2):
                    z3(s, n).wait_recv()
            finish(zr3)

        @pl.when(is_mid)
        def _():
            if begin:
                for n in range(2):
                    z3(s, n).wait_send()
            finish(zs3)

    def load_g(l, n):
        return pltpu.make_async_copy(gd.at[l, n, 0], left.at[n], gsem.at[n])

    def load_o(l, n):
        return pltpu.make_async_copy(qkvo.at[l, n, 3], left.at[32 + n], osem4.at[n])

    def load_h(l):
        return pltpu.make_async_copy(hbs.at[l], right.at[1], bsem.at[0])

    def load_x(source):
        return pltpu.make_async_copy(source, right.at[3], bsem.at[1])

    def load_u(l, which):
        return pltpu.make_async_copy(us.at[l, which], u, bsem.at[2])

    def ffn(l, n, slot):
        return weight_copies(full, l, 1, lax.rem(n, 4), n // 4, wf.at[slot], wfsem.at[slot], wide) + [
            pltpu.make_async_copy(gd.at[l, 4 * lax.rem(n, 4) + n // 4, 1], df.at[slot], dfsem.at[slot])
        ]

    def attn(l, q, slot):
        return weight_copies(full, l, 0, q, 0, wa.at[slot], wasem.at[slot], wide) + [
            pltpu.make_async_copy(qkvo.at[l, q], da.at[slot], dasem.at[slot]),
            pltpu.make_async_copy(logs.at[l, q], dl.at[slot], dlsem.at[slot]),
        ]

    def store_dx(l, begin):
        @pl.when(l == c)
        def _():
            copy = pltpu.make_async_copy(g, grads.at[c], gds.at[0])
            copy.start() if begin else copy.wait()

        @pl.when(l != c)
        def _():
            copy = remote(g, grads.at[c], gds.at[0], gdr.at[0], near["core"])
            copy.start() if begin else copy.wait_send()

    def give(begin):
        @pl.when(c == 1)
        def _():
            copy = pltpu.make_async_copy(g, acts.at[1], as_.at[0])
            copy.start() if begin else copy.wait()

        @pl.when(c == 0)
        def _():
            copy = remote(g, acts.at[0], as_.at[0], ar.at[0], near["core"])
            copy.start() if begin else copy.wait_send()

    def output():
        load_u(1, 1).wait()
        store_dx(0, False)

        def run(r):
            g[r] = low(standard(u[r])[0] * norms[1, 3:4] + norms[1, 5:6])

        by_rows(u.shape[0], 64, run)
        give(True)

    def ahead(l):
        load_u(l, 1).start()
        for copy in ffn(l, 0, 0) + attn(l, 0, 0):
            copy.start()

    def operands(l):
        def run(n, carry):
            load_g(l, n).start()
            return carry

        lax.fori_loop(0, 16, run, 0)
        for n in range(4):
            load_o(l, n).start()
        load_h(l).start()

    def operands_there(l):
        def run(n, carry):
            load_g(l, n).wait()
            return carry

        lax.fori_loop(0, 16, run, 0)
        for n in range(4):
            load_o(l, n).wait()
        load_h(l).wait()

    def top_segment(l):
        load_u(l, 1).wait()
        norm_back(u, g, norms[l, 3:4], totals.at[l], (1, 3, 5), right.at[0], acc)
        load_u(l, 0).start()

        @pl.when(l == 1)
        def _():
            operands_there(1)

    def ffn_segment(l, b):
        def run(q, carry):
            n = 4 * b + q
            slot = lax.rem(n, 2)
            for copy in ffn(l, n, slot):
                copy.wait()

            @pl.when(n < 15)
            def _():
                for copy in ffn(l, n + 1, 1 - slot):
                    copy.start()

            row = ffn_back_block(right.at[0], wf.at[slot], df[slot], acc, left.at[16 + 4 * q + b])
            totals[l, pl.ds(10 + b, 1), pl.ds(pl.multiple_of(q * wide, wide), wide)] = row
            return carry

        lax.fori_loop(0, 4, run, 0)

    def middle_segment(l):
        load_u(l, 0).wait()
        norm_back(u, acc, norms[l, 2:3], totals.at[l], (0, 2, 4), right.at[2], acc)

    def attention_segment(l, q):
        slot = lax.rem(q, 2)
        for copy in attn(l, q, slot):
            copy.wait()

        @pl.when(q < 3)
        def _():
            for copy in attn(l, q + 1, 1 - slot):
                copy.start()

        dq, dk, dv = left.at[36 + q], left.at[40 + q], left.at[44 + q]
        attention_back_block(right.at[2], wa.at[slot], da.at[slot], dl[slot], dq, dk, dv, acc, dim)
        cols = pl.ds(pl.multiple_of(q * wide, wide), wide)
        totals[l, 8:9, cols] = jnp.sum(high(dq[...]), axis=0, keepdims=True)
        totals[l, 9:10, cols] = jnp.sum(high(dv[...]), axis=0, keepdims=True)

    def end_segment(l):
        by_rows(acc.shape[0], 64, lambda r: g.__setitem__(r, low(acc[r])))
        store_dx(l, True)
        if l == 1:
            ahead(0)

    def segment(i):
        l = jnp.where(i < 8, 1, 0)
        j = jnp.where(i < 8, i, i - 9)
        q = jnp.where(i < 8, i - 4, i - 14)

        @pl.when(i == 8)
        def _():
            end_segment(1)
            operands(0)
            store_dx(1, False)

        @pl.when(i == 7)
        def _():
            load_x(between).wait()

        @pl.when(j == -1)
        def _():
            top_segment(l)

        @pl.when((j >= 0) & (j < 4))
        def _():
            ffn_segment(l, j)

        @pl.when((i == 3) | (i == 13))
        def _():
            middle_segment(l)

        @pl.when((q >= 0) & (q < 4))
        def _():
            attention_segment(l, q)

        @pl.when(i == 18)
        def _():
            end_segment(0)

        @pl.when(i == 10)
        def _():
            operands_there(0)

        @pl.when(i == 12)
        def _():
            load_x(tokens.at[c]).start()

        @pl.when(i == 16)
        def _():
            load_x(tokens.at[c]).wait()

    def trade(k):
        return remote(totals, trades.at[k], tss.at[k], trs.at[k], near[("core", "x", "y", "pair", "far")[k]])

    first_rows = pltpu.make_async_copy(cots.at[c], g, bsem.at[3])
    first_rows.start()
    ahead(1)
    operands(1)
    load_x(between).start()
    totals[...] = jnp.zeros_like(totals)
    barrier = pltpu.get_barrier_semaphore()

    def signal(device):
        pl.semaphore_signal(barrier, inc=1, device_id=device, device_id_type=MESH)

    for name in ("core", "x", "y", "pair", "far"):
        signal(near[name])

    @pl.when(is_end)
    def _():
        pl.semaphore_wait(barrier, 5)

    @pl.when(is_mid)
    def _():
        signal(near["across"])
        pl.semaphore_wait(barrier, 6)

    first_rows.wait()

    def step(count, carry):
        i = count - 1

        def run(stage, lag, *extra):
            @pl.when((i >= lag) & (i < CHUNKS + lag))
            def _():
                stage(i - lag, *extra)

        for lag, stage in enumerate((stage1, stage2, stage3, stage4, stage5)):
            run(stage, lag + 1)
        run(stage6, 6, True)
        run(stage6, 7, False)
        for k in range(6):

            @pl.when(i == 20 + k)
            def _():
                if k:
                    trade(k - 1).wait()
                    totals[...] += trades[k - 1]
                if k < 5:
                    trade(k).start()

        run(stage0, 0)

        @pl.when((i < 20) & (i != 0))
        def _():
            segment(jnp.where(i < 0, i, i - 1))

        @pl.when(i == 20)
        def _():
            load_u(1, 1).start()

        @pl.when(i == 22)
        def _():
            output()


        return carry

    lax.fori_loop(0, CHUNKS + 9, step, 0)
    give(False)

    @pl.when(c == 1)
    def _():
        remote(g, acts.at[0], as_.at[0], ar.at[0], near["core"]).wait_recv()

    remote(g, grads.at[1 - c], gds.at[0], gdr.at[0], near["core"]).wait_recv()
    for k in range(12):
        remote(zs3.at[0], out.at[k, 1 - c], os.at[0], orr.at[k], near["core"]).wait_recv()


def backward_reduce(dim, tokens, cots, full, norms, saved):
    seq, width = tokens.shape[1:]
    wide = width // 4
    block, half = wide // 2, wide // 4
    bf, f32, dma, v = jnp.bfloat16, jnp.float32, pltpu.SemaphoreType.DMA, pltpu.VMEM
    hbm, vmem = pl.BlockSpec(memory_space=pl.ANY), pl.BlockSpec(memory_space=pltpu.VMEM)
    S = jax.ShapeDtypeStruct
    return pl.pallas_call(
        functools.partial(backward_reduce_kernel, dim),
        out_shape=(S((12, 2, 2, half, width), bf), S((2, seq, width), bf), S((2, seq, width), bf),
                   S((2, 16, width), f32)),
        in_specs=[hbm, hbm, hbm, vmem] + [hbm] * 6,
        out_specs=[hbm, hbm, hbm, vmem],
        scratch_shapes=[
            v((48, seq, wide), bf), v((4, seq, width), bf), v((seq, width), f32), v((seq, width), bf),
            v((seq, width), f32),
            v((2, 4, wide, width), bf), v((2, 2, wide, width), bf), v((2, 4, seq, wide), bf), v((2, seq, wide), bf),
            v((2, seq, 128), f32), dma((2,)), v((5, 2, 16, width), f32),
            v((2, 4, block, width), bf), v((4, 4, block, width), bf), v((2, 4, block, width), f32),
            v((2, 2, half, width), bf), v((4, 2, half, width), bf), v((2, 2, half, width), bf), v((4, 2, half, width), bf),
            v((2, 2, half, width), f32), v((2, block, width), f32),
            v((2, half, width), bf), v((4, half, width), bf), v((2, half, width), bf), v((4, half, width), bf),
            v((2, 2, half, width), f32),
            v((2, 2, half, width), f32), v((2, 2, half, width), bf), v((4, 2, half, width), bf),
            v((2, 2, half, width), bf), v((4, 2, half, width), bf), v((6, 2, half, width), bf), v((6, 2, half, width), bf),
            dma((2, 4)), dma((2, 2)), dma((2,)), dma((2,)), dma((16,)), dma((4,)), dma((4,)), dma((1,)), dma((1,)), dma((1,)), dma((1,)),
            dma((5,)), dma((5,)),
        ] + [dma((n,)) for n in (2, 4)] + [dma((n, 2)) for n in (2, 4) * 2] + [dma((n,)) for n in (2, 4) * 2]
        + [dma((n, 2)) for n in (2, 4, 2, 4, 6, 6)] + [dma((6,)), dma((12,))],
        compiler_params=pltpu.CompilerParams(collective_id=1, has_side_effects=True, vmem_limit_bytes=63 * 2**20),
    )(tokens, cots, full, norms, *saved)


def finish_kernel(parts, acts_zero, acts_one, grads_in, totals, acts, grads, g_qkv, g_out, g_up, g_down, g_qv, g_bias,
                  g_biases, g_gains, g_shifts, pb, ab, gb, qb, ob, ub, db, psem, asem, osem):
    def load(k):
        return pltpu.make_async_copy(parts.at[k], pb.at[k], psem.at[k])

    c, p, d = lax.axis_index("section"), lax.axis_index("mp"), lax.axis_index("dp")
    order = (4, 5, 6, 7, 9, 10, 11, 0, 1, 2, 3, 8)
    for k in order:
        load(k).start()

    @pl.when(c == 0)
    def _():
        pltpu.make_async_copy(acts_zero, ab, asem.at[0]).start()

    @pl.when(c == 1)
    def _():
        pltpu.make_async_copy(acts_one, ab, asem.at[0]).start()

    pltpu.make_async_copy(grads_in, gb, asem.at[1]).start()
    others = [(acts_zero, ab, acts, 0), (grads_in, gb, grads, 1)]
    stores = []
    rows = pb.shape[1]
    mine = totals.at[c]
    own = mine[8:16, pl.ds(pl.multiple_of(p * rows, rows), rows)]
    g_qv[...] = own[0:2]
    for b in range(4):
        g_bias[:, b * rows : (b + 1) * rows] = own[2 + b : 3 + b]
    piece = g_gains.shape[1]
    both = mine[0:8, pl.ds(pl.multiple_of(p * rows + d // 2 * 2 * piece, 2 * piece), 2 * piece)]
    both = jnp.where(lax.rem(d, 2) == 0, both[:, :piece], both[:, piece:])
    g_biases[...], g_gains[...], g_shifts[...] = both[0:2], both[2:4], both[4:6]

    def store(source, place):
        copy = pltpu.make_async_copy(source, place, osem.at[len(stores)])
        copy.start()
        stores.append(copy)

    for k in order:
        load(k).wait()
        if k < 4:
            span = pl.ds(k * rows, rows)
            db[span] = high(pb[k])
            store(db.at[span], g_down.at[span])
        elif k < 8:
            ub[:, pl.ds((k - 4) * rows, rows)] = high(pb[k].T)
            if k == 7:
                store(ub, g_up)
        elif k == 8:
            ob[...] = high(pb[k])
            store(ob, g_out)
        else:
            qb[k - 9] = high(pb[k].T)
            store(qb.at[k - 9], g_qkv.at[k - 9])
        if k == 7:
            for source, buffer, place, n in others:
                pltpu.make_async_copy(source, buffer, asem.at[n]).wait()
                store(buffer, place)
    for copy in stores:
        copy.wait()


def finish(parts, acts, acts_one, grads, totals):
    count, rows, width = parts.shape
    bf, f32, dma, v = jnp.bfloat16, jnp.float32, pltpu.SemaphoreType.DMA, pltpu.VMEM
    S = jax.ShapeDtypeStruct
    shapes = [(3, width, rows), (rows, width), (width, width), (width, width)]
    piece = width // (lax.axis_size("mp") * lax.axis_size("dp"))
    hbm, vmem = pl.BlockSpec(memory_space=pl.ANY), pl.BlockSpec(memory_space=pltpu.VMEM)
    vectors = [(2, rows), (1, 4 * rows)] + [(2, piece)] * 3
    return pl.pallas_call(
        finish_kernel,
        out_shape=[S(acts.shape, bf), S(grads.shape, bf)] + [S(shape, f32) for shape in shapes + vectors],
        in_specs=[hbm] * 4 + [vmem],
        out_specs=[hbm] * 6 + [vmem] * 5,
        scratch_shapes=[v(parts.shape, bf), v(acts.shape, bf), v(grads.shape, bf)] + [v(shape, f32) for shape in shapes]
        + [dma((12,)), dma((2,)), dma((11,))],
        compiler_params=pltpu.CompilerParams(vmem_limit_bytes=63 * 2**20),
    )(parts, acts, acts_one, grads, totals)


def by_page(
    token_in,
    cotangent,
    w_qkv,
    qv_bias,
    w_attn_out,
    w_ffn_in,
    ffn_in_bias,
    w_ffn_out,
    out_biases,
    norm_gains,
    norm_shifts,
):
    width = token_in.shape[2]
    full, vecs, norms, *saved, acts = gather_forward(
        HEAD_DIM,
        token_in,
        w_qkv[0],
        w_attn_out[0],
        w_ffn_in[0],
        w_ffn_out[0],
        qv_bias[0],
        ffn_in_bias,
        out_biases[0],
        norm_gains[0],
        norm_shifts[0],
    )
    parts, grads, acts_one, totals = backward_reduce(HEAD_DIM, token_in, cotangent, full, norms, saved)
    results = finish(parts.reshape(12, width // 4, width), acts, acts_one, grads, totals)
    acts, grads, grad_qkv, grad_out, grad_up, grad_down, grad_qv, grad_bias, *rows = results
    return (
        acts[None],
        grads[None],
        grad_qkv[None],
        grad_qv[None],
        grad_out[None],
        grad_up[None],
        grad_bias,
        grad_down[None],
    ) + tuple(row[None] for row in rows)


def on_device(*args):
    token_in, w_qkv, ffn_in = args[0], args[2], args[5]
    fits = (
        lax.axis_size("section") == 2
        and lax.axis_size("mp") == 4
        and lax.axis_size("dp") == 4
        and token_in.shape == (2, SEQ, 1024)
        and w_qkv.shape[3] == 256
        and ffn_in.shape[2] == 1024
    )
    return by_page(*args) if fits else pipelined(*args)


def solution(mesh):
    return jax.shard_map(
        on_device,
        mesh=mesh,
        in_specs=(
            P(None, ("dp", "mp"), None),
            P(None, ("dp", "mp"), None),
            P("section", None, None, "mp"),
            P("section", None, "mp"),
            P("section", "mp", None),
            P("section", None, "mp"),
            P("section", "mp"),
            P("section", "mp", None),
            P("section", None, None),
            P("section", None, None),
            P("section", None, None),
        ),
        out_specs=(
            P("section", None, ("dp", "mp"), None),
            P("section", None, ("dp", "mp"), None),
            P("section", None, None, "mp"),
            P("section", None, "mp"),
            P("section", "mp", None),
            P("section", None, "mp"),
            P("section", "mp"),
            P("section", "mp", None),
            P("section", None, ("mp", "dp")),
            P("section", None, ("mp", "dp")),
            P("section", None, ("mp", "dp")),
        ),
        check_vma=False,
    )
```

```python
import functools
from functools import partial
import math

import jax
import jax.numpy as jnp
from jax import lax
from jax.experimental import pallas as pl
from jax.experimental.pallas import tpu as pltpu
from jax.sharding import PartitionSpec as P

HEAD_DIM = 64
SEQ = 512


def from_behind(value, axis, by):
    devices = lax.axis_size(axis)
    pairs = [(i, i + by) for i in range(devices) if 0 <= i + by < devices]
    return lax.ppermute(value, axis, pairs)


def norm_rows(values, gain_row, shift_row):
    average = jnp.mean(values, axis=-1, keepdims=True)
    centered = values - average
    variance = jnp.mean(centered * centered, axis=-1, keepdims=True)
    return centered * lax.rsqrt(variance + 1e-05) * gain_row + shift_row


def exact_gelu(values):
    return jax.nn.gelu(values, approximate=False)


def layer_forward(params, token_rows):
    (
        w_qkv,
        qv_bias,
        w_attn_out,
        w_ffn_in,
        ffn_in_bias,
        w_ffn_out,
        out_biases,
        norm_gains,
        norm_shifts,
    ) = params
    gathered = lax.all_gather(token_rows, "mp", axis=0, tiled=True)
    rows_all = gathered.shape[0]
    local_width = w_qkv.shape[2]
    local_heads = local_width // HEAD_DIM
    page_count = rows_all // SEQ
    scale_factor = 1.0 / math.sqrt(HEAD_DIM)
    bias_full = jnp.stack([qv_bias[0], jnp.zeros_like(qv_bias[0]), qv_bias[1]]).astype(jnp.float32)
    projected = (
        jnp.einsum("rd,cde->cre", gathered, w_qkv, preferred_element_type=jnp.float32)
        + bias_full[:, None, :]
    )
    heads_view = projected.astype(jnp.bfloat16).reshape(3, page_count, SEQ, local_heads, HEAD_DIM)
    scores = (
        jnp.einsum(
            "pqhe,pkhe->phqk", heads_view[0], heads_view[1], preferred_element_type=jnp.float32
        )
        * scale_factor
    )
    top_score = jnp.max(scores, axis=-1, keepdims=True)
    exponent = jnp.exp(scores - top_score)
    weights_soft = exponent / jnp.sum(exponent, axis=-1, keepdims=True)
    weights_low = weights_soft.astype(jnp.bfloat16)
    attended = jnp.einsum(
        "phqk,pkhe->pqhe", weights_low, heads_view[2], preferred_element_type=jnp.float32
    )
    attended = attended.reshape(rows_all, local_width).astype(jnp.bfloat16)
    attn_part = jnp.dot(attended, w_attn_out, preferred_element_type=jnp.float32)
    attn_rows = lax.psum_scatter(
        attn_part.astype(jnp.bfloat16), "mp", scatter_dimension=0, tiled=True
    ).astype(jnp.float32)
    residual_one = attn_rows + out_biases[0] + token_rows.astype(jnp.float32)
    first = norm_rows(residual_one, norm_gains[0], norm_shifts[0])
    first_all = lax.all_gather(first.astype(jnp.bfloat16), "mp", axis=0, tiled=True)
    pre_act = jnp.dot(first_all, w_ffn_in, preferred_element_type=jnp.float32) + ffn_in_bias.astype(
        jnp.float32
    )
    activated = exact_gelu(pre_act).astype(jnp.bfloat16)
    ffn_part = jnp.dot(activated, w_ffn_out, preferred_element_type=jnp.float32)
    ffn_rows = lax.psum_scatter(
        ffn_part.astype(jnp.bfloat16), "mp", scatter_dimension=0, tiled=True
    ).astype(jnp.float32)
    residual_two = ffn_rows + out_biases[1] + first
    result = norm_rows(residual_two, norm_gains[1], norm_shifts[1])
    kept_values = (
        gathered,
        heads_view,
        weights_soft,
        attended,
        residual_one,
        first_all,
        pre_act,
        activated,
        residual_two,
    )
    return (result, kept_values)


def layer_backward(params, kept_values, grad_out):
    (
        w_qkv,
        qv_bias,
        w_attn_out,
        w_ffn_in,
        ffn_in_bias,
        w_ffn_out,
        out_biases,
        norm_gains,
        norm_shifts,
    ) = params
    (
        gathered,
        heads_view,
        weights_soft,
        attended,
        residual_one,
        first_all,
        pre_act,
        activated,
        residual_two,
    ) = kept_values
    rows_all = gathered.shape[0]
    local_width = w_qkv.shape[2]
    local_heads = local_width // HEAD_DIM
    page_count = rows_all // SEQ
    scale_factor = 1.0 / math.sqrt(HEAD_DIM)
    unused_two, norm_two_back = jax.vjp(norm_rows, residual_two, norm_gains[1], norm_shifts[1])
    grad_res_two, grad_gain_two, grad_shift_two = norm_two_back(grad_out)
    grad_bias_two = jnp.sum(grad_res_two, axis=0)
    ffn_grad_all = lax.all_gather(grad_res_two.astype(jnp.bfloat16), "mp", axis=0, tiled=True)
    grad_w_ffn_out = jnp.einsum(
        "rf,rd->fd", activated, ffn_grad_all, preferred_element_type=jnp.float32
    )
    grad_act = jnp.einsum("rd,fd->rf", ffn_grad_all, w_ffn_out, preferred_element_type=jnp.float32)
    unused_gelu, gelu_back = jax.vjp(exact_gelu, pre_act)
    grad_pre = gelu_back(grad_act)[0].astype(jnp.bfloat16)
    grad_ffn_in_bias = jnp.sum(grad_pre.astype(jnp.float32), axis=0)
    grad_w_ffn_in = jnp.einsum("rd,rf->df", first_all, grad_pre, preferred_element_type=jnp.float32)
    first_part = jnp.einsum("rf,df->rd", grad_pre, w_ffn_in, preferred_element_type=jnp.float32)
    first_grad_rows = lax.psum_scatter(
        first_part.astype(jnp.bfloat16), "mp", scatter_dimension=0, tiled=True
    ).astype(jnp.float32)
    grad_first = first_grad_rows + grad_res_two
    unused_one, norm_one_back = jax.vjp(norm_rows, residual_one, norm_gains[0], norm_shifts[0])
    grad_res_one, grad_gain_one, grad_shift_one = norm_one_back(grad_first)
    grad_bias_one = jnp.sum(grad_res_one, axis=0)
    attn_grad_all = lax.all_gather(grad_res_one.astype(jnp.bfloat16), "mp", axis=0, tiled=True)
    grad_w_attn_out = jnp.einsum(
        "rk,rd->kd", attended, attn_grad_all, preferred_element_type=jnp.float32
    )
    grad_attended = jnp.einsum(
        "rd,kd->rk", attn_grad_all, w_attn_out, preferred_element_type=jnp.float32
    )
    grad_attended = grad_attended.astype(jnp.bfloat16).reshape(
        page_count, SEQ, local_heads, HEAD_DIM
    )
    weights_low = weights_soft.astype(jnp.bfloat16)
    grad_weights = jnp.einsum(
        "pqhe,pkhe->phqk", grad_attended, heads_view[2], preferred_element_type=jnp.float32
    )
    grad_values = jnp.einsum(
        "phqk,pqhe->pkhe", weights_low, grad_attended, preferred_element_type=jnp.float32
    )
    inner_total = jnp.sum(weights_soft * grad_weights, axis=-1, keepdims=True)
    grad_scores = (weights_soft * (grad_weights - inner_total)).astype(jnp.bfloat16)
    grad_queries = (
        jnp.einsum(
            "phqk,pkhe->pqhe", grad_scores, heads_view[1], preferred_element_type=jnp.float32
        )
        * scale_factor
    )
    grad_keys = (
        jnp.einsum(
            "phqk,pqhe->pkhe", grad_scores, heads_view[0], preferred_element_type=jnp.float32
        )
        * scale_factor
    )
    grad_proj = (
        jnp.stack([grad_queries, grad_keys, grad_values])
        .reshape(3, rows_all, local_width)
        .astype(jnp.bfloat16)
    )
    proj_sums = jnp.sum(grad_proj.astype(jnp.float32), axis=1)
    grad_qv_bias = jnp.stack([proj_sums[0], proj_sums[2]])
    grad_w_qkv = jnp.einsum("rd,cre->cde", gathered, grad_proj, preferred_element_type=jnp.float32)
    input_part = jnp.einsum("cre,cde->rd", grad_proj, w_qkv, preferred_element_type=jnp.float32)
    input_grad_rows = lax.psum_scatter(
        input_part.astype(jnp.bfloat16), "mp", scatter_dimension=0, tiled=True
    ).astype(jnp.float32)
    grad_in = input_grad_rows + grad_res_one
    matrix_grads = (
        grad_w_qkv,
        grad_qv_bias,
        grad_w_attn_out,
        grad_w_ffn_in,
        grad_ffn_in_bias,
        grad_w_ffn_out,
    )
    vector_grads = (
        jnp.stack([grad_bias_one, grad_bias_two]),
        jnp.stack([grad_gain_one, grad_gain_two]),
        jnp.stack([grad_shift_one, grad_shift_two]),
    )
    return (grad_in, matrix_grads, vector_grads)


def pipelined(
    token_in,
    cotangent,
    w_qkv,
    qv_bias,
    w_attn_out,
    w_ffn_in,
    ffn_in_bias,
    w_ffn_out,
    out_biases,
    norm_gains,
    norm_shifts,
):
    params = (
        w_qkv[0],
        qv_bias[0],
        w_attn_out[0],
        w_ffn_in[0],
        ffn_in_bias[0],
        w_ffn_out[0],
        out_biases[0],
        norm_gains[0],
        norm_shifts[0],
    )
    micro_count = token_in.shape[0]
    section_index = lax.axis_index("section")
    is_first = section_index == 0
    zero_rows = jnp.zeros(token_in.shape[1:], jnp.bfloat16)
    run_forward = partial(layer_forward, params)
    run_backward = partial(layer_backward, params)

    def forward_step(step_index, carry):
        received, saved, stored = carry
        own_micro = step_index - section_index
        is_valid = (own_micro >= 0) & (own_micro < micro_count)
        slot_index = jnp.clip(own_micro, 0, micro_count - 1)
        first_rows = lax.dynamic_index_in_dim(
            token_in, jnp.minimum(step_index, micro_count - 1).astype(jnp.int32), 0, keepdims=False
        )
        layer_in = jnp.where(is_first, first_rows, received)
        result, unused_kept = run_forward(layer_in)
        result_low = result.astype(jnp.bfloat16)
        old_saved = lax.dynamic_index_in_dim(saved, slot_index, 0, keepdims=False)
        saved = lax.dynamic_update_index_in_dim(
            saved, jnp.where(is_valid, layer_in, old_saved), slot_index, 0
        )
        old_stored = lax.dynamic_index_in_dim(stored, slot_index, 0, keepdims=False)
        stored = lax.dynamic_update_index_in_dim(
            stored, jnp.where(is_valid, result_low, old_stored), slot_index, 0
        )
        received = from_behind(result_low, "section", 1)
        return (received, saved, stored)

    start_carry = (zero_rows, jnp.zeros_like(token_in), jnp.zeros_like(token_in))
    unused_received, saved, stored = lax.fori_loop(0, micro_count + 1, forward_step, start_carry)
    matrix_zero = tuple((jnp.zeros(entry.shape, jnp.float32) for entry in params[:6]))
    vector_zero = (
        jnp.zeros(out_biases.shape[1:], jnp.float32),
        jnp.zeros(norm_gains.shape[1:], jnp.float32),
        jnp.zeros(norm_shifts.shape[1:], jnp.float32),
    )

    def backward_step(step_index, carry):
        received_grad, grad_store, matrix_sums, vector_sums = carry
        own_micro = step_index - (1 - section_index)
        is_valid = (own_micro >= 0) & (own_micro < micro_count)
        slot_index = jnp.clip(own_micro, 0, micro_count - 1)
        layer_in = lax.dynamic_index_in_dim(saved, slot_index, 0, keepdims=False)
        from_last = lax.dynamic_index_in_dim(cotangent, slot_index, 0, keepdims=False)
        grad_out = jnp.where(is_first, received_grad, from_last).astype(jnp.float32)
        unused_result, kept_values = run_forward(layer_in)
        grad_in, matrix_grads, vector_grads = run_backward(kept_values, grad_out)
        matrix_grads = tuple((jnp.where(is_valid, entry, 0.0) for entry in matrix_grads))
        vector_grads = tuple((jnp.where(is_valid, entry, 0.0) for entry in vector_grads))
        grad_low = grad_in.astype(jnp.bfloat16)
        old_piece = lax.dynamic_index_in_dim(grad_store, slot_index, 0, keepdims=False)
        grad_store = lax.dynamic_update_index_in_dim(
            grad_store, jnp.where(is_valid, grad_low, old_piece), slot_index, 0
        )
        grad_one, grad_two, grad_three, grad_four, grad_five, grad_six = matrix_grads
        matrix_grads = (
            lax.psum(grad_one.astype(jnp.bfloat16), "dp").astype(jnp.float32),
            lax.psum(grad_two.astype(jnp.bfloat16), "dp").astype(jnp.float32),
            lax.psum(grad_three.astype(jnp.bfloat16), "dp").astype(jnp.float32),
            lax.psum(grad_four.astype(jnp.bfloat16), "dp").astype(jnp.float32),
            lax.psum(grad_five.astype(jnp.bfloat16), "dp").astype(jnp.float32),
            lax.psum(grad_six.astype(jnp.bfloat16), "dp").astype(jnp.float32),
        )
        matrix_sums = tuple((total + extra for total, extra in zip(matrix_sums, matrix_grads)))
        vector_sums = tuple((total + extra for total, extra in zip(vector_sums, vector_grads)))
        received_grad = from_behind(grad_low, "section", -1)
        return (received_grad, grad_store, matrix_sums, vector_sums)

    back_carry = (zero_rows, jnp.zeros_like(token_in), matrix_zero, vector_zero)
    unused_grad, grad_store, matrix_sums, vector_sums = lax.fori_loop(
        0, micro_count + 1, backward_step, back_carry
    )
    bias_total, gain_total, shift_total = vector_sums
    bias_part, gain_part, shift_part = (
        lax.psum_scatter(bias_total, ("mp", "dp"), scatter_dimension=1, tiled=True),
        lax.psum_scatter(gain_total, ("mp", "dp"), scatter_dimension=1, tiled=True),
        lax.psum_scatter(shift_total, ("mp", "dp"), scatter_dimension=1, tiled=True),
    )
    return (
        stored[None],
        grad_store[None],
        matrix_sums[0][None],
        matrix_sums[1][None],
        matrix_sums[2][None],
        matrix_sums[3][None],
        matrix_sums[4][None],
        matrix_sums[5][None],
        bias_part[None],
        gain_part[None],
        shift_part[None],
    )


MESH = pl.DeviceIdType.MESH
CHUNKS = 24
TRIPLES = 8
SCALE = 0.125


def low(value):
    return value.astype(jnp.bfloat16)


def high(value):
    return value.astype(jnp.float32)


def remote(src, dst, send, recv, device):
    return pltpu.make_async_remote_copy(
        src_ref=src, dst_ref=dst, send_sem=send, recv_sem=recv, device_id=device, device_id_type=MESH
    )


def neighbours():
    c, p, d = lax.axis_index("section"), lax.axis_index("mp"), lax.axis_index("dp")
    return {
        "core": (1 - c, p, d),
        "x": (c, p + 1 - 2 * lax.rem(p, 2), d),
        "y": (c, lax.rem(p + 2, 4), d),
        "across": (c, p, 3 - d),
        "inner": (c, p, jnp.where(d == 0, 1, 2)),
        "outer": (c, p, jnp.where(d == 1, 0, 3)),
    }


def places():
    p = lax.axis_index("mp")
    return [p, p + 1 - 2 * lax.rem(p, 2), lax.rem(p + 2, 4), 3 - p]


def dot(a, b):
    return jnp.dot(a, b, preferred_element_type=jnp.float32)


def dot_tn(a, b):
    return lax.dot_general(a, b, (((0,), (0,)), ((), ())), preferred_element_type=jnp.float32)


def dot_nt(a, b):
    return lax.dot_general(a, b, (((1,), (1,)), ((), ())), preferred_element_type=jnp.float32)


def standard(values):
    average = jnp.mean(values, axis=-1, keepdims=True)
    centered = values - average
    variance = jnp.mean(centered * centered, axis=-1, keepdims=True)
    scale = lax.rsqrt(variance + 1e-05)
    return centered * scale, scale


def softmax(q, k):
    scores = dot_nt(q * jnp.asarray(SCALE, q.dtype), k)
    top = jnp.max(scores, axis=-1, keepdims=True)
    exponent = jnp.exp(scores - top)
    total = jnp.sum(exponent, axis=-1, keepdims=True)
    return exponent * (1.0 / total), top + jnp.log(total)


def by_rows(rows, step, body):
    def run(i, carry):
        body(pl.ds(pl.multiple_of(i * step, step), step))
        return carry

    lax.fori_loop(0, rows // step, run, 0)


def first_norm(x, nrm, acc, u1, hb):
    def run(rows):
        u = acc[rows] + nrm[0:1] + high(x[rows])
        u1[rows] = u
        h = standard(u)[0] * nrm[2:3] + nrm[4:5]
        hb[rows] = low(h)
        acc[rows] = h + nrm[1:2]

    by_rows(acc.shape[0], 64, run)


def second_norm(nrm, acc, u2, out):
    def run(rows):
        u = acc[rows]
        u2[rows] = u
        out[rows] = low(standard(u)[0] * nrm[3:4] + nrm[5:6])

    by_rows(acc.shape[0], 64, run)


def norm_back(u, grad, gain, sums, at, out_low, out_acc):
    def run(rows):
        g = high(grad[rows])
        xhat, scale = standard(u[rows])
        scaled = g * gain
        du = scale * (
            scaled
            - jnp.mean(scaled, axis=-1, keepdims=True)
            - xhat * jnp.mean(scaled * xhat, axis=-1, keepdims=True)
        )
        out_low[rows] = low(du)
        out_acc[rows] = du
        for row, term in ((at[0], du), (at[1], g * xhat), (at[2], g)):
            sums[row : row + 1] += jnp.sum(term, axis=0, keepdims=True)

    by_rows(u.shape[0], 64, run)


def ffn_back_block(dfb, w, gd, acc, dz_out):
    dz = low(dot_nt(dfb[...], w[1]) * high(gd))
    dz_out[...] = dz
    acc[...] += dot(dz, w[0])
    return jnp.sum(high(dz), axis=0, keepdims=True)


def attention_back_block(dab, w, qkv, logs, dq_out, dk_out, dv_out, acc, dim):
    dob = low(dot_nt(dab[...], w[3]))
    for j in range(dob.shape[1] // dim):
        cols = slice(j * dim, (j + 1) * dim)
        q, k, v, do = qkv[0, :, cols], qkv[1, :, cols], qkv[2, :, cols], dob[:, cols]
        a = jnp.exp(dot_nt(q * jnp.asarray(SCALE, q.dtype), k) - logs[:, j : j + 1])
        da = dot_nt(do, v)
        ds = low(a * (da - jnp.sum(a * da, axis=-1, keepdims=True)))
        dv_out[:, cols] = low(dot_tn(low(a), do))
        dq_out[:, cols] = low(dot(ds, k) * SCALE)
        dk_out[:, cols] = low(dot_tn(ds, q) * SCALE)
    acc[...] += dot(dq_out[...], w[0]) + dot(dk_out[...], w[1]) + dot(dv_out[...], w[2])


def weight_copies(full, layer, kind, p, b, buf, sem, rows):
    width = 4 * rows
    if kind == 0:
        starts = [c * width + p * rows for c in range(4)]
    else:
        starts = [4 * width + t * 4 * width + p * width + b * rows for t in range(2)]
    return [
        pltpu.make_async_copy(full.at[layer, pl.ds(pl.multiple_of(start, rows), rows)], buf.at[n], sem.at[n])
        for n, start in enumerate(starts)
    ]


def project_block(x, w, vec, save, logs, dim):
    rows = x[...]
    q = low(dot_nt(rows, w[0]) + vec[0:1])
    k = low(dot_nt(rows, w[1]))
    v = low(dot_nt(rows, w[2]) + vec[1:2])
    save[0], save[1], save[2] = q, k, v
    for j in range(q.shape[1] // dim):
        cols = slice(j * dim, (j + 1) * dim)
        soft, logs[:, j : j + 1] = softmax(q[:, cols], k[:, cols])
        save[3, :, cols] = low(dot(low(soft), v[:, cols]))


def unit_values(hb, w, bias):
    z = dot_nt(hb[...], w) + bias
    inner = 0.5 + 0.5 * lax.erf(z * math.sqrt(0.5))
    slope = inner + z * jnp.exp(-0.5 * z * z) * (1.0 / math.sqrt(2.0 * math.pi))
    return low(z * inner), low(slope)


def gather_forward_kernel(
    dim, tokens, qkv_in, out_in, up_in, down_in, qv, up_bias, biases, gains, shifts, full, vecs, norms, qkvo, logs, gd, us, hbs, between, acts,
    turned, x, acc, u, hb, wa, wf, sa, gb, sd, wasem, wfsem, sasem, gbsem, sdsem, usem, vec, norm_in, lb, lbsem,
    w_qkv, w_out, w_up, w_down, rawsem,
    ini_s, ini_r, loc, x1ss, x1rs, y1ss, y1rs, x2ss, x2rs, y2ss, y2rs, zs, zr, cs, cr, vs, vr, vloc, as_, ar,
):
    c, p, d = lax.axis_index("section"), lax.axis_index("mp"), lax.axis_index("dp")
    near = neighbours()
    near["pair"] = (c, p, d + 1 - 2 * lax.rem(d, 2))
    spots = places()
    rows = w_out.shape[0] // 2
    half = rows // 2
    odd = lax.rem(d, 2)
    others = [(cc, spots[r], d) for r in range(4) for cc in (c, 1 - c)][1:]

    def place_of(s, spot, h):
        k = lax.rem(s, 12)
        row = jnp.where(k < 4, k * 8 + spot * 2, 32 + (k // 4 - 1) * 32 + spot * 8 + lax.rem(k, 4) * 2)
        return s // 12, (row + h) * rows

    def block(s, spot, h, start=0, size=rows):
        layer, row = place_of(s, spot, h)
        return full.at[layer, pl.ds(pl.multiple_of(row + start, half), size)]

    def init_place(k, layer):
        row = place_of(12 * layer + k, p, 0)[1]
        return full.at[layer, pl.ds(pl.multiple_of(row, half), 2 * rows)]

    def turn(k):
        if k < 3:
            turned[k] = w_qkv[k].T
        elif 4 <= k < 8:
            turned[k - 1] = w_up[:, 2 * rows * (k - 4) : 2 * rows * (k - 3)].T

    def chunk(k):
        if k == 3:
            return w_out
        if k < 8:
            return turned.at[k if k < 3 else k - 1]
        return w_down.at[pl.ds(2 * rows * (k - 8), 2 * rows)]

    def init_start(k):
        if k > 2:
            turn(k)
        pltpu.make_async_copy(chunk(k), init_place(k, c), loc.at[k]).start()
        remote(chunk(k), init_place(k, c), ini_s.at[k], ini_r.at[k], near["core"]).start()

    def init_local(k):
        return pltpu.make_async_copy(init_place(k, c), init_place(k, c), loc.at[k])

    def init_wait(k):
        there = init_place(k, 1 - c)
        remote(there, there, ini_s.at[k], ini_r.at[k], near["core"]).wait_recv()

    def small():
        copies = [remote(vec, vecs.at[c, p], vs.at[i], vr.at[c, p], device) for i, device in enumerate(others)]
        copies.append(remote(norm_in, norms.at[c], vs.at[7], vr.at[0, 4], near["core"]))
        return copies

    def small_local():
        return [
            pltpu.make_async_copy(vec, vecs.at[c, p], vloc.at[0]),
            pltpu.make_async_copy(norm_in, norms.at[c], vloc.at[1]),
        ]

    def hop(s, spot, name, pick):
        ss, rs = (x1ss, x1rs) if pick == "x" else (y1ss, y1rs)
        b = block(s, spot, c)
        return remote(b, b, ss.at[s], rs.at[s], near[name])

    def first(s, name):
        return hop(s, p, name, name)

    def arrived(s, name):
        return hop(s, spots[1] if name == "x" else spots[2], name, name)

    def relay(s, name, spot=None):
        if name == "x":
            b = block(s, spots[2] if spot is None else spot, c, 0, half)
            return remote(b, b, x2ss.at[s], x2rs.at[s], near["x"])
        b = block(s, spots[1] if spot is None else spot, c, half, half)
        return remote(b, b, y2ss.at[s], y2rs.at[s], near["y"])

    def relayed(s, name):
        return relay(s, name, spots[3])

    def to_pair(s, r):
        b = block(s, spots[r], c)
        return remote(b, b, zs.at[s, r - 1], zr.at[s, r - 1], near["pair"])

    def to_core(s, r):
        b = block(s, spots[r], c)
        return remote(b, b, cs.at[s, r - 1], cr.at[s, r - 1], near["core"])

    def from_core(s, r):
        b = block(s, spots[r], 1 - c)
        return remote(b, b, cs.at[s, r - 1], cr.at[s, r - 1], near["core"])

    def sent_chunk(j):
        t, n = j // 2, lax.rem(j, 2)
        return 3 * t + (1 - n) * (1 + odd), n == 0

    def stage_a(j):
        s = sent_chunk(j)[0]
        for m in range(3):
            own = 3 * (j // 2) + m

            @pl.when((own // 12 != c) & (lax.rem(j, 2) == 0))
            def _():
                init_wait(lax.rem(own, 12))

            @pl.when((own // 12 == c) & (lax.rem(j, 2) == 0))
            def _():
                init_local(lax.rem(own, 12)).wait()

        first(s, "x").start()
        first(s, "y").start()

    def stage_b(j):
        s, shared = sent_chunk(j)
        arrived(s, "x").wait_recv()
        relay(s, "y").start()
        arrived(s, "y").wait_recv()
        relay(s, "x").start()
        for r in (1, 2):
            to_core(s, r).start()

        @pl.when(shared)
        def _():
            for r in (1, 2):
                to_pair(s, r).start()

    def stage_c(j):
        s, shared = sent_chunk(j)
        relayed(s, "x").wait_recv()
        relayed(s, "y").wait_recv()
        to_core(s, 3).start()

        @pl.when(shared)
        def _():
            to_pair(s, 3).start()

    def stage_d(t):
        s = 3 * t + 2 - odd
        for r in (1, 2, 3):
            to_pair(s, r).wait_recv()
            to_core(s, r).start()

    def stage_e(t):
        for j in range(3):
            for r in (1, 2, 3):
                from_core(3 * t + j, r).wait_recv()

    def stage_f(t):
        for n, s in enumerate((3 * t, 3 * t + 1 + odd)):
            first(s, "x").wait_send()
            first(s, "y").wait_send()
            relay(s, "x").wait_send()
            relay(s, "y").wait_send()
            for r in (1, 2, 3):
                if n:
                    to_pair(s, r).wait_send()
        for j in range(3):
            for r in (1, 2, 3):
                to_core(3 * t + j, r).wait_send()

    wide = 2 * rows

    def weights(l, number, place, sem):
        begin = pl.multiple_of(number * wide, wide)
        return pltpu.make_async_copy(full.at[l, pl.ds(begin, wide)], place, sem)

    def load_qkv(l, q):
        return [weights(l, 4 * n + q, wa.at[q, n], wasem.at[q, n]) for n in range(3)]

    def load(l, number, slot):
        return weights(l, number, wf.at[slot], wfsem.at[slot])

    def load_out(l, q):
        return load(l, 12 + q, q)

    def load_in(l, b, q, slot):
        return load(l, 16 + 4 * q + b, slot)

    def load_down(l, b, q, slot):
        return load(l, 32 + 4 * q + b, slot)

    def load_last(l, q):
        return weights(l, 32 + 4 * q + 3, wa.at[q, 0], wasem.at[q, 0])

    def save_attn(l, q):
        return pltpu.make_async_copy(sa.at[q], qkvo.at[l, q], sasem.at[q])

    def save_logs(l, q):
        return pltpu.make_async_copy(lb.at[q], logs.at[l, q], lbsem.at[q])

    def save_g(l, n):
        return pltpu.make_async_copy(gb.at[n], gd.at[l, n, 0], gbsem.at[n])

    def save_d(l, n, slot):
        return pltpu.make_async_copy(sd.at[slot], gd.at[l, n, 1], sdsem.at[slot])

    def keep(l, which):
        if which == 2:
            return pltpu.make_async_copy(hb, hbs.at[l], usem.at[2])
        if which == 3:
            return pltpu.make_async_copy(x, between, usem.at[3])
        return pltpu.make_async_copy(u, us.at[l, which], usem.at[which])

    def give(begin):
        @pl.when(c == 0)
        def _():
            copy = pltpu.make_async_copy(x, acts.at[0], as_.at[0])
            copy.start() if begin else copy.wait()

        @pl.when(c == 1)
        def _():
            copy = remote(x, acts.at[1], as_.at[0], ar.at[0], near["core"])
            copy.start() if begin else copy.wait_send()

    def last_sum():
        return pltpu.make_async_copy(acc, us.at[1, 1], usem.at[1])

    def each(count, body):
        def run(q, carry):
            body(q)
            return carry

        lax.fori_loop(0, count, run, 0)

    def attention_segment(l, q):
        for copy in load_qkv(l, q):
            copy.wait()
        project_block(x, wa.at[q], vecs[l, q], sa.at[q], lb.at[q], dim)
        save_attn(l, q).start()
        save_logs(l, q).start()

    def out_segment(l):
        @pl.when(l == 1)
        def _():
            keep(0, 1).wait()

        acc[...] = jnp.zeros_like(acc)

        def branch(q):
            load_out(l, q).wait()
            acc[...] += dot(sa[q, 3], wf[q])
            load_in(l, 1, q, q).start()

        each(4, branch)
        first_norm(x, norms.at[l], acc, u, hb)
        keep(l, 0).start()
        keep(l, 2).start()

    def up_segment(l, b, slot):
        for q in range(4):
            load_in(l, b, q, slot + q).wait()
        for q in range(4):
            g, slope = unit_values(hb, wf[slot + q], vecs[l, q, pl.ds(2 + b, 1)])
            gb[4 * q + b] = g
            sd[q] = slope
        for q in range(4):
            save_g(l, 4 * q + b).start()
            save_d(l, 4 * q + b, q).start()

    def up_saved(l, b):
        for q in range(4):
            save_d(l, 4 * q + b, q).wait()

    def down_segment(l, b, slot):
        for q in range(4):
            load_down(l, b, q, slot + q).wait()
        first_two = dot(gb[b], wf[slot]) + dot(gb[4 + b], wf[slot + 1])
        acc[...] += first_two + dot(gb[8 + b], wf[slot + 2]) + dot(gb[12 + b], wf[slot + 3])

    def end_segment(l):
        keep(l, 0).wait()
        keep(l, 2).wait()
        each(4, lambda q: save_attn(l, q).wait())
        each(4, lambda q: save_logs(l, q).wait())
        each(16, lambda n: save_g(l, n).wait())

        @pl.when(l == 0)
        def _():
            second_norm(norms.at[0], acc, u, x)
            keep(0, 1).start()
            give(True)
            keep(0, 3).start()

        @pl.when(l == 1)
        def _():
            last_sum().start()

    def small_there():
        for copy in small_local():
            copy.wait()
        for copy in small():
            copy.wait_send()
        for cc, spot in [(cc, spots[r]) for r in range(4) for cc in (c, 1 - c)][1:]:
            remote(vec, vecs.at[cc, spot], vs.at[0], vr.at[cc, spot], near["core"]).wait_recv()
        remote(norm_in, norms.at[1 - c], vs.at[7], vr.at[0, 4], near["core"]).wait_recv()

    def compute(m):
        l, part = m // 8, lax.rem(m, 8)

        def at(number, body):
            @pl.when(part == number)
            def _():
                body()

        def attention_first():
            for q in range(4):
                for copy in load_qkv(l, q):
                    copy.start()

            @pl.when(m == 0)
            def _():
                small_there()
                first_rows.wait()

        def attention_half(begin):
            each(2, lambda q: attention_segment(l, begin + q))

        def out_part():
            for q in range(4):
                load_out(l, q).start()
            for q in range(4):
                load_in(l, 0, q, 4 + q).start()
            out_segment(l)

        def up_part():
            for q in range(4):
                load_in(l, 2, q, q).start()
            for q in range(4):
                load_in(l, 3, q, 4 + q).start()
            up_saved(l, 1)
            up_segment(l, 2, 0)
            for q in range(4):
                load_down(l, 0, q, q).start()

        def turn_part():
            up_saved(l, 2)
            up_segment(l, 3, 4)
            down_segment(l, 0, 0)

        def down_part():
            for b in (1, 2):
                for q in range(4):
                    load_down(l, b, q, 4 * (b - 1) + q).start()
            for q in range(4):
                load_last(l, q).start()
            up_saved(l, 3)
            down_segment(l, 1, 0)
            down_segment(l, 2, 4)

        def end_part():
            for q in range(4):
                load_last(l, q).wait()
            first_two = dot(gb[3], wa[0, 0]) + dot(gb[7], wa[1, 0])
            acc[...] += first_two + dot(gb[11], wa[2, 0]) + dot(gb[15], wa[3, 0])
            end_segment(l)

        at(0, attention_first)

        @pl.when(part < 2)
        def _():
            attention_half(2 * part)

        at(2, out_part)

        @pl.when((part == 2) | (part == 3))
        def _():
            b = part - 2

            @pl.when(b == 1)
            def _():
                up_saved(l, 0)

            up_segment(l, b, 4 - 4 * b)

        at(4, up_part)
        at(5, turn_part)
        at(6, down_part)
        at(7, end_part)

    first_rows = pltpu.make_async_copy(tokens.at[c], x, usem.at[4])
    raw = [
        pltpu.make_async_copy(source, place, rawsem.at[n])
        for n, (source, place) in enumerate(
            ((qkv_in, w_qkv), (out_in, w_out), (up_in, w_up), (down_in, w_down))
        )
    ]
    for copy in raw:
        copy.start()
    first_rows.start()
    vec[...] = jnp.zeros_like(vec)
    vec[0:2] = high(qv[...])
    for b in range(4):
        vec[2 + b : 3 + b] = high(up_bias[:, 2 * rows * b : 2 * rows * (b + 1)])
    norm_in[...] = jnp.zeros_like(norm_in)
    norm_in[0:2], norm_in[2:4], norm_in[4:6] = biases[...], gains[...], shifts[...]
    barrier = pltpu.get_barrier_semaphore()
    for device in others + [near["pair"]]:
        pl.semaphore_signal(barrier, inc=1, device_id=device, device_id_type=MESH)
    raw[0].wait()
    for k in range(3):
        turn(k)
    pl.semaphore_wait(barrier, 8)
    for k in range(3):
        init_start(k)
    for copy in small_local() + small():
        copy.start()

    def step(count, carry):
        i = count - 1

        def run(stage, lag):
            @pl.when((i >= lag) & (i < 2 * TRIPLES + lag))
            def _():
                stage(i - lag)

        def run_late(stage, lag):
            @pl.when((i >= lag) & (i < 2 * TRIPLES + lag) & (lax.rem(i - lag, 2) == 0))
            def _():
                stage((i - lag) // 2)

        run(stage_b, 1)
        run(stage_a, -1)
        run(stage_c, 2)
        run_late(stage_e, 4)
        run_late(stage_f, 6)
        for t in range(3):

            @pl.when(i == 2 * t)
            def _():
                if t == 0:
                    for copy in raw[1:]:
                        copy.wait()
                for k in range(3 * t + 3, 3 * t + 6):
                    init_start(k)

        run(compute, 4)
        run_late(stage_d, 3)
        return carry

    lax.fori_loop(0, 2 * TRIPLES + 6, step, 0)

    for k in range(12):
        remote(chunk(k), init_place(k, c), ini_s.at[k], ini_r.at[k], near["core"]).wait_send()
    keep(0, 3).wait()
    give(False)
    last_sum().wait()

    @pl.when(c == 0)
    def _():
        remote(x, acts.at[1], as_.at[0], ar.at[0], near["core"]).wait_recv()


def gather_forward(dim, tokens, w_qkv, w_out, w_up, w_down, qv, up_bias, biases, gains, shifts):
    rows, width = w_out.shape
    seq = tokens.shape[1]
    bf, f32, dma, v = jnp.bfloat16, jnp.float32, pltpu.SemaphoreType.DMA, pltpu.VMEM
    hbm, vmem = pl.BlockSpec(memory_space=pl.ANY), pl.BlockSpec(memory_space=pltpu.VMEM)
    S = jax.ShapeDtypeStruct
    return pl.pallas_call(
        functools.partial(gather_forward_kernel, dim),
        out_shape=(
            S((2, 48 * rows, width), bf), S((2, 4, 8, rows), f32), S((2, 8, width), f32),
            S((2, 4, 4, seq, rows), bf), S((2, 4, seq, 128), f32), S((2, 16, 2, seq, rows), bf), S((2, 2, seq, width), f32),
            S((2, seq, width), bf), S((seq, width), bf), S((2, seq, width), bf),
        ),
        in_specs=[hbm] * 5 + [vmem] * 5,
        out_specs=[hbm, vmem, vmem] + [hbm] * 7,
        scratch_shapes=[
            v((7, rows, width), bf),
            v((seq, width), bf), v((seq, width), f32), v((seq, width), f32), v((seq, width), bf),
            v((4, 3, rows, width), bf), v((8, rows, width), bf), v((4, 4, seq, rows), bf), v((16, seq, rows), bf),
            v((4, seq, rows), bf), dma((4, 3)), dma((8,)), dma((4,)), dma((16,)), dma((4,)), dma((5,)),
            v((8, rows), f32), v((8, width), f32), v((4, seq, 128), f32), dma((4,)),
            v(w_qkv.shape, bf), v(w_out.shape, bf), v(w_up.shape, bf), v(w_down.shape, bf), dma((4,)),
        ] + [dma((12,))] * 3 + [dma((24,))] * 8 + [dma((24, 3))] * 4
        + [dma((8,)), dma((2, 5)), dma((2,)), dma((1,)), dma((1,))],
        compiler_params=pltpu.CompilerParams(collective_id=0, has_side_effects=True, vmem_limit_bytes=60 * 2**20),
    )(tokens, w_qkv, w_out, w_up, w_down, qv, up_bias, biases, gains, shifts)


def backward_reduce_kernel(
    dim, tokens, cots, full, norms, qkvo, logs, gd, us, hbs, between, out, grads, acts, totals,
    left, right, acc, g, u, wa, wf, da, df, dl, dlsem, trades,
    sendc, recvc, keep, x1s, x1r, y1s, y1r, part, base, x2s, x2r, y2s, y2r, mid,
    zk, zs1, zr1, zs2, zr2, zs3, zr3,
    wasem, wfsem, dasem, dfsem, gsem, osem4, bsem, gds, gdr, as_, ar, tss, trs,
    cs, cr, x1ss, x1rs, y1ss, y1rs, x2ss, x2rs, y2ss, y2rs, z1ss, z1rs, z2ss, z2rs, z3ss, z3rs, os, orr,
):
    c, p, d = lax.axis_index("section"), lax.axis_index("mp"), lax.axis_index("dp")
    near = neighbours()
    near["pair"] = (c, p, d + 1 - 2 * lax.rem(d, 2))
    near["far"] = (c, p, lax.rem(d + 2, 4))
    spots = places()
    is_end = (d == 0) | (d == 3)
    is_mid = jnp.logical_not(is_end)
    rows = sendc.shape[2]
    half = rows // 2
    wide = 2 * rows

    def core_copy(s):
        a, b = lax.rem(s, 2), lax.rem(s, 4)
        return remote(sendc.at[a], recvc.at[b], cs.at[a], cr.at[b], near["core"])

    def link_copy(s, src, dst, ss, rs, name):
        a, b = lax.rem(s, 2), lax.rem(s, 4)
        return remote(src.at[a], dst.at[b], ss.at[a], rs.at[b], near[name])

    def first_copy(s, n, src, dst, ss, rs, name):
        a, b = lax.rem(s, 2), lax.rem(s, 4)
        return remote(src.at[a, n], dst.at[b, n], ss.at[a, n], rs.at[b, n], near[name])

    x1 = lambda s, n: first_copy(s, n, x1s, x1r, x1ss, x1rs, "x")
    y1 = lambda s, n: first_copy(s, n, y1s, y1r, y1ss, y1rs, "y")
    x2 = lambda s: link_copy(s, x2s, x2r, x2ss, x2rs, "x")
    y2 = lambda s: link_copy(s, y2s, y2r, y2ss, y2rs, "y")
    z1 = lambda s, n: first_copy(s, n, zs1, zr1, z1ss, z1rs, "inner")
    z2 = lambda s, n: first_copy(s, n, zs2, zr2, z2ss, z2rs, "across")

    def z3(s, n):
        b = lax.rem(s, 6)
        return remote(zs3.at[b, n], zr3.at[b, n], z3ss.at[b, n], z3rs.at[b, n], near["outer"])

    def stage0(s):
        k, slot = lax.rem(s, 12), lax.rem(s, 2)
        stride = jnp.where(k < 8, 4, 1)
        first = jnp.where(k < 4, k, jnp.where(k < 8, 12 + k, jnp.where(k == 8, 32, 36 + 4 * (k - 9))))
        kind = jnp.where(k < 4, 0, jnp.where(k < 8, 1, jnp.where(k == 8, 2, 3)))
        for r in range(4):
            whole = dot_tn(left[first + stride * spots[r]], right[kind])
            keep[slot, r] = jnp.where(c == 0, whole[:rows], whole[rows:])
            sendc[slot, r] = low(jnp.where(c == 0, whole[rows:], whole[:rows]))
        core_copy(s).start()

    def stage1(s):
        a, b = lax.rem(s, 2), lax.rem(s, 4)
        core_copy(s).wait()
        far = keep[a, 3] + high(recvc[b, 3])
        x1s[a, 0] = low(far[:half])
        y1s[a, 0] = low(far[half:])
        x1(s, 0).start()
        y1(s, 0).start()
        by_x = keep[a, 1] + high(recvc[b, 1])
        x1s[a, 1] = low(by_x[:half])
        part[a, 0] = by_x[half:]
        by_y = keep[a, 2] + high(recvc[b, 2])
        y1s[a, 1] = low(by_y[half:])
        part[a, 1] = by_y[:half]
        x1(s, 1).start()
        y1(s, 1).start()
        base[a] = keep[a, 0] + high(recvc[b, 0])

    def stage2(s):
        a, b = lax.rem(s, 2), lax.rem(s, 4)
        x1(s, 0).wait()
        y2s[a] = low(part[a, 1] + high(x1r[b, 0]))
        y2(s).start()
        y1(s, 0).wait()
        x2s[a] = low(part[a, 0] + high(y1r[b, 0]))
        x2(s).start()
        x1(s, 1).wait()
        y1(s, 1).wait()
        own = base[a]
        mid[a, 0] = own[:half] + high(x1r[b, 1])
        mid[a, 1] = own[half:] + high(y1r[b, 1])

    def stage3(s):
        a, b = lax.rem(s, 2), lax.rem(s, 4)
        for n, copy, got in ((0, y2, y2r), (1, x2, x2r)):
            copy(s).wait()
            total = mid[a, n] + high(got[b])

            @pl.when(is_end)
            def _():
                zs1[a, n] = low(total)
                z1(s, n).start()

            @pl.when(is_mid)
            def _():
                zk[a, n] = total

    def stage4(s):
        a, b = lax.rem(s, 2), lax.rem(s, 4)
        for n in range(2):

            @pl.when(is_end)
            def _():
                z1(s, n).wait_send()

            @pl.when(is_mid)
            def _():
                z1(s, n).wait_recv()
                zs2[a, n] = low(zk[a, n] + high(zr1[b, n]))
                z2(s, n).start()

    def stage5(s):
        a, b, to = lax.rem(s, 2), lax.rem(s, 4), lax.rem(s, 6)

        @pl.when(is_mid)
        def _():
            for n in range(2):
                z2(s, n).wait()
                zs3[to, n] = low(high(zs2[a, n]) + high(zr2[b, n]))
                z3(s, n).start()

    def stage6(s, begin):
        layer, k, b = 1 - s // 12, lax.rem(s, 12), lax.rem(s, 6)

        def finish(source):
            @pl.when(layer == c)
            def _():
                copy = pltpu.make_async_copy(source.at[b], out.at[k, c], os.at[b])
                copy.start() if begin else copy.wait()

            @pl.when(layer != c)
            def _():
                copy = remote(source.at[b], out.at[k, c], os.at[b], orr.at[k], near["core"])
                copy.start() if begin else copy.wait_send()

        @pl.when(is_end)
        def _():
            if begin:
                for n in range(2):
                    z3(s, n).wait_recv()
            finish(zr3)

        @pl.when(is_mid)
        def _():
            if begin:
                for n in range(2):
                    z3(s, n).wait_send()
            finish(zs3)

    def load_g(l, n):
        return pltpu.make_async_copy(gd.at[l, n, 0], left.at[n], gsem.at[n])

    def load_o(l, n):
        return pltpu.make_async_copy(qkvo.at[l, n, 3], left.at[32 + n], osem4.at[n])

    def load_h(l):
        return pltpu.make_async_copy(hbs.at[l], right.at[1], bsem.at[0])

    def load_x(source):
        return pltpu.make_async_copy(source, right.at[3], bsem.at[1])

    def load_u(l, which):
        return pltpu.make_async_copy(us.at[l, which], u, bsem.at[2])

    def ffn(l, n, slot):
        return weight_copies(full, l, 1, lax.rem(n, 4), n // 4, wf.at[slot], wfsem.at[slot], wide) + [
            pltpu.make_async_copy(gd.at[l, 4 * lax.rem(n, 4) + n // 4, 1], df.at[slot], dfsem.at[slot])
        ]

    def attn(l, q, slot):
        return weight_copies(full, l, 0, q, 0, wa.at[slot], wasem.at[slot], wide) + [
            pltpu.make_async_copy(qkvo.at[l, q], da.at[slot], dasem.at[slot]),
            pltpu.make_async_copy(logs.at[l, q], dl.at[slot], dlsem.at[slot]),
        ]

    def store_dx(l, begin):
        @pl.when(l == c)
        def _():
            copy = pltpu.make_async_copy(g, grads.at[c], gds.at[0])
            copy.start() if begin else copy.wait()

        @pl.when(l != c)
        def _():
            copy = remote(g, grads.at[c], gds.at[0], gdr.at[0], near["core"])
            copy.start() if begin else copy.wait_send()

    def give(begin):
        @pl.when(c == 1)
        def _():
            copy = pltpu.make_async_copy(g, acts.at[1], as_.at[0])
            copy.start() if begin else copy.wait()

        @pl.when(c == 0)
        def _():
            copy = remote(g, acts.at[0], as_.at[0], ar.at[0], near["core"])
            copy.start() if begin else copy.wait_send()

    def output():
        load_u(1, 1).wait()
        store_dx(0, False)

        def run(r):
            g[r] = low(standard(u[r])[0] * norms[1, 3:4] + norms[1, 5:6])

        by_rows(u.shape[0], 64, run)
        give(True)

    def ahead(l):
        load_u(l, 1).start()
        for copy in ffn(l, 0, 0) + attn(l, 0, 0):
            copy.start()

    def operands(l):
        def run(n, carry):
            load_g(l, n).start()
            return carry

        lax.fori_loop(0, 16, run, 0)
        for n in range(4):
            load_o(l, n).start()
        load_h(l).start()

    def operands_there(l):
        def run(n, carry):
            load_g(l, n).wait()
            return carry

        lax.fori_loop(0, 16, run, 0)
        for n in range(4):
            load_o(l, n).wait()
        load_h(l).wait()

    def top_segment(l):
        load_u(l, 1).wait()
        norm_back(u, g, norms[l, 3:4], totals.at[l], (1, 3, 5), right.at[0], acc)
        load_u(l, 0).start()

        @pl.when(l == 1)
        def _():
            operands_there(1)

    def ffn_segment(l, b):
        def run(q, carry):
            n = 4 * b + q
            slot = lax.rem(n, 2)
            for copy in ffn(l, n, slot):
                copy.wait()

            @pl.when(n < 15)
            def _():
                for copy in ffn(l, n + 1, 1 - slot):
                    copy.start()

            row = ffn_back_block(right.at[0], wf.at[slot], df[slot], acc, left.at[16 + 4 * q + b])
            totals[l, pl.ds(10 + b, 1), pl.ds(pl.multiple_of(q * wide, wide), wide)] = row
            return carry

        lax.fori_loop(0, 4, run, 0)

    def middle_segment(l):
        load_u(l, 0).wait()
        norm_back(u, acc, norms[l, 2:3], totals.at[l], (0, 2, 4), right.at[2], acc)

    def attention_segment(l, q):
        slot = lax.rem(q, 2)
        for copy in attn(l, q, slot):
            copy.wait()

        @pl.when(q < 3)
        def _():
            for copy in attn(l, q + 1, 1 - slot):
                copy.start()

        dq, dk, dv = left.at[36 + q], left.at[40 + q], left.at[44 + q]
        attention_back_block(right.at[2], wa.at[slot], da.at[slot], dl[slot], dq, dk, dv, acc, dim)
        cols = pl.ds(pl.multiple_of(q * wide, wide), wide)
        totals[l, 8:9, cols] = jnp.sum(high(dq[...]), axis=0, keepdims=True)
        totals[l, 9:10, cols] = jnp.sum(high(dv[...]), axis=0, keepdims=True)

    def end_segment(l):
        by_rows(acc.shape[0], 64, lambda r: g.__setitem__(r, low(acc[r])))
        store_dx(l, True)
        if l == 1:
            ahead(0)

    def segment(i):
        l = jnp.where(i < 8, 1, 0)
        j = jnp.where(i < 8, i, i - 9)
        q = jnp.where(i < 8, i - 4, i - 14)

        @pl.when(i == 8)
        def _():
            end_segment(1)
            operands(0)
            store_dx(1, False)

        @pl.when(i == 7)
        def _():
            load_x(between).wait()

        @pl.when(j == -1)
        def _():
            top_segment(l)

        @pl.when((j >= 0) & (j < 4))
        def _():
            ffn_segment(l, j)

        @pl.when((i == 3) | (i == 13))
        def _():
            middle_segment(l)

        @pl.when((q >= 0) & (q < 4))
        def _():
            attention_segment(l, q)

        @pl.when(i == 18)
        def _():
            end_segment(0)

        @pl.when(i == 10)
        def _():
            operands_there(0)

        @pl.when(i == 12)
        def _():
            load_x(tokens.at[c]).start()

        @pl.when(i == 16)
        def _():
            load_x(tokens.at[c]).wait()

    def trade(k):
        return remote(totals, trades.at[k], tss.at[k], trs.at[k], near[("core", "x", "y", "pair", "far")[k]])

    first_rows = pltpu.make_async_copy(cots.at[c], g, bsem.at[3])
    first_rows.start()
    ahead(1)
    operands(1)
    load_x(between).start()
    totals[...] = jnp.zeros_like(totals)
    barrier = pltpu.get_barrier_semaphore()

    def signal(device):
        pl.semaphore_signal(barrier, inc=1, device_id=device, device_id_type=MESH)

    for name in ("core", "x", "y", "pair", "far"):
        signal(near[name])

    @pl.when(is_end)
    def _():
        pl.semaphore_wait(barrier, 5)

    @pl.when(is_mid)
    def _():
        signal(near["across"])
        pl.semaphore_wait(barrier, 6)

    first_rows.wait()

    def step(count, carry):
        i = count - 1

        def run(stage, lag, *extra):
            @pl.when((i >= lag) & (i < CHUNKS + lag))
            def _():
                stage(i - lag, *extra)

        for lag, stage in enumerate((stage1, stage2, stage3, stage4, stage5)):
            run(stage, lag + 1)
        run(stage6, 6, True)
        run(stage6, 7, False)
        for k in range(6):

            @pl.when(i == 20 + k)
            def _():
                if k:
                    trade(k - 1).wait()
                    totals[...] += trades[k - 1]
                if k < 5:
                    trade(k).start()

        run(stage0, 0)

        @pl.when((i < 20) & (i != 0))
        def _():
            segment(jnp.where(i < 0, i, i - 1))

        @pl.when(i == 20)
        def _():
            load_u(1, 1).start()

        @pl.when(i == 22)
        def _():
            output()


        return carry

    lax.fori_loop(0, CHUNKS + 9, step, 0)
    give(False)

    @pl.when(c == 1)
    def _():
        remote(g, acts.at[0], as_.at[0], ar.at[0], near["core"]).wait_recv()

    remote(g, grads.at[1 - c], gds.at[0], gdr.at[0], near["core"]).wait_recv()
    for k in range(12):
        remote(zs3.at[0], out.at[k, 1 - c], os.at[0], orr.at[k], near["core"]).wait_recv()


def backward_reduce(dim, tokens, cots, full, norms, saved):
    seq, width = tokens.shape[1:]
    wide = width // 4
    block, half = wide // 2, wide // 4
    bf, f32, dma, v = jnp.bfloat16, jnp.float32, pltpu.SemaphoreType.DMA, pltpu.VMEM
    hbm, vmem = pl.BlockSpec(memory_space=pl.ANY), pl.BlockSpec(memory_space=pltpu.VMEM)
    S = jax.ShapeDtypeStruct
    return pl.pallas_call(
        functools.partial(backward_reduce_kernel, dim),
        out_shape=(S((12, 2, 2, half, width), bf), S((2, seq, width), bf), S((2, seq, width), bf),
                   S((2, 16, width), f32)),
        in_specs=[hbm, hbm, hbm, vmem] + [hbm] * 6,
        out_specs=[hbm, hbm, hbm, vmem],
        scratch_shapes=[
            v((48, seq, wide), bf), v((4, seq, width), bf), v((seq, width), f32), v((seq, width), bf),
            v((seq, width), f32),
            v((2, 4, wide, width), bf), v((2, 2, wide, width), bf), v((2, 4, seq, wide), bf), v((2, seq, wide), bf),
            v((2, seq, 128), f32), dma((2,)), v((5, 2, 16, width), f32),
            v((2, 4, block, width), bf), v((4, 4, block, width), bf), v((2, 4, block, width), f32),
            v((2, 2, half, width), bf), v((4, 2, half, width), bf), v((2, 2, half, width), bf), v((4, 2, half, width), bf),
            v((2, 2, half, width), f32), v((2, block, width), f32),
            v((2, half, width), bf), v((4, half, width), bf), v((2, half, width), bf), v((4, half, width), bf),
            v((2, 2, half, width), f32),
            v((2, 2, half, width), f32), v((2, 2, half, width), bf), v((4, 2, half, width), bf),
            v((2, 2, half, width), bf), v((4, 2, half, width), bf), v((6, 2, half, width), bf), v((6, 2, half, width), bf),
            dma((2, 4)), dma((2, 2)), dma((2,)), dma((2,)), dma((16,)), dma((4,)), dma((4,)), dma((1,)), dma((1,)), dma((1,)), dma((1,)),
            dma((5,)), dma((5,)),
        ] + [dma((n,)) for n in (2, 4)] + [dma((n, 2)) for n in (2, 4) * 2] + [dma((n,)) for n in (2, 4) * 2]
        + [dma((n, 2)) for n in (2, 4, 2, 4, 6, 6)] + [dma((6,)), dma((12,))],
        compiler_params=pltpu.CompilerParams(collective_id=1, has_side_effects=True, vmem_limit_bytes=63 * 2**20),
    )(tokens, cots, full, norms, *saved)


def finish_kernel(parts, acts_zero, acts_one, grads_in, totals, acts, grads, g_qkv, g_out, g_up, g_down, g_qv, g_bias,
                  g_biases, g_gains, g_shifts, pb, ab, gb, qb, ob, ub, db, psem, asem, osem):
    def load(k):
        return pltpu.make_async_copy(parts.at[k], pb.at[k], psem.at[k])

    c, p, d = lax.axis_index("section"), lax.axis_index("mp"), lax.axis_index("dp")
    order = (4, 5, 6, 7, 9, 10, 11, 0, 1, 2, 3, 8)
    for k in order:
        load(k).start()

    @pl.when(c == 0)
    def _():
        pltpu.make_async_copy(acts_zero, ab, asem.at[0]).start()

    @pl.when(c == 1)
    def _():
        pltpu.make_async_copy(acts_one, ab, asem.at[0]).start()

    pltpu.make_async_copy(grads_in, gb, asem.at[1]).start()
    others = [(acts_zero, ab, acts, 0), (grads_in, gb, grads, 1)]
    stores = []
    rows = pb.shape[1]
    mine = totals.at[c]
    own = mine[8:16, pl.ds(pl.multiple_of(p * rows, rows), rows)]
    g_qv[...] = own[0:2]
    for b in range(4):
        g_bias[:, b * rows : (b + 1) * rows] = own[2 + b : 3 + b]
    piece = g_gains.shape[1]
    both = mine[0:8, pl.ds(pl.multiple_of(p * rows + d // 2 * 2 * piece, 2 * piece), 2 * piece)]
    both = jnp.where(lax.rem(d, 2) == 0, both[:, :piece], both[:, piece:])
    g_biases[...], g_gains[...], g_shifts[...] = both[0:2], both[2:4], both[4:6]

    def store(source, place):
        copy = pltpu.make_async_copy(source, place, osem.at[len(stores)])
        copy.start()
        stores.append(copy)

    for k in order:
        load(k).wait()
        if k < 4:
            span = pl.ds(k * rows, rows)
            db[span] = high(pb[k])
            store(db.at[span], g_down.at[span])
        elif k < 8:
            ub[:, pl.ds((k - 4) * rows, rows)] = high(pb[k].T)
            if k == 7:
                store(ub, g_up)
        elif k == 8:
            ob[...] = high(pb[k])
            store(ob, g_out)
        else:
            qb[k - 9] = high(pb[k].T)
            store(qb.at[k - 9], g_qkv.at[k - 9])
        if k == 7:
            for source, buffer, place, n in others:
                pltpu.make_async_copy(source, buffer, asem.at[n]).wait()
                store(buffer, place)
    for copy in stores:
        copy.wait()


def finish(parts, acts, acts_one, grads, totals):
    count, rows, width = parts.shape
    bf, f32, dma, v = jnp.bfloat16, jnp.float32, pltpu.SemaphoreType.DMA, pltpu.VMEM
    S = jax.ShapeDtypeStruct
    shapes = [(3, width, rows), (rows, width), (width, width), (width, width)]
    piece = width // (lax.axis_size("mp") * lax.axis_size("dp"))
    hbm, vmem = pl.BlockSpec(memory_space=pl.ANY), pl.BlockSpec(memory_space=pltpu.VMEM)
    vectors = [(2, rows), (1, 4 * rows)] + [(2, piece)] * 3
    return pl.pallas_call(
        finish_kernel,
        out_shape=[S(acts.shape, bf), S(grads.shape, bf)] + [S(shape, f32) for shape in shapes + vectors],
        in_specs=[hbm] * 4 + [vmem],
        out_specs=[hbm] * 6 + [vmem] * 5,
        scratch_shapes=[v(parts.shape, bf), v(acts.shape, bf), v(grads.shape, bf)] + [v(shape, f32) for shape in shapes]
        + [dma((12,)), dma((2,)), dma((11,))],
        compiler_params=pltpu.CompilerParams(vmem_limit_bytes=63 * 2**20),
    )(parts, acts, acts_one, grads, totals)


def by_page(
    token_in,
    cotangent,
    w_qkv,
    qv_bias,
    w_attn_out,
    w_ffn_in,
    ffn_in_bias,
    w_ffn_out,
    out_biases,
    norm_gains,
    norm_shifts,
):
    width = token_in.shape[2]
    full, vecs, norms, *saved, acts = gather_forward(
        HEAD_DIM,
        token_in,
        w_qkv[0],
        w_attn_out[0],
        w_ffn_in[0],
        w_ffn_out[0],
        qv_bias[0],
        ffn_in_bias,
        out_biases[0],
        norm_gains[0],
        norm_shifts[0],
    )
    parts, grads, acts_one, totals = backward_reduce(HEAD_DIM, token_in, cotangent, full, norms, saved)
    results = finish(parts.reshape(12, width // 4, width), acts, acts_one, grads, totals)
    acts, grads, grad_qkv, grad_out, grad_up, grad_down, grad_qv, grad_bias, *rows = results
    return (
        acts[None],
        grads[None],
        grad_qkv[None],
        grad_qv[None],
        grad_out[None],
        grad_up[None],
        grad_bias,
        grad_down[None],
    ) + tuple(row[None] for row in rows)


def on_device(*args):
    token_in, w_qkv, ffn_in = args[0], args[2], args[5]
    fits = (
        lax.axis_size("section") == 2
        and lax.axis_size("mp") == 4
        and lax.axis_size("dp") == 4
        and token_in.shape == (2, SEQ, 1024)
        and w_qkv.shape[3] == 256
        and ffn_in.shape[2] == 1024
    )
    return by_page(*args) if fits else pipelined(*args)


def solution(mesh):
    return jax.shard_map(
        on_device,
        mesh=mesh,
        in_specs=(
            P(None, ("dp", "mp"), None),
            P(None, ("dp", "mp"), None),
            P("section", None, None, "mp"),
            P("section", None, "mp"),
            P("section", "mp", None),
            P("section", None, "mp"),
            P("section", "mp"),
            P("section", "mp", None),
            P("section", None, None),
            P("section", None, None),
            P("section", None, None),
        ),
        out_specs=(
            P("section", None, ("dp", "mp"), None),
            P("section", None, ("dp", "mp"), None),
            P("section", None, None, "mp"),
            P("section", None, "mp"),
            P("section", "mp", None),
            P("section", None, "mp"),
            P("section", "mp"),
            P("section", "mp", None),
            P("section", None, ("mp", "dp")),
            P("section", None, ("mp", "dp")),
            P("section", None, ("mp", "dp")),
        ),
        check_vma=False,
    )
```

```python
import functools
from functools import partial
import math

import jax
import jax.numpy as jnp
from jax import lax
from jax.experimental import pallas as pl
from jax.experimental.pallas import tpu as pltpu
from jax.sharding import PartitionSpec as P

HEAD_DIM = 64
SEQ = 512


def from_behind(value, axis, by):
    devices = lax.axis_size(axis)
    pairs = [(i, i + by) for i in range(devices) if 0 <= i + by < devices]
    return lax.ppermute(value, axis, pairs)


def norm_rows(values, gain_row, shift_row):
    average = jnp.mean(values, axis=-1, keepdims=True)
    centered = values - average
    variance = jnp.mean(centered * centered, axis=-1, keepdims=True)
    return centered * lax.rsqrt(variance + 1e-05) * gain_row + shift_row


def exact_gelu(values):
    return jax.nn.gelu(values, approximate=False)


def layer_forward(params, token_rows):
    (
        w_qkv,
        qv_bias,
        w_attn_out,
        w_ffn_in,
        ffn_in_bias,
        w_ffn_out,
        out_biases,
        norm_gains,
        norm_shifts,
    ) = params
    gathered = lax.all_gather(token_rows, "mp", axis=0, tiled=True)
    rows_all = gathered.shape[0]
    local_width = w_qkv.shape[2]
    local_heads = local_width // HEAD_DIM
    page_count = rows_all // SEQ
    scale_factor = 1.0 / math.sqrt(HEAD_DIM)
    bias_full = jnp.stack([qv_bias[0], jnp.zeros_like(qv_bias[0]), qv_bias[1]]).astype(jnp.float32)
    projected = (
        jnp.einsum("rd,cde->cre", gathered, w_qkv, preferred_element_type=jnp.float32)
        + bias_full[:, None, :]
    )
    heads_view = projected.astype(jnp.bfloat16).reshape(3, page_count, SEQ, local_heads, HEAD_DIM)
    scores = (
        jnp.einsum(
            "pqhe,pkhe->phqk", heads_view[0], heads_view[1], preferred_element_type=jnp.float32
        )
        * scale_factor
    )
    top_score = jnp.max(scores, axis=-1, keepdims=True)
    exponent = jnp.exp(scores - top_score)
    weights_soft = exponent / jnp.sum(exponent, axis=-1, keepdims=True)
    weights_low = weights_soft.astype(jnp.bfloat16)
    attended = jnp.einsum(
        "phqk,pkhe->pqhe", weights_low, heads_view[2], preferred_element_type=jnp.float32
    )
    attended = attended.reshape(rows_all, local_width).astype(jnp.bfloat16)
    attn_part = jnp.dot(attended, w_attn_out, preferred_element_type=jnp.float32)
    attn_rows = lax.psum_scatter(
        attn_part.astype(jnp.bfloat16), "mp", scatter_dimension=0, tiled=True
    ).astype(jnp.float32)
    residual_one = attn_rows + out_biases[0] + token_rows.astype(jnp.float32)
    first = norm_rows(residual_one, norm_gains[0], norm_shifts[0])
    first_all = lax.all_gather(first.astype(jnp.bfloat16), "mp", axis=0, tiled=True)
    pre_act = jnp.dot(first_all, w_ffn_in, preferred_element_type=jnp.float32) + ffn_in_bias.astype(
        jnp.float32
    )
    activated = exact_gelu(pre_act).astype(jnp.bfloat16)
    ffn_part = jnp.dot(activated, w_ffn_out, preferred_element_type=jnp.float32)
    ffn_rows = lax.psum_scatter(
        ffn_part.astype(jnp.bfloat16), "mp", scatter_dimension=0, tiled=True
    ).astype(jnp.float32)
    residual_two = ffn_rows + out_biases[1] + first
    result = norm_rows(residual_two, norm_gains[1], norm_shifts[1])
    kept_values = (
        gathered,
        heads_view,
        weights_soft,
        attended,
        residual_one,
        first_all,
        pre_act,
        activated,
        residual_two,
    )
    return (result, kept_values)


def layer_backward(params, kept_values, grad_out):
    (
        w_qkv,
        qv_bias,
        w_attn_out,
        w_ffn_in,
        ffn_in_bias,
        w_ffn_out,
        out_biases,
        norm_gains,
        norm_shifts,
    ) = params
    (
        gathered,
        heads_view,
        weights_soft,
        attended,
        residual_one,
        first_all,
        pre_act,
        activated,
        residual_two,
    ) = kept_values
    rows_all = gathered.shape[0]
    local_width = w_qkv.shape[2]
    local_heads = local_width // HEAD_DIM
    page_count = rows_all // SEQ
    scale_factor = 1.0 / math.sqrt(HEAD_DIM)
    unused_two, norm_two_back = jax.vjp(norm_rows, residual_two, norm_gains[1], norm_shifts[1])
    grad_res_two, grad_gain_two, grad_shift_two = norm_two_back(grad_out)
    grad_bias_two = jnp.sum(grad_res_two, axis=0)
    ffn_grad_all = lax.all_gather(grad_res_two.astype(jnp.bfloat16), "mp", axis=0, tiled=True)
    grad_w_ffn_out = jnp.einsum(
        "rf,rd->fd", activated, ffn_grad_all, preferred_element_type=jnp.float32
    )
    grad_act = jnp.einsum("rd,fd->rf", ffn_grad_all, w_ffn_out, preferred_element_type=jnp.float32)
    unused_gelu, gelu_back = jax.vjp(exact_gelu, pre_act)
    grad_pre = gelu_back(grad_act)[0].astype(jnp.bfloat16)
    grad_ffn_in_bias = jnp.sum(grad_pre.astype(jnp.float32), axis=0)
    grad_w_ffn_in = jnp.einsum("rd,rf->df", first_all, grad_pre, preferred_element_type=jnp.float32)
    first_part = jnp.einsum("rf,df->rd", grad_pre, w_ffn_in, preferred_element_type=jnp.float32)
    first_grad_rows = lax.psum_scatter(
        first_part.astype(jnp.bfloat16), "mp", scatter_dimension=0, tiled=True
    ).astype(jnp.float32)
    grad_first = first_grad_rows + grad_res_two
    unused_one, norm_one_back = jax.vjp(norm_rows, residual_one, norm_gains[0], norm_shifts[0])
    grad_res_one, grad_gain_one, grad_shift_one = norm_one_back(grad_first)
    grad_bias_one = jnp.sum(grad_res_one, axis=0)
    attn_grad_all = lax.all_gather(grad_res_one.astype(jnp.bfloat16), "mp", axis=0, tiled=True)
    grad_w_attn_out = jnp.einsum(
        "rk,rd->kd", attended, attn_grad_all, preferred_element_type=jnp.float32
    )
    grad_attended = jnp.einsum(
        "rd,kd->rk", attn_grad_all, w_attn_out, preferred_element_type=jnp.float32
    )
    grad_attended = grad_attended.astype(jnp.bfloat16).reshape(
        page_count, SEQ, local_heads, HEAD_DIM
    )
    weights_low = weights_soft.astype(jnp.bfloat16)
    grad_weights = jnp.einsum(
        "pqhe,pkhe->phqk", grad_attended, heads_view[2], preferred_element_type=jnp.float32
    )
    grad_values = jnp.einsum(
        "phqk,pqhe->pkhe", weights_low, grad_attended, preferred_element_type=jnp.float32
    )
    inner_total = jnp.sum(weights_soft * grad_weights, axis=-1, keepdims=True)
    grad_scores = (weights_soft * (grad_weights - inner_total)).astype(jnp.bfloat16)
    grad_queries = (
        jnp.einsum(
            "phqk,pkhe->pqhe", grad_scores, heads_view[1], preferred_element_type=jnp.float32
        )
        * scale_factor
    )
    grad_keys = (
        jnp.einsum(
            "phqk,pqhe->pkhe", grad_scores, heads_view[0], preferred_element_type=jnp.float32
        )
        * scale_factor
    )
    grad_proj = (
        jnp.stack([grad_queries, grad_keys, grad_values])
        .reshape(3, rows_all, local_width)
        .astype(jnp.bfloat16)
    )
    proj_sums = jnp.sum(grad_proj.astype(jnp.float32), axis=1)
    grad_qv_bias = jnp.stack([proj_sums[0], proj_sums[2]])
    grad_w_qkv = jnp.einsum("rd,cre->cde", gathered, grad_proj, preferred_element_type=jnp.float32)
    input_part = jnp.einsum("cre,cde->rd", grad_proj, w_qkv, preferred_element_type=jnp.float32)
    input_grad_rows = lax.psum_scatter(
        input_part.astype(jnp.bfloat16), "mp", scatter_dimension=0, tiled=True
    ).astype(jnp.float32)
    grad_in = input_grad_rows + grad_res_one
    matrix_grads = (
        grad_w_qkv,
        grad_qv_bias,
        grad_w_attn_out,
        grad_w_ffn_in,
        grad_ffn_in_bias,
        grad_w_ffn_out,
    )
    vector_grads = (
        jnp.stack([grad_bias_one, grad_bias_two]),
        jnp.stack([grad_gain_one, grad_gain_two]),
        jnp.stack([grad_shift_one, grad_shift_two]),
    )
    return (grad_in, matrix_grads, vector_grads)


def pipelined(
    token_in,
    cotangent,
    w_qkv,
    qv_bias,
    w_attn_out,
    w_ffn_in,
    ffn_in_bias,
    w_ffn_out,
    out_biases,
    norm_gains,
    norm_shifts,
):
    params = (
        w_qkv[0],
        qv_bias[0],
        w_attn_out[0],
        w_ffn_in[0],
        ffn_in_bias[0],
        w_ffn_out[0],
        out_biases[0],
        norm_gains[0],
        norm_shifts[0],
    )
    micro_count = token_in.shape[0]
    section_index = lax.axis_index("section")
    is_first = section_index == 0
    zero_rows = jnp.zeros(token_in.shape[1:], jnp.bfloat16)
    run_forward = partial(layer_forward, params)
    run_backward = partial(layer_backward, params)

    def forward_step(step_index, carry):
        received, saved, stored = carry
        own_micro = step_index - section_index
        is_valid = (own_micro >= 0) & (own_micro < micro_count)
        slot_index = jnp.clip(own_micro, 0, micro_count - 1)
        first_rows = lax.dynamic_index_in_dim(
            token_in, jnp.minimum(step_index, micro_count - 1).astype(jnp.int32), 0, keepdims=False
        )
        layer_in = jnp.where(is_first, first_rows, received)
        result, unused_kept = run_forward(layer_in)
        result_low = result.astype(jnp.bfloat16)
        old_saved = lax.dynamic_index_in_dim(saved, slot_index, 0, keepdims=False)
        saved = lax.dynamic_update_index_in_dim(
            saved, jnp.where(is_valid, layer_in, old_saved), slot_index, 0
        )
        old_stored = lax.dynamic_index_in_dim(stored, slot_index, 0, keepdims=False)
        stored = lax.dynamic_update_index_in_dim(
            stored, jnp.where(is_valid, result_low, old_stored), slot_index, 0
        )
        received = from_behind(result_low, "section", 1)
        return (received, saved, stored)

    start_carry = (zero_rows, jnp.zeros_like(token_in), jnp.zeros_like(token_in))
    unused_received, saved, stored = lax.fori_loop(0, micro_count + 1, forward_step, start_carry)
    matrix_zero = tuple((jnp.zeros(entry.shape, jnp.float32) for entry in params[:6]))
    vector_zero = (
        jnp.zeros(out_biases.shape[1:], jnp.float32),
        jnp.zeros(norm_gains.shape[1:], jnp.float32),
        jnp.zeros(norm_shifts.shape[1:], jnp.float32),
    )

    def backward_step(step_index, carry):
        received_grad, grad_store, matrix_sums, vector_sums = carry
        own_micro = step_index - (1 - section_index)
        is_valid = (own_micro >= 0) & (own_micro < micro_count)
        slot_index = jnp.clip(own_micro, 0, micro_count - 1)
        layer_in = lax.dynamic_index_in_dim(saved, slot_index, 0, keepdims=False)
        from_last = lax.dynamic_index_in_dim(cotangent, slot_index, 0, keepdims=False)
        grad_out = jnp.where(is_first, received_grad, from_last).astype(jnp.float32)
        unused_result, kept_values = run_forward(layer_in)
        grad_in, matrix_grads, vector_grads = run_backward(kept_values, grad_out)
        matrix_grads = tuple((jnp.where(is_valid, entry, 0.0) for entry in matrix_grads))
        vector_grads = tuple((jnp.where(is_valid, entry, 0.0) for entry in vector_grads))
        grad_low = grad_in.astype(jnp.bfloat16)
        old_piece = lax.dynamic_index_in_dim(grad_store, slot_index, 0, keepdims=False)
        grad_store = lax.dynamic_update_index_in_dim(
            grad_store, jnp.where(is_valid, grad_low, old_piece), slot_index, 0
        )
        grad_one, grad_two, grad_three, grad_four, grad_five, grad_six = matrix_grads
        matrix_grads = (
            lax.psum(grad_one.astype(jnp.bfloat16), "dp").astype(jnp.float32),
            lax.psum(grad_two.astype(jnp.bfloat16), "dp").astype(jnp.float32),
            lax.psum(grad_three.astype(jnp.bfloat16), "dp").astype(jnp.float32),
            lax.psum(grad_four.astype(jnp.bfloat16), "dp").astype(jnp.float32),
            lax.psum(grad_five.astype(jnp.bfloat16), "dp").astype(jnp.float32),
            lax.psum(grad_six.astype(jnp.bfloat16), "dp").astype(jnp.float32),
        )
        matrix_sums = tuple((total + extra for total, extra in zip(matrix_sums, matrix_grads)))
        vector_sums = tuple((total + extra for total, extra in zip(vector_sums, vector_grads)))
        received_grad = from_behind(grad_low, "section", -1)
        return (received_grad, grad_store, matrix_sums, vector_sums)

    back_carry = (zero_rows, jnp.zeros_like(token_in), matrix_zero, vector_zero)
    unused_grad, grad_store, matrix_sums, vector_sums = lax.fori_loop(
        0, micro_count + 1, backward_step, back_carry
    )
    bias_total, gain_total, shift_total = vector_sums
    bias_part, gain_part, shift_part = (
        lax.psum_scatter(bias_total, ("mp", "dp"), scatter_dimension=1, tiled=True),
        lax.psum_scatter(gain_total, ("mp", "dp"), scatter_dimension=1, tiled=True),
        lax.psum_scatter(shift_total, ("mp", "dp"), scatter_dimension=1, tiled=True),
    )
    return (
        stored[None],
        grad_store[None],
        matrix_sums[0][None],
        matrix_sums[1][None],
        matrix_sums[2][None],
        matrix_sums[3][None],
        matrix_sums[4][None],
        matrix_sums[5][None],
        bias_part[None],
        gain_part[None],
        shift_part[None],
    )


MESH = pl.DeviceIdType.MESH
CHUNKS = 24
TRIPLES = 8
SCALE = 0.125


def low(value):
    return value.astype(jnp.bfloat16)


def high(value):
    return value.astype(jnp.float32)


def remote(src, dst, send, recv, device):
    return pltpu.make_async_remote_copy(
        src_ref=src, dst_ref=dst, send_sem=send, recv_sem=recv, device_id=device, device_id_type=MESH
    )


def neighbours():
    c, p, d = lax.axis_index("section"), lax.axis_index("mp"), lax.axis_index("dp")
    return {
        "core": (1 - c, p, d),
        "x": (c, p + 1 - 2 * lax.rem(p, 2), d),
        "y": (c, lax.rem(p + 2, 4), d),
        "across": (c, p, 3 - d),
        "inner": (c, p, jnp.where(d == 0, 1, 2)),
        "outer": (c, p, jnp.where(d == 1, 0, 3)),
    }


def places():
    p = lax.axis_index("mp")
    return [p, p + 1 - 2 * lax.rem(p, 2), lax.rem(p + 2, 4), 3 - p]


def dot(a, b):
    return jnp.dot(a, b, preferred_element_type=jnp.float32)


def dot_tn(a, b):
    return lax.dot_general(a, b, (((0,), (0,)), ((), ())), preferred_element_type=jnp.float32)


def dot_nt(a, b):
    return lax.dot_general(a, b, (((1,), (1,)), ((), ())), preferred_element_type=jnp.float32)


def standard(values):
    average = jnp.mean(values, axis=-1, keepdims=True)
    centered = values - average
    variance = jnp.mean(centered * centered, axis=-1, keepdims=True)
    scale = lax.rsqrt(variance + 1e-05)
    return centered * scale, scale


def softmax(q, k):
    scores = dot_nt(q * jnp.asarray(SCALE, q.dtype), k)
    top = jnp.max(scores, axis=-1, keepdims=True)
    exponent = jnp.exp(scores - top)
    total = jnp.sum(exponent, axis=-1, keepdims=True)
    return exponent * (1.0 / total), top + jnp.log(total)


def by_rows(rows, step, body):
    def run(i, carry):
        body(pl.ds(pl.multiple_of(i * step, step), step))
        return carry

    lax.fori_loop(0, rows // step, run, 0)


def first_norm(x, nrm, acc, u1, hb):
    def run(rows):
        u = acc[rows] + nrm[0:1] + high(x[rows])
        u1[rows] = u
        h = standard(u)[0] * nrm[2:3] + nrm[4:5]
        hb[rows] = low(h)
        acc[rows] = h + nrm[1:2]

    by_rows(acc.shape[0], 64, run)


def second_norm(nrm, acc, u2, out):
    def run(rows):
        u = acc[rows]
        u2[rows] = u
        out[rows] = low(standard(u)[0] * nrm[3:4] + nrm[5:6])

    by_rows(acc.shape[0], 64, run)


def norm_back(u, grad, gain, sums, at, out_low, out_acc):
    def run(rows):
        g = high(grad[rows])
        xhat, scale = standard(u[rows])
        scaled = g * gain
        du = scale * (
            scaled
            - jnp.mean(scaled, axis=-1, keepdims=True)
            - xhat * jnp.mean(scaled * xhat, axis=-1, keepdims=True)
        )
        out_low[rows] = low(du)
        out_acc[rows] = du
        for row, term in ((at[0], du), (at[1], g * xhat), (at[2], g)):
            sums[row : row + 1] += jnp.sum(term, axis=0, keepdims=True)

    by_rows(u.shape[0], 64, run)


def ffn_back_block(dfb, w, gd, acc, dz_out):
    dz = low(dot_nt(dfb[...], w[1]) * high(gd))
    dz_out[...] = dz
    acc[...] += dot(dz, w[0])
    return jnp.sum(high(dz), axis=0, keepdims=True)


def attention_back_block(dab, w, qkv, logs, dq_out, dk_out, dv_out, acc, dim):
    dob = low(dot_nt(dab[...], w[3]))
    for j in range(dob.shape[1] // dim):
        cols = slice(j * dim, (j + 1) * dim)
        q, k, v, do = qkv[0, :, cols], qkv[1, :, cols], qkv[2, :, cols], dob[:, cols]
        a = jnp.exp(dot_nt(q * jnp.asarray(SCALE, q.dtype), k) - logs[:, j : j + 1])
        da = dot_nt(do, v)
        ds = low(a * (da - jnp.sum(a * da, axis=-1, keepdims=True)))
        dv_out[:, cols] = low(dot_tn(low(a), do))
        dq_out[:, cols] = low(dot(ds, k) * SCALE)
        dk_out[:, cols] = low(dot_tn(ds, q) * SCALE)
    acc[...] += dot(dq_out[...], w[0]) + dot(dk_out[...], w[1]) + dot(dv_out[...], w[2])


def weight_copies(full, layer, kind, p, b, buf, sem, rows):
    width = 4 * rows
    if kind == 0:
        starts = [c * width + p * rows for c in range(4)]
    else:
        starts = [4 * width + t * 4 * width + p * width + b * rows for t in range(2)]
    return [
        pltpu.make_async_copy(full.at[layer, pl.ds(pl.multiple_of(start, rows), rows)], buf.at[n], sem.at[n])
        for n, start in enumerate(starts)
    ]


def project_block(x, w, vec, save, logs, dim):
    rows = x[...]
    q = low(dot_nt(rows, w[0]) + vec[0:1])
    k = low(dot_nt(rows, w[1]))
    v = low(dot_nt(rows, w[2]) + vec[1:2])
    save[0], save[1], save[2] = q, k, v
    for j in range(q.shape[1] // dim):
        cols = slice(j * dim, (j + 1) * dim)
        soft, logs[:, j : j + 1] = softmax(q[:, cols], k[:, cols])
        save[3, :, cols] = low(dot(low(soft), v[:, cols]))


def unit_values(hb, w, bias):
    z = dot_nt(hb[...], w) + bias
    inner = 0.5 + 0.5 * lax.erf(z * math.sqrt(0.5))
    slope = inner + z * jnp.exp(-0.5 * z * z) * (1.0 / math.sqrt(2.0 * math.pi))
    return low(z * inner), low(slope)


def gather_forward_kernel(
    dim, tokens, qkv_in, out_in, up_in, down_in, qv, up_bias, biases, gains, shifts, full, vecs, norms, qkvo, logs, gd, us, hbs, between, acts,
    turned, x, acc, u, hb, wa, wf, sa, gb, sd, wasem, wfsem, sasem, gbsem, sdsem, usem, vec, norm_in, lb, lbsem,
    w_qkv, w_out, w_up, w_down, rawsem,
    ini_s, ini_r, loc, x1ss, x1rs, y1ss, y1rs, x2ss, x2rs, y2ss, y2rs, zs, zr, cs, cr, vs, vr, vloc, as_, ar,
):
    c, p, d = lax.axis_index("section"), lax.axis_index("mp"), lax.axis_index("dp")
    near = neighbours()
    near["pair"] = (c, p, d + 1 - 2 * lax.rem(d, 2))
    spots = places()
    rows = w_out.shape[0] // 2
    half = rows // 2
    odd = lax.rem(d, 2)
    others = [(cc, spots[r], d) for r in range(4) for cc in (c, 1 - c)][1:]

    def place_of(s, spot, h):
        k = lax.rem(s, 12)
        row = jnp.where(k < 4, k * 8 + spot * 2, 32 + (k // 4 - 1) * 32 + spot * 8 + lax.rem(k, 4) * 2)
        return s // 12, (row + h) * rows

    def block(s, spot, h, start=0, size=rows):
        layer, row = place_of(s, spot, h)
        return full.at[layer, pl.ds(pl.multiple_of(row + start, half), size)]

    def init_place(k, layer):
        row = place_of(12 * layer + k, p, 0)[1]
        return full.at[layer, pl.ds(pl.multiple_of(row, half), 2 * rows)]

    def turn(k):
        if k < 3:
            turned[k] = w_qkv[k].T
        elif 4 <= k < 8:
            turned[k - 1] = w_up[:, 2 * rows * (k - 4) : 2 * rows * (k - 3)].T

    def chunk(k):
        if k == 3:
            return w_out
        if k < 8:
            return turned.at[k if k < 3 else k - 1]
        return w_down.at[pl.ds(2 * rows * (k - 8), 2 * rows)]

    def init_start(k):
        if k > 2:
            turn(k)
        pltpu.make_async_copy(chunk(k), init_place(k, c), loc.at[k]).start()
        remote(chunk(k), init_place(k, c), ini_s.at[k], ini_r.at[k], near["core"]).start()

    def init_local(k):
        return pltpu.make_async_copy(init_place(k, c), init_place(k, c), loc.at[k])

    def init_wait(k):
        there = init_place(k, 1 - c)
        remote(there, there, ini_s.at[k], ini_r.at[k], near["core"]).wait_recv()

    def small():
        copies = [remote(vec, vecs.at[c, p], vs.at[i], vr.at[c, p], device) for i, device in enumerate(others)]
        copies.append(remote(norm_in, norms.at[c], vs.at[7], vr.at[0, 4], near["core"]))
        return copies

    def small_local():
        return [
            pltpu.make_async_copy(vec, vecs.at[c, p], vloc.at[0]),
            pltpu.make_async_copy(norm_in, norms.at[c], vloc.at[1]),
        ]

    def hop(s, spot, name, pick):
        ss, rs = (x1ss, x1rs) if pick == "x" else (y1ss, y1rs)
        b = block(s, spot, c)
        return remote(b, b, ss.at[s], rs.at[s], near[name])

    def first(s, name):
        return hop(s, p, name, name)

    def arrived(s, name):
        return hop(s, spots[1] if name == "x" else spots[2], name, name)

    def relay(s, name, spot=None):
        if name == "x":
            b = block(s, spots[2] if spot is None else spot, c, 0, half)
            return remote(b, b, x2ss.at[s], x2rs.at[s], near["x"])
        b = block(s, spots[1] if spot is None else spot, c, half, half)
        return remote(b, b, y2ss.at[s], y2rs.at[s], near["y"])

    def relayed(s, name):
        return relay(s, name, spots[3])

    def to_pair(s, r):
        b = block(s, spots[r], c)
        return remote(b, b, zs.at[s, r - 1], zr.at[s, r - 1], near["pair"])

    def to_core(s, r):
        b = block(s, spots[r], c)
        return remote(b, b, cs.at[s, r - 1], cr.at[s, r - 1], near["core"])

    def from_core(s, r):
        b = block(s, spots[r], 1 - c)
        return remote(b, b, cs.at[s, r - 1], cr.at[s, r - 1], near["core"])

    def sent_chunk(j):
        t, n = j // 2, lax.rem(j, 2)
        return 3 * t + (1 - n) * (1 + odd), n == 0

    def stage_a(j):
        s = sent_chunk(j)[0]
        for m in range(3):
            own = 3 * (j // 2) + m

            @pl.when((own // 12 != c) & (lax.rem(j, 2) == 0))
            def _():
                init_wait(lax.rem(own, 12))

            @pl.when((own // 12 == c) & (lax.rem(j, 2) == 0))
            def _():
                init_local(lax.rem(own, 12)).wait()

        first(s, "x").start()
        first(s, "y").start()

    def stage_b(j):
        s, shared = sent_chunk(j)
        arrived(s, "x").wait_recv()
        relay(s, "y").start()
        arrived(s, "y").wait_recv()
        relay(s, "x").start()
        for r in (1, 2):
            to_core(s, r).start()

        @pl.when(shared)
        def _():
            for r in (1, 2):
                to_pair(s, r).start()

    def stage_c(j):
        s, shared = sent_chunk(j)
        relayed(s, "x").wait_recv()
        relayed(s, "y").wait_recv()
        to_core(s, 3).start()

        @pl.when(shared)
        def _():
            to_pair(s, 3).start()

    def stage_d(t):
        s = 3 * t + 2 - odd
        for r in (1, 2, 3):
            to_pair(s, r).wait_recv()
            to_core(s, r).start()

    def stage_e(t):
        for j in range(3):
            for r in (1, 2, 3):
                from_core(3 * t + j, r).wait_recv()

    def stage_f(t):
        for n, s in enumerate((3 * t, 3 * t + 1 + odd)):
            first(s, "x").wait_send()
            first(s, "y").wait_send()
            relay(s, "x").wait_send()
            relay(s, "y").wait_send()
            for r in (1, 2, 3):
                if n:
                    to_pair(s, r).wait_send()
        for j in range(3):
            for r in (1, 2, 3):
                to_core(3 * t + j, r).wait_send()

    wide = 2 * rows

    def weights(l, number, place, sem):
        begin = pl.multiple_of(number * wide, wide)
        return pltpu.make_async_copy(full.at[l, pl.ds(begin, wide)], place, sem)

    def load_qkv(l, q):
        return [weights(l, 4 * n + q, wa.at[q, n], wasem.at[q, n]) for n in range(3)]

    def load(l, number, slot):
        return weights(l, number, wf.at[slot], wfsem.at[slot])

    def load_out(l, q):
        return load(l, 12 + q, q)

    def load_in(l, b, q, slot):
        return load(l, 16 + 4 * q + b, slot)

    def load_down(l, b, q, slot):
        return load(l, 32 + 4 * q + b, slot)

    def load_last(l, q):
        return weights(l, 32 + 4 * q + 3, wa.at[q, 0], wasem.at[q, 0])

    def save_attn(l, q):
        return pltpu.make_async_copy(sa.at[q], qkvo.at[l, q], sasem.at[q])

    def save_logs(l, q):
        return pltpu.make_async_copy(lb.at[q], logs.at[l, q], lbsem.at[q])

    def save_g(l, n):
        return pltpu.make_async_copy(gb.at[n], gd.at[l, n, 0], gbsem.at[n])

    def save_d(l, n, slot):
        return pltpu.make_async_copy(sd.at[slot], gd.at[l, n, 1], sdsem.at[slot])

    def keep(l, which):
        if which == 2:
            return pltpu.make_async_copy(hb, hbs.at[l], usem.at[2])
        if which == 3:
            return pltpu.make_async_copy(x, between, usem.at[3])
        return pltpu.make_async_copy(u, us.at[l, which], usem.at[which])

    def give(begin):
        @pl.when(c == 0)
        def _():
            copy = pltpu.make_async_copy(x, acts.at[0], as_.at[0])
            copy.start() if begin else copy.wait()

        @pl.when(c == 1)
        def _():
            copy = remote(x, acts.at[1], as_.at[0], ar.at[0], near["core"])
            copy.start() if begin else copy.wait_send()

    def last_sum():
        return pltpu.make_async_copy(acc, us.at[1, 1], usem.at[1])

    def each(count, body):
        def run(q, carry):
            body(q)
            return carry

        lax.fori_loop(0, count, run, 0)

    def attention_segment(l, q):
        for copy in load_qkv(l, q):
            copy.wait()
        project_block(x, wa.at[q], vecs[l, q], sa.at[q], lb.at[q], dim)
        save_attn(l, q).start()
        save_logs(l, q).start()

    def out_segment(l):
        @pl.when(l == 1)
        def _():
            keep(0, 1).wait()

        acc[...] = jnp.zeros_like(acc)

        def branch(q):
            load_out(l, q).wait()
            acc[...] += dot(sa[q, 3], wf[q])
            load_in(l, 1, q, q).start()

        each(4, branch)
        first_norm(x, norms.at[l], acc, u, hb)
        keep(l, 0).start()
        keep(l, 2).start()

    def up_segment(l, b, slot):
        for q in range(4):
            load_in(l, b, q, slot + q).wait()
        for q in range(4):
            g, slope = unit_values(hb, wf[slot + q], vecs[l, q, pl.ds(2 + b, 1)])
            gb[4 * q + b] = g
            sd[q] = slope
        for q in range(4):
            save_g(l, 4 * q + b).start()
            save_d(l, 4 * q + b, q).start()

    def up_saved(l, b):
        for q in range(4):
            save_d(l, 4 * q + b, q).wait()

    def down_segment(l, b, slot):
        for q in range(4):
            load_down(l, b, q, slot + q).wait()
        first_two = dot(gb[b], wf[slot]) + dot(gb[4 + b], wf[slot + 1])
        acc[...] += first_two + dot(gb[8 + b], wf[slot + 2]) + dot(gb[12 + b], wf[slot + 3])

    def end_segment(l):
        keep(l, 0).wait()
        keep(l, 2).wait()
        each(4, lambda q: save_attn(l, q).wait())
        each(4, lambda q: save_logs(l, q).wait())
        each(16, lambda n: save_g(l, n).wait())

        @pl.when(l == 0)
        def _():
            second_norm(norms.at[0], acc, u, x)
            keep(0, 1).start()
            give(True)
            keep(0, 3).start()

        @pl.when(l == 1)
        def _():
            last_sum().start()

    def small_there():
        for copy in small_local():
            copy.wait()
        for copy in small():
            copy.wait_send()
        for cc, spot in [(cc, spots[r]) for r in range(4) for cc in (c, 1 - c)][1:]:
            remote(vec, vecs.at[cc, spot], vs.at[0], vr.at[cc, spot], near["core"]).wait_recv()
        remote(norm_in, norms.at[1 - c], vs.at[7], vr.at[0, 4], near["core"]).wait_recv()

    def compute(m):
        l, part = m // 8, lax.rem(m, 8)

        def at(number, body):
            @pl.when(part == number)
            def _():
                body()

        def attention_first():
            for q in range(4):
                for copy in load_qkv(l, q):
                    copy.start()

            @pl.when(m == 0)
            def _():
                small_there()
                first_rows.wait()

        def attention_half(begin):
            each(2, lambda q: attention_segment(l, begin + q))

        def out_part():
            for q in range(4):
                load_out(l, q).start()
            for q in range(4):
                load_in(l, 0, q, 4 + q).start()
            out_segment(l)

        def up_part():
            for q in range(4):
                load_in(l, 2, q, q).start()
            for q in range(4):
                load_in(l, 3, q, 4 + q).start()
            up_saved(l, 1)
            up_segment(l, 2, 0)
            for q in range(4):
                load_down(l, 0, q, q).start()

        def turn_part():
            up_saved(l, 2)
            up_segment(l, 3, 4)
            down_segment(l, 0, 0)

        def down_part():
            for b in (1, 2):
                for q in range(4):
                    load_down(l, b, q, 4 * (b - 1) + q).start()
            for q in range(4):
                load_last(l, q).start()
            up_saved(l, 3)
            down_segment(l, 1, 0)
            down_segment(l, 2, 4)

        def end_part():
            for q in range(4):
                load_last(l, q).wait()
            first_two = dot(gb[3], wa[0, 0]) + dot(gb[7], wa[1, 0])
            acc[...] += first_two + dot(gb[11], wa[2, 0]) + dot(gb[15], wa[3, 0])
            end_segment(l)

        at(0, attention_first)

        @pl.when(part < 2)
        def _():
            attention_half(2 * part)

        at(2, out_part)

        @pl.when((part == 2) | (part == 3))
        def _():
            b = part - 2

            @pl.when(b == 1)
            def _():
                up_saved(l, 0)

            up_segment(l, b, 4 - 4 * b)

        at(4, up_part)
        at(5, turn_part)
        at(6, down_part)
        at(7, end_part)

    first_rows = pltpu.make_async_copy(tokens.at[c], x, usem.at[4])
    raw = [
        pltpu.make_async_copy(source, place, rawsem.at[n])
        for n, (source, place) in enumerate(
            ((qkv_in, w_qkv), (out_in, w_out), (up_in, w_up), (down_in, w_down))
        )
    ]
    for copy in raw:
        copy.start()
    first_rows.start()
    vec[...] = jnp.zeros_like(vec)
    vec[0:2] = high(qv[...])
    for b in range(4):
        vec[2 + b : 3 + b] = high(up_bias[:, 2 * rows * b : 2 * rows * (b + 1)])
    norm_in[...] = jnp.zeros_like(norm_in)
    norm_in[0:2], norm_in[2:4], norm_in[4:6] = biases[...], gains[...], shifts[...]
    barrier = pltpu.get_barrier_semaphore()
    for device in others + [near["pair"]]:
        pl.semaphore_signal(barrier, inc=1, device_id=device, device_id_type=MESH)
    raw[0].wait()
    for k in range(3):
        turn(k)
    pl.semaphore_wait(barrier, 8)
    for k in range(3):
        init_start(k)
    for copy in small_local() + small():
        copy.start()

    def step(count, carry):
        i = count - 1

        def run(stage, lag):
            @pl.when((i >= lag) & (i < 2 * TRIPLES + lag))
            def _():
                stage(i - lag)

        def run_late(stage, lag):
            @pl.when((i >= lag) & (i < 2 * TRIPLES + lag) & (lax.rem(i - lag, 2) == 0))
            def _():
                stage((i - lag) // 2)

        run(stage_b, 1)
        run(stage_a, -1)
        run(stage_c, 2)
        run_late(stage_e, 4)
        run_late(stage_f, 6)
        for t in range(3):

            @pl.when(i == 2 * t)
            def _():
                if t == 0:
                    for copy in raw[1:]:
                        copy.wait()
                for k in range(3 * t + 3, 3 * t + 6):
                    init_start(k)

        run_late(stage_d, 3)
        run(compute, 4)
        return carry

    lax.fori_loop(0, 2 * TRIPLES + 6, step, 0)

    for k in range(12):
        remote(chunk(k), init_place(k, c), ini_s.at[k], ini_r.at[k], near["core"]).wait_send()
    keep(0, 3).wait()
    give(False)
    last_sum().wait()

    @pl.when(c == 0)
    def _():
        remote(x, acts.at[1], as_.at[0], ar.at[0], near["core"]).wait_recv()


def gather_forward(dim, tokens, w_qkv, w_out, w_up, w_down, qv, up_bias, biases, gains, shifts):
    rows, width = w_out.shape
    seq = tokens.shape[1]
    bf, f32, dma, v = jnp.bfloat16, jnp.float32, pltpu.SemaphoreType.DMA, pltpu.VMEM
    hbm, vmem = pl.BlockSpec(memory_space=pl.ANY), pl.BlockSpec(memory_space=pltpu.VMEM)
    S = jax.ShapeDtypeStruct
    return pl.pallas_call(
        functools.partial(gather_forward_kernel, dim),
        out_shape=(
            S((2, 48 * rows, width), bf), S((2, 4, 8, rows), f32), S((2, 8, width), f32),
            S((2, 4, 4, seq, rows), bf), S((2, 4, seq, 128), f32), S((2, 16, 2, seq, rows), bf), S((2, 2, seq, width), f32),
            S((2, seq, width), bf), S((seq, width), bf), S((2, seq, width), bf),
        ),
        in_specs=[hbm] * 5 + [vmem] * 5,
        out_specs=[hbm, vmem, vmem] + [hbm] * 7,
        scratch_shapes=[
            v((7, rows, width), bf),
            v((seq, width), bf), v((seq, width), f32), v((seq, width), f32), v((seq, width), bf),
            v((4, 3, rows, width), bf), v((8, rows, width), bf), v((4, 4, seq, rows), bf), v((16, seq, rows), bf),
            v((4, seq, rows), bf), dma((4, 3)), dma((8,)), dma((4,)), dma((16,)), dma((4,)), dma((5,)),
            v((8, rows), f32), v((8, width), f32), v((4, seq, 128), f32), dma((4,)),
            v(w_qkv.shape, bf), v(w_out.shape, bf), v(w_up.shape, bf), v(w_down.shape, bf), dma((4,)),
        ] + [dma((12,))] * 3 + [dma((24,))] * 8 + [dma((24, 3))] * 4
        + [dma((8,)), dma((2, 5)), dma((2,)), dma((1,)), dma((1,))],
        compiler_params=pltpu.CompilerParams(collective_id=0, has_side_effects=True, vmem_limit_bytes=60 * 2**20),
    )(tokens, w_qkv, w_out, w_up, w_down, qv, up_bias, biases, gains, shifts)


def backward_reduce_kernel(
    dim, tokens, cots, full, norms, qkvo, logs, gd, us, hbs, between, out, grads, acts, totals,
    left, right, acc, g, u, wa, wf, da, df, dl, dlsem, trades,
    sendc, recvc, keep, x1s, x1r, y1s, y1r, part, base, x2s, x2r, y2s, y2r, mid,
    zk, zs1, zr1, zs2, zr2, zs3, zr3,
    wasem, wfsem, dasem, dfsem, gsem, osem4, bsem, gds, gdr, as_, ar, tss, trs,
    cs, cr, x1ss, x1rs, y1ss, y1rs, x2ss, x2rs, y2ss, y2rs, z1ss, z1rs, z2ss, z2rs, z3ss, z3rs, os, orr,
):
    c, p, d = lax.axis_index("section"), lax.axis_index("mp"), lax.axis_index("dp")
    near = neighbours()
    near["pair"] = (c, p, d + 1 - 2 * lax.rem(d, 2))
    near["far"] = (c, p, lax.rem(d + 2, 4))
    spots = places()
    is_end = (d == 0) | (d == 3)
    is_mid = jnp.logical_not(is_end)
    rows = sendc.shape[2]
    half = rows // 2
    wide = 2 * rows

    def core_copy(s):
        a, b = lax.rem(s, 2), lax.rem(s, 4)
        return remote(sendc.at[a], recvc.at[b], cs.at[a], cr.at[b], near["core"])

    def link_copy(s, src, dst, ss, rs, name):
        a, b = lax.rem(s, 2), lax.rem(s, 4)
        return remote(src.at[a], dst.at[b], ss.at[a], rs.at[b], near[name])

    def first_copy(s, n, src, dst, ss, rs, name):
        a, b = lax.rem(s, 2), lax.rem(s, 4)
        return remote(src.at[a, n], dst.at[b, n], ss.at[a, n], rs.at[b, n], near[name])

    x1 = lambda s, n: first_copy(s, n, x1s, x1r, x1ss, x1rs, "x")
    y1 = lambda s, n: first_copy(s, n, y1s, y1r, y1ss, y1rs, "y")
    x2 = lambda s: link_copy(s, x2s, x2r, x2ss, x2rs, "x")
    y2 = lambda s: link_copy(s, y2s, y2r, y2ss, y2rs, "y")
    z1 = lambda s, n: first_copy(s, n, zs1, zr1, z1ss, z1rs, "inner")
    z2 = lambda s, n: first_copy(s, n, zs2, zr2, z2ss, z2rs, "across")

    def z3(s, n):
        b = lax.rem(s, 6)
        return remote(zs3.at[b, n], zr3.at[b, n], z3ss.at[b, n], z3rs.at[b, n], near["outer"])

    def stage0(s):
        k, slot = lax.rem(s, 12), lax.rem(s, 2)
        stride = jnp.where(k < 8, 4, 1)
        first = jnp.where(k < 4, k, jnp.where(k < 8, 12 + k, jnp.where(k == 8, 32, 36 + 4 * (k - 9))))
        kind = jnp.where(k < 4, 0, jnp.where(k < 8, 1, jnp.where(k == 8, 2, 3)))
        for r in range(4):
            whole = dot_tn(left[first + stride * spots[r]], right[kind])
            keep[slot, r] = jnp.where(c == 0, whole[:rows], whole[rows:])
            sendc[slot, r] = low(jnp.where(c == 0, whole[rows:], whole[:rows]))
        core_copy(s).start()

    def stage1(s):
        a, b = lax.rem(s, 2), lax.rem(s, 4)
        core_copy(s).wait()
        far = keep[a, 3] + high(recvc[b, 3])
        x1s[a, 0] = low(far[:half])
        y1s[a, 0] = low(far[half:])
        x1(s, 0).start()
        y1(s, 0).start()
        by_x = keep[a, 1] + high(recvc[b, 1])
        x1s[a, 1] = low(by_x[:half])
        part[a, 0] = by_x[half:]
        by_y = keep[a, 2] + high(recvc[b, 2])
        y1s[a, 1] = low(by_y[half:])
        part[a, 1] = by_y[:half]
        x1(s, 1).start()
        y1(s, 1).start()
        base[a] = keep[a, 0] + high(recvc[b, 0])

    def stage2(s):
        a, b = lax.rem(s, 2), lax.rem(s, 4)
        x1(s, 0).wait()
        y2s[a] = low(part[a, 1] + high(x1r[b, 0]))
        y2(s).start()
        y1(s, 0).wait()
        x2s[a] = low(part[a, 0] + high(y1r[b, 0]))
        x2(s).start()
        x1(s, 1).wait()
        y1(s, 1).wait()
        own = base[a]
        mid[a, 0] = own[:half] + high(x1r[b, 1])
        mid[a, 1] = own[half:] + high(y1r[b, 1])

    def stage3(s):
        a, b = lax.rem(s, 2), lax.rem(s, 4)
        for n, copy, got in ((0, y2, y2r), (1, x2, x2r)):
            copy(s).wait()
            total = mid[a, n] + high(got[b])

            @pl.when(is_end)
            def _():
                zs1[a, n] = low(total)
                z1(s, n).start()

            @pl.when(is_mid)
            def _():
                zk[a, n] = total

    def stage4(s):
        a, b = lax.rem(s, 2), lax.rem(s, 4)
        for n in range(2):

            @pl.when(is_end)
            def _():
                z1(s, n).wait_send()

            @pl.when(is_mid)
            def _():
                z1(s, n).wait_recv()
                zs2[a, n] = low(zk[a, n] + high(zr1[b, n]))
                z2(s, n).start()

    def stage5(s):
        a, b, to = lax.rem(s, 2), lax.rem(s, 4), lax.rem(s, 6)

        @pl.when(is_mid)
        def _():
            for n in range(2):
                z2(s, n).wait()
                zs3[to, n] = low(high(zs2[a, n]) + high(zr2[b, n]))
                z3(s, n).start()

    def stage6(s, begin):
        layer, k, b = 1 - s // 12, lax.rem(s, 12), lax.rem(s, 6)

        def finish(source):
            @pl.when(layer == c)
            def _():
                copy = pltpu.make_async_copy(source.at[b], out.at[k, c], os.at[b])
                copy.start() if begin else copy.wait()

            @pl.when(layer != c)
            def _():
                copy = remote(source.at[b], out.at[k, c], os.at[b], orr.at[k], near["core"])
                copy.start() if begin else copy.wait_send()

        @pl.when(is_end)
        def _():
            if begin:
                for n in range(2):
                    z3(s, n).wait_recv()
            finish(zr3)

        @pl.when(is_mid)
        def _():
            if begin:
                for n in range(2):
                    z3(s, n).wait_send()
            finish(zs3)

    def load_g(l, n):
        return pltpu.make_async_copy(gd.at[l, n, 0], left.at[n], gsem.at[n])

    def load_o(l, n):
        return pltpu.make_async_copy(qkvo.at[l, n, 3], left.at[32 + n], osem4.at[n])

    def load_h(l):
        return pltpu.make_async_copy(hbs.at[l], right.at[1], bsem.at[0])

    def load_x(source):
        return pltpu.make_async_copy(source, right.at[3], bsem.at[1])

    def load_u(l, which):
        return pltpu.make_async_copy(us.at[l, which], u, bsem.at[2])

    def ffn(l, n, slot):
        return weight_copies(full, l, 1, lax.rem(n, 4), n // 4, wf.at[slot], wfsem.at[slot], wide) + [
            pltpu.make_async_copy(gd.at[l, 4 * lax.rem(n, 4) + n // 4, 1], df.at[slot], dfsem.at[slot])
        ]

    def attn(l, q, slot):
        return weight_copies(full, l, 0, q, 0, wa.at[slot], wasem.at[slot], wide) + [
            pltpu.make_async_copy(qkvo.at[l, q], da.at[slot], dasem.at[slot]),
            pltpu.make_async_copy(logs.at[l, q], dl.at[slot], dlsem.at[slot]),
        ]

    def store_dx(l, begin):
        @pl.when(l == c)
        def _():
            copy = pltpu.make_async_copy(g, grads.at[c], gds.at[0])
            copy.start() if begin else copy.wait()

        @pl.when(l != c)
        def _():
            copy = remote(g, grads.at[c], gds.at[0], gdr.at[0], near["core"])
            copy.start() if begin else copy.wait_send()

    def give(begin):
        @pl.when(c == 1)
        def _():
            copy = pltpu.make_async_copy(g, acts.at[1], as_.at[0])
            copy.start() if begin else copy.wait()

        @pl.when(c == 0)
        def _():
            copy = remote(g, acts.at[0], as_.at[0], ar.at[0], near["core"])
            copy.start() if begin else copy.wait_send()

    def output():
        load_u(1, 1).wait()
        store_dx(0, False)

        def run(r):
            g[r] = low(standard(u[r])[0] * norms[1, 3:4] + norms[1, 5:6])

        by_rows(u.shape[0], 64, run)
        give(True)

    def ahead(l):
        load_u(l, 1).start()
        for copy in ffn(l, 0, 0) + attn(l, 0, 0):
            copy.start()

    def operands(l):
        def run(n, carry):
            load_g(l, n).start()
            return carry

        lax.fori_loop(0, 16, run, 0)
        for n in range(4):
            load_o(l, n).start()
        load_h(l).start()

    def operands_there(l):
        def run(n, carry):
            load_g(l, n).wait()
            return carry

        lax.fori_loop(0, 16, run, 0)
        for n in range(4):
            load_o(l, n).wait()
        load_h(l).wait()

    def top_segment(l):
        load_u(l, 1).wait()
        norm_back(u, g, norms[l, 3:4], totals.at[l], (1, 3, 5), right.at[0], acc)
        load_u(l, 0).start()

        @pl.when(l == 1)
        def _():
            operands_there(1)

    def ffn_segment(l, b):
        def run(q, carry):
            n = 4 * b + q
            slot = lax.rem(n, 2)
            for copy in ffn(l, n, slot):
                copy.wait()

            @pl.when(n < 15)
            def _():
                for copy in ffn(l, n + 1, 1 - slot):
                    copy.start()

            row = ffn_back_block(right.at[0], wf.at[slot], df[slot], acc, left.at[16 + 4 * q + b])
            totals[l, pl.ds(10 + b, 1), pl.ds(pl.multiple_of(q * wide, wide), wide)] = row
            return carry

        lax.fori_loop(0, 4, run, 0)

    def middle_segment(l):
        load_u(l, 0).wait()
        norm_back(u, acc, norms[l, 2:3], totals.at[l], (0, 2, 4), right.at[2], acc)

    def attention_segment(l, q):
        slot = lax.rem(q, 2)
        for copy in attn(l, q, slot):
            copy.wait()

        @pl.when(q < 3)
        def _():
            for copy in attn(l, q + 1, 1 - slot):
                copy.start()

        dq, dk, dv = left.at[36 + q], left.at[40 + q], left.at[44 + q]
        attention_back_block(right.at[2], wa.at[slot], da.at[slot], dl[slot], dq, dk, dv, acc, dim)
        cols = pl.ds(pl.multiple_of(q * wide, wide), wide)
        totals[l, 8:9, cols] = jnp.sum(high(dq[...]), axis=0, keepdims=True)
        totals[l, 9:10, cols] = jnp.sum(high(dv[...]), axis=0, keepdims=True)

    def end_segment(l):
        by_rows(acc.shape[0], 64, lambda r: g.__setitem__(r, low(acc[r])))
        store_dx(l, True)
        if l == 1:
            ahead(0)

    def segment(i):
        l = jnp.where(i < 8, 1, 0)
        j = jnp.where(i < 8, i, i - 9)
        q = jnp.where(i < 8, i - 4, i - 14)

        @pl.when(i == 8)
        def _():
            end_segment(1)
            operands(0)
            store_dx(1, False)

        @pl.when(i == 7)
        def _():
            load_x(between).wait()

        @pl.when(j == -1)
        def _():
            top_segment(l)

        @pl.when((j >= 0) & (j < 4))
        def _():
            ffn_segment(l, j)

        @pl.when((i == 3) | (i == 13))
        def _():
            middle_segment(l)

        @pl.when((q >= 0) & (q < 4))
        def _():
            attention_segment(l, q)

        @pl.when(i == 18)
        def _():
            end_segment(0)

        @pl.when(i == 10)
        def _():
            operands_there(0)

        @pl.when(i == 12)
        def _():
            load_x(tokens.at[c]).start()

        @pl.when(i == 16)
        def _():
            load_x(tokens.at[c]).wait()

    def trade(k):
        return remote(totals, trades.at[k], tss.at[k], trs.at[k], near[("core", "x", "y", "pair", "far")[k]])

    first_rows = pltpu.make_async_copy(cots.at[c], g, bsem.at[3])
    first_rows.start()
    ahead(1)
    operands(1)
    load_x(between).start()
    totals[...] = jnp.zeros_like(totals)
    barrier = pltpu.get_barrier_semaphore()

    def signal(device):
        pl.semaphore_signal(barrier, inc=1, device_id=device, device_id_type=MESH)

    for name in ("core", "x", "y", "pair", "far"):
        signal(near[name])

    @pl.when(is_end)
    def _():
        pl.semaphore_wait(barrier, 5)

    @pl.when(is_mid)
    def _():
        signal(near["across"])
        pl.semaphore_wait(barrier, 6)

    first_rows.wait()

    def step(count, carry):
        i = count - 1

        def run(stage, lag, *extra):
            @pl.when((i >= lag) & (i < CHUNKS + lag))
            def _():
                stage(i - lag, *extra)

        for lag, stage in enumerate((stage1, stage2, stage3, stage4, stage5)):
            run(stage, lag + 1)
        run(stage6, 6, True)
        run(stage6, 7, False)
        for k in range(6):

            @pl.when(i == 20 + k)
            def _():
                if k:
                    trade(k - 1).wait()
                    totals[...] += trades[k - 1]
                if k < 5:
                    trade(k).start()

        run(stage0, 0)

        @pl.when((i < 20) & (i != 0))
        def _():
            segment(jnp.where(i < 0, i, i - 1))

        @pl.when(i == 20)
        def _():
            load_u(1, 1).start()

        @pl.when(i == 22)
        def _():
            output()


        return carry

    lax.fori_loop(0, CHUNKS + 9, step, 0)
    give(False)

    @pl.when(c == 1)
    def _():
        remote(g, acts.at[0], as_.at[0], ar.at[0], near["core"]).wait_recv()

    remote(g, grads.at[1 - c], gds.at[0], gdr.at[0], near["core"]).wait_recv()
    for k in range(12):
        remote(zs3.at[0], out.at[k, 1 - c], os.at[0], orr.at[k], near["core"]).wait_recv()


def backward_reduce(dim, tokens, cots, full, norms, saved):
    seq, width = tokens.shape[1:]
    wide = width // 4
    block, half = wide // 2, wide // 4
    bf, f32, dma, v = jnp.bfloat16, jnp.float32, pltpu.SemaphoreType.DMA, pltpu.VMEM
    hbm, vmem = pl.BlockSpec(memory_space=pl.ANY), pl.BlockSpec(memory_space=pltpu.VMEM)
    S = jax.ShapeDtypeStruct
    return pl.pallas_call(
        functools.partial(backward_reduce_kernel, dim),
        out_shape=(S((12, 2, 2, half, width), bf), S((2, seq, width), bf), S((2, seq, width), bf),
                   S((2, 16, width), f32)),
        in_specs=[hbm, hbm, hbm, vmem] + [hbm] * 6,
        out_specs=[hbm, hbm, hbm, vmem],
        scratch_shapes=[
            v((48, seq, wide), bf), v((4, seq, width), bf), v((seq, width), f32), v((seq, width), bf),
            v((seq, width), f32),
            v((2, 4, wide, width), bf), v((2, 2, wide, width), bf), v((2, 4, seq, wide), bf), v((2, seq, wide), bf),
            v((2, seq, 128), f32), dma((2,)), v((5, 2, 16, width), f32),
            v((2, 4, block, width), bf), v((4, 4, block, width), bf), v((2, 4, block, width), f32),
            v((2, 2, half, width), bf), v((4, 2, half, width), bf), v((2, 2, half, width), bf), v((4, 2, half, width), bf),
            v((2, 2, half, width), f32), v((2, block, width), f32),
            v((2, half, width), bf), v((4, half, width), bf), v((2, half, width), bf), v((4, half, width), bf),
            v((2, 2, half, width), f32),
            v((2, 2, half, width), f32), v((2, 2, half, width), bf), v((4, 2, half, width), bf),
            v((2, 2, half, width), bf), v((4, 2, half, width), bf), v((6, 2, half, width), bf), v((6, 2, half, width), bf),
            dma((2, 4)), dma((2, 2)), dma((2,)), dma((2,)), dma((16,)), dma((4,)), dma((4,)), dma((1,)), dma((1,)), dma((1,)), dma((1,)),
            dma((5,)), dma((5,)),
        ] + [dma((n,)) for n in (2, 4)] + [dma((n, 2)) for n in (2, 4) * 2] + [dma((n,)) for n in (2, 4) * 2]
        + [dma((n, 2)) for n in (2, 4, 2, 4, 6, 6)] + [dma((6,)), dma((12,))],
        compiler_params=pltpu.CompilerParams(collective_id=1, has_side_effects=True, vmem_limit_bytes=63 * 2**20),
    )(tokens, cots, full, norms, *saved)


def finish_kernel(parts, acts_zero, acts_one, grads_in, totals, acts, grads, g_qkv, g_out, g_up, g_down, g_qv, g_bias,
                  g_biases, g_gains, g_shifts, pb, ab, gb, qb, ob, ub, db, psem, asem, osem):
    def load(k):
        return pltpu.make_async_copy(parts.at[k], pb.at[k], psem.at[k])

    c, p, d = lax.axis_index("section"), lax.axis_index("mp"), lax.axis_index("dp")
    order = (4, 5, 6, 7, 9, 10, 11, 0, 1, 2, 3, 8)
    for k in order:
        load(k).start()

    @pl.when(c == 0)
    def _():
        pltpu.make_async_copy(acts_zero, ab, asem.at[0]).start()

    @pl.when(c == 1)
    def _():
        pltpu.make_async_copy(acts_one, ab, asem.at[0]).start()

    pltpu.make_async_copy(grads_in, gb, asem.at[1]).start()
    others = [(acts_zero, ab, acts, 0), (grads_in, gb, grads, 1)]
    stores = []
    rows = pb.shape[1]
    mine = totals.at[c]
    own = mine[8:16, pl.ds(pl.multiple_of(p * rows, rows), rows)]
    g_qv[...] = own[0:2]
    for b in range(4):
        g_bias[:, b * rows : (b + 1) * rows] = own[2 + b : 3 + b]
    piece = g_gains.shape[1]
    both = mine[0:8, pl.ds(pl.multiple_of(p * rows + d // 2 * 2 * piece, 2 * piece), 2 * piece)]
    both = jnp.where(lax.rem(d, 2) == 0, both[:, :piece], both[:, piece:])
    g_biases[...], g_gains[...], g_shifts[...] = both[0:2], both[2:4], both[4:6]

    def store(source, place):
        copy = pltpu.make_async_copy(source, place, osem.at[len(stores)])
        copy.start()
        stores.append(copy)

    for k in order:
        load(k).wait()
        if k < 4:
            span = pl.ds(k * rows, rows)
            db[span] = high(pb[k])
            store(db.at[span], g_down.at[span])
        elif k < 8:
            ub[:, pl.ds((k - 4) * rows, rows)] = high(pb[k].T)
            if k == 7:
                store(ub, g_up)
        elif k == 8:
            ob[...] = high(pb[k])
            store(ob, g_out)
        else:
            qb[k - 9] = high(pb[k].T)
            store(qb.at[k - 9], g_qkv.at[k - 9])
        if k == 7:
            for source, buffer, place, n in others:
                pltpu.make_async_copy(source, buffer, asem.at[n]).wait()
                store(buffer, place)
    for copy in stores:
        copy.wait()


def finish(parts, acts, acts_one, grads, totals):
    count, rows, width = parts.shape
    bf, f32, dma, v = jnp.bfloat16, jnp.float32, pltpu.SemaphoreType.DMA, pltpu.VMEM
    S = jax.ShapeDtypeStruct
    shapes = [(3, width, rows), (rows, width), (width, width), (width, width)]
    piece = width // (lax.axis_size("mp") * lax.axis_size("dp"))
    hbm, vmem = pl.BlockSpec(memory_space=pl.ANY), pl.BlockSpec(memory_space=pltpu.VMEM)
    vectors = [(2, rows), (1, 4 * rows)] + [(2, piece)] * 3
    return pl.pallas_call(
        finish_kernel,
        out_shape=[S(acts.shape, bf), S(grads.shape, bf)] + [S(shape, f32) for shape in shapes + vectors],
        in_specs=[hbm] * 4 + [vmem],
        out_specs=[hbm] * 6 + [vmem] * 5,
        scratch_shapes=[v(parts.shape, bf), v(acts.shape, bf), v(grads.shape, bf)] + [v(shape, f32) for shape in shapes]
        + [dma((12,)), dma((2,)), dma((11,))],
        compiler_params=pltpu.CompilerParams(vmem_limit_bytes=63 * 2**20),
    )(parts, acts, acts_one, grads, totals)


def by_page(
    token_in,
    cotangent,
    w_qkv,
    qv_bias,
    w_attn_out,
    w_ffn_in,
    ffn_in_bias,
    w_ffn_out,
    out_biases,
    norm_gains,
    norm_shifts,
):
    width = token_in.shape[2]
    full, vecs, norms, *saved, acts = gather_forward(
        HEAD_DIM,
        token_in,
        w_qkv[0],
        w_attn_out[0],
        w_ffn_in[0],
        w_ffn_out[0],
        qv_bias[0],
        ffn_in_bias,
        out_biases[0],
        norm_gains[0],
        norm_shifts[0],
    )
    parts, grads, acts_one, totals = backward_reduce(HEAD_DIM, token_in, cotangent, full, norms, saved)
    results = finish(parts.reshape(12, width // 4, width), acts, acts_one, grads, totals)
    acts, grads, grad_qkv, grad_out, grad_up, grad_down, grad_qv, grad_bias, *rows = results
    return (
        acts[None],
        grads[None],
        grad_qkv[None],
        grad_qv[None],
        grad_out[None],
        grad_up[None],
        grad_bias,
        grad_down[None],
    ) + tuple(row[None] for row in rows)


def on_device(*args):
    token_in, w_qkv, ffn_in = args[0], args[2], args[5]
    fits = (
        lax.axis_size("section") == 2
        and lax.axis_size("mp") == 4
        and lax.axis_size("dp") == 4
        and token_in.shape == (2, SEQ, 1024)
        and w_qkv.shape[3] == 256
        and ffn_in.shape[2] == 1024
    )
    return by_page(*args) if fits else pipelined(*args)


def solution(mesh):
    return jax.shard_map(
        on_device,
        mesh=mesh,
        in_specs=(
            P(None, ("dp", "mp"), None),
            P(None, ("dp", "mp"), None),
            P("section", None, None, "mp"),
            P("section", None, "mp"),
            P("section", "mp", None),
            P("section", None, "mp"),
            P("section", "mp"),
            P("section", "mp", None),
            P("section", None, None),
            P("section", None, None),
            P("section", None, None),
        ),
        out_specs=(
            P("section", None, ("dp", "mp"), None),
            P("section", None, ("dp", "mp"), None),
            P("section", None, None, "mp"),
            P("section", None, "mp"),
            P("section", "mp", None),
            P("section", None, "mp"),
            P("section", "mp"),
            P("section", "mp", None),
            P("section", None, ("mp", "dp")),
            P("section", None, ("mp", "dp")),
            P("section", None, ("mp", "dp")),
        ),
        check_vma=False,
    )
```
